32 devices in a mesh: dp: 8 (over z, y), fsdp: 4 (over x, core).
Axes of the slice: x: 2, y: 2, z: 4, core: 2. Of those that a mesh axis runs over, the one named last changes fastest.
Arguments:
- tokens: bfloat16 [64, 192, 1024], P(('dp', 'fsdp')), may hold values from -6 to 6
- encoder: bfloat16 [64, 384, 1024], P(('dp', 'fsdp')), may hold values from -6 to 6
- cotangent: bfloat16 [64, 192, 1024], P(('dp', 'fsdp')), may hold values from -6 to 6
- lengths: int32 [64], P(('dp', 'fsdp')), may hold values from 48 to 192
- enc_lengths: int32 [64], P(('dp', 'fsdp')), may hold values from 96 to 384
- bucket_ids: int32 [192], replicated, may hold values from 0 to 31
- self_qkv: bfloat16 [1024, 3072], P(('dp', 'fsdp')), may hold values from -0.1875 to 0.1875
- self_out: bfloat16 [1024, 1024], P(('dp', 'fsdp')), may hold values from -0.5 to 0.5
- cross_q: bfloat16 [1024, 1024], P(('dp', 'fsdp')), may hold values from -0.1875 to 0.1875
- cross_kv: bfloat16 [1024, 2048], P(('dp', 'fsdp')), may hold values from -0.1875 to 0.1875
- cross_out: bfloat16 [1024, 1024], P(('dp', 'fsdp')), may hold values from -0.5 to 0.5
- ff_in: bfloat16 [1024, 5632], P(('dp', 'fsdp')), may hold values from -0.1875 to 0.1875
- ff_out: bfloat16 [2816, 1024], P(('dp', 'fsdp')), may hold values from -0.109375 to 0.109375
- norm_gains: bfloat16 [3, 1024], P(None, ('dp', 'fsdp')), may hold values from 0.5 to 1.5
- rel_bias: bfloat16 [512], P(('dp', 'fsdp')), may hold values from -4 to 4
Outputs:
- output: float32 [64, 192, 1024], P(('dp', 'fsdp'))
- grad_tokens: float32 [64, 192, 1024], P(('dp', 'fsdp'))
- grad_encoder: float32 [64, 384, 1024], P(('dp', 'fsdp'))
- grad_self_qkv: float32 [1024, 3072], P(('dp', 'fsdp'))
- grad_self_out: float32 [1024, 1024], P(('dp', 'fsdp'))
- grad_cross_q: float32 [1024, 1024], P(('dp', 'fsdp'))
- grad_cross_kv: float32 [1024, 2048], P(('dp', 'fsdp'))
- grad_cross_out: float32 [1024, 1024], P(('dp', 'fsdp'))
- grad_ff_in: float32 [1024, 5632], P(('dp', 'fsdp'))
- grad_ff_out: float32 [2816, 1024], P(('dp', 'fsdp'))
- grad_norm_gains: float32 [3, 1024], P(None, ('dp', 'fsdp'))
- grad_rel_bias: float32 [512], P(('dp', 'fsdp'))
The draws below stay inside these ranges and needn't reach their ends.
All inputs are finite; a program needn't handle non-finite values.
Results may differ from the reference program's by a relative error of at most 0.022.
Values may be sent and summed in bfloat16 or wider, within the bound.
A program may use at most 200 MiB of HBM per device.

```python
import jax
import jax.numpy as jnp
from jax import lax

D = 1024
HEADS = 16
HEAD = 64
FF = 2816
BUCKETS = 32
SLOT = 192
ENC = 384
SEQS = 64


def plant(values, stream_key, least, largest):
    place = [jax.random.randint(jax.random.fold_in(stream_key, axis), (), 0, length) for axis, length in enumerate(values.shape)]
    widest = values.shape.index(max(values.shape))
    neighbour = place[:widest] + [(place[widest] + 1) % values.shape[widest]] + place[widest + 1:]
    return values.at[tuple(place)].set(least).at[tuple(neighbour)].set(largest)


def shard_levels(key, shape, pieces, low, largest):
    factor_of, own = 1.0, jax.random.fold_in(key, 6)
    for position, parts in pieces:
        steps = jnp.exp(jax.random.uniform(jax.random.fold_in(own, position), (parts,), jnp.float32, low / len(pieces), largest / len(pieces)))
        factor_of = factor_of * jnp.repeat(steps, shape[position] // parts).reshape([-1 if axis == position else 1 for axis in range(len(shape))])
    return factor_of


def scatter_about(key, dims, spread, bound, shards=(), kind=jnp.bfloat16):
    result = jax.random.normal(key, dims, jnp.float32) * spread
    if len(shards) > 0:
        result = shard_levels(key, dims, shards, -0.22, 0.18) * result
    return jnp.clip(result, min=-bound, max=bound).astype(kind)


def setup_inputs(seed: int = 0) -> dict:
    streams_of = jax.random.split(jax.random.key(seed), 16)
    tokens = scatter_about(streams_of[0], (SEQS, SLOT, D), 1.0, 6.0, ((0, 32),))
    encoder = scatter_about(streams_of[1], (SEQS, ENC, D), 1.0, 6.0, ((0, 32),))
    cotangent = scatter_about(streams_of[2], (SEQS, SLOT, D), 1.0, 6.0, ((0, 32),))
    lengths = plant(jax.random.randint(streams_of[3], (SEQS,), SLOT // 4, SLOT + 1), jax.random.fold_in(streams_of[3], 1), SLOT // 4, SLOT).astype(jnp.int32)
    enc_lengths = plant(jax.random.randint(streams_of[4], (SEQS,), ENC // 4, ENC + 1), jax.random.fold_in(streams_of[4], 1), ENC // 4, ENC).astype(jnp.int32)
    bucket_ids = plant(jax.random.randint(streams_of[5], (SLOT,), 0, BUCKETS), jax.random.fold_in(streams_of[5], 1), 0, BUCKETS - 1).astype(jnp.int32)
    self_qkv = scatter_about(streams_of[6], (D, 3 * D), D ** -0.5, 0.1875, ((0, 32),))
    self_out = scatter_about(streams_of[7], (D, D), (D // 8) ** -0.5, 0.5, ((0, 32),))
    cross_q = scatter_about(streams_of[8], (D, D), D ** -0.5, 0.1875, ((0, 32),))
    cross_kv = scatter_about(streams_of[9], (D, 2 * D), D ** -0.5, 0.1875, ((0, 32),))
    cross_out = scatter_about(streams_of[10], (D, D), (D // 8) ** -0.5, 0.5, ((0, 32),))
    ff_in = scatter_about(streams_of[11], (D, 2 * FF), D ** -0.5, 0.1875, ((0, 32),))
    ff_out = scatter_about(streams_of[12], (FF, D), FF ** -0.5, 0.109375, ((0, 32),))
    norm_gains = jnp.clip(1.0 + 0.1 * jax.random.normal(streams_of[13], (3, D), jnp.float32), 0.5, 1.5).astype(jnp.bfloat16)
    rel_bias = scatter_about(streams_of[14], (HEADS * BUCKETS,), 1.0, 4.0, ((0, 32),))
    return {"tokens": tokens, "encoder": encoder, "cotangent": cotangent, "lengths": lengths, "enc_lengths": enc_lengths, "bucket_ids": bucket_ids, "self_qkv": self_qkv, "self_out": self_out, "cross_q": cross_q, "cross_kv": cross_kv, "cross_out": cross_out, "ff_in": ff_in, "ff_out": ff_out, "norm_gains": norm_gains, "rel_bias": rel_bias}


@jax.custom_vjp
def low(v):
    return lax.optimization_barrier(v.astype(jnp.bfloat16)).astype(jnp.float32)

@jax.custom_vjp
def low_back(v):
    return v

def low_keep(v):
    return (low(v), None)

def low_pass(kept, grad):
    return (grad,)

def back_keep(v):
    return (v, None)

def back_low(kept, grad):
    return (low(grad),)
low.defvjp(low_keep, low_pass)
low_back.defvjp(back_keep, back_low)

def matmul(left, right):
    return jnp.dot(left, right, precision=lax.Precision.HIGHEST)

def norm_scale(stream, gain):
    return stream * lax.rsqrt(lax.optimization_barrier(jnp.mean(stream * stream, axis=-1, keepdims=True)) + 1e-06) * gain

def gelu_tanh(values):
    return 0.5 * values * (1.0 + jnp.tanh(0.7978845608028654 * (values + 0.044715 * values * values * values)))

def attention(queries, key_rows, value_rows, keep_mask, pos_bias):
    row_count = queries.shape[0]
    scores = jnp.einsum('ihc,jhc->hij', queries, key_rows, precision=lax.Precision.HIGHEST) * HEAD ** (-0.5)
    if pos_bias is not None:
        scores = scores + pos_bias
    scores = low_back(scores)
    masked = jnp.where(keep_mask[None], scores, -1e+30)
    row_max = lax.optimization_barrier(jnp.max(masked, axis=-1, keepdims=True))
    exponent = jnp.exp(masked - row_max)
    probs = exponent / lax.optimization_barrier(jnp.sum(exponent, axis=-1, keepdims=True))
    mixed = jnp.einsum('hij,jhc->ihc', low(probs), value_rows, precision=lax.Precision.HIGHEST)
    return low(low_back(mixed.reshape(row_count, HEADS * HEAD)))

def group_forward(weight_set, tok_group, enc_group, len_group, enc_len_group, onehot):
    self_qkv, self_out, cross_q, cross_kv, cross_out, ff_in, ff_out, norm_gains, rel_bias = weight_set
    pos_bias = matmul(rel_bias.reshape(HEADS, BUCKETS), onehot).reshape(HEADS, SLOT, SLOT)
    row_ids = jnp.arange(SLOT, dtype=jnp.int32)
    enc_ids = jnp.arange(ENC, dtype=jnp.int32)

    def sequence(stream, enc_rows, length, enc_length):
        self_mask = (row_ids[None, :] <= row_ids[:, None]) & (row_ids[None, :] < length)
        cross_mask = jnp.broadcast_to(enc_ids[None, :] < enc_length, (SLOT, ENC))
        normed = low(norm_scale(stream, norm_gains[0]))
        qkv_all = low(low_back(matmul(normed, self_qkv))).reshape(SLOT, 3, HEADS, HEAD)
        mixed = attention(qkv_all[:, 0], qkv_all[:, 1], qkv_all[:, 2], self_mask, pos_bias)
        second = stream + low_back(matmul(mixed, self_out))
        normed = low(norm_scale(second, norm_gains[1]))
        queries = low(low_back(matmul(normed, cross_q))).reshape(SLOT, HEADS, HEAD)
        enc_pairs = low(low_back(matmul(enc_rows, cross_kv))).reshape(ENC, 2, HEADS, HEAD)
        mixed = attention(queries, enc_pairs[:, 0], enc_pairs[:, 1], cross_mask, None)
        third = second + low_back(matmul(mixed, cross_out))
        normed = low(norm_scale(third, norm_gains[2]))
        gate_up = low_back(matmul(normed, ff_in))
        hidden = low(gelu_tanh(gate_up[:, :FF]) * gate_up[:, FF:])
        return third + low_back(matmul(hidden, ff_out))
    return jax.vmap(sequence)(tok_group, enc_group, len_group, enc_len_group)

def reference(tokens, encoder, cotangent, lengths, enc_lengths, bucket_ids, self_qkv, self_out, cross_q, cross_kv, cross_out, ff_in, ff_out, norm_gains, rel_bias):
    weight_set = tuple((matrix.astype(jnp.float32) for matrix in (self_qkv, self_out, cross_q, cross_kv, cross_out, ff_in, ff_out, norm_gains, rel_bias)))
    row_ids = jnp.arange(SLOT, dtype=jnp.int32)
    distance = jnp.maximum(row_ids[:, None] - row_ids[None, :], 0)
    bucket_map = bucket_ids[distance].reshape(-1)
    onehot = (jnp.arange(BUCKETS, dtype=jnp.int32)[:, None] == bucket_map[None, :]).astype(jnp.float32)
    group_size = 16 if SEQS % 16 == 0 else 1
    group_count = SEQS // group_size

    def grouped(array):
        return array.reshape((group_count, group_size) + array.shape[1:])
    scanned = (grouped(tokens.astype(jnp.float32)), grouped(encoder.astype(jnp.float32)), grouped(cotangent.astype(jnp.float32)), grouped(lengths), grouped(enc_lengths))
    initial = tuple((jnp.zeros_like(matrix) for matrix in weight_set))

    def micro_step(totals, element):
        tok_group, enc_group, cot_group, len_group, enc_len_group = element

        def run(weights_in, tok_in, enc_in):
            return group_forward(weights_in, tok_in, enc_in, len_group, enc_len_group, onehot)
        outcome, pullback = jax.vjp(run, weight_set, tok_group, enc_group)
        valid = (row_ids[None, :] < len_group[:, None]).astype(jnp.float32)[:, :, None]
        grad_weights, grad_tok, grad_enc = pullback(cot_group * valid)
        totals = tuple((accum + extra for accum, extra in zip(totals, grad_weights)))
        return (totals, (outcome, grad_tok, grad_enc))
    totals, (outcomes, grad_toks, grad_encs) = lax.scan(micro_step, initial, scanned)
    return (outcomes.reshape(SEQS, SLOT, D), grad_toks.reshape(SEQS, SLOT, D), grad_encs.reshape(SEQS, ENC, D), totals[0], totals[1], totals[2], totals[3], totals[4], totals[5], totals[6], totals[7], totals[8])
```

```python
import functools

import jax
import jax.numpy as jnp
from jax import lax
from jax.experimental import pallas as pl
from jax.experimental.pallas import tpu as pltpu
from jax.sharding import PartitionSpec as P

HEADS = 16
HEAD = 64
BUCKETS = 32
PACK = 32
LANES = 128
PIECE = 32 * 1024

MESH = pl.DeviceIdType.MESH


class Place:
    def __init__(self, dp, fsdp):
        self.sizes = (dp // 2, 2, fsdp // 2, 2)

    def locate(self):
        row, column = lax.axis_index("dp"), lax.axis_index("fsdp")
        sizes = self.sizes
        self.here = (row // sizes[1], row % sizes[1], column // sizes[3], column % sizes[3])

    def moved(self, axis, step):
        coords = list(self.here)
        coords[axis] = (coords[axis] + step) % self.sizes[axis]
        return coords

    def device(self, coords):
        return (coords[0] * self.sizes[1] + coords[1], coords[2] * self.sizes[3] + coords[3])

    def peers(self):
        return [(axis, step) for axis in range(4) for step in range(1, self.sizes[axis])]

    def greet(self):
        barrier = pltpu.get_barrier_semaphore()
        for axis, step in self.peers():
            pl.semaphore_signal(
                barrier, inc=1, device_id=self.device(self.moved(axis, step)), device_id_type=MESH
            )
        pl.semaphore_wait(barrier, len(self.peers()))


class Unit:
    def __init__(self, owner, block, start, count):
        self.owner, self.start, self.count = owner, start, count
        self.grouped = len(block) == 3
        self.shape = (count,) + block[1:] if self.grouped else (block[0], count)
        width = self.shape[-1]
        self.halves = 2 if width % 256 == 0 else 1
        self.half = width // self.halves

    def part(self, half=None):
        low, size = (0, self.shape[-1]) if half is None else (half * self.half, self.half)
        if self.grouped:
            return (pl.ds(self.start, self.count), slice(None), pl.ds(low, size))
        return (slice(None), pl.ds(self.start + low, size))

    def local(self, half):
        return (slice(None),) * (len(self.shape) - 1) + (pl.ds(half * self.half, self.half),)

    def half_shape(self):
        return self.shape[:-1] + (self.half,)


def make_units(blocks, piece):
    units = []
    for owner, block in enumerate(blocks):
        total, most = (block[0], piece // 8 // block[2] or 1) if len(block) == 3 else (block[1], piece // block[0])
        start = 0
        while start < total:
            count = min(most, total - start)
            units.append(Unit(owner, block, start, count))
            start += count
    return units


def gather_kernel(place, units, count, *refs):
    shards, wholes = refs[:count], refs[count : 2 * count]
    send_sems, recv_sems, local_sems = refs[2 * count :]
    place.locate()
    place.greet()
    zi, yi, xi, ci = place.here
    sizes = place.sizes
    started = []
    serial = [0]

    def send(source, target, axis, step):
        spot = serial[0]
        serial[0] += 1
        copy = pltpu.make_async_remote_copy(
            src_ref=source,
            dst_ref=target,
            send_sem=send_sems.at[spot],
            recv_sem=recv_sems.at[spot],
            device_id=place.device(place.moved(axis, step)),
            device_id_type=MESH,
        )
        copy.start()
        started.append(copy)
        return copy

    pending = {}

    def along(axis, source, target):
        return [send(source, target, axis, step) for step in range(1, sizes[axis])]

    def first(u):
        unit = units[u]
        shard = shards[unit.owner].at[unit.part()]
        own = wholes[unit.owner].at[(zi, yi, xi, ci) + unit.part()]
        copy = pltpu.make_async_copy(shard, own, local_sems.at[u])
        copy.start()
        pending[u] = (copy, along(0, shard, own))

    def settle(u):
        for copy in pending[u]:
            copy.wait_recv()

    def second(u):
        copy, others = pending[u]
        copy.wait()
        for other in others:
            other.wait_recv()
        unit = units[u]
        whole = wholes[unit.owner]
        pending[u] = []
        for half in range(unit.halves):
            ref = whole.at[(slice(None), yi, xi, ci) + unit.part(half)]
            pending[u] += along(2 - half, ref, ref)

    def third(u):
        settle(u)
        unit = units[u]
        whole = wholes[unit.owner]
        pending[u] = []
        for half in range(unit.halves):
            index = (slice(None), yi, slice(None), ci) if half == 0 else (slice(None), slice(None), xi, ci)
            ref = whole.at[index + unit.part(half)]
            pending[u] += along(1 + half, ref, ref)

    def fourth(u):
        settle(u)
        unit = units[u]
        ref = wholes[unit.owner].at[(slice(None), slice(None), slice(None), ci) + unit.part()]
        pending[u] = along(3, ref, ref)

    stages = (first, second, third, fourth, settle)
    for tick in range(len(units) + len(stages) - 1):
        for lag, stage in enumerate(stages):
            if 0 <= tick - lag < len(units):
                stage(tick - lag)
    for copy in started:
        copy.wait_send()


def scatter_kernel(place, units, count, slot_of, *refs):
    wholes, owned = refs[:count], refs[count : 2 * count]
    refs = refs[2 * count :]
    scratch = [refs[6 * u : 6 * u + 6] for u in range(len(units))]
    slots = refs[6 * len(units) : -3]
    send_sems, recv_sems, local_sems = refs[-3:]
    place.locate()
    place.greet()
    zi, yi, xi, ci = place.here
    sizes = place.sizes
    full = slice(None)
    started, serial, pending = [], [0], {}

    def send(source, target, axis, step):
        spot = serial[0]
        serial[0] += 1
        copy = pltpu.make_async_remote_copy(
            src_ref=source,
            dst_ref=target,
            send_sem=send_sems.at[spot],
            recv_sem=recv_sems.at[spot],
            device_id=place.device(place.moved(axis, step)),
            device_id_type=MESH,
        )
        copy.start()
        started.append(copy)
        return copy

    def settle(u):
        for copy in pending[u]:
            copy.wait_recv()
        pending[u] = []

    def add(total, target, terms, kind=jnp.bfloat16):
        def body(spot, carry):
            value = sum(term(spot).astype(jnp.float32) for term in terms)
            ref, index = target(spot)
            ref[index] = value.astype(kind)
            return carry

        lax.fori_loop(0, total, body, 0)

    def slot(u):
        kind, place_in = slot_of[u]
        return slots[kind].at[place_in]

    def first(u):
        unit = units[u]
        whole = wholes[unit.owner]
        arrived = scratch[u][0]
        mine = pltpu.make_async_copy(
            whole.at[(full, full, full, ci) + unit.part()], slot(u), local_sems.at[u]
        )
        mine.start()
        theirs = send(
            whole.at[(full, full, full, (ci + 1) % 2) + unit.part()], arrived, 3, 1
        )
        pending[u] = (mine, theirs)

    def second(u):
        unit = units[u]
        arrived, one_a, one_b = scratch[u][:3]
        own = slot(u)
        mine, theirs = pending[u]
        mine.wait()
        theirs.wait_recv()
        flat = lambda b: (b // (sizes[1] * sizes[2]), (b // sizes[2]) % sizes[1], b % sizes[2])
        add(
            sizes[0] * sizes[1] * sizes[2],
            lambda b: (arrived, flat(b)),
            [lambda b: arrived[flat(b)], lambda b: own[flat(b)]],
        )
        pending[u] = []
        for half in range(unit.halves):
            axis, target = (1, one_a) if half == 0 else (2, one_b)
            for step in range(1, sizes[axis]):
                there = place.moved(axis, step)[axis]
                index = (full, there, full) if half == 0 else (full, full, there)
                pending[u].append(
                    send(arrived.at[index + unit.local(half)], target.at[step - 1], axis, step)
                )

    def third(u):
        settle(u)
        unit = units[u]
        arrived, one_a, one_b, two_a, two_b = scratch[u][:5]
        for half in range(unit.halves):
            axis, other = (1, 2) if half == 0 else (2, 1)
            one, two = (one_a, two_a) if half == 0 else (one_b, two_b)
            wide = sizes[other]

            def mine(b, half=half, wide=wide):
                middle = (yi, b % wide) if half == 0 else (b % wide, xi)
                return arrived[(b // wide,) + middle + unit.local(half)]

            add(
                sizes[0] * wide,
                lambda b: (one, (0, b // wide, b % wide)),
                [mine]
                + [
                    lambda b, step=step: one[step, b // wide, b % wide]
                    for step in range(sizes[axis] - 1)
                ],
            )
            for step in range(1, wide):
                there = place.moved(other, step)[other]
                pending[u].append(send(one.at[0, :, there], two.at[step - 1], other, step))

    def fourth(u):
        settle(u)
        unit = units[u]
        one_a, one_b, two_a, two_b, last = scratch[u][1:]
        for half in range(unit.halves):
            axis, here = (2, xi) if half == 0 else (1, yi)
            one, two = (one_a, two_a) if half == 0 else (one_b, two_b)
            add(
                sizes[0],
                lambda b: (two, (0, b)),
                [lambda b: one[0, b, here]]
                + [lambda b, step=step: two[step, b] for step in range(sizes[axis] - 1)],
            )
            for step in range(1, sizes[0]):
                there = place.moved(0, step)[0]
                pending[u].append(
                    send(two.at[0, there], last.at[(step - 1,) + unit.local(half)], 0, step)
                )

    def fifth(u):
        settle(u)
        unit = units[u]
        two_a, two_b, last = scratch[u][3:]
        for half in range(unit.halves):
            two = two_a if half == 0 else two_b
            value = two[0, zi].astype(jnp.float32)
            for step in range(sizes[0] - 1):
                value = value + last[(step,) + unit.local(half)].astype(jnp.float32)
            owned[unit.owner][unit.part(half)] = value

    stages = (first, second, third, fourth, fifth)
    for tick in range(len(units) + len(stages) - 1):
        for lag, stage in enumerate(stages):
            if 0 <= tick - lag < len(units):
                stage(tick - lag)
    for copy in started:
        copy.wait_send()


def copies_of(units, sizes, per_z):
    total = 0
    for unit in units:
        total += (sizes[0] - 1) * (unit.halves if per_z else 1) + 1
        total += unit.halves * (sizes[1] - 1 + sizes[2] - 1)
    return total


def gather_all(place, blocks, shards):
    units = make_units(blocks, PIECE)
    total = copies_of(units, place.sizes, False)
    anywhere = pl.BlockSpec(memory_space=pl.ANY)
    return pl.pallas_call(
        functools.partial(gather_kernel, place, units, len(blocks)),
        out_shape=[jax.ShapeDtypeStruct(place.sizes + block, jnp.bfloat16) for block in blocks],
        in_specs=[anywhere] * len(blocks),
        out_specs=[anywhere] * len(blocks),
        scratch_shapes=[
            pltpu.SemaphoreType.DMA((total,)),
            pltpu.SemaphoreType.DMA((total,)),
            pltpu.SemaphoreType.DMA((len(units),)),
        ],
        compiler_params=pltpu.CompilerParams(collective_id=0, has_side_effects=True),
        name="gather_all",
    )(*shards)


def scatter_all(place, blocks, wholes):
    units = make_units(blocks, PIECE)
    sizes = place.sizes
    total = copies_of(units, sizes, True)
    scratch, kinds, slot_of = [], [], []
    seen = {}
    for unit in units:
        half = unit.half_shape()
        for shape in (
            sizes[:3] + unit.shape,
            (sizes[1] - 1, sizes[0], sizes[2]) + half,
            (sizes[2] - 1, sizes[0], sizes[1]) + half,
            (sizes[2] - 1, sizes[0]) + half,
            (sizes[1] - 1, sizes[0]) + half,
            (sizes[0] - 1,) + unit.shape,
        ):
            scratch.append(pltpu.VMEM(shape, jnp.bfloat16))
        if unit.shape not in seen:
            seen[unit.shape] = [len(kinds), 0]
            kinds.append(pltpu.VMEM((3,) + sizes[:3] + unit.shape, jnp.bfloat16))
        kind = seen[unit.shape]
        slot_of.append((kind[0], kind[1] % 3))
        kind[1] += 1
    anywhere = pl.BlockSpec(memory_space=pl.ANY)
    return pl.pallas_call(
        functools.partial(scatter_kernel, place, units, len(blocks), slot_of),
        out_shape=[jax.ShapeDtypeStruct(block, jnp.float32) for block in blocks],
        in_specs=[anywhere] * len(blocks),
        out_specs=[pl.BlockSpec(memory_space=pltpu.VMEM)] * len(blocks),
        scratch_shapes=scratch
        + kinds
        + [
            pltpu.SemaphoreType.DMA((total,)),
            pltpu.SemaphoreType.DMA((total,)),
            pltpu.SemaphoreType.DMA((len(units),)),
        ],
        compiler_params=pltpu.CompilerParams(
            collective_id=1, has_side_effects=True, vmem_limit_bytes=60 * 2**20
        ),
        name="scatter_all",
    )(*wholes)


def norm_scale(stream, gain):
    return stream * lax.rsqrt(jnp.mean(stream * stream, axis=-1, keepdims=True) + 1e-06) * gain


def gelu_tanh(values):
    return (
        0.5
        * values
        * (1.0 + jnp.tanh(0.7978845608028654 * (values + 0.044715 * values * values * values)))
    )


def gated(gate_up):
    half_width = gate_up.shape[1] // 2
    return gelu_tanh(gate_up[:, :half_width]) * gate_up[:, half_width:]


def product(spec, left, right):
    return jnp.einsum(spec, left, right, preferred_element_type=jnp.float32)


def attend(queries, key_rows, value_rows, pos_bias, keep_mask):
    scores = product("bihc,bjhc->bhij", queries, key_rows) * HEAD ** (-0.5)
    if pos_bias is not None:
        scores = scores + pos_bias
    masked = jnp.where(keep_mask[:, None], scores, -1e30)
    row_max = jnp.max(masked, axis=-1, keepdims=True)
    powers = jnp.exp(masked - row_max)
    probs = powers / jnp.sum(powers, axis=-1, keepdims=True)
    low_probs = probs.astype(jnp.bfloat16)
    mixed = product("bhij,bjhc->bihc", low_probs, value_rows)
    return mixed.astype(jnp.bfloat16), low_probs


def attend_back(queries, key_rows, value_rows, low_probs, grad_mixed):
    probs = low_probs.astype(jnp.float32)
    grad_values = product("bhij,bihc->bjhc", low_probs, grad_mixed)
    grad_probs = product("bihc,bjhc->bhij", grad_mixed, value_rows)
    grad_scores = (
        probs * (grad_probs - jnp.sum(probs * grad_probs, axis=-1, keepdims=True))
    ).astype(jnp.bfloat16)
    grad_queries = product("bhij,bjhc->bihc", grad_scores, key_rows) * HEAD ** (-0.5)
    grad_keys = product("bhij,bihc->bjhc", grad_scores, queries) * HEAD ** (-0.5)
    return grad_queries, grad_keys, grad_values, grad_scores


def toeplitz(table, size):
    lead = table.shape[:-1]
    row = jnp.concatenate(
        [table[..., ::-1], jnp.broadcast_to(table[..., :1], lead + (size,))], axis=-1
    )
    tiled = jnp.broadcast_to(row[..., None, :], lead + (size, 2 * size)).reshape(lead + (-1,))
    tiled = jnp.concatenate([tiled[..., size - 1 :], row[..., :1]], axis=-1)
    tiled = tiled[..., : size * (2 * size - 1)]
    return tiled.reshape(lead + (size, 2 * size - 1))[..., :size]


def layer(weights, gains, rel_bias, tokens, encoder, cotangent, lengths, enc_lengths, bucket_ids):
    self_qkv, self_out, cross_q, cross_kv, cross_out, ff_in, ff_out = weights
    count, slots, width = tokens.shape
    enc_count = encoder.shape[1]
    bucket_map = toeplitz(bucket_ids, slots).reshape(-1)
    onehot = (lax.iota(jnp.int32, BUCKETS)[:, None] == bucket_map[None, :]).astype(jnp.bfloat16)
    pos_bias = jnp.dot(rel_bias, onehot, preferred_element_type=jnp.float32).reshape(
        HEADS, slots, slots
    )
    row_ids = lax.iota(jnp.int32, slots)
    self_mask = (row_ids[None, None, :] <= row_ids[None, :, None]) & (
        row_ids[None, None, :] < lengths[:, None, None]
    )
    cross_mask = lax.iota(jnp.int32, enc_count)[None, None, :] < enc_lengths[:, None, None]
    enc_rows = encoder.reshape(count * enc_count, width)
    dot = functools.partial(jnp.dot, preferred_element_type=jnp.float32)
    low = lambda value: value.astype(jnp.bfloat16)
    stream = tokens.reshape(count * slots, width).astype(jnp.float32)
    normed_self, back_self = jax.vjp(norm_scale, stream, gains[0])
    normed_self = low(normed_self)
    qkv = low(dot(normed_self, self_qkv)).reshape(count, slots, 3, HEADS, HEAD)
    mixed_self, probs_self = attend(qkv[:, :, 0], qkv[:, :, 1], qkv[:, :, 2], pos_bias, self_mask)
    mixed_self = mixed_self.reshape(count * slots, width)
    second = stream + dot(mixed_self, self_out)
    normed_cross, back_cross = jax.vjp(norm_scale, second, gains[1])
    normed_cross = low(normed_cross)
    queries = low(dot(normed_cross, cross_q)).reshape(count, slots, HEADS, HEAD)
    pairs = low(dot(enc_rows, cross_kv)).reshape(count, enc_count, 2, HEADS, HEAD)
    mixed_cross, probs_cross = attend(queries, pairs[:, :, 0], pairs[:, :, 1], None, cross_mask)
    mixed_cross = mixed_cross.reshape(count * slots, width)
    third = second + dot(mixed_cross, cross_out)
    normed_ffn, back_ffn = jax.vjp(norm_scale, third, gains[2])
    normed_ffn = low(normed_ffn)
    gate_up = dot(normed_ffn, ff_in)
    activated, back_gate = jax.vjp(gated, gate_up)
    hidden = low(activated)
    outcome = third + dot(hidden, ff_out)

    valid = (row_ids[None, :] < lengths[:, None]).astype(jnp.float32)[:, :, None]
    grad_out = (cotangent.astype(jnp.float32) * valid).reshape(count * slots, width)
    branch = low(grad_out)
    grad_ff_out = product("lf,ld->fd", hidden, branch)
    grad_hidden = product("ld,fd->lf", branch, ff_out)
    (grad_gate_up,) = back_gate(grad_hidden)
    grad_gate_up = low(grad_gate_up)
    grad_ff_in = product("ld,lf->df", normed_ffn, grad_gate_up)
    grad_stream, gain_ffn = back_ffn(product("lf,df->ld", grad_gate_up, ff_in))
    grad_third = grad_out + grad_stream
    branch = low(grad_third)
    grad_cross_out = product("le,ld->ed", mixed_cross, branch)
    grad_mixed = low(product("ld,ed->le", branch, cross_out)).reshape(count, slots, HEADS, HEAD)
    grad_queries, grad_keys, grad_values, unused = attend_back(
        queries, pairs[:, :, 0], pairs[:, :, 1], probs_cross, grad_mixed
    )
    grad_query_rows = low(grad_queries.reshape(count * slots, width))
    grad_pair_rows = low(
        jnp.concatenate(
            [
                grad_keys.reshape(count * enc_count, width),
                grad_values.reshape(count * enc_count, width),
            ],
            axis=1,
        )
    )
    grad_cross_q = product("ld,le->de", normed_cross, grad_query_rows)
    grad_cross_kv = product("ed,ef->df", enc_rows, grad_pair_rows)
    grad_enc = product("ef,df->ed", grad_pair_rows, cross_kv)
    grad_stream, gain_cross = back_cross(product("le,de->ld", grad_query_rows, cross_q))
    grad_second = grad_third + grad_stream
    branch = low(grad_second)
    grad_self_out = product("le,ld->ed", mixed_self, branch)
    grad_mixed = low(product("ld,ed->le", branch, self_out)).reshape(count, slots, HEADS, HEAD)
    grad_queries, grad_keys, grad_values, grad_scores = attend_back(
        qkv[:, :, 0], qkv[:, :, 1], qkv[:, :, 2], probs_self, grad_mixed
    )
    score_sums = jnp.sum(grad_scores.astype(jnp.float32), axis=0).reshape(HEADS, slots * slots)
    grad_rel_bias = product("hn,bn->hb", low(score_sums), onehot)
    grad_qkv = low(
        jnp.concatenate(
            [part.reshape(count * slots, width) for part in (grad_queries, grad_keys, grad_values)],
            axis=1,
        )
    )
    grad_self_qkv = product("ld,lf->df", normed_self, grad_qkv)
    grad_stream, gain_self = back_self(product("lf,df->ld", grad_qkv, self_qkv))
    grad_tok = grad_second + grad_stream
    grad_gains = jnp.stack([gain_self, gain_cross, gain_ffn], axis=0)
    grads = (
        grad_self_qkv,
        grad_self_out,
        grad_cross_q,
        grad_cross_kv,
        grad_cross_out,
        grad_ff_in,
        grad_ff_out,
    )
    return (
        outcome.reshape(tokens.shape),
        grad_tok.reshape(tokens.shape),
        grad_enc.reshape(encoder.shape),
        grads,
        grad_gains,
        grad_rel_bias,
    )


AXES = ("dp", "fsdp")


def by_collectives(data, shards):
    whole = lambda shard, axis=0: lax.all_gather(shard, AXES, axis=axis, tiled=True)
    weights = tuple(whole(shard) for shard in shards[:7])
    gains = whole(shards[7], 1).astype(jnp.float32)
    rel_bias = whole(shards[8]).reshape(HEADS, BUCKETS)
    outcome, grad_tok, grad_enc, grads, grad_gains, grad_rel_bias = layer(
        weights, gains, rel_bias, *data
    )
    settle = lambda total, axis=0: lax.psum_scatter(
        total, AXES, scatter_dimension=axis, tiled=True
    )
    return (
        (outcome, grad_tok, grad_enc)
        + tuple(settle(grad) for grad in grads)
        + (settle(grad_gains, 1), settle(grad_rel_bias.reshape(-1)))
    )


def by_kernels(place, data, shards):
    norm_gains, rel_bias = shards[7:]
    count = place.sizes[0] * place.sizes[1] * place.sizes[2] * place.sizes[3]
    me = lax.axis_index(AXES)
    norms, per = norm_gains.shape
    group = LANES // per
    rel_per = rel_bias.shape[0]
    pack = jnp.zeros((PACK, LANES), jnp.bfloat16)
    pack = lax.dynamic_update_slice(pack, norm_gains, (0, (me % group) * per))
    rel_row, rel_column = HEADS + me * rel_per // BUCKETS, (me * rel_per) % BUCKETS
    pack = lax.dynamic_update_slice(pack, rel_bias.reshape(1, rel_per), (rel_row, rel_column))
    ff_rows, width = shards[6].shape
    ff_shape = (ff_rows // 8, 8, width)
    sent = (pack,) + shards[:6] + (shards[6].reshape(ff_shape),)
    blocks = [piece.shape for piece in sent]
    packs, *wholes = gather_all(place, blocks, sent)
    weights = tuple(
        whole.reshape(count * shard.shape[0], shard.shape[1])
        for whole, shard in zip(wholes, shards[:7])
    )
    packs = packs.reshape(count // group, group, PACK, LANES).astype(jnp.float32).sum(axis=1)
    gains = packs[:, :norms].transpose(1, 0, 2).reshape(norms, -1)
    rel_table = packs.sum(axis=0)[HEADS:, :BUCKETS].astype(jnp.bfloat16)
    outcome, grad_tok, grad_enc, grads, grad_gains, grad_rel_bias = layer(
        weights, gains, rel_table, *data
    )
    top = grad_gains.reshape(norms, count // group, LANES).transpose(1, 0, 2)
    top = jnp.pad(top, ((0, 0), (0, HEADS - norms), (0, 0)))
    low_part = jnp.pad(grad_rel_bias, ((0, 0), (0, LANES - BUCKETS)))
    low_part = jnp.broadcast_to(low_part, (count // group, HEADS, LANES))
    tiles = jnp.concatenate([top, low_part], axis=1)[:, None]
    tiles = jnp.broadcast_to(tiles, (count // group, group, PACK, LANES))
    sums = scatter_all(
        place,
        blocks,
        [
            piece.astype(jnp.bfloat16).reshape(place.sizes + block)
            for piece, block in zip((tiles,) + grads, blocks)
        ],
    )
    packed, *owned = sums
    own_gains = lax.dynamic_slice(packed, (0, (me % group) * per), (norms, per))
    own_rel = lax.dynamic_slice(packed, (rel_row, rel_column), (1, rel_per)).reshape(-1)
    owned[6] = owned[6].reshape(ff_rows, width)
    return (outcome, grad_tok, grad_enc) + tuple(owned) + (own_gains, own_rel)


def on_device(place, *args):
    data, shards = args[:6], args[6:]
    per = shards[7].shape[1]
    regular = all(shard.shape[0] % 16 == 0 for shard in shards[:6])
    if regular and shards[6].shape[0] % 8 == 0 and LANES % per == 0:
        return by_kernels(place, data, shards)
    return by_collectives(data, shards)


def solution(mesh):
    rows = P(AXES, None, None)
    flat = P(AXES)
    matrix = P(AXES, None)
    split = P(None, AXES)
    place = Place(mesh.shape["dp"], mesh.shape["fsdp"])
    return jax.shard_map(
        functools.partial(on_device, place),
        mesh=mesh,
        in_specs=(rows, rows, rows, flat, flat, P()) + (matrix,) * 7 + (split, flat),
        out_specs=(rows, rows, rows) + (matrix,) * 7 + (split, flat),
        check_vma=False,
    )
```

```python
import functools

import jax
import jax.numpy as jnp
from jax import lax
from jax.experimental import pallas as pl
from jax.experimental.pallas import tpu as pltpu
from jax.sharding import PartitionSpec as P

HEADS = 16
HEAD = 64
BUCKETS = 32
PACK = 32
LANES = 128
PIECE = 32 * 1024

MESH = pl.DeviceIdType.MESH


class Place:
    def __init__(self, dp, fsdp):
        self.sizes = (dp // 2, 2, fsdp // 2, 2)

    def locate(self):
        row, column = lax.axis_index("dp"), lax.axis_index("fsdp")
        sizes = self.sizes
        self.here = (row // sizes[1], row % sizes[1], column // sizes[3], column % sizes[3])

    def moved(self, axis, step):
        coords = list(self.here)
        coords[axis] = (coords[axis] + step) % self.sizes[axis]
        return coords

    def device(self, coords):
        return (coords[0] * self.sizes[1] + coords[1], coords[2] * self.sizes[3] + coords[3])

    def peers(self):
        return [(axis, step) for axis in range(4) for step in range(1, self.sizes[axis])]

    def greet(self):
        barrier = pltpu.get_barrier_semaphore()
        for axis, step in self.peers():
            pl.semaphore_signal(
                barrier, inc=1, device_id=self.device(self.moved(axis, step)), device_id_type=MESH
            )
        pl.semaphore_wait(barrier, len(self.peers()))


class Unit:
    def __init__(self, owner, block, start, count):
        self.owner, self.start, self.count = owner, start, count
        self.grouped = len(block) == 3
        self.shape = (count,) + block[1:] if self.grouped else (block[0], count)
        width = self.shape[-1]
        self.halves = 2 if width % 256 == 0 else 1
        self.half = width // self.halves

    def part(self, half=None):
        low, size = (0, self.shape[-1]) if half is None else (half * self.half, self.half)
        if self.grouped:
            return (pl.ds(self.start, self.count), slice(None), pl.ds(low, size))
        return (slice(None), pl.ds(self.start + low, size))

    def local(self, half):
        return (slice(None),) * (len(self.shape) - 1) + (pl.ds(half * self.half, self.half),)

    def half_shape(self):
        return self.shape[:-1] + (self.half,)


def make_units(blocks, piece, order):
    units = []
    for owner in order:
        block = blocks[owner]
        total, most = (block[0], piece // 8 // block[2] or 1) if len(block) == 3 else (block[1], piece // block[0])
        start = 0
        while start < total:
            count = min(most, total - start)
            units.append(Unit(owner, block, start, count))
            start += count
    return units


class Wires:
    def __init__(self, place, send_sems, recv_sems):
        self.place, self.send_sems, self.recv_sems = place, send_sems, recv_sems
        self.started = []

    def send(self, source, target, axis, step):
        spot = len(self.started)
        copy = pltpu.make_async_remote_copy(
            src_ref=source,
            dst_ref=target,
            send_sem=self.send_sems.at[spot],
            recv_sem=self.recv_sems.at[spot],
            device_id=self.place.device(self.place.moved(axis, step)),
            device_id_type=MESH,
        )
        copy.start()
        self.started.append(copy)
        return copy

    def along(self, axis, source, target):
        return [
            self.send(source, target, axis, step) for step in range(1, self.place.sizes[axis])
        ]

    def finish(self):
        for copy in self.started:
            copy.wait_send()


def gather_stages(place, units, shards, wholes, wires, local_sems):
    zi, yi, xi, ci = place.here
    full = slice(None)
    pending = {}

    def first(u):
        unit = units[u]
        shard = shards[unit.owner].at[unit.part()]
        own = wholes[unit.owner].at[(zi, yi, xi, ci) + unit.part()]
        copy = pltpu.make_async_copy(shard, own, local_sems.at[u])
        copy.start()
        pending[u] = (copy, wires.along(0, shard, own))

    def settle(u):
        for copy in pending[u]:
            copy.wait_recv()

    def second(u):
        copy, others = pending[u]
        copy.wait()
        for other in others:
            other.wait_recv()
        unit = units[u]
        whole = wholes[unit.owner]
        pending[u] = []
        for half in range(unit.halves):
            ref = whole.at[(full, yi, xi, ci) + unit.part(half)]
            pending[u] += wires.along(2 - half, ref, ref)

    def third(u):
        settle(u)
        unit = units[u]
        whole = wholes[unit.owner]
        pending[u] = []
        for half in range(unit.halves):
            index = (full, yi, full, ci) if half == 0 else (full, full, xi, ci)
            ref = whole.at[index + unit.part(half)]
            pending[u] += wires.along(1 + half, ref, ref)

    def fourth(u):
        settle(u)
        unit = units[u]
        ref = wholes[unit.owner].at[(full, full, full, ci) + unit.part()]
        pending[u] = wires.along(3, ref, ref)

    return (first, second, third, fourth, settle)


def mul(left, right, left_dim=1, right_dim=0):
    return lax.dot_general(
        left, right, (((left_dim,), (right_dim,)), ((), ())), preferred_element_type=jnp.float32
    )


def low(value):
    return value.astype(jnp.bfloat16)


def wide(value):
    return value.astype(jnp.float32)


def rms_rows(source, target, gain, rows=64):
    def body(step, carry):
        at = pl.ds(pl.multiple_of(step * rows, rows), rows)
        value = wide(source[at, :])
        scale = lax.rsqrt(jnp.mean(value * value, axis=-1, keepdims=True) + 1e-06)
        target[at, :] = low(value * scale * gain)
        return carry

    lax.fori_loop(0, source.shape[0] // rows, body, 0)


def tiles(total, size, body):
    def step(spot, carry):
        body(pl.ds(pl.multiple_of(spot * size, size), size))
        return carry

    lax.fori_loop(0, total // size, step, 0)


def flat_rows(value):
    return value.reshape(-1, value.shape[-1])


def attend_pair(queries, key_rows, value_rows, bias, mask):
    rows = queries.shape[0]
    left = lax.broadcasted_iota(jnp.int32, (1, LANES), 1) < HEAD
    zero = jnp.zeros_like(queries)
    scaled = queries * jnp.bfloat16(HEAD ** (-0.5))
    stacked = jnp.concatenate(
        [jnp.where(left, scaled, zero), jnp.where(left, zero, scaled)], axis=0
    )
    scores = mul(stacked, key_rows, 1, 1)
    if bias is not None:
        scores = scores + bias
    scores = jnp.where(mask, scores, -1e30)
    powers = jnp.exp(scores - jnp.max(scores, axis=-1, keepdims=True))
    probs = low(powers / jnp.sum(powers, axis=-1, keepdims=True))
    none = jnp.zeros_like(value_rows)
    mixed = mul(probs[:rows], jnp.where(left, value_rows, none)) + mul(
        probs[rows:], jnp.where(left, none, value_rows)
    )
    return probs, low(mixed)


class Driver:
    def __init__(self, units, stages, lead):
        self.units, self.stages, self.lead = units, stages, lead
        self.tick, self.debt = 0, 0.0

    def done(self):
        return self.tick >= len(self.units) + len(self.stages) - 1

    def settled(self):
        return self.tick - len(self.stages)

    def advance(self):
        for lag, stage in enumerate(self.stages):
            if 0 <= self.tick - lag < len(self.units):
                stage(self.tick - lag)
        self.tick += 1

    def until(self, unit):
        while self.settled() < unit:
            self.advance()

    def spent(self, cost):
        self.debt += cost
        while self.debt >= self.lead:
            self.debt -= self.lead
            if not self.done():
                self.advance()


KEPT = (
    "normed_self", "qkv", "probs_self", "mixed_self", "second", "normed_cross", "queries", "pairs",
    "probs_cross", "mixed_cross", "third", "normed_ffn", "branch", "hidden", "grad_gate_up",
    "grad_normed", "gains",
)
CHUNK = 256
ORDER = (0, 1, 2, 3, 4, 5, 7, 6)


def forward_kernel(place, units, count, seqs, *refs):
    shards, refs = refs[:count], refs[count:]
    tokens, encoder, cotangent, lengths, enc_lengths, spread_ids = refs[:6]
    wholes, refs = refs[6 : 6 + count], refs[6 + count :]
    outcome, refs = refs[0], refs[1:]
    stored, refs = refs[: len(KEPT)], refs[len(KEPT) :]
    vmem, refs = dict(zip(KEPT, refs)), refs[len(KEPT) :]
    bias_rows, slots, raw_out, ff_out, pack = refs[:5]
    send_sems, recv_sems, local_sems, fetch_sems, keep_sems = refs[5:]
    place.locate()
    place.greet()
    wires = Wires(place, send_sems, recv_sems)
    driver = Driver(units, gather_stages(place, units, shards, wholes, wires, local_sems), 5.0)
    rows, width = tokens.shape
    slot_rows, enc_rows = rows // seqs, encoder.shape[0] // seqs
    pairs_of_heads = width // LANES
    norms = vmem["gains"].shape[0]
    keeping = []

    def keep(name):
        copy = pltpu.make_async_copy(
            vmem[name], stored[KEPT.index(name)], keep_sems.at[KEPT.index(name)]
        )
        copy.start()
        keeping.append(copy)

    first_of = {}
    for u, unit in enumerate(units):
        first_of.setdefault(unit.owner, u)
    last_of = {unit.owner: u for u, unit in enumerate(units)}
    slotted = [u for u, unit in enumerate(units) if unit.owner not in (0, 7)]
    state = dict(fetched=0, used=0)
    depth = slots.shape[0]

    def fetch(u):
        unit = units[u]
        spot = slotted.index(u) % depth
        return pltpu.make_async_copy(
            wholes[unit.owner].at[(slice(None),) * 4 + unit.part()],
            slots.at[(spot,) + (slice(None),) * 5 + (pl.ds(0, unit.shape[1]),)],
            fetch_sems.at[spot],
        )

    def pump():
        while (
            state["fetched"] < len(slotted)
            and slotted[state["fetched"]] <= driver.settled()
            and state["fetched"] < state["used"] + depth
        ):
            fetch(slotted[state["fetched"]]).start()
            state["fetched"] += 1

    def spent(cost):
        driver.spent(cost)
        pump()

    def weight(u):
        driver.until(u)
        pump()
        fetch(u).wait()
        spot = slotted.index(u) % depth
        return lambda at: slots[spot, :, :, :, :, :, at].reshape(width, -1)

    def release():
        state["used"] += 1
        pump()

    def project(source, u, target, tile, cost):
        matrix = weight(u)
        size = units[u].shape[1]

        def body(at):
            target[:, at] = low(mul(source[...], matrix(at)))

        tiles(size, tile, body)
        release()
        spent(cost)

    def residual(source, u, before, target, cost):
        matrix = weight(u)

        def body(at):
            target[:, at] = wide(before[:, at]) + mul(source[...], matrix(at))

        tiles(width, CHUNK, body)
        release()
        spent(cost)

    driver.until(0)
    copy = pltpu.make_async_copy(wholes[0], pack, fetch_sems.at[depth])
    copy.start()
    copy.wait()
    packs = wide(pack[...]).reshape(width // LANES, -1, PACK, LANES)
    summed = jnp.sum(packs, axis=1)
    for group in range(summed.shape[0]):
        vmem["gains"][:, group * LANES : (group + 1) * LANES] = summed[group, :norms]
    table = low(jnp.sum(summed, axis=0)[HEADS:, :BUCKETS])
    spread = spread_ids[...]
    onehot = (lax.broadcasted_iota(jnp.int32, (BUCKETS, spread.shape[1]), 0) == spread).astype(
        jnp.bfloat16
    )
    bias_rows[...] = mul(table, onehot)
    keep("gains")
    rms_rows(tokens, vmem["normed_self"], vmem["gains"][0:1])
    keep("normed_self")

    for sequence in range(seqs):
        at = pl.ds(sequence * slot_rows, slot_rows)
        valid = lax.broadcasted_iota(jnp.int32, (slot_rows, 1), 0) < lengths[sequence]
        vmem["branch"][at, :] = low(jnp.where(valid, wide(cotangent[at, :]), 0.0))
    keep("branch")

    for part in range(3):
        project(vmem["normed_self"], first_of[1] + part, vmem["qkv"].at[part], CHUNK, 2.0)
    keep("qkv")
    for part in range(2):
        project(encoder, first_of[2] + part, vmem["pairs"].at[part], CHUNK, 3.0)
    keep("pairs")

    def self_pair(pair, carry):
        lanes = pl.ds(pl.multiple_of(pair * LANES, LANES), LANES)
        row = lax.broadcasted_iota(jnp.int32, (slot_rows, slot_rows), 0)
        column = lax.broadcasted_iota(jnp.int32, (slot_rows, slot_rows), 1)
        period = bias_rows.shape[1]
        bias = jnp.concatenate(
            [
                pltpu.roll(
                    jnp.broadcast_to(bias_rows[2 * pair + head, :][None], (slot_rows, period)),
                    0,
                    1,
                    stride=1,
                    stride_axis=0,
                )[:, :slot_rows]
                for head in range(2)
            ],
            axis=0,
        )
        for sequence in range(seqs):
            at = pl.ds(sequence * slot_rows, slot_rows)
            mask = (column <= row) & (column < lengths[sequence])
            probs, mixed = attend_pair(
                vmem["qkv"][0, at, lanes],
                vmem["qkv"][1, at, lanes],
                vmem["qkv"][2, at, lanes],
                bias,
                jnp.concatenate([mask, mask], axis=0),
            )
            vmem["probs_self"][sequence, pair] = probs
            vmem["mixed_self"][at, lanes] = mixed
        return carry

    for pair in range(0, pairs_of_heads, 2):
        lax.fori_loop(pair, pair + 2, self_pair, 0)
        spent(3.0)
    keep("probs_self")
    keep("mixed_self")
    residual(vmem["mixed_self"], first_of[3], tokens, vmem["second"], 1.0)
    keep("second")
    rms_rows(vmem["second"], vmem["normed_cross"], vmem["gains"][1:2])
    keep("normed_cross")
    project(vmem["normed_cross"], first_of[4], vmem["queries"], CHUNK, 2.0)
    keep("queries")

    def cross_pair(pair, carry):
        lanes = pl.ds(pl.multiple_of(pair * LANES, LANES), LANES)
        column = lax.broadcasted_iota(jnp.int32, (1, enc_rows), 1)
        for sequence in range(seqs):
            at = pl.ds(sequence * slot_rows, slot_rows)
            keys = pl.ds(sequence * enc_rows, enc_rows)
            probs, mixed = attend_pair(
                vmem["queries"][at, lanes],
                vmem["pairs"][0, keys, lanes],
                vmem["pairs"][1, keys, lanes],
                None,
                column < enc_lengths[sequence],
            )
            vmem["probs_cross"][sequence, pair] = probs
            vmem["mixed_cross"][at, lanes] = mixed
        return carry

    for pair in range(0, pairs_of_heads, 2):
        lax.fori_loop(pair, pair + 2, cross_pair, 0)
        spent(4.0)
    keep("probs_cross")
    keep("mixed_cross")
    residual(vmem["mixed_cross"], first_of[5], vmem["second"], vmem["third"], 1.0)
    keep("third")
    rms_rows(vmem["third"], vmem["normed_ffn"], vmem["gains"][2:3])
    keep("normed_ffn")

    driver.until(last_of[7])
    copy = pltpu.make_async_copy(wholes[7], raw_out, fetch_sems.at[depth])
    copy.start()
    copy.wait()
    sizes = place.sizes
    joined = 2 * raw_out.shape[4] * 8

    def unpack(step, carry):
        at = (step // (sizes[1] * sizes[2]), (step // sizes[2]) % sizes[1], step % sizes[2])
        ff_out[pl.ds(pl.multiple_of(step * joined, 16), joined), :] = low(
            wide(raw_out[at]).reshape(joined, width)
        )
        return carry

    lax.fori_loop(0, sizes[0] * sizes[1] * sizes[2], unpack, 0)
    spent(3.0)
    outcome[...] = vmem["third"][...]
    vmem["grad_normed"][...] = jnp.zeros_like(vmem["grad_normed"])

    def ffn_chunk(matrix, chunk, lane):
        gate_at = pl.ds(pl.multiple_of(lane, 2 * CHUNK), CHUNK)
        up_at = pl.ds(pl.multiple_of(lane + CHUNK, CHUNK), CHUNK)
        normed = vmem["normed_ffn"][...]
        gate = mul(normed, matrix(gate_at))
        up = mul(normed, matrix(up_at))
        square = gate * gate
        curve = jnp.tanh(0.7978845608028654 * gate * (1.0 + 0.044715 * square))
        half = 0.5 * (1.0 + curve)
        gelu = gate * half
        slope = half + 0.5 * gate * (1.0 - curve * curve) * (
            0.7978845608028654 * (1.0 + 3 * 0.044715 * square)
        )
        hidden = low(gelu * up)
        vmem["hidden"][chunk] = hidden
        down_at = pl.ds(pl.multiple_of(chunk * CHUNK, CHUNK), CHUNK)
        grad_hidden = mul(vmem["branch"][...], ff_out[down_at, :], 1, 1)
        grads = jnp.concatenate([low(grad_hidden * up * slope), low(grad_hidden * gelu)], axis=1)
        vmem["grad_gate_up"][chunk] = grads

        def add_out(at):
            outcome[:, at] += mul(vmem["hidden"][chunk], ff_out[down_at, at])

        tiles(width, CHUNK, add_out)

        def add_back(at):
            vmem["grad_normed"][at, :] += mul(
                vmem["grad_gate_up"][chunk, at, :],
                matrix(pl.ds(pl.multiple_of(lane, 2 * CHUNK), 2 * CHUNK)),
                1,
                1,
            )

        tiles(rows, LANES, add_back)

    chunk = 0
    for u in range(first_of[6], last_of[6] + 1):
        matrix = weight(u)
        inside = units[u].shape[1] // (2 * CHUNK)

        def step(spot, carry, matrix=matrix, chunk=chunk):
            ffn_chunk(matrix, chunk + spot, spot * 2 * CHUNK)
            return carry

        lax.fori_loop(0, inside, step, 0)
        chunk += inside
        release()
        spent(3.0 * inside)
    for name in ("hidden", "grad_gate_up", "grad_normed"):
        keep(name)
    while not driver.done():
        driver.advance()
    for copy in keeping:
        copy.wait()
    wires.finish()


def kept_shapes(seqs, slot_rows, enc_rows, width, hidden, norms):
    rows = seqs * slot_rows
    pairs = width // LANES
    low_type, wide_type = jnp.bfloat16, jnp.float32
    return {
        "normed_self": ((rows, width), low_type),
        "qkv": ((3, rows, width), low_type),
        "probs_self": ((seqs, pairs, 2 * slot_rows, slot_rows), low_type),
        "mixed_self": ((rows, width), low_type),
        "second": ((rows, width), wide_type),
        "normed_cross": ((rows, width), low_type),
        "queries": ((rows, width), low_type),
        "pairs": ((2, seqs * enc_rows, width), low_type),
        "probs_cross": ((seqs, pairs, 2 * slot_rows, enc_rows), low_type),
        "mixed_cross": ((rows, width), low_type),
        "third": ((rows, width), wide_type),
        "normed_ffn": ((rows, width), low_type),
        "branch": ((rows, width), low_type),
        "hidden": ((hidden // CHUNK, rows, CHUNK), low_type),
        "grad_gate_up": ((hidden // CHUNK, rows, 2 * CHUNK), low_type),
        "grad_normed": ((rows, width), wide_type),
        "gains": ((norms, width), wide_type),
    }


def forward_all(place, shards, tokens, encoder, cotangent, lengths, enc_lengths, bucket_ids, norms):
    blocks = [shard.shape for shard in shards]
    units = make_units(blocks, PIECE, ORDER)
    total = copies_of(units, place.sizes, False)
    anywhere = pl.BlockSpec(memory_space=pl.ANY)
    inside = pl.BlockSpec(memory_space=pltpu.VMEM)
    scalars = pl.BlockSpec(memory_space=pltpu.SMEM)
    seqs, slot_rows, width = tokens.shape
    rows = seqs * slot_rows
    hidden = blocks[6][1] // 2
    kept = kept_shapes(seqs, slot_rows, encoder.shape[1], width, hidden, norms)
    spread = jnp.concatenate(
        [bucket_ids[:1], jnp.broadcast_to(bucket_ids[:1], (slot_rows,)), bucket_ids[:0:-1]]
    )[None]
    depth = 3
    results = pl.pallas_call(
        functools.partial(forward_kernel, place, units, len(blocks), seqs),
        out_shape=[jax.ShapeDtypeStruct(place.sizes + block, jnp.bfloat16) for block in blocks]
        + [jax.ShapeDtypeStruct((rows, width), jnp.float32)]
        + [jax.ShapeDtypeStruct(*kept[name]) for name in KEPT],
        in_specs=[anywhere] * len(blocks) + [inside] * 3 + [scalars] * 2 + [inside],
        out_specs=[anywhere] * len(blocks) + [inside] + [anywhere] * len(KEPT),
        scratch_shapes=[pltpu.VMEM(*kept[name]) for name in KEPT]
        + [
            pltpu.VMEM((HEADS, 2 * slot_rows), jnp.float32),
            pltpu.VMEM((depth,) + place.sizes + (blocks[1][0], PIECE // blocks[1][0]), jnp.bfloat16),
            pltpu.VMEM(place.sizes + blocks[7], jnp.bfloat16),
            pltpu.VMEM((hidden, width), jnp.bfloat16),
            pltpu.VMEM(place.sizes + blocks[0], jnp.bfloat16),
            pltpu.SemaphoreType.DMA((total,)),
            pltpu.SemaphoreType.DMA((total,)),
            pltpu.SemaphoreType.DMA((len(units),)),
            pltpu.SemaphoreType.DMA((depth + 1,)),
            pltpu.SemaphoreType.DMA((len(KEPT),)),
        ],
        compiler_params=pltpu.CompilerParams(
            collective_id=0, has_side_effects=True, vmem_limit_bytes=63 * 2**20
        ),
        name="forward_all",
    )(
        *shards,
        tokens.reshape(rows, width),
        encoder.reshape(-1, width),
        cotangent.reshape(rows, width),
        lengths,
        enc_lengths,
        spread,
    )
    count = len(blocks)
    return results[:count], results[count], dict(zip(KEPT, results[count + 1 :]))


def scatter_kernel(place, units, count, slot_of, *refs):
    wholes, owned = refs[:count], refs[count : 2 * count]
    refs = refs[2 * count :]
    scratch = [refs[6 * u : 6 * u + 6] for u in range(len(units))]
    slots = refs[6 * len(units) : -3]
    send_sems, recv_sems, local_sems = refs[-3:]
    place.locate()
    place.greet()
    zi, yi, xi, ci = place.here
    sizes = place.sizes
    full = slice(None)
    started, serial, pending = [], [0], {}

    def send(source, target, axis, step):
        spot = serial[0]
        serial[0] += 1
        copy = pltpu.make_async_remote_copy(
            src_ref=source,
            dst_ref=target,
            send_sem=send_sems.at[spot],
            recv_sem=recv_sems.at[spot],
            device_id=place.device(place.moved(axis, step)),
            device_id_type=MESH,
        )
        copy.start()
        started.append(copy)
        return copy

    def settle(u):
        for copy in pending[u]:
            copy.wait_recv()
        pending[u] = []

    def add(total, target, terms, kind=jnp.bfloat16):
        def body(spot, carry):
            value = sum(term(spot).astype(jnp.float32) for term in terms)
            ref, index = target(spot)
            ref[index] = value.astype(kind)
            return carry

        lax.fori_loop(0, total, body, 0)

    def slot(u):
        kind, place_in = slot_of[u]
        return slots[kind].at[place_in]

    def first(u):
        unit = units[u]
        whole = wholes[unit.owner]
        arrived = scratch[u][0]
        mine = pltpu.make_async_copy(
            whole.at[(full, full, full, ci) + unit.part()], slot(u), local_sems.at[u]
        )
        mine.start()
        theirs = send(
            whole.at[(full, full, full, (ci + 1) % 2) + unit.part()], arrived, 3, 1
        )
        pending[u] = (mine, theirs)

    def second(u):
        unit = units[u]
        arrived, one_a, one_b = scratch[u][:3]
        own = slot(u)
        mine, theirs = pending[u]
        mine.wait()
        theirs.wait_recv()
        flat = lambda b: (b // (sizes[1] * sizes[2]), (b // sizes[2]) % sizes[1], b % sizes[2])
        add(
            sizes[0] * sizes[1] * sizes[2],
            lambda b: (arrived, flat(b)),
            [lambda b: arrived[flat(b)], lambda b: own[flat(b)]],
        )
        pending[u] = []
        for half in range(unit.halves):
            axis, target = (1, one_a) if half == 0 else (2, one_b)
            for step in range(1, sizes[axis]):
                there = place.moved(axis, step)[axis]
                index = (full, there, full) if half == 0 else (full, full, there)
                pending[u].append(
                    send(arrived.at[index + unit.local(half)], target.at[step - 1], axis, step)
                )

    def third(u):
        settle(u)
        unit = units[u]
        arrived, one_a, one_b, two_a, two_b = scratch[u][:5]
        for half in range(unit.halves):
            axis, other = (1, 2) if half == 0 else (2, 1)
            one, two = (one_a, two_a) if half == 0 else (one_b, two_b)
            wide = sizes[other]

            def mine(b, half=half, wide=wide):
                middle = (yi, b % wide) if half == 0 else (b % wide, xi)
                return arrived[(b // wide,) + middle + unit.local(half)]

            add(
                sizes[0] * wide,
                lambda b: (one, (0, b // wide, b % wide)),
                [mine]
                + [
                    lambda b, step=step: one[step, b // wide, b % wide]
                    for step in range(sizes[axis] - 1)
                ],
            )
            for step in range(1, wide):
                there = place.moved(other, step)[other]
                pending[u].append(send(one.at[0, :, there], two.at[step - 1], other, step))

    def fourth(u):
        settle(u)
        unit = units[u]
        one_a, one_b, two_a, two_b, last = scratch[u][1:]
        for half in range(unit.halves):
            axis, here = (2, xi) if half == 0 else (1, yi)
            one, two = (one_a, two_a) if half == 0 else (one_b, two_b)
            add(
                sizes[0],
                lambda b: (two, (0, b)),
                [lambda b: one[0, b, here]]
                + [lambda b, step=step: two[step, b] for step in range(sizes[axis] - 1)],
            )
            for step in range(1, sizes[0]):
                there = place.moved(0, step)[0]
                pending[u].append(
                    send(two.at[0, there], last.at[(step - 1,) + unit.local(half)], 0, step)
                )

    def fifth(u):
        settle(u)
        unit = units[u]
        two_a, two_b, last = scratch[u][3:]
        for half in range(unit.halves):
            two = two_a if half == 0 else two_b
            value = two[0, zi].astype(jnp.float32)
            for step in range(sizes[0] - 1):
                value = value + last[(step,) + unit.local(half)].astype(jnp.float32)
            owned[unit.owner][unit.part(half)] = value

    stages = (first, second, third, fourth, fifth)
    for tick in range(len(units) + len(stages) - 1):
        for lag, stage in enumerate(stages):
            if 0 <= tick - lag < len(units):
                stage(tick - lag)
    for copy in started:
        copy.wait_send()


def copies_of(units, sizes, per_z):
    total = 0
    for unit in units:
        total += (sizes[0] - 1) * (unit.halves if per_z else 1) + 1
        total += unit.halves * (sizes[1] - 1 + sizes[2] - 1)
    return total


def scatter_all(place, blocks, wholes):
    units = make_units(blocks, PIECE, ORDER)
    sizes = place.sizes
    total = copies_of(units, sizes, True)
    scratch, kinds, slot_of = [], [], []
    seen = {}
    for unit in units:
        half = unit.half_shape()
        for shape in (
            sizes[:3] + unit.shape,
            (sizes[1] - 1, sizes[0], sizes[2]) + half,
            (sizes[2] - 1, sizes[0], sizes[1]) + half,
            (sizes[2] - 1, sizes[0]) + half,
            (sizes[1] - 1, sizes[0]) + half,
            (sizes[0] - 1,) + unit.shape,
        ):
            scratch.append(pltpu.VMEM(shape, jnp.bfloat16))
        if unit.shape not in seen:
            seen[unit.shape] = [len(kinds), 0]
            kinds.append(pltpu.VMEM((3,) + sizes[:3] + unit.shape, jnp.bfloat16))
        kind = seen[unit.shape]
        slot_of.append((kind[0], kind[1] % 3))
        kind[1] += 1
    anywhere = pl.BlockSpec(memory_space=pl.ANY)
    return pl.pallas_call(
        functools.partial(scatter_kernel, place, units, len(blocks), slot_of),
        out_shape=[jax.ShapeDtypeStruct(block, jnp.float32) for block in blocks],
        in_specs=[anywhere] * len(blocks),
        out_specs=[pl.BlockSpec(memory_space=pltpu.VMEM)] * len(blocks),
        scratch_shapes=scratch
        + kinds
        + [
            pltpu.SemaphoreType.DMA((total,)),
            pltpu.SemaphoreType.DMA((total,)),
            pltpu.SemaphoreType.DMA((len(units),)),
        ],
        compiler_params=pltpu.CompilerParams(
            collective_id=1, has_side_effects=True, vmem_limit_bytes=60 * 2**20
        ),
        name="scatter_all",
    )(*wholes)


def norm_scale(stream, gain):
    return stream * lax.rsqrt(jnp.mean(stream * stream, axis=-1, keepdims=True) + 1e-06) * gain


def gelu_tanh(values):
    return (
        0.5
        * values
        * (1.0 + jnp.tanh(0.7978845608028654 * (values + 0.044715 * values * values * values)))
    )


def gated(gate_up):
    half_width = gate_up.shape[1] // 2
    return gelu_tanh(gate_up[:, :half_width]) * gate_up[:, half_width:]


def product(spec, left, right):
    return jnp.einsum(spec, left, right, preferred_element_type=jnp.float32)


def attend(queries, key_rows, value_rows, pos_bias, keep_mask):
    scores = product("bihc,bjhc->bhij", queries, key_rows) * HEAD ** (-0.5)
    if pos_bias is not None:
        scores = scores + pos_bias
    masked = jnp.where(keep_mask[:, None], scores, -1e30)
    row_max = jnp.max(masked, axis=-1, keepdims=True)
    powers = jnp.exp(masked - row_max)
    probs = powers / jnp.sum(powers, axis=-1, keepdims=True)
    low_probs = probs.astype(jnp.bfloat16)
    mixed = product("bhij,bjhc->bihc", low_probs, value_rows)
    return mixed.astype(jnp.bfloat16), low_probs


def attend_back(queries, key_rows, value_rows, low_probs, grad_mixed):
    probs = low_probs.astype(jnp.float32)
    grad_values = product("bhij,bihc->bjhc", low_probs, grad_mixed)
    grad_probs = product("bihc,bjhc->bhij", grad_mixed, value_rows)
    grad_scores = (
        probs * (grad_probs - jnp.sum(probs * grad_probs, axis=-1, keepdims=True))
    ).astype(jnp.bfloat16)
    grad_queries = product("bhij,bjhc->bihc", grad_scores, key_rows) * HEAD ** (-0.5)
    grad_keys = product("bhij,bihc->bjhc", grad_scores, queries) * HEAD ** (-0.5)
    return grad_queries, grad_keys, grad_values, grad_scores


def toeplitz(table, size):
    lead = table.shape[:-1]
    row = jnp.concatenate(
        [table[..., ::-1], jnp.broadcast_to(table[..., :1], lead + (size,))], axis=-1
    )
    tiled = jnp.broadcast_to(row[..., None, :], lead + (size, 2 * size)).reshape(lead + (-1,))
    tiled = jnp.concatenate([tiled[..., size - 1 :], row[..., :1]], axis=-1)
    tiled = tiled[..., : size * (2 * size - 1)]
    return tiled.reshape(lead + (size, 2 * size - 1))[..., :size]


def layer(weights, gains, rel_bias, tokens, encoder, cotangent, lengths, enc_lengths, bucket_ids):
    self_qkv, self_out, cross_q, cross_kv, cross_out, ff_in, ff_out = weights
    count, slots, width = tokens.shape
    enc_count = encoder.shape[1]
    bucket_map = toeplitz(bucket_ids, slots).reshape(-1)
    onehot = (lax.iota(jnp.int32, BUCKETS)[:, None] == bucket_map[None, :]).astype(jnp.bfloat16)
    pos_bias = jnp.dot(rel_bias, onehot, preferred_element_type=jnp.float32).reshape(
        HEADS, slots, slots
    )
    row_ids = lax.iota(jnp.int32, slots)
    self_mask = (row_ids[None, None, :] <= row_ids[None, :, None]) & (
        row_ids[None, None, :] < lengths[:, None, None]
    )
    cross_mask = lax.iota(jnp.int32, enc_count)[None, None, :] < enc_lengths[:, None, None]
    enc_rows = encoder.reshape(count * enc_count, width)
    dot = functools.partial(jnp.dot, preferred_element_type=jnp.float32)
    low = lambda value: value.astype(jnp.bfloat16)
    stream = tokens.reshape(count * slots, width).astype(jnp.float32)
    normed_self, back_self = jax.vjp(norm_scale, stream, gains[0])
    normed_self = low(normed_self)
    qkv = low(dot(normed_self, self_qkv)).reshape(count, slots, 3, HEADS, HEAD)
    mixed_self, probs_self = attend(qkv[:, :, 0], qkv[:, :, 1], qkv[:, :, 2], pos_bias, self_mask)
    mixed_self = mixed_self.reshape(count * slots, width)
    second = stream + dot(mixed_self, self_out)
    normed_cross, back_cross = jax.vjp(norm_scale, second, gains[1])
    normed_cross = low(normed_cross)
    queries = low(dot(normed_cross, cross_q)).reshape(count, slots, HEADS, HEAD)
    pairs = low(dot(enc_rows, cross_kv)).reshape(count, enc_count, 2, HEADS, HEAD)
    mixed_cross, probs_cross = attend(queries, pairs[:, :, 0], pairs[:, :, 1], None, cross_mask)
    mixed_cross = mixed_cross.reshape(count * slots, width)
    third = second + dot(mixed_cross, cross_out)
    normed_ffn, back_ffn = jax.vjp(norm_scale, third, gains[2])
    normed_ffn = low(normed_ffn)
    gate_up = dot(normed_ffn, ff_in)
    activated, back_gate = jax.vjp(gated, gate_up)
    hidden = low(activated)
    outcome = third + dot(hidden, ff_out)

    valid = (row_ids[None, :] < lengths[:, None]).astype(jnp.float32)[:, :, None]
    grad_out = (cotangent.astype(jnp.float32) * valid).reshape(count * slots, width)
    branch = low(grad_out)
    grad_ff_out = product("lf,ld->fd", hidden, branch)
    grad_hidden = product("ld,fd->lf", branch, ff_out)
    (grad_gate_up,) = back_gate(grad_hidden)
    grad_gate_up = low(grad_gate_up)
    grad_ff_in = product("ld,lf->df", normed_ffn, grad_gate_up)
    grad_stream, gain_ffn = back_ffn(product("lf,df->ld", grad_gate_up, ff_in))
    grad_third = grad_out + grad_stream
    branch = low(grad_third)
    grad_cross_out = product("le,ld->ed", mixed_cross, branch)
    grad_mixed = low(product("ld,ed->le", branch, cross_out)).reshape(count, slots, HEADS, HEAD)
    grad_queries, grad_keys, grad_values, unused = attend_back(
        queries, pairs[:, :, 0], pairs[:, :, 1], probs_cross, grad_mixed
    )
    grad_query_rows = low(grad_queries.reshape(count * slots, width))
    grad_pair_rows = low(
        jnp.concatenate(
            [
                grad_keys.reshape(count * enc_count, width),
                grad_values.reshape(count * enc_count, width),
            ],
            axis=1,
        )
    )
    grad_cross_q = product("ld,le->de", normed_cross, grad_query_rows)
    grad_cross_kv = product("ed,ef->df", enc_rows, grad_pair_rows)
    grad_enc = product("ef,df->ed", grad_pair_rows, cross_kv)
    grad_stream, gain_cross = back_cross(product("le,de->ld", grad_query_rows, cross_q))
    grad_second = grad_third + grad_stream
    branch = low(grad_second)
    grad_self_out = product("le,ld->ed", mixed_self, branch)
    grad_mixed = low(product("ld,ed->le", branch, self_out)).reshape(count, slots, HEADS, HEAD)
    grad_queries, grad_keys, grad_values, grad_scores = attend_back(
        qkv[:, :, 0], qkv[:, :, 1], qkv[:, :, 2], probs_self, grad_mixed
    )
    score_sums = jnp.sum(grad_scores.astype(jnp.float32), axis=0).reshape(HEADS, slots * slots)
    grad_rel_bias = product("hn,bn->hb", low(score_sums), onehot)
    grad_qkv = low(
        jnp.concatenate(
            [part.reshape(count * slots, width) for part in (grad_queries, grad_keys, grad_values)],
            axis=1,
        )
    )
    grad_self_qkv = product("ld,lf->df", normed_self, grad_qkv)
    grad_stream, gain_self = back_self(product("lf,df->ld", grad_qkv, self_qkv))
    grad_tok = grad_second + grad_stream
    grad_gains = jnp.stack([gain_self, gain_cross, gain_ffn], axis=0)
    grads = (
        grad_self_qkv,
        grad_self_out,
        grad_cross_q,
        grad_cross_kv,
        grad_cross_out,
        grad_ff_in,
        grad_ff_out,
    )
    return (
        outcome.reshape(tokens.shape),
        grad_tok.reshape(tokens.shape),
        grad_enc.reshape(encoder.shape),
        grads,
        grad_gains,
        grad_rel_bias,
    )


AXES = ("dp", "fsdp")


def by_collectives(data, shards):
    whole = lambda shard, axis=0: lax.all_gather(shard, AXES, axis=axis, tiled=True)
    weights = tuple(whole(shard) for shard in shards[:7])
    gains = whole(shards[7], 1).astype(jnp.float32)
    rel_bias = whole(shards[8]).reshape(HEADS, BUCKETS)
    outcome, grad_tok, grad_enc, grads, grad_gains, grad_rel_bias = layer(
        weights, gains, rel_bias, *data
    )
    settle = lambda total, axis=0: lax.psum_scatter(
        total, AXES, scatter_dimension=axis, tiled=True
    )
    return (
        (outcome, grad_tok, grad_enc)
        + tuple(settle(grad) for grad in grads)
        + (settle(grad_gains, 1), settle(grad_rel_bias.reshape(-1)))
    )


def back(kept, weights, gains, data):
    self_qkv, cross_kv, self_out, cross_q, cross_out, ff_in, ff_out = weights
    tokens, encoder, cotangent, lengths, enc_lengths, bucket_ids = data
    count, slots, width = tokens.shape
    enc_count = encoder.shape[1]
    heads = lambda a, n: a.reshape(count, n, HEADS, HEAD)
    probs_of = lambda a: a.reshape(count, HEADS, slots, -1)
    bucket_map = toeplitz(bucket_ids, slots).reshape(-1)
    onehot = (lax.iota(jnp.int32, BUCKETS)[:, None] == bucket_map[None, :]).astype(jnp.bfloat16)
    enc_rows = encoder.reshape(count * enc_count, width)
    low = lambda value: value.astype(jnp.bfloat16)
    stream = tokens.reshape(count * slots, width).astype(jnp.float32)
    unused, back_self = jax.vjp(norm_scale, stream, gains[0])
    unused, back_cross = jax.vjp(norm_scale, kept["second"], gains[1])
    unused, back_ffn = jax.vjp(norm_scale, kept["third"], gains[2])
    hidden = kept["hidden"].transpose(1, 0, 2).reshape(count * slots, -1)
    grad_gate_up = kept["grad_gate_up"].transpose(1, 0, 2).reshape(count * slots, -1)
    row_ids = lax.iota(jnp.int32, slots)
    valid = (row_ids[None, :] < lengths[:, None]).astype(jnp.float32)[:, :, None]
    grad_out = (cotangent.astype(jnp.float32) * valid).reshape(count * slots, width)
    grad_ff_out = product("lf,ld->fd", hidden, kept["branch"])
    grad_ff_in = product("ld,lf->df", kept["normed_ffn"], grad_gate_up)
    grad_stream, gain_ffn = back_ffn(kept["grad_normed"])
    grad_third = grad_out + grad_stream
    branch = low(grad_third)
    grad_cross_out = product("le,ld->ed", kept["mixed_cross"], branch)
    grad_mixed = heads(low(product("ld,ed->le", branch, cross_out)), slots)
    grad_queries, grad_keys, grad_values, unused = attend_back(
        heads(kept["queries"], slots),
        heads(kept["pairs"][0], enc_count),
        heads(kept["pairs"][1], enc_count),
        probs_of(kept["probs_cross"]),
        grad_mixed,
    )
    grad_query_rows = low(grad_queries.reshape(count * slots, width))
    grad_pair_rows = low(
        jnp.concatenate(
            [
                grad_keys.reshape(count * enc_count, width),
                grad_values.reshape(count * enc_count, width),
            ],
            axis=1,
        )
    )
    grad_cross_q = product("ld,le->de", kept["normed_cross"], grad_query_rows)
    grad_cross_kv = product("ed,ef->df", enc_rows, grad_pair_rows)
    grad_enc = product("ef,df->ed", grad_pair_rows, cross_kv)
    grad_stream, gain_cross = back_cross(product("le,de->ld", grad_query_rows, cross_q))
    grad_second = grad_third + grad_stream
    branch = low(grad_second)
    grad_self_out = product("le,ld->ed", kept["mixed_self"], branch)
    grad_mixed = heads(low(product("ld,ed->le", branch, self_out)), slots)
    grad_queries, grad_keys, grad_values, grad_scores = attend_back(
        heads(kept["qkv"][0], slots),
        heads(kept["qkv"][1], slots),
        heads(kept["qkv"][2], slots),
        probs_of(kept["probs_self"]),
        grad_mixed,
    )
    score_sums = jnp.sum(grad_scores.astype(jnp.float32), axis=0).reshape(HEADS, slots * slots)
    grad_rel_bias = product("hn,bn->hb", low(score_sums), onehot)
    grad_qkv = low(
        jnp.concatenate(
            [part.reshape(count * slots, width) for part in (grad_queries, grad_keys, grad_values)],
            axis=1,
        )
    )
    grad_self_qkv = product("ld,lf->df", kept["normed_self"], grad_qkv)
    grad_stream, gain_self = back_self(product("lf,df->ld", grad_qkv, self_qkv))
    grad_tok = grad_second + grad_stream
    grad_gains = jnp.stack([gain_self, gain_cross, gain_ffn], axis=0)
    grads = (
        grad_self_qkv,
        grad_cross_kv,
        grad_self_out,
        grad_cross_q,
        grad_cross_out,
        grad_ff_in,
        grad_ff_out,
    )
    return grad_tok.reshape(tokens.shape), grad_enc.reshape(encoder.shape), grads, grad_gains, grad_rel_bias


def by_kernels(place, data, shards):
    norm_gains, rel_bias = shards[7:]
    count = place.sizes[0] * place.sizes[1] * place.sizes[2] * place.sizes[3]
    me = lax.axis_index(AXES)
    norms, per = norm_gains.shape
    group = LANES // per
    rel_per = rel_bias.shape[0]
    pack = jnp.zeros((PACK, LANES), jnp.bfloat16)
    pack = lax.dynamic_update_slice(pack, norm_gains, (0, (me % group) * per))
    rel_row, rel_column = HEADS + me * rel_per // BUCKETS, (me * rel_per) % BUCKETS
    pack = lax.dynamic_update_slice(pack, rel_bias.reshape(1, rel_per), (rel_row, rel_column))
    ff_rows, width = shards[6].shape
    ff_shape = (ff_rows // 8, 8, width)
    self_qkv, self_out, cross_q, cross_kv, cross_out, ff_in, ff_out = shards[:7]
    chunks = ff_in.shape[1] // (2 * CHUNK)
    laced = ff_in.reshape(-1, 2, chunks, CHUNK).transpose(0, 2, 1, 3).reshape(ff_in.shape)
    sent = (pack, self_qkv, cross_kv, self_out, cross_q, cross_out, laced, ff_out.reshape(ff_shape))
    blocks = [piece.shape for piece in sent]
    wholes, outcome, kept = forward_all(place, sent, *data, norms)
    weights = tuple(
        whole.reshape(count * shard.shape[0], shard.shape[1])
        for whole, shard in zip(
            wholes[1:], (self_qkv, cross_kv, self_out, cross_q, cross_out, ff_in, ff_out)
        )
    )
    outcome = outcome.reshape(data[0].shape)
    grad_tok, grad_enc, grads, grad_gains, grad_rel_bias = back(kept, weights, kept["gains"], data)
    top = grad_gains.reshape(norms, count // group, LANES).transpose(1, 0, 2)
    top = jnp.pad(top, ((0, 0), (0, HEADS - norms), (0, 0)))
    low_part = jnp.pad(grad_rel_bias, ((0, 0), (0, LANES - BUCKETS)))
    low_part = jnp.broadcast_to(low_part, (count // group, HEADS, LANES))
    tiles = jnp.concatenate([top, low_part], axis=1)[:, None]
    tiles = jnp.broadcast_to(tiles, (count // group, group, PACK, LANES))
    sums = scatter_all(
        place,
        blocks,
        [
            piece.astype(jnp.bfloat16).reshape(place.sizes + block)
            for piece, block in zip((tiles,) + grads, blocks)
        ],
    )
    packed, g_qkv, g_kv, g_so, g_cq, g_co, g_in, g_out = sums
    g_in = g_in.reshape(-1, chunks, 2, CHUNK).transpose(0, 2, 1, 3).reshape(ff_in.shape)
    owned = [g_qkv, g_so, g_cq, g_kv, g_co, g_in, g_out.reshape(ff_rows, width)]
    own_gains = lax.dynamic_slice(packed, (0, (me % group) * per), (norms, per))
    own_rel = lax.dynamic_slice(packed, (rel_row, rel_column), (1, rel_per)).reshape(-1)
    return (outcome, grad_tok, grad_enc) + tuple(owned) + (own_gains, own_rel)


def on_device(place, *args):
    data, shards = args[:6], args[6:]
    per = shards[7].shape[1]
    regular = all(shard.shape[0] % 16 == 0 for shard in shards[:6])
    if regular and shards[6].shape[0] % 8 == 0 and LANES % per == 0:
        return by_kernels(place, data, shards)
    return by_collectives(data, shards)


def solution(mesh):
    rows = P(AXES, None, None)
    flat = P(AXES)
    matrix = P(AXES, None)
    split = P(None, AXES)
    place = Place(mesh.shape["dp"], mesh.shape["fsdp"])
    return jax.shard_map(
        functools.partial(on_device, place),
        mesh=mesh,
        in_specs=(rows, rows, rows, flat, flat, P()) + (matrix,) * 7 + (split, flat),
        out_specs=(rows, rows, rows) + (matrix,) * 7 + (split, flat),
        check_vma=False,
    )
```

```python
import functools

import jax
import jax.numpy as jnp
from jax import lax
from jax.experimental import pallas as pl
from jax.experimental.pallas import tpu as pltpu
from jax.sharding import PartitionSpec as P

HEADS = 16
HEAD = 64
BUCKETS = 32
PACK = 32
LANES = 128
PIECE = 32 * 1024

MESH = pl.DeviceIdType.MESH


class Place:
    def __init__(self, dp, fsdp):
        self.sizes = (dp // 2, 2, fsdp // 2, 2)

    def locate(self):
        row, column = lax.axis_index("dp"), lax.axis_index("fsdp")
        sizes = self.sizes
        self.here = (row // sizes[1], row % sizes[1], column // sizes[3], column % sizes[3])

    def moved(self, axis, step):
        coords = list(self.here)
        coords[axis] = (coords[axis] + step) % self.sizes[axis]
        return coords

    def device(self, coords):
        return (coords[0] * self.sizes[1] + coords[1], coords[2] * self.sizes[3] + coords[3])

    def peers(self):
        return [(axis, step) for axis in range(4) for step in range(1, self.sizes[axis])]

    def greet(self):
        barrier = pltpu.get_barrier_semaphore()
        for axis, step in self.peers():
            pl.semaphore_signal(
                barrier, inc=1, device_id=self.device(self.moved(axis, step)), device_id_type=MESH
            )
        pl.semaphore_wait(barrier, len(self.peers()))


class Unit:
    def __init__(self, owner, block, start, count):
        self.owner, self.start, self.count = owner, start, count
        self.grouped = len(block) == 3
        self.shape = (count,) + block[1:] if self.grouped else (block[0], count)
        width = self.shape[-1]
        self.halves = 2 if width % 256 == 0 else 1
        self.half = width // self.halves

    def part(self, half=None):
        low, size = (0, self.shape[-1]) if half is None else (half * self.half, self.half)
        if self.grouped:
            return (pl.ds(self.start, self.count), slice(None), pl.ds(low, size))
        return (slice(None), pl.ds(self.start + low, size))

    def local(self, half):
        return (slice(None),) * (len(self.shape) - 1) + (pl.ds(half * self.half, self.half),)

    def half_shape(self):
        return self.shape[:-1] + (self.half,)


def make_units(blocks, piece, order):
    units = []
    for owner in order:
        block = blocks[owner]
        total, most = (block[0], piece // 8 // block[2] or 1) if len(block) == 3 else (block[1], piece // block[0])
        start = 0
        while start < total:
            count = min(most, total - start)
            units.append(Unit(owner, block, start, count))
            start += count
    return units


class Wires:
    def __init__(self, place, send_sems, recv_sems):
        self.place, self.send_sems, self.recv_sems = place, send_sems, recv_sems
        self.started = []

    def send(self, source, target, axis, step):
        spot = len(self.started)
        copy = pltpu.make_async_remote_copy(
            src_ref=source,
            dst_ref=target,
            send_sem=self.send_sems.at[spot],
            recv_sem=self.recv_sems.at[spot],
            device_id=self.place.device(self.place.moved(axis, step)),
            device_id_type=MESH,
        )
        copy.start()
        self.started.append(copy)
        return copy

    def along(self, axis, source, target):
        return [
            self.send(source, target, axis, step) for step in range(1, self.place.sizes[axis])
        ]

    def finish(self):
        for copy in self.started:
            copy.wait_send()


def gather_stages(place, units, shards, wholes, wires, local_sems):
    zi, yi, xi, ci = place.here
    full = slice(None)
    pending = {}

    def first(u):
        unit = units[u]
        shard = shards[unit.owner].at[unit.part()]
        own = wholes[unit.owner].at[(zi, yi, xi, ci) + unit.part()]
        copy = pltpu.make_async_copy(shard, own, local_sems.at[u])
        copy.start()
        pending[u] = (copy, wires.along(0, shard, own))

    def settle(u):
        for copy in pending[u]:
            copy.wait_recv()

    def second(u):
        copy, others = pending[u]
        copy.wait()
        for other in others:
            other.wait_recv()
        unit = units[u]
        whole = wholes[unit.owner]
        pending[u] = []
        for half in range(unit.halves):
            ref = whole.at[(full, yi, xi, ci) + unit.part(half)]
            pending[u] += wires.along(2 - half, ref, ref)

    def third(u):
        settle(u)
        unit = units[u]
        whole = wholes[unit.owner]
        pending[u] = []
        for half in range(unit.halves):
            index = (full, yi, full, ci) if half == 0 else (full, full, xi, ci)
            ref = whole.at[index + unit.part(half)]
            pending[u] += wires.along(1 + half, ref, ref)

    def fourth(u):
        settle(u)
        unit = units[u]
        ref = wholes[unit.owner].at[(full, full, full, ci) + unit.part()]
        pending[u] = wires.along(3, ref, ref)

    return (first, second, third, fourth, settle)


def copies_of(units, sizes, per_z):
    total = 0
    for unit in units:
        total += (sizes[0] - 1) * (unit.halves if per_z else 1) + 1
        total += unit.halves * (sizes[1] - 1 + sizes[2] - 1)
    return total


def mul(left, right, left_dim=1, right_dim=0):
    return lax.dot_general(
        left, right, (((left_dim,), (right_dim,)), ((), ())), preferred_element_type=jnp.float32
    )


def low(value):
    return value.astype(jnp.bfloat16)


def wide(value):
    return value.astype(jnp.float32)


def rms_rows(source, target, gain, rows=64):
    def body(step, carry):
        at = pl.ds(pl.multiple_of(step * rows, rows), rows)
        value = wide(source[at, :])
        scale = lax.rsqrt(jnp.mean(value * value, axis=-1, keepdims=True) + 1e-06)
        target[at, :] = low(value * scale * gain)
        return carry

    lax.fori_loop(0, source.shape[0] // rows, body, 0)


def tiles(total, size, body):
    def step(spot, carry):
        body(pl.ds(pl.multiple_of(spot * size, size), size))
        return carry

    lax.fori_loop(0, total // size, step, 0)


def flat_rows(value):
    return value.reshape(-1, value.shape[-1])


def attend_pair(queries, key_rows, value_rows, bias, mask):
    rows = queries.shape[0]
    left = lax.broadcasted_iota(jnp.int32, (1, LANES), 1) < HEAD
    zero = jnp.zeros_like(queries)
    scaled = queries * jnp.bfloat16(HEAD ** (-0.5))
    stacked = jnp.concatenate(
        [jnp.where(left, scaled, zero), jnp.where(left, zero, scaled)], axis=0
    )
    scores = mul(stacked, key_rows, 1, 1)
    if bias is not None:
        scores = scores + bias
    scores = jnp.where(mask, scores, -1e30)
    powers = jnp.exp(scores - jnp.max(scores, axis=-1, keepdims=True))
    probs = low(powers / jnp.sum(powers, axis=-1, keepdims=True))
    none = jnp.zeros_like(value_rows)
    mixed = mul(probs[:rows], jnp.where(left, value_rows, none)) + mul(
        probs[rows:], jnp.where(left, none, value_rows)
    )
    return probs, low(mixed)


class Driver:
    def __init__(self, units, stages, lead):
        self.units, self.stages, self.lead = units, stages, lead
        self.tick, self.debt = 0, 0.0

    def done(self):
        return self.tick >= len(self.units) + len(self.stages) - 1

    def settled(self):
        return self.tick - len(self.stages)

    def advance(self):
        for lag, stage in enumerate(self.stages):
            if 0 <= self.tick - lag < len(self.units):
                stage(self.tick - lag)
        self.tick += 1

    def until(self, unit):
        while self.settled() < unit:
            self.advance()

    def spent(self, cost):
        self.debt += cost
        while self.debt >= self.lead:
            self.debt -= self.lead
            if not self.done():
                self.advance()


KEPT = (
    "normed_self", "qkv", "probs_self", "mixed_self", "second", "normed_cross", "queries", "pairs",
    "probs_cross", "mixed_cross", "third", "normed_ffn", "branch", "hidden", "grad_gate_up",
    "grad_normed", "gains",
)
CHUNK = 256
ORDER = (0, 1, 2, 3, 4, 5, 7, 6)


def forward_kernel(place, units, count, seqs, *refs):
    shards, refs = refs[:count], refs[count:]
    tokens, encoder, cotangent, lengths, enc_lengths, spread_ids = refs[:6]
    wholes, refs = refs[6 : 6 + count], refs[6 + count :]
    outcome, refs = refs[0], refs[1:]
    stored, refs = refs[: len(KEPT)], refs[len(KEPT) :]
    vmem, refs = dict(zip(KEPT, refs)), refs[len(KEPT) :]
    bias_rows, slots, raw_out, ff_out, pack = refs[:5]
    send_sems, recv_sems, local_sems, fetch_sems, keep_sems = refs[5:]
    place.locate()
    place.greet()
    wires = Wires(place, send_sems, recv_sems)
    driver = Driver(units, gather_stages(place, units, shards, wholes, wires, local_sems), 5.0)
    rows, width = tokens.shape
    slot_rows, enc_rows = rows // seqs, encoder.shape[0] // seqs
    pairs_of_heads = width // LANES
    norms = vmem["gains"].shape[0]
    keeping = []

    def keep(name):
        copy = pltpu.make_async_copy(
            vmem[name], stored[KEPT.index(name)], keep_sems.at[KEPT.index(name)]
        )
        copy.start()
        keeping.append(copy)

    first_of = {}
    for u, unit in enumerate(units):
        first_of.setdefault(unit.owner, u)
    last_of = {unit.owner: u for u, unit in enumerate(units)}
    slotted = [u for u, unit in enumerate(units) if unit.owner not in (0, 7)]
    state = dict(fetched=0, used=0)
    depth = slots.shape[0]

    def fetch(u):
        unit = units[u]
        spot = slotted.index(u) % depth
        return pltpu.make_async_copy(
            wholes[unit.owner].at[(slice(None),) * 4 + unit.part()],
            slots.at[(spot,) + (slice(None),) * 5 + (pl.ds(0, unit.shape[1]),)],
            fetch_sems.at[spot],
        )

    def pump():
        while (
            state["fetched"] < len(slotted)
            and slotted[state["fetched"]] <= driver.settled()
            and state["fetched"] < state["used"] + depth
        ):
            fetch(slotted[state["fetched"]]).start()
            state["fetched"] += 1

    def spent(cost):
        driver.spent(cost)
        pump()

    def weight(u):
        driver.until(u)
        pump()
        fetch(u).wait()
        spot = slotted.index(u) % depth
        return lambda at: slots[spot, :, :, :, :, :, at].reshape(width, -1)

    def release():
        state["used"] += 1
        pump()

    def project(source, u, target, tile, cost):
        matrix = weight(u)
        size = units[u].shape[1]

        def body(at):
            target[:, at] = low(mul(source[...], matrix(at)))

        tiles(size, tile, body)
        release()
        spent(cost)

    def residual(source, u, before, target, cost):
        matrix = weight(u)

        def body(at):
            target[:, at] = wide(before[:, at]) + mul(source[...], matrix(at))

        tiles(width, CHUNK, body)
        release()
        spent(cost)

    driver.until(0)
    copy = pltpu.make_async_copy(wholes[0], pack, fetch_sems.at[depth])
    copy.start()
    copy.wait()
    packs = wide(pack[...]).reshape(width // LANES, -1, PACK, LANES)
    summed = jnp.sum(packs, axis=1)
    for group in range(summed.shape[0]):
        vmem["gains"][:, group * LANES : (group + 1) * LANES] = summed[group, :norms]
    table = low(jnp.sum(summed, axis=0)[HEADS:, :BUCKETS])
    spread = spread_ids[...]
    onehot = (lax.broadcasted_iota(jnp.int32, (BUCKETS, spread.shape[1]), 0) == spread).astype(
        jnp.bfloat16
    )
    bias_rows[...] = mul(table, onehot)
    keep("gains")
    rms_rows(tokens, vmem["normed_self"], vmem["gains"][0:1])
    keep("normed_self")

    for sequence in range(seqs):
        at = pl.ds(sequence * slot_rows, slot_rows)
        valid = lax.broadcasted_iota(jnp.int32, (slot_rows, 1), 0) < lengths[sequence]
        vmem["branch"][at, :] = low(jnp.where(valid, wide(cotangent[at, :]), 0.0))
    keep("branch")

    for part in range(3):
        project(vmem["normed_self"], first_of[1] + part, vmem["qkv"].at[part], CHUNK, 2.0)
    keep("qkv")
    for part in range(2):
        project(encoder, first_of[2] + part, vmem["pairs"].at[part], CHUNK, 3.0)
    keep("pairs")

    def self_pair(pair, carry):
        lanes = pl.ds(pl.multiple_of(pair * LANES, LANES), LANES)
        row = lax.broadcasted_iota(jnp.int32, (slot_rows, slot_rows), 0)
        column = lax.broadcasted_iota(jnp.int32, (slot_rows, slot_rows), 1)
        period = bias_rows.shape[1]
        bias = jnp.concatenate(
            [
                pltpu.roll(
                    jnp.broadcast_to(bias_rows[2 * pair + head, :][None], (slot_rows, period)),
                    0,
                    1,
                    stride=1,
                    stride_axis=0,
                )[:, :slot_rows]
                for head in range(2)
            ],
            axis=0,
        )
        for sequence in range(seqs):
            at = pl.ds(sequence * slot_rows, slot_rows)
            mask = (column <= row) & (column < lengths[sequence])
            probs, mixed = attend_pair(
                vmem["qkv"][0, at, lanes],
                vmem["qkv"][1, at, lanes],
                vmem["qkv"][2, at, lanes],
                bias,
                jnp.concatenate([mask, mask], axis=0),
            )
            vmem["probs_self"][sequence, pair] = probs
            vmem["mixed_self"][at, lanes] = mixed
        return carry

    for pair in range(0, pairs_of_heads, 2):
        lax.fori_loop(pair, pair + 2, self_pair, 0)
        spent(3.0)
    keep("probs_self")
    keep("mixed_self")
    residual(vmem["mixed_self"], first_of[3], tokens, vmem["second"], 1.0)
    keep("second")
    rms_rows(vmem["second"], vmem["normed_cross"], vmem["gains"][1:2])
    keep("normed_cross")
    project(vmem["normed_cross"], first_of[4], vmem["queries"], CHUNK, 2.0)
    keep("queries")

    def cross_pair(pair, carry):
        lanes = pl.ds(pl.multiple_of(pair * LANES, LANES), LANES)
        column = lax.broadcasted_iota(jnp.int32, (1, enc_rows), 1)
        for sequence in range(seqs):
            at = pl.ds(sequence * slot_rows, slot_rows)
            keys = pl.ds(sequence * enc_rows, enc_rows)
            probs, mixed = attend_pair(
                vmem["queries"][at, lanes],
                vmem["pairs"][0, keys, lanes],
                vmem["pairs"][1, keys, lanes],
                None,
                column < enc_lengths[sequence],
            )
            vmem["probs_cross"][sequence, pair] = probs
            vmem["mixed_cross"][at, lanes] = mixed
        return carry

    for pair in range(0, pairs_of_heads, 2):
        lax.fori_loop(pair, pair + 2, cross_pair, 0)
        spent(4.0)
    keep("probs_cross")
    keep("mixed_cross")
    residual(vmem["mixed_cross"], first_of[5], vmem["second"], vmem["third"], 1.0)
    keep("third")
    rms_rows(vmem["third"], vmem["normed_ffn"], vmem["gains"][2:3])
    keep("normed_ffn")

    driver.until(last_of[7])
    copy = pltpu.make_async_copy(wholes[7], raw_out, fetch_sems.at[depth])
    copy.start()
    copy.wait()
    sizes = place.sizes
    joined = 2 * raw_out.shape[4] * 8

    def unpack(step, carry):
        at = (step // (sizes[1] * sizes[2]), (step // sizes[2]) % sizes[1], step % sizes[2])
        ff_out[pl.ds(pl.multiple_of(step * joined, 16), joined), :] = low(
            wide(raw_out[at]).reshape(joined, width)
        )
        return carry

    lax.fori_loop(0, sizes[0] * sizes[1] * sizes[2], unpack, 0)
    spent(3.0)
    outcome[...] = vmem["third"][...]
    vmem["grad_normed"][...] = jnp.zeros_like(vmem["grad_normed"])

    def ffn_chunk(matrix, chunk, lane):
        gate_at = pl.ds(pl.multiple_of(lane, 2 * CHUNK), CHUNK)
        up_at = pl.ds(pl.multiple_of(lane + CHUNK, CHUNK), CHUNK)
        normed = vmem["normed_ffn"][...]
        gate = mul(normed, matrix(gate_at))
        up = mul(normed, matrix(up_at))
        square = gate * gate
        curve = jnp.tanh(0.7978845608028654 * gate * (1.0 + 0.044715 * square))
        half = 0.5 * (1.0 + curve)
        gelu = gate * half
        slope = half + 0.5 * gate * (1.0 - curve * curve) * (
            0.7978845608028654 * (1.0 + 3 * 0.044715 * square)
        )
        hidden = low(gelu * up)
        vmem["hidden"][chunk] = hidden
        down_at = pl.ds(pl.multiple_of(chunk * CHUNK, CHUNK), CHUNK)
        grad_hidden = mul(vmem["branch"][...], ff_out[down_at, :], 1, 1)
        grads = jnp.concatenate([low(grad_hidden * up * slope), low(grad_hidden * gelu)], axis=1)
        vmem["grad_gate_up"][chunk] = grads

        def add_out(at):
            outcome[:, at] += mul(vmem["hidden"][chunk], ff_out[down_at, at])

        tiles(width, CHUNK, add_out)

        def add_back(at):
            vmem["grad_normed"][at, :] += mul(
                vmem["grad_gate_up"][chunk, at, :],
                matrix(pl.ds(pl.multiple_of(lane, 2 * CHUNK), 2 * CHUNK)),
                1,
                1,
            )

        tiles(rows, LANES, add_back)

    chunk = 0
    for u in range(first_of[6], last_of[6] + 1):
        matrix = weight(u)
        inside = units[u].shape[1] // (2 * CHUNK)

        def step(spot, carry, matrix=matrix, chunk=chunk):
            ffn_chunk(matrix, chunk + spot, spot * 2 * CHUNK)
            return carry

        lax.fori_loop(0, inside, step, 0)
        chunk += inside
        release()
        spent(3.0 * inside)
    for name in ("hidden", "grad_gate_up", "grad_normed"):
        keep(name)
    while not driver.done():
        driver.advance()
    for copy in keeping:
        copy.wait()
    wires.finish()


def kept_shapes(seqs, slot_rows, enc_rows, width, hidden, norms):
    rows = seqs * slot_rows
    pairs = width // LANES
    low_type, wide_type = jnp.bfloat16, jnp.float32
    return {
        "normed_self": ((rows, width), low_type),
        "qkv": ((3, rows, width), low_type),
        "probs_self": ((seqs, pairs, 2 * slot_rows, slot_rows), low_type),
        "mixed_self": ((rows, width), low_type),
        "second": ((rows, width), wide_type),
        "normed_cross": ((rows, width), low_type),
        "queries": ((rows, width), low_type),
        "pairs": ((2, seqs * enc_rows, width), low_type),
        "probs_cross": ((seqs, pairs, 2 * slot_rows, enc_rows), low_type),
        "mixed_cross": ((rows, width), low_type),
        "third": ((rows, width), wide_type),
        "normed_ffn": ((rows, width), low_type),
        "branch": ((rows, width), low_type),
        "hidden": ((hidden // CHUNK, rows, CHUNK), low_type),
        "grad_gate_up": ((hidden // CHUNK, rows, 2 * CHUNK), low_type),
        "grad_normed": ((rows, width), wide_type),
        "gains": ((norms, width), wide_type),
    }


def forward_all(place, shards, tokens, encoder, cotangent, lengths, enc_lengths, spread, norms):
    blocks = [shard.shape for shard in shards]
    units = make_units(blocks, PIECE, ORDER)
    total = copies_of(units, place.sizes, False)
    anywhere = pl.BlockSpec(memory_space=pl.ANY)
    inside = pl.BlockSpec(memory_space=pltpu.VMEM)
    scalars = pl.BlockSpec(memory_space=pltpu.SMEM)
    seqs, slot_rows, width = tokens.shape
    rows = seqs * slot_rows
    hidden = blocks[6][1] // 2
    kept = kept_shapes(seqs, slot_rows, encoder.shape[1], width, hidden, norms)
    depth = 3
    results = pl.pallas_call(
        functools.partial(forward_kernel, place, units, len(blocks), seqs),
        out_shape=[jax.ShapeDtypeStruct(place.sizes + block, jnp.bfloat16) for block in blocks]
        + [jax.ShapeDtypeStruct((rows, width), jnp.float32)]
        + [jax.ShapeDtypeStruct(*kept[name]) for name in KEPT],
        in_specs=[anywhere] * len(blocks) + [inside] * 3 + [scalars] * 2 + [inside],
        out_specs=[anywhere] * len(blocks) + [inside] + [anywhere] * len(KEPT),
        scratch_shapes=[pltpu.VMEM(*kept[name]) for name in KEPT]
        + [
            pltpu.VMEM((HEADS, 2 * slot_rows), jnp.float32),
            pltpu.VMEM((depth,) + place.sizes + (blocks[1][0], PIECE // blocks[1][0]), jnp.bfloat16),
            pltpu.VMEM(place.sizes + blocks[7], jnp.bfloat16),
            pltpu.VMEM((hidden, width), jnp.bfloat16),
            pltpu.VMEM(place.sizes + blocks[0], jnp.bfloat16),
            pltpu.SemaphoreType.DMA((total,)),
            pltpu.SemaphoreType.DMA((total,)),
            pltpu.SemaphoreType.DMA((len(units),)),
            pltpu.SemaphoreType.DMA((depth + 1,)),
            pltpu.SemaphoreType.DMA((len(KEPT),)),
        ],
        compiler_params=pltpu.CompilerParams(
            collective_id=0, has_side_effects=True, vmem_limit_bytes=63 * 2**20
        ),
        name="forward_all",
    )(
        *shards,
        tokens.reshape(rows, width),
        encoder.reshape(-1, width),
        cotangent.reshape(rows, width),
        lengths,
        enc_lengths,
        spread,
    )
    count = len(blocks)
    return results[:count], results[count], dict(zip(KEPT, results[count + 1 :]))


RING = 5
BACK_ORDER = (6, 7, 5, 2, 4, 3, 1, 0)
READ = (
    "branch", "normed_ffn", "grad_gate_up", "hidden", "third", "grad_normed", "mixed_cross", "queries",
    "pairs", "encoder", "second", "normed_cross", "mixed_self", "qkv", "tokens", "normed_self", "gains",
)
STREAMED = ("probs_cross", "probs_self")


def scatter_stages(place, units, whole_slots, rings, finish, wires):
    zi, yi, xi, ci = place.here
    sizes = place.sizes
    full = slice(None)
    arrived, one_a, one_b, two_a, two_b, last = rings
    pending = {}

    def settle(u):
        for copy in pending[u]:
            copy.wait()
        pending[u] = []

    def lanes(u, half=None):
        unit = units[u]
        return (full, pl.ds(0, unit.shape[1] if half is None else unit.half))

    def inner(u, half):
        return (full, pl.ds(half * units[u].half, units[u].half))

    def add(total, target, terms):
        def body(spot, carry):
            value = sum(wide(term(spot)) for term in terms)
            ref, index = target(spot)
            ref[index] = low(value)
            return carry

        lax.fori_loop(0, total, body, 0)

    def slot(u):
        return whole_slots.at[u % whole_slots.shape[0]]

    def first(u):
        source = slot(u).at[(full, full, full, (ci + 1) % 2) + lanes(u)]
        target = arrived.at[(u % RING, full, full, full) + lanes(u)]
        pending[u] = [wires.send(source, target, 3, 1)]

    def second(u):
        settle(u)
        ring, own = u % RING, slot(u)

        def flat(b):
            return (b // (sizes[1] * sizes[2]), (b // sizes[2]) % sizes[1], b % sizes[2])

        add(
            sizes[0] * sizes[1] * sizes[2],
            lambda b: (arrived, (ring,) + flat(b) + lanes(u)),
            [
                lambda b: arrived[(ring,) + flat(b) + lanes(u)],
                lambda b: own[flat(b) + (ci,) + lanes(u)],
            ],
        )
        for half in range(units[u].halves):
            axis, target = (1, one_a) if half == 0 else (2, one_b)
            for step in range(1, sizes[axis]):
                there = place.moved(axis, step)[axis]
                index = (full, there, full) if half == 0 else (full, full, there)
                pending[u].append(
                    wires.send(
                        arrived.at[(ring,) + index + inner(u, half)],
                        target.at[(ring, step - 1, full, full) + lanes(u, 0)],
                        axis,
                        step,
                    )
                )

    def third(u):
        settle(u)
        ring = u % RING
        for half in range(units[u].halves):
            axis, other = (1, 2) if half == 0 else (2, 1)
            one, two = (one_a, two_a) if half == 0 else (one_b, two_b)
            across = sizes[other]

            def mine(b, half=half, across=across):
                middle = (yi, b % across) if half == 0 else (b % across, xi)
                return arrived[(ring, b // across) + middle + inner(u, half)]

            def theirs(b, step=0, one=one, across=across):
                return one[(ring, step, b // across, b % across) + lanes(u, 0)]

            add(
                sizes[0] * across,
                lambda b: (one, (ring, 0, b // across, b % across) + lanes(u, 0)),
                [mine] + [functools.partial(theirs, step=step) for step in range(sizes[axis] - 1)],
            )
            for step in range(1, across):
                there = place.moved(other, step)[other]
                pending[u].append(
                    wires.send(
                        one.at[(ring, 0, full, there) + lanes(u, 0)],
                        two.at[(ring, step - 1, full) + lanes(u, 0)],
                        other,
                        step,
                    )
                )

    def fourth(u):
        settle(u)
        ring = u % RING
        for half in range(units[u].halves):
            axis, here = (2, xi) if half == 0 else (1, yi)
            one, two = (one_a, two_a) if half == 0 else (one_b, two_b)

            def mine(b, one=one, here=here):
                return one[(ring, 0, b, here) + lanes(u, 0)]

            def theirs(b, step=0, two=two):
                return two[(ring, step, b) + lanes(u, 0)]

            add(
                sizes[0],
                lambda b: (two, (ring, 0, b) + lanes(u, 0)),
                [mine] + [functools.partial(theirs, step=step) for step in range(sizes[axis] - 1)],
            )
            for step in range(1, sizes[0]):
                there = place.moved(0, step)[0]
                pending[u].append(
                    wires.send(
                        two.at[(ring, 0, there) + lanes(u, 0)],
                        last.at[(ring, step - 1) + inner(u, half)],
                        0,
                        step,
                    )
                )

    def fifth(u):
        settle(u)
        ring = u % RING
        for half in range(units[u].halves):
            two = two_a if half == 0 else two_b
            value = wide(two[(ring, 0, zi) + lanes(u, 0)])
            for step in range(sizes[0] - 1):
                value = value + wide(last[(ring, step) + inner(u, half)])
            finish(u, half, value)

    return (first, second, third, fourth, fifth)


def backward_kernel(place, units, seqs, *refs):
    weights, refs = refs[:5], refs[5:]
    sources, refs = dict(zip(READ, refs)), refs[len(READ) :]
    probs_from, spread_ids, refs = refs[:2], refs[2], refs[3:]
    grad_tokens, grad_encoder, refs = refs[0], refs[1], refs[2:]
    owned, refs = refs[:8], refs[8:]
    vmem, refs = dict(zip(READ, refs)), refs[len(READ) :]
    probs_cross, probs_self, dx, rounded, grad_mixed, grad_enc, down_grads, diag, gain_grads = refs[:9]
    weight_slots, whole_slots = refs[9:11]
    rings, refs = refs[11:17], refs[17:]
    send_sems, recv_sems, read_sems, probs_sems, weight_sems, out_sems = refs
    place.locate()
    place.greet()
    wires = Wires(place, send_sems, recv_sems)
    rows, width = dx.shape
    slot_rows, enc_rows = rows // seqs, vmem["encoder"].shape[0] // seqs
    count_pairs = width // LANES
    sizes = place.sizes
    norms = vmem["gains"].shape[0]
    hidden_width = vmem["hidden"].shape[0] * CHUNK
    per_z = width // sizes[0]

    def reading(name):
        at = READ.index(name)
        return pltpu.make_async_copy(sources[name], vmem[name], read_sems.at[at])

    for name in READ:
        reading(name).start()
    ready = set()

    def need(*names):
        for name in names:
            if name not in ready:
                reading(name).wait()
                ready.add(name)

    def finish(u, half, value):
        unit = units[u]
        start = unit.start + half * unit.half
        if unit.owner == 6:
            for block in range(unit.half // CHUNK):
                spot = start // CHUNK + block
                at = (spot % 2) * hidden_width + (spot // 2) * CHUNK
                owned[6][:, at : at + CHUNK] = value[:, block * CHUNK : (block + 1) * CHUNK]
        elif unit.owner == 7:
            row = unit.row
            kept = min(value.shape[0], owned[7].shape[0] - row)
            at = half * unit.half
            owned[7][row : row + kept, at : at + unit.half] = value[:kept]
        else:
            owned[unit.owner][:, start : start + unit.half] = value

    driver = Driver(units, scatter_stages(place, units, whole_slots, rings, finish, wires), 1.0)

    wanted = [(4, 0), (1, 0), (1, 1), (3, 0), (2, 0), (0, 0), (0, 1), (0, 2)]
    depth = weight_slots.shape[0]
    state = dict(fetched=0, used=0)

    def fetch(spot):
        which, part = wanted[spot]
        return pltpu.make_async_copy(
            weights[which].at[(slice(None),) * 5 + (pl.ds(part * width, width),)],
            weight_slots.at[spot % depth],
            weight_sems.at[spot % depth],
        )

    def pump():
        while state["fetched"] < min(len(wanted), state["used"] + depth):
            fetch(state["fetched"]).start()
            state["fetched"] += 1

    def weight(spot):
        fetch(spot).wait()
        return lambda z: weight_slots[spot % depth, z].reshape(per_z, width)

    def release():
        state["used"] += 1
        pump()

    pump()

    def weight_grad(u, left, right):
        slot = u % whole_slots.shape[0]

        def columns(spot, carry):
            at = pl.ds(pl.multiple_of(spot * CHUNK, CHUNK), CHUNK)
            moving = right(spot)

            def planes(z, inner):
                piece = left[:, pl.ds(pl.multiple_of(z * per_z, per_z), per_z)]
                block = low(mul(piece, moving, 0, 0))
                whole_slots[slot, z, :, :, :, :, at] = block.reshape(sizes[1:] + (-1, CHUNK))
                return inner

            return lax.fori_loop(0, sizes[0], planes, carry)

        lax.fori_loop(0, units[u].shape[1] // CHUNK, columns, 0)

    def columns_of(ref, base=0):
        return lambda spot: ref[:, pl.ds(pl.multiple_of(base + spot * CHUNK, CHUNK), CHUNK)]

    def norm_back(which, stream, before, last):
        gain = vmem["gains"][which : which + 1]
        step_rows = 64

        def body(step, total):
            at = pl.ds(pl.multiple_of(step * step_rows, step_rows), step_rows)
            value = wide(stream[at, :])
            scale = lax.rsqrt(jnp.mean(value * value, axis=-1, keepdims=True) + 1e-06)
            unit = value * scale
            grad = vmem["grad_normed"][at, :]
            scaled = grad * gain
            result = wide(before[at, :]) + scale * (
                scaled - unit * jnp.mean(scaled * unit, axis=-1, keepdims=True)
            )
            dx[at, :] = result
            if not last:
                rounded[2 - which, at, :] = low(result)
            return total + jnp.sum(grad * unit, axis=0, keepdims=True)

        total = lax.fori_loop(0, rows // step_rows, body, jnp.zeros((1, width), jnp.float32))
        gain_grads[which : which + 1, :] = total

    def through(spot, source, target, add, rounding):
        matrix = weight(spot)

        def body(z, carry):
            at = pl.ds(pl.multiple_of(z * per_z, per_z), per_z)
            value = mul(source[...], matrix(z), 1, 1)
            if add:
                value = value + target[:, at]
            target[:, at] = low(value) if rounding else value
            return carry

        lax.fori_loop(0, sizes[0], body, 0)
        release()

    left = lax.broadcasted_iota(jnp.int32, (1, LANES), 1) < HEAD

    def stack(value):
        zero = jnp.zeros_like(value)
        return jnp.concatenate([jnp.where(left, value, zero), jnp.where(left, zero, value)], axis=0)

    def pair_back(queries, keys, values, probs, grad):
        count = queries.shape[0]
        stacked = stack(grad)
        spread = mul(stacked, values, 1, 1)
        wide_probs = wide(probs)
        product = wide_probs * spread
        scores = low(product - wide_probs * jnp.sum(product, axis=-1, keepdims=True))
        grad_values = low(mul(probs, stacked, 0, 0))
        both = mul(scores, keys)
        grad_queries = low(jnp.where(left, both[:count], both[count:]) * HEAD ** (-0.5))
        grad_keys = low(mul(scores, stack(queries * jnp.bfloat16(HEAD ** (-0.5))), 0, 0))
        return grad_queries, grad_keys, grad_values, scores

    def probs_copy(kind, pair):
        target = (probs_cross, probs_self)[kind]
        return pltpu.make_async_copy(
            probs_from[kind].at[:, pair], target.at[pair % 2], probs_sems.at[2 * kind + pair % 2]
        )

    def cross_back(pair):
        if pair + 1 < count_pairs:
            probs_copy(0, pair + 1).start()
        probs_copy(0, pair).wait()
        lanes = pl.ds(pair * LANES, LANES)

        def body(sequence, carry):
            at = pl.ds(pl.multiple_of(sequence * slot_rows, slot_rows), slot_rows)
            keys = pl.ds(pl.multiple_of(sequence * enc_rows, enc_rows), enc_rows)
            queries, pairs = vmem["queries"], vmem["pairs"]
            grads = pair_back(
                queries[at, lanes],
                pairs[0, keys, lanes],
                pairs[1, keys, lanes],
                probs_cross[pair % 2, sequence],
                grad_mixed[at, lanes],
            )
            queries[at, lanes], pairs[0, keys, lanes], pairs[1, keys, lanes] = grads[:3]
            return carry

        lax.fori_loop(0, seqs, body, 0)

    def self_back(pair):
        if pair + 1 < count_pairs:
            probs_copy(1, pair + 1).start()
        probs_copy(1, pair).wait()
        lanes = pl.ds(pair * LANES, LANES)
        total = 0.0
        for sequence in range(seqs):
            at = pl.ds(sequence * slot_rows, slot_rows)
            qkv = vmem["qkv"]
            grads = pair_back(
                qkv[0, at, lanes],
                qkv[1, at, lanes],
                qkv[2, at, lanes],
                probs_self[pair % 2, sequence],
                grad_mixed[at, lanes],
            )
            qkv[0, at, lanes], qkv[1, at, lanes], qkv[2, at, lanes] = grads[:3]
            total = total + wide(grads[3])
        period = spread_ids.shape[1]
        total = jnp.concatenate(
            [total, jnp.zeros((total.shape[0], period - slot_rows), jnp.float32)], axis=1
        )
        for head in range(2):
            sums = 0.0
            for group in range(slot_rows // 8):
                start = head * slot_rows + group * 8
                piece = total[start : start + 8]
                sums = sums + (pltpu.roll(piece, period - group * 8, 1) if group else piece)
            diag[2 * pair + head] = sums

    chain, produced = [], []

    def then(cost, step):
        chain.append((cost, step))

    def start_ffn():
        need("third", "grad_normed", "gains")
        norm_back(2, vmem["third"], vmem["branch"], False)

    def start_cross():
        probs_copy(0, 0).start()
        through(0, rounded.at[0], grad_mixed, False, True)
        need("queries", "pairs")

    def encoder_back():
        keys, values = weight(1), weight(2)

        def body(z, carry):
            at = pl.ds(pl.multiple_of(z * per_z, per_z), per_z)
            grad_enc[:, at] = mul(vmem["pairs"][0], keys(z), 1, 1) + mul(
                vmem["pairs"][1], values(z), 1, 1
            )
            return carry

        lax.fori_loop(0, sizes[0], body, 0)
        release()
        release()
        pltpu.make_async_copy(grad_enc, grad_encoder, out_sems.at[0]).start()

    def end_cross():
        need("second")
        through(3, vmem["queries"], vmem["grad_normed"], False, False)

    def start_self():
        norm_back(1, vmem["second"], dx, False)

    def self_mixed():
        probs_copy(1, 0).start()
        need("qkv")
        through(4, rounded.at[1], grad_mixed, False, True)

    def self_normed(part):
        through(5 + part, vmem["qkv"].at[part], vmem["grad_normed"], part > 0, False)

    def end_self():
        need("tokens")
        norm_back(0, vmem["tokens"], dx, True)
        pltpu.make_async_copy(dx, grad_tokens, out_sems.at[1]).start()

    then(1.5, start_ffn)
    marks = {}
    marks[5] = len(chain)
    then(1.5, start_cross)
    for pair in range(count_pairs):
        then(3.0, functools.partial(cross_back, pair))
    marks[2] = marks[4] = len(chain)
    then(4.0, encoder_back)
    then(1.5, end_cross)
    then(1.5, start_self)
    marks[3] = len(chain)
    then(1.5, self_mixed)
    for pair in range(count_pairs):
        then(3.0, functools.partial(self_back, pair))
    marks[1] = len(chain)
    for part in range(3):
        then(1.2, functools.partial(self_normed, part))
    then(1.5, end_self)
    marks[0] = len(chain)
    marks[6] = marks[7] = 0

    def pack_grad(u):
        slot = u % whole_slots.shape[0]
        period = spread_ids.shape[1]
        table = 0.0
        for row in range(8):
            part = diag[:, row, :]
            table = table + (pltpu.roll(part, period - row, 1) if row else part)
        spread = spread_ids[...]
        onehot = (lax.broadcasted_iota(jnp.int32, (LANES, period), 0) == spread).astype(jnp.bfloat16)
        high = low(table)
        rel = mul(high, onehot, 1, 1) + mul(low(table - wide(high)), onehot, 1, 1)
        for z in range(sizes[0]):
            for y in range(sizes[1]):
                at = slice((z * sizes[1] + y) * LANES, (z * sizes[1] + y + 1) * LANES)
                top = jnp.concatenate(
                    [gain_grads[:, at], jnp.zeros((HEADS - norms, LANES), jnp.float32)], axis=0
                )
                tile = low(jnp.concatenate([top, rel], axis=0))
                for x in range(sizes[2]):
                    for core in range(sizes[3]):
                        whole_slots[slot, z, y, x, core, :, 0:LANES] = tile

    groups = owned[7].shape[0] // 8

    def down_chunk(spot, carry):
        block = mul(vmem["hidden"][spot], vmem["branch"][...], 0, 0)
        per = CHUNK // 8
        down_grads[pl.ds(spot * per, per)] = low(block.reshape(per, 8, width))
        return carry

    def down_grad(u):
        slot = u % whole_slots.shape[0]
        start = units[u].row // 8

        block_rows = whole_slots.shape[5]

        def body(device, carry):
            piece = down_grads[pl.ds(device * groups + start, block_rows // 8)]
            c, rest = device % sizes[3], device // sizes[3]
            x, rest = rest % sizes[2], rest // sizes[2]
            whole_slots[slot, rest // sizes[1], rest % sizes[1], x, c, :, :] = low(
                wide(piece).reshape(block_rows, width)
            )
            return carry

        lax.fori_loop(0, sizes[0] * sizes[1] * sizes[2] * sizes[3], body, 0)

    def grad_of(u):
        unit = units[u]
        owner = unit.owner
        part = unit.start // width
        if owner == 6:
            need("branch", "normed_ffn", "grad_gate_up")
            base = unit.start // (2 * CHUNK)
            grads = vmem["grad_gate_up"]

            def right(spot):
                lane = pl.multiple_of((spot % 2) * CHUNK, CHUNK)
                return grads[base + spot // 2, :, pl.ds(lane, CHUNK)]

            weight_grad(u, vmem["normed_ffn"], right)
        elif owner == 7:
            if unit.row == 0:
                need("hidden")
                down_grads[down_grads.shape[0] - 8 :] = jnp.zeros((8, 8, width), jnp.bfloat16)
                lax.fori_loop(0, hidden_width // CHUNK, down_chunk, 0)
            down_grad(u)
        elif owner == 5:
            need("mixed_cross")
            weight_grad(u, vmem["mixed_cross"], columns_of(rounded.at[0]))
        elif owner == 2:
            need("encoder")
            weight_grad(u, vmem["encoder"], columns_of(vmem["pairs"].at[part]))
        elif owner == 4:
            need("normed_cross")
            weight_grad(u, vmem["normed_cross"], columns_of(vmem["queries"]))
        elif owner == 3:
            need("mixed_self")
            weight_grad(u, vmem["mixed_self"], columns_of(rounded.at[1]))
        elif owner == 1:
            need("normed_self")
            weight_grad(u, vmem["normed_self"], columns_of(vmem["qkv"].at[part]))
        else:
            pack_grad(u)

    position = 0
    budget = 6.0
    for u, unit in enumerate(units):
        while position < marks[unit.owner]:
            chain[position][1]()
            position += 1
        grad_of(u)
        driver.advance()
        spent = 0.0
        while unit.owner in (6, 7) and position < len(chain) and spent < budget:
            spent += chain[position][0]
            chain[position][1]()
            position += 1
    while not driver.done():
        driver.advance()
    pltpu.make_async_copy(grad_enc, grad_encoder, out_sems.at[0]).wait()
    pltpu.make_async_copy(dx, grad_tokens, out_sems.at[1]).wait()


def backward_all(place, wholes, kept, probs, spread, data, blocks):
    tokens, encoder = data[:2]
    seqs, slot_rows, width = tokens.shape
    rows = seqs * slot_rows
    sources = dict(kept, tokens=tokens.reshape(rows, width), encoder=encoder.reshape(-1, width))
    low_type, wide_type = jnp.bfloat16, jnp.float32
    sizes = place.sizes
    block_rows = blocks[1][0]
    units = []
    for owner in BACK_ORDER:
        if owner == 7:
            height = blocks[7][0] * 8
            for row in range(0, height, block_rows):
                unit = Unit(7, (block_rows, width), 0, width)
                unit.row = row
                units.append(unit)
        else:
            units += make_units(blocks, PIECE, (owner,))
    total = copies_of(units, sizes, True)
    anywhere = pl.BlockSpec(memory_space=pl.ANY)
    inside = pl.BlockSpec(memory_space=pltpu.VMEM)
    down_rows = blocks[7][0] * 8
    owned = [(block[0], block[1]) for block in blocks[:7]] + [(down_rows, width)]
    count = sizes[0] * sizes[1] * sizes[2] * sizes[3]
    size = PIECE // block_rows
    half = size // 2
    rings = [
        sizes[:3] + (block_rows, size),
        (sizes[1] - 1, sizes[0], sizes[2], block_rows, half),
        (sizes[2] - 1, sizes[0], sizes[1], block_rows, half),
        (sizes[2] - 1, sizes[0], block_rows, half),
        (sizes[1] - 1, sizes[0], block_rows, half),
        (sizes[0] - 1, block_rows, size),
    ]
    like = lambda array: pltpu.VMEM(array.shape, array.dtype)
    results = pl.pallas_call(
        functools.partial(backward_kernel, place, units, seqs),
        out_shape=[
            jax.ShapeDtypeStruct((rows, width), wide_type),
            jax.ShapeDtypeStruct((sources["encoder"].shape), wide_type),
        ]
        + [jax.ShapeDtypeStruct(block, wide_type) for block in owned],
        in_specs=[anywhere] * (5 + len(READ) + 2) + [inside],
        out_specs=[anywhere] * 2 + [inside] * len(owned),
        scratch_shapes=[like(sources[name]) for name in READ]
        + [
            pltpu.VMEM((2,) + probs[0].shape[:1] + probs[0].shape[2:], low_type),
            pltpu.VMEM((2,) + probs[1].shape[:1] + probs[1].shape[2:], low_type),
            pltpu.VMEM((rows, width), wide_type),
            pltpu.VMEM((2, rows, width), low_type),
            pltpu.VMEM((rows, width), low_type),
            pltpu.VMEM(sources["encoder"].shape, wide_type),
            pltpu.VMEM((count * blocks[7][0] + 8, 8, width), low_type),
            pltpu.VMEM((HEADS, 8, spread.shape[1]), wide_type),
            pltpu.VMEM(kept["gains"].shape, wide_type),
            pltpu.VMEM((2,) + sizes + (block_rows, width), low_type),
            pltpu.VMEM((2,) + sizes + (block_rows, size), low_type),
        ]
        + [pltpu.VMEM((RING,) + shape, low_type) for shape in rings]
        + [
            pltpu.SemaphoreType.DMA((total,)),
            pltpu.SemaphoreType.DMA((total,)),
            pltpu.SemaphoreType.DMA((len(READ),)),
            pltpu.SemaphoreType.DMA((4,)),
            pltpu.SemaphoreType.DMA((2,)),
            pltpu.SemaphoreType.DMA((2,)),
        ],
        compiler_params=pltpu.CompilerParams(
            collective_id=1, has_side_effects=True, vmem_limit_bytes=63 * 2**20
        ),
        name="backward_all",
    )(*wholes[1:6], *[sources[name] for name in READ], *probs, spread)
    return results[0], results[1], results[2:]


def norm_scale(stream, gain):
    return stream * lax.rsqrt(jnp.mean(stream * stream, axis=-1, keepdims=True) + 1e-06) * gain


def gelu_tanh(values):
    return (
        0.5
        * values
        * (1.0 + jnp.tanh(0.7978845608028654 * (values + 0.044715 * values * values * values)))
    )


def gated(gate_up):
    half_width = gate_up.shape[1] // 2
    return gelu_tanh(gate_up[:, :half_width]) * gate_up[:, half_width:]


def product(spec, left, right):
    return jnp.einsum(spec, left, right, preferred_element_type=jnp.float32)


def attend(queries, key_rows, value_rows, pos_bias, keep_mask):
    scores = product("bihc,bjhc->bhij", queries, key_rows) * HEAD ** (-0.5)
    if pos_bias is not None:
        scores = scores + pos_bias
    masked = jnp.where(keep_mask[:, None], scores, -1e30)
    row_max = jnp.max(masked, axis=-1, keepdims=True)
    powers = jnp.exp(masked - row_max)
    probs = powers / jnp.sum(powers, axis=-1, keepdims=True)
    low_probs = probs.astype(jnp.bfloat16)
    mixed = product("bhij,bjhc->bihc", low_probs, value_rows)
    return mixed.astype(jnp.bfloat16), low_probs


def attend_back(queries, key_rows, value_rows, low_probs, grad_mixed):
    probs = low_probs.astype(jnp.float32)
    grad_values = product("bhij,bihc->bjhc", low_probs, grad_mixed)
    grad_probs = product("bihc,bjhc->bhij", grad_mixed, value_rows)
    grad_scores = (
        probs * (grad_probs - jnp.sum(probs * grad_probs, axis=-1, keepdims=True))
    ).astype(jnp.bfloat16)
    grad_queries = product("bhij,bjhc->bihc", grad_scores, key_rows) * HEAD ** (-0.5)
    grad_keys = product("bhij,bihc->bjhc", grad_scores, queries) * HEAD ** (-0.5)
    return grad_queries, grad_keys, grad_values, grad_scores


def toeplitz(table, size):
    lead = table.shape[:-1]
    row = jnp.concatenate(
        [table[..., ::-1], jnp.broadcast_to(table[..., :1], lead + (size,))], axis=-1
    )
    tiled = jnp.broadcast_to(row[..., None, :], lead + (size, 2 * size)).reshape(lead + (-1,))
    tiled = jnp.concatenate([tiled[..., size - 1 :], row[..., :1]], axis=-1)
    tiled = tiled[..., : size * (2 * size - 1)]
    return tiled.reshape(lead + (size, 2 * size - 1))[..., :size]


def layer(weights, gains, rel_bias, tokens, encoder, cotangent, lengths, enc_lengths, bucket_ids):
    self_qkv, self_out, cross_q, cross_kv, cross_out, ff_in, ff_out = weights
    count, slots, width = tokens.shape
    enc_count = encoder.shape[1]
    bucket_map = toeplitz(bucket_ids, slots).reshape(-1)
    onehot = (lax.iota(jnp.int32, BUCKETS)[:, None] == bucket_map[None, :]).astype(jnp.bfloat16)
    pos_bias = jnp.dot(rel_bias, onehot, preferred_element_type=jnp.float32).reshape(
        HEADS, slots, slots
    )
    row_ids = lax.iota(jnp.int32, slots)
    self_mask = (row_ids[None, None, :] <= row_ids[None, :, None]) & (
        row_ids[None, None, :] < lengths[:, None, None]
    )
    cross_mask = lax.iota(jnp.int32, enc_count)[None, None, :] < enc_lengths[:, None, None]
    enc_rows = encoder.reshape(count * enc_count, width)
    dot = functools.partial(jnp.dot, preferred_element_type=jnp.float32)
    low = lambda value: value.astype(jnp.bfloat16)
    stream = tokens.reshape(count * slots, width).astype(jnp.float32)
    normed_self, back_self = jax.vjp(norm_scale, stream, gains[0])
    normed_self = low(normed_self)
    qkv = low(dot(normed_self, self_qkv)).reshape(count, slots, 3, HEADS, HEAD)
    mixed_self, probs_self = attend(qkv[:, :, 0], qkv[:, :, 1], qkv[:, :, 2], pos_bias, self_mask)
    mixed_self = mixed_self.reshape(count * slots, width)
    second = stream + dot(mixed_self, self_out)
    normed_cross, back_cross = jax.vjp(norm_scale, second, gains[1])
    normed_cross = low(normed_cross)
    queries = low(dot(normed_cross, cross_q)).reshape(count, slots, HEADS, HEAD)
    pairs = low(dot(enc_rows, cross_kv)).reshape(count, enc_count, 2, HEADS, HEAD)
    mixed_cross, probs_cross = attend(queries, pairs[:, :, 0], pairs[:, :, 1], None, cross_mask)
    mixed_cross = mixed_cross.reshape(count * slots, width)
    third = second + dot(mixed_cross, cross_out)
    normed_ffn, back_ffn = jax.vjp(norm_scale, third, gains[2])
    normed_ffn = low(normed_ffn)
    gate_up = dot(normed_ffn, ff_in)
    activated, back_gate = jax.vjp(gated, gate_up)
    hidden = low(activated)
    outcome = third + dot(hidden, ff_out)

    valid = (row_ids[None, :] < lengths[:, None]).astype(jnp.float32)[:, :, None]
    grad_out = (cotangent.astype(jnp.float32) * valid).reshape(count * slots, width)
    branch = low(grad_out)
    grad_ff_out = product("lf,ld->fd", hidden, branch)
    grad_hidden = product("ld,fd->lf", branch, ff_out)
    (grad_gate_up,) = back_gate(grad_hidden)
    grad_gate_up = low(grad_gate_up)
    grad_ff_in = product("ld,lf->df", normed_ffn, grad_gate_up)
    grad_stream, gain_ffn = back_ffn(product("lf,df->ld", grad_gate_up, ff_in))
    grad_third = grad_out + grad_stream
    branch = low(grad_third)
    grad_cross_out = product("le,ld->ed", mixed_cross, branch)
    grad_mixed = low(product("ld,ed->le", branch, cross_out)).reshape(count, slots, HEADS, HEAD)
    grad_queries, grad_keys, grad_values, unused = attend_back(
        queries, pairs[:, :, 0], pairs[:, :, 1], probs_cross, grad_mixed
    )
    grad_query_rows = low(grad_queries.reshape(count * slots, width))
    grad_pair_rows = low(
        jnp.concatenate(
            [
                grad_keys.reshape(count * enc_count, width),
                grad_values.reshape(count * enc_count, width),
            ],
            axis=1,
        )
    )
    grad_cross_q = product("ld,le->de", normed_cross, grad_query_rows)
    grad_cross_kv = product("ed,ef->df", enc_rows, grad_pair_rows)
    grad_enc = product("ef,df->ed", grad_pair_rows, cross_kv)
    grad_stream, gain_cross = back_cross(product("le,de->ld", grad_query_rows, cross_q))
    grad_second = grad_third + grad_stream
    branch = low(grad_second)
    grad_self_out = product("le,ld->ed", mixed_self, branch)
    grad_mixed = low(product("ld,ed->le", branch, self_out)).reshape(count, slots, HEADS, HEAD)
    grad_queries, grad_keys, grad_values, grad_scores = attend_back(
        qkv[:, :, 0], qkv[:, :, 1], qkv[:, :, 2], probs_self, grad_mixed
    )
    score_sums = jnp.sum(grad_scores.astype(jnp.float32), axis=0).reshape(HEADS, slots * slots)
    grad_rel_bias = product("hn,bn->hb", low(score_sums), onehot)
    grad_qkv = low(
        jnp.concatenate(
            [part.reshape(count * slots, width) for part in (grad_queries, grad_keys, grad_values)],
            axis=1,
        )
    )
    grad_self_qkv = product("ld,lf->df", normed_self, grad_qkv)
    grad_stream, gain_self = back_self(product("lf,df->ld", grad_qkv, self_qkv))
    grad_tok = grad_second + grad_stream
    grad_gains = jnp.stack([gain_self, gain_cross, gain_ffn], axis=0)
    grads = (
        grad_self_qkv,
        grad_self_out,
        grad_cross_q,
        grad_cross_kv,
        grad_cross_out,
        grad_ff_in,
        grad_ff_out,
    )
    return (
        outcome.reshape(tokens.shape),
        grad_tok.reshape(tokens.shape),
        grad_enc.reshape(encoder.shape),
        grads,
        grad_gains,
        grad_rel_bias,
    )


AXES = ("dp", "fsdp")


def by_collectives(data, shards):
    whole = lambda shard, axis=0: lax.all_gather(shard, AXES, axis=axis, tiled=True)
    weights = tuple(whole(shard) for shard in shards[:7])
    gains = whole(shards[7], 1).astype(jnp.float32)
    rel_bias = whole(shards[8]).reshape(HEADS, BUCKETS)
    outcome, grad_tok, grad_enc, grads, grad_gains, grad_rel_bias = layer(
        weights, gains, rel_bias, *data
    )
    settle = lambda total, axis=0: lax.psum_scatter(
        total, AXES, scatter_dimension=axis, tiled=True
    )
    return (
        (outcome, grad_tok, grad_enc)
        + tuple(settle(grad) for grad in grads)
        + (settle(grad_gains, 1), settle(grad_rel_bias.reshape(-1)))
    )


def by_kernels(place, data, shards):
    norm_gains, rel_bias = shards[7:]
    count = place.sizes[0] * place.sizes[1] * place.sizes[2] * place.sizes[3]
    me = lax.axis_index(AXES)
    norms, per = norm_gains.shape
    group = LANES // per
    rel_per = rel_bias.shape[0]
    pack = jnp.zeros((PACK, LANES), jnp.bfloat16)
    pack = lax.dynamic_update_slice(pack, norm_gains, (0, (me % group) * per))
    rel_row, rel_column = HEADS + me * rel_per // BUCKETS, (me * rel_per) % BUCKETS
    pack = lax.dynamic_update_slice(pack, rel_bias.reshape(1, rel_per), (rel_row, rel_column))
    ff_rows, width = shards[6].shape
    ff_shape = (ff_rows // 8, 8, width)
    self_qkv, self_out, cross_q, cross_kv, cross_out, ff_in, ff_out = shards[:7]
    chunks = ff_in.shape[1] // (2 * CHUNK)
    laced = ff_in.reshape(-1, 2, chunks, CHUNK).transpose(0, 2, 1, 3).reshape(ff_in.shape)
    sent = (pack, self_qkv, cross_kv, self_out, cross_q, cross_out, laced, ff_out.reshape(ff_shape))
    blocks = [piece.shape for piece in sent]
    bucket_ids = data[5]
    spread = jnp.concatenate(
        [bucket_ids[:1], jnp.broadcast_to(bucket_ids[:1], bucket_ids.shape), bucket_ids[:0:-1]]
    )[None]
    wholes, outcome, kept = forward_all(place, sent, *data[:5], spread, norms)
    grad_tok, grad_enc, sums = backward_all(
        place,
        wholes,
        kept,
        (kept["probs_cross"], kept["probs_self"]),
        spread,
        data,
        blocks,
    )
    packed, g_qkv, g_kv, g_so, g_cq, g_co, g_in, g_out = sums
    owned = [g_qkv, g_so, g_cq, g_kv, g_co, g_in, g_out]
    own_gains = lax.dynamic_slice(packed, (0, (me % group) * per), (norms, per))
    own_rel = lax.dynamic_slice(packed, (rel_row, rel_column), (1, rel_per)).reshape(-1)
    shaped = (
        outcome.reshape(data[0].shape),
        grad_tok.reshape(data[0].shape),
        grad_enc.reshape(data[1].shape),
    )
    return shaped + tuple(owned) + (own_gains, own_rel)


def on_device(place, *args):
    data, shards = args[:6], args[6:]
    per = shards[7].shape[1]
    regular = all(shard.shape[0] % 16 == 0 for shard in shards[:6])
    if regular and shards[6].shape[0] % 8 == 0 and LANES % per == 0:
        return by_kernels(place, data, shards)
    return by_collectives(data, shards)


def solution(mesh):
    rows = P(AXES, None, None)
    flat = P(AXES)
    matrix = P(AXES, None)
    split = P(None, AXES)
    place = Place(mesh.shape["dp"], mesh.shape["fsdp"])
    return jax.shard_map(
        functools.partial(on_device, place),
        mesh=mesh,
        in_specs=(rows, rows, rows, flat, flat, P()) + (matrix,) * 7 + (split, flat),
        out_specs=(rows, rows, rows) + (matrix,) * 7 + (split, flat),
        check_vma=False,
    )
```

```python
import functools

import jax
import jax.numpy as jnp
from jax import lax
from jax.experimental import pallas as pl
from jax.experimental.pallas import tpu as pltpu
from jax.sharding import PartitionSpec as P

HEADS = 16
HEAD = 64
BUCKETS = 32
PACK = 32
LANES = 128
PIECE = 32 * 1024

MESH = pl.DeviceIdType.MESH


class Place:
    def __init__(self, dp, fsdp):
        self.sizes = (dp // 2, 2, fsdp // 2, 2)

    def locate(self):
        row, column = lax.axis_index("dp"), lax.axis_index("fsdp")
        sizes = self.sizes
        self.here = (row // sizes[1], row % sizes[1], column // sizes[3], column % sizes[3])

    def moved(self, axis, step):
        coords = list(self.here)
        coords[axis] = (coords[axis] + step) % self.sizes[axis]
        return coords

    def device(self, coords):
        return (coords[0] * self.sizes[1] + coords[1], coords[2] * self.sizes[3] + coords[3])

    def peers(self):
        return [(axis, step) for axis in range(4) for step in range(1, self.sizes[axis])]

    def greet(self):
        barrier = pltpu.get_barrier_semaphore()
        for axis, step in self.peers():
            pl.semaphore_signal(
                barrier, inc=1, device_id=self.device(self.moved(axis, step)), device_id_type=MESH
            )
        pl.semaphore_wait(barrier, len(self.peers()))


def split_lanes(width, parity):
    if width == 8 * LANES:
        more, less = (4 - parity) * LANES, (3 + parity) * LANES
        third = ((2, 1, 0), (1, 2, 0))[parity]
        return ((0, more, (0, 2, 1)), (more, less, (0, 1, 2)), (7 * LANES, LANES, third))
    if width % (2 * LANES) == 0:
        return ((0, width // 2, (0, 2, 1)), (width // 2, width // 2, (0, 1, 2)))
    return ((0, width, (0, 2, 1)),)


class Unit:
    def __init__(self, owner, block, start, count, parity=0):
        self.owner, self.start, self.count = owner, start, count
        self.grouped = len(block) == 3
        self.shape = (count,) + block[1:] if self.grouped else (block[0], count)
        self.paths = split_lanes(self.shape[-1], parity)

    def part(self, start=0, size=None):
        size = self.shape[-1] if size is None else size
        if self.grouped:
            return (pl.ds(self.start, self.count), slice(None), pl.ds(start, size))
        return (slice(None), pl.ds(self.start + start, size))


def make_units(blocks, piece, order, before=0):
    units = []
    for owner in order:
        block = blocks[owner]
        total, most = (block[0], piece // 8 // block[2] or 1) if len(block) == 3 else (block[1], piece // block[0])
        start = 0
        while start < total:
            count = min(most, total - start)
            units.append(Unit(owner, block, start, count, (before + len(units)) % 2))
            start += count
    return units


class Wires:
    def __init__(self, place, send_sems, recv_sems):
        self.place, self.send_sems, self.recv_sems = place, send_sems, recv_sems
        self.started = []

    def send(self, source, target, axis, step):
        spot = len(self.started)
        copy = pltpu.make_async_remote_copy(
            src_ref=source,
            dst_ref=target,
            send_sem=self.send_sems.at[spot],
            recv_sem=self.recv_sems.at[spot],
            device_id=self.place.device(self.place.moved(axis, step)),
            device_id_type=MESH,
        )
        copy.start()
        self.started.append(copy)
        return copy

    def along(self, axis, source, target):
        return [
            self.send(source, target, axis, step) for step in range(1, self.place.sizes[axis])
        ]

    def finish(self):
        for copy in self.started:
            copy.wait_send()


def gather_stages(place, units, shards, wholes, wires, local_sems):
    full = slice(None)
    pending = {}

    def settle(u):
        for copy in pending[u]:
            copy.wait_recv()
        pending[u] = []

    def first(u):
        unit = units[u]
        shard, whole = shards[unit.owner], wholes[unit.owner]
        own = pltpu.make_async_copy(
            shard.at[unit.part()], whole.at[place.here + unit.part()], local_sems.at[u]
        )
        own.start()
        pending[u] = [own]
        for start, size, axes in unit.paths:
            part = unit.part(start, size)
            pending[u] += wires.along(axes[0], shard.at[part], whole.at[place.here + part])

    def later(u, stage):
        if stage == 1:
            pending[u].pop(0).wait()
        settle(u)
        unit = units[u]
        for start, size, axes in unit.paths:
            index = tuple(
                full if axis in axes[:stage] else place.here[axis] for axis in range(3)
            ) + (place.here[3],)
            ref = wholes[unit.owner].at[index + unit.part(start, size)]
            pending[u] += wires.along(axes[stage], ref, ref)

    def across(u):
        settle(u)
        unit = units[u]
        ref = wholes[unit.owner].at[(full, full, full, place.here[3]) + unit.part()]
        pending[u] = wires.along(3, ref, ref)

    return (
        first,
        functools.partial(later, stage=1),
        functools.partial(later, stage=2),
        across,
        settle,
    )


def copies_of(units, sizes):
    return sum(1 + len(unit.paths) * (sizes[0] + sizes[1] + sizes[2] - 3) for unit in units)


def mul(left, right, left_dim=1, right_dim=0):
    return lax.dot_general(
        left, right, (((left_dim,), (right_dim,)), ((), ())), preferred_element_type=jnp.float32
    )


def low(value):
    return value.astype(jnp.bfloat16)


def wide(value):
    return value.astype(jnp.float32)


def rms_rows(source, target, gain, rows=64):
    def body(step, carry):
        at = pl.ds(pl.multiple_of(step * rows, rows), rows)
        value = wide(source[at, :])
        scale = lax.rsqrt(jnp.mean(value * value, axis=-1, keepdims=True) + 1e-06)
        target[at, :] = low(value * scale * gain)
        return carry

    lax.fori_loop(0, source.shape[0] // rows, body, 0)


def tiles(total, size, body):
    def step(spot, carry):
        body(pl.ds(pl.multiple_of(spot * size, size), size))
        return carry

    lax.fori_loop(0, total // size, step, 0)


def flat_rows(value):
    return value.reshape(-1, value.shape[-1])


def attend_pair(queries, key_rows, value_rows, bias, mask):
    rows = queries.shape[0]
    left = lax.broadcasted_iota(jnp.int32, (1, LANES), 1) < HEAD
    zero = jnp.zeros_like(queries)
    scaled = queries * jnp.bfloat16(HEAD ** (-0.5))
    stacked = jnp.concatenate(
        [jnp.where(left, scaled, zero), jnp.where(left, zero, scaled)], axis=0
    )
    scores = mul(stacked, key_rows, 1, 1)
    if bias is not None:
        scores = scores + bias
    scores = jnp.where(mask, scores, -1e30)
    powers = jnp.exp(scores - jnp.max(scores, axis=-1, keepdims=True))
    probs = low(powers / jnp.sum(powers, axis=-1, keepdims=True))
    none = jnp.zeros_like(value_rows)
    mixed = mul(probs[:rows], jnp.where(left, value_rows, none)) + mul(
        probs[rows:], jnp.where(left, none, value_rows)
    )
    return probs, low(mixed)


class Driver:
    def __init__(self, units, stages, lead):
        self.units, self.stages, self.lead = units, stages, lead
        self.tick, self.debt = 0, 0.0

    def done(self):
        return self.tick >= len(self.units) + len(self.stages) - 1

    def settled(self):
        return self.tick - len(self.stages)

    def advance(self):
        for lag, stage in enumerate(self.stages):
            if 0 <= self.tick - lag < len(self.units):
                stage(self.tick - lag)
        self.tick += 1

    def until(self, unit):
        while self.settled() < unit:
            self.advance()

    def spent(self, cost):
        self.debt += cost
        while self.debt >= self.lead:
            self.debt -= self.lead
            if not self.done():
                self.advance()


KEPT = (
    "normed_self", "qkv", "probs_self", "mixed_self", "second", "normed_cross", "queries", "pairs",
    "probs_cross", "mixed_cross", "third", "normed_ffn", "branch", "hidden", "grad_gate_up",
    "grad_normed", "gains",
)
CHUNK = 256
ORDER = (0, 1, 2, 3, 4, 5, 7, 6)


def forward_kernel(place, units, count, seqs, *refs):
    shards, refs = refs[:count], refs[count:]
    tokens, encoder, cotangent, lengths, enc_lengths, spread_ids = refs[:6]
    wholes, refs = refs[6 : 6 + count], refs[6 + count :]
    outcome, refs = refs[0], refs[1:]
    stored, refs = refs[: len(KEPT)], refs[len(KEPT) :]
    vmem, refs = dict(zip(KEPT, refs)), refs[len(KEPT) :]
    bias_rows, slots, raw_out, ff_out, pack = refs[:5]
    send_sems, recv_sems, local_sems, fetch_sems, keep_sems = refs[5:]
    place.locate()
    place.greet()
    wires = Wires(place, send_sems, recv_sems)
    driver = Driver(units, gather_stages(place, units, shards, wholes, wires, local_sems), 5.0)
    rows, width = tokens.shape
    slot_rows, enc_rows = rows // seqs, encoder.shape[0] // seqs
    pairs_of_heads = width // LANES
    norms = vmem["gains"].shape[0]
    keeping = []

    def keep(name):
        copy = pltpu.make_async_copy(
            vmem[name], stored[KEPT.index(name)], keep_sems.at[KEPT.index(name)]
        )
        copy.start()
        keeping.append(copy)

    first_of = {}
    for u, unit in enumerate(units):
        first_of.setdefault(unit.owner, u)
    last_of = {unit.owner: u for u, unit in enumerate(units)}
    slotted = [u for u, unit in enumerate(units) if unit.owner not in (0, 7)]
    state = dict(fetched=0, used=0, raw=False)
    depth = slots.shape[0]

    def fetch(u):
        unit = units[u]
        spot = slotted.index(u) % depth
        return pltpu.make_async_copy(
            wholes[unit.owner].at[(slice(None),) * 4 + unit.part()],
            slots.at[(spot,) + (slice(None),) * 5 + (pl.ds(0, unit.shape[1]),)],
            fetch_sems.at[spot],
        )

    def pump():
        while (
            state["fetched"] < len(slotted)
            and slotted[state["fetched"]] <= driver.settled()
            and state["fetched"] < state["used"] + depth
        ):
            fetch(slotted[state["fetched"]]).start()
            state["fetched"] += 1
        if not state["raw"] and driver.settled() >= last_of[7]:
            state["raw"] = True
            raw_copy().start()

    def raw_copy():
        return pltpu.make_async_copy(wholes[7], raw_out, fetch_sems.at[depth])

    def spent(cost):
        driver.spent(cost)
        pump()

    def weight(u):
        driver.until(u)
        pump()
        fetch(u).wait()
        spot = slotted.index(u) % depth
        size = units[u].shape[1]
        return lambda: slots[spot, :, :, :, :, :, 0:size].reshape(width, size)

    def release():
        state["used"] += 1
        pump()

    def project(source, u, target, cost):
        matrix = weight(u)
        target[...] = low(mul(source[...], matrix()))
        release()
        spent(cost)

    def residual(source, u, before, target, cost):
        matrix = weight(u)
        target[...] = wide(before[...]) + mul(source[...], matrix())
        release()
        spent(cost)

    driver.until(0)
    copy = pltpu.make_async_copy(wholes[0], pack, fetch_sems.at[depth + 1])
    copy.start()
    copy.wait()
    packs = wide(pack[...]).reshape(width // LANES, -1, PACK, LANES)
    summed = jnp.sum(packs, axis=1)
    for group in range(summed.shape[0]):
        vmem["gains"][:, group * LANES : (group + 1) * LANES] = summed[group, :norms]
    table = low(jnp.sum(summed, axis=0)[HEADS:, :BUCKETS])
    spread = spread_ids[...]
    onehot = (lax.broadcasted_iota(jnp.int32, (BUCKETS, spread.shape[1]), 0) == spread).astype(
        jnp.bfloat16
    )
    bias_rows[...] = mul(table, onehot)
    keep("gains")
    rms_rows(tokens, vmem["normed_self"], vmem["gains"][0:1])
    keep("normed_self")

    for sequence in range(seqs):
        at = pl.ds(sequence * slot_rows, slot_rows)
        valid = lax.broadcasted_iota(jnp.int32, (slot_rows, 1), 0) < lengths[sequence]
        vmem["branch"][at, :] = low(jnp.where(valid, wide(cotangent[at, :]), 0.0))
    keep("branch")

    for part in range(3):
        project(vmem["normed_self"], first_of[1] + part, vmem["qkv"].at[part], 1.5)
    keep("qkv")
    for part in range(2):
        project(encoder, first_of[2] + part, vmem["pairs"].at[part], 2.5)
    keep("pairs")

    def self_pair(pair, carry):
        lanes = pl.ds(pl.multiple_of(pair * LANES, LANES), LANES)
        row = lax.broadcasted_iota(jnp.int32, (slot_rows, slot_rows), 0)
        column = lax.broadcasted_iota(jnp.int32, (slot_rows, slot_rows), 1)
        period = bias_rows.shape[1]
        bias = jnp.concatenate(
            [
                pltpu.roll(
                    jnp.broadcast_to(bias_rows[2 * pair + head, :][None], (slot_rows, period)),
                    0,
                    1,
                    stride=1,
                    stride_axis=0,
                )[:, :slot_rows]
                for head in range(2)
            ],
            axis=0,
        )
        for sequence in range(seqs):
            at = pl.ds(sequence * slot_rows, slot_rows)
            mask = (column <= row) & (column < lengths[sequence])
            probs, mixed = attend_pair(
                vmem["qkv"][0, at, lanes],
                vmem["qkv"][1, at, lanes],
                vmem["qkv"][2, at, lanes],
                bias,
                jnp.concatenate([mask, mask], axis=0),
            )
            vmem["probs_self"][sequence, pair] = probs
            vmem["mixed_self"][at, lanes] = mixed
        return carry

    for pair in range(0, pairs_of_heads, 2):
        lax.fori_loop(pair, pair + 2, self_pair, 0)
        spent(3.0)
    keep("probs_self")
    keep("mixed_self")
    residual(vmem["mixed_self"], first_of[3], tokens, vmem["second"], 1.0)
    keep("second")
    rms_rows(vmem["second"], vmem["normed_cross"], vmem["gains"][1:2])
    keep("normed_cross")
    project(vmem["normed_cross"], first_of[4], vmem["queries"], 2.0)
    keep("queries")

    def cross_pair(pair, carry):
        lanes = pl.ds(pl.multiple_of(pair * LANES, LANES), LANES)
        column = lax.broadcasted_iota(jnp.int32, (1, enc_rows), 1)
        for sequence in range(seqs):
            at = pl.ds(sequence * slot_rows, slot_rows)
            keys = pl.ds(sequence * enc_rows, enc_rows)
            probs, mixed = attend_pair(
                vmem["queries"][at, lanes],
                vmem["pairs"][0, keys, lanes],
                vmem["pairs"][1, keys, lanes],
                None,
                column < enc_lengths[sequence],
            )
            vmem["probs_cross"][sequence, pair] = probs
            vmem["mixed_cross"][at, lanes] = mixed
        return carry

    for pair in range(0, pairs_of_heads, 2):
        lax.fori_loop(pair, pair + 2, cross_pair, 0)
        spent(4.0)
    keep("probs_cross")
    keep("mixed_cross")
    residual(vmem["mixed_cross"], first_of[5], vmem["second"], vmem["third"], 1.0)
    keep("third")
    rms_rows(vmem["third"], vmem["normed_ffn"], vmem["gains"][2:3])
    keep("normed_ffn")

    driver.until(last_of[7])
    pump()
    raw_copy().wait()
    sizes = place.sizes
    joined = 2 * raw_out.shape[4] * 8

    def unpack(step, carry):
        at = (step // (sizes[1] * sizes[2]), (step // sizes[2]) % sizes[1], step % sizes[2])
        ff_out[pl.ds(pl.multiple_of(step * joined, 16), joined), :] = low(
            wide(raw_out[at]).reshape(joined, width)
        )
        return carry

    lax.fori_loop(0, sizes[0] * sizes[1] * sizes[2], unpack, 0)
    spent(3.0)
    outcome[...] = vmem["third"][...]
    vmem["grad_normed"][...] = jnp.zeros_like(vmem["grad_normed"])

    def activate(spot, gate_up, grad_hidden, chunk):
        gate = gate_up[:, 2 * chunk * CHUNK : (2 * chunk + 1) * CHUNK]
        up = gate_up[:, (2 * chunk + 1) * CHUNK : (2 * chunk + 2) * CHUNK]
        grad = grad_hidden[:, chunk * CHUNK : (chunk + 1) * CHUNK]
        square = gate * gate
        curve = jnp.tanh(0.7978845608028654 * gate * (1.0 + 0.044715 * square))
        half = 0.5 * (1.0 + curve)
        gelu = gate * half
        slope = half + 0.5 * gate * (1.0 - curve * curve) * (
            0.7978845608028654 * (1.0 + 3 * 0.044715 * square)
        )
        hidden, grads = vmem["hidden"], vmem["grad_gate_up"]
        hidden[spot, :, chunk * CHUNK : (chunk + 1) * CHUNK] = low(gelu * up)
        grads[spot, :, 2 * chunk * CHUNK : (2 * chunk + 1) * CHUNK] = low(grad * up * slope)
        grads[spot, :, (2 * chunk + 1) * CHUNK : (2 * chunk + 2) * CHUNK] = low(grad * gelu)

    for u in range(first_of[6], last_of[6] + 1):
        matrix = weight(u)
        spot, size = u - first_of[6], units[u].shape[1]
        down = slice(units[u].start // 2, (units[u].start + size) // 2)
        gate_up = mul(vmem["normed_ffn"][...], matrix())
        grad_hidden = mul(vmem["branch"][...], ff_out[down, :], 1, 1)
        for chunk in range(size // (2 * CHUNK)):
            activate(spot, gate_up, grad_hidden, chunk)
        spent(5.0)
        vmem["grad_normed"][...] += mul(vmem["grad_gate_up"][spot, :, 0:size], matrix(), 1, 1)
        release()
        outcome[...] += mul(vmem["hidden"][spot, :, 0 : size // 2], ff_out[down, :])
    for name in ("hidden", "grad_gate_up", "grad_normed"):
        keep(name)
    while not driver.done():
        driver.advance()
    for copy in keeping:
        copy.wait()
    wires.finish()


def kept_shapes(seqs, slot_rows, enc_rows, width, hidden, norms, piece):
    steps = -(-2 * hidden // piece)
    rows = seqs * slot_rows
    pairs = width // LANES
    low_type, wide_type = jnp.bfloat16, jnp.float32
    return {
        "normed_self": ((rows, width), low_type),
        "qkv": ((3, rows, width), low_type),
        "probs_self": ((seqs, pairs, 2 * slot_rows, slot_rows), low_type),
        "mixed_self": ((rows, width), low_type),
        "second": ((rows, width), wide_type),
        "normed_cross": ((rows, width), low_type),
        "queries": ((rows, width), low_type),
        "pairs": ((2, seqs * enc_rows, width), low_type),
        "probs_cross": ((seqs, pairs, 2 * slot_rows, enc_rows), low_type),
        "mixed_cross": ((rows, width), low_type),
        "third": ((rows, width), wide_type),
        "normed_ffn": ((rows, width), low_type),
        "branch": ((rows, width), low_type),
        "hidden": ((steps, rows, piece // 2), low_type),
        "grad_gate_up": ((steps, rows, piece), low_type),
        "grad_normed": ((rows, width), wide_type),
        "gains": ((norms, width), wide_type),
    }


def forward_all(place, shards, tokens, encoder, cotangent, lengths, enc_lengths, spread, norms):
    blocks = [shard.shape for shard in shards]
    units = make_units(blocks, PIECE, ORDER)
    total = copies_of(units, place.sizes)
    anywhere = pl.BlockSpec(memory_space=pl.ANY)
    inside = pl.BlockSpec(memory_space=pltpu.VMEM)
    scalars = pl.BlockSpec(memory_space=pltpu.SMEM)
    seqs, slot_rows, width = tokens.shape
    rows = seqs * slot_rows
    hidden = blocks[6][1] // 2
    piece = PIECE // blocks[1][0]
    kept = kept_shapes(seqs, slot_rows, encoder.shape[1], width, hidden, norms, piece)
    depth = 3
    results = pl.pallas_call(
        functools.partial(forward_kernel, place, units, len(blocks), seqs),
        out_shape=[jax.ShapeDtypeStruct(place.sizes + block, jnp.bfloat16) for block in blocks]
        + [jax.ShapeDtypeStruct((rows, width), jnp.float32)]
        + [jax.ShapeDtypeStruct(*kept[name]) for name in KEPT],
        in_specs=[anywhere] * len(blocks) + [inside] * 3 + [scalars] * 2 + [inside],
        out_specs=[anywhere] * len(blocks) + [inside] + [anywhere] * len(KEPT),
        scratch_shapes=[pltpu.VMEM(*kept[name]) for name in KEPT]
        + [
            pltpu.VMEM((HEADS, 2 * slot_rows), jnp.float32),
            pltpu.VMEM((depth,) + place.sizes + (blocks[1][0], PIECE // blocks[1][0]), jnp.bfloat16),
            pltpu.VMEM(place.sizes + blocks[7], jnp.bfloat16),
            pltpu.VMEM((hidden, width), jnp.bfloat16),
            pltpu.VMEM(place.sizes + blocks[0], jnp.bfloat16),
            pltpu.SemaphoreType.DMA((total,)),
            pltpu.SemaphoreType.DMA((total,)),
            pltpu.SemaphoreType.DMA((len(units),)),
            pltpu.SemaphoreType.DMA((depth + 2,)),
            pltpu.SemaphoreType.DMA((len(KEPT),)),
        ],
        compiler_params=pltpu.CompilerParams(
            collective_id=0, has_side_effects=True, vmem_limit_bytes=63 * 2**20
        ),
        name="forward_all",
    )(
        *shards,
        tokens.reshape(rows, width),
        encoder.reshape(-1, width),
        cotangent.reshape(rows, width),
        lengths,
        enc_lengths,
        spread,
    )
    count = len(blocks)
    return results[:count], results[count], dict(zip(KEPT, results[count + 1 :]))


RING = 5
BACK_ORDER = (6, 7, 5, 2, 4, 3, 1, 0)
READ = (
    "branch", "normed_ffn", "grad_gate_up", "third", "grad_normed", "gains", "mixed_cross", "queries",
    "pairs", "hidden", "encoder", "second", "normed_cross", "mixed_self", "qkv", "tokens", "normed_self",
)


def ring_shapes(sizes, block_rows, width):
    shapes = {}
    for parity in range(2):
        for start, lanes, axes in split_lanes(width, parity):
            for hop in range(3):
                axis = axes[2 - hop]
                rest = tuple(sizes[other] for other in range(3) if other in axes[: 2 - hop])
                shape = (sizes[axis] - 1,) + rest + (block_rows,)
                key = (axes, hop)
                old = shapes.get(key, (0,))[-1]
                shapes[key] = shape + (max(lanes, old),)
    return shapes


def scatter_stages(place, units, whole_slots, arrived, rings, finish, wires):
    sizes, full = place.sizes, slice(None)
    here = place.here
    pending = {}

    def settle(u):
        for copy in pending[u]:
            copy.wait()
        pending[u] = []

    def lanes(u):
        return (full, pl.ds(0, units[u].shape[1]))

    def slot(u):
        return whole_slots.at[u % whole_slots.shape[0]]

    def spread(b, axes):
        coords = {}
        for axis in reversed(axes):
            coords[axis] = b % sizes[axis]
            b = b // sizes[axis]
        return coords

    def count(axes):
        total = 1
        for axis in axes:
            total *= sizes[axis]
        return total

    def held(u, path, hop):
        start, size, axes = path
        ring = u % RING
        if hop == 0:
            return lambda at: (arrived, (ring,) + tuple(at[a] for a in range(3)) + (full, pl.ds(start, size)))
        rest = sorted(axes[: 3 - hop])
        ref = rings[axes, hop - 1]
        return lambda at: (ref, (ring, 0) + tuple(at[a] for a in rest) + (full, pl.ds(0, size)))

    def first(u):
        source = slot(u).at[(full, full, full, (here[3] + 1) % 2) + lanes(u)]
        target = arrived.at[(u % RING, full, full, full) + lanes(u)]
        pending[u] = [wires.send(source, target, 3, 1)]

    def pass_on(u, hop):
        for path in units[u].paths:
            start, size, axes = path
            axis = axes[2 - hop]
            where = held(u, path, hop)
            ref = rings[axes, hop]
            rest = sorted(axes[: 2 - hop])
            for step in range(1, sizes[axis]):
                at = {a: full for a in rest}
                at[axis] = place.moved(axis, step)[axis]
                source, index = where(at)
                target = ref.at[
                    (u % RING, step - 1) + (full,) * len(rest) + (full, pl.ds(0, size))
                ]
                pending[u].append(wires.send(source.at[index], target, axis, step))

    def merge(u, path, hop):
        start, size, axes = path
        axis = axes[2 - hop]
        rest = sorted(axes[: 2 - hop])
        before, after = held(u, path, hop), held(u, path, hop + 1)
        ref = rings[axes, hop]

        def body(b, carry):
            at = spread(b, rest)
            source, index = before({**at, axis: here[axis]})
            value = wide(source[index])
            for step in range(sizes[axis] - 1):
                value = value + wide(
                    ref[(u % RING, step) + tuple(at[a] for a in rest) + (full, pl.ds(0, size))]
                )
            if hop == 2:
                finish(u, start, size, value)
            else:
                target, index = after(at)
                target[index] = low(value)
            return carry

        if hop == 2:
            body(0, 0)
        else:
            lax.fori_loop(0, count(rest), body, 0)

    def second(u):
        settle(u)
        ring, own = u % RING, slot(u)

        def body(b, carry):
            at = spread(b, (0, 1, 2))
            index = tuple(at[a] for a in range(3))
            target = (ring,) + index + lanes(u)
            arrived[target] = low(wide(arrived[target]) + wide(own[index + (here[3],) + lanes(u)]))
            return carry

        lax.fori_loop(0, count((0, 1, 2)), body, 0)
        pass_on(u, 0)

    def later(u, hop):
        settle(u)
        for path in units[u].paths:
            merge(u, path, hop)
        if hop < 2:
            pass_on(u, hop + 1)

    return (first, second) + tuple(functools.partial(later, hop=hop) for hop in range(3))


def backward_kernel(place, units, seqs, ring_keys, *refs):
    weights, refs = refs[:5], refs[5:]
    sources, refs = dict(zip(READ, refs)), refs[len(READ) :]
    probs_from, spread_ids, refs = refs[:2], refs[2], refs[3:]
    grad_tokens, grad_encoder, refs = refs[0], refs[1], refs[2:]
    owned, refs = refs[:8], refs[8:]
    vmem, refs = dict(zip(READ, refs)), refs[len(READ) :]
    probs_cross, probs_self, dx, rounded, grad_mixed, grad_enc, down_grads, diag, gain_grads = refs[:9]
    weight_slots, whole_slots, arrived = refs[9:12]
    refs = refs[12:]
    rings = dict(zip(ring_keys, refs))
    refs = refs[len(ring_keys) :]
    send_sems, recv_sems, read_sems, probs_sems, weight_sems, out_sems = refs
    place.locate()
    place.greet()
    wires = Wires(place, send_sems, recv_sems)
    rows, width = dx.shape
    slot_rows, enc_rows = rows // seqs, vmem["encoder"].shape[0] // seqs
    count_pairs = width // LANES
    sizes = place.sizes
    norms = vmem["gains"].shape[0]
    hidden_width = owned[6].shape[1] // 2

    def reading(name):
        at = READ.index(name)
        return pltpu.make_async_copy(sources[name], vmem[name], read_sems.at[at])

    ready, begun = set(), [0]

    def begin(name):
        while begun[0] <= READ.index(name):
            reading(READ[begun[0]]).start()
            begun[0] += 1

    def need(*names):
        for name in names:
            if name not in ready:
                begin(name)
                reading(name).wait()
                ready.add(name)

    begin("grad_gate_up")

    def finish(u, lane, size, value):
        unit = units[u]
        start = unit.start + lane
        if unit.owner == 6:
            for at in range(start, start + size, LANES):
                spot, rest = at // CHUNK, at % CHUNK
                to = (spot % 2) * hidden_width + (spot // 2) * CHUNK + rest
                owned[6][:, to : to + LANES] = value[:, at - start : at - start + LANES]
        elif unit.owner == 7:
            kept = min(value.shape[0], owned[7].shape[0] - unit.row)
            owned[7][unit.row : unit.row + kept, lane : lane + size] = value[:kept]
        else:
            owned[unit.owner][:, start : start + size] = value

    driver = Driver(units, scatter_stages(place, units, whole_slots, arrived, rings, finish, wires), 1.0)

    wanted = [(4, 0), (1, 0), (1, 1), (3, 0), (2, 0), (0, 0), (0, 1), (0, 2)]
    depth = weight_slots.shape[0]
    state = dict(fetched=0, used=0)

    def fetch(spot):
        which, part = wanted[spot]
        return pltpu.make_async_copy(
            weights[which].at[(slice(None),) * 5 + (pl.ds(part * width, width),)],
            weight_slots.at[spot % depth],
            weight_sems.at[spot % depth],
        )

    def pump():
        while state["fetched"] < min(len(wanted), state["used"] + depth):
            fetch(state["fetched"]).start()
            state["fetched"] += 1

    def weight(spot):
        fetch(spot).wait()
        return lambda: weight_slots[spot % depth].reshape(width, width)

    def release():
        state["used"] += 1
        pump()

    pump()

    def weight_grad(u, name, right):
        need(name)
        size = units[u].shape[1]
        block = low(mul(vmem[name][...], right, 0, 0))
        whole_slots[u % whole_slots.shape[0], :, :, :, :, :, 0:size] = block.reshape(
            sizes + (-1, size)
        )

    def norm_back(which, stream, before, last):
        gain = vmem["gains"][which : which + 1]
        step_rows = 64

        def body(step, total):
            at = pl.ds(pl.multiple_of(step * step_rows, step_rows), step_rows)
            value = wide(stream[at, :])
            scale = lax.rsqrt(jnp.mean(value * value, axis=-1, keepdims=True) + 1e-06)
            unit = value * scale
            grad = vmem["grad_normed"][at, :]
            scaled = grad * gain
            result = wide(before[at, :]) + scale * (
                scaled - unit * jnp.mean(scaled * unit, axis=-1, keepdims=True)
            )
            dx[at, :] = result
            if not last:
                rounded[2 - which, at, :] = low(result)
            return total + jnp.sum(grad * unit, axis=0, keepdims=True)

        total = lax.fori_loop(0, rows // step_rows, body, jnp.zeros((1, width), jnp.float32))
        gain_grads[which : which + 1, :] = total

    def through(spot, source, target, add, rounding):
        value = mul(source[...], weight(spot)(), 1, 1)
        if add:
            value = value + target[...]
        target[...] = low(value) if rounding else value
        release()

    left = lax.broadcasted_iota(jnp.int32, (1, LANES), 1) < HEAD

    def stack(value):
        zero = jnp.zeros_like(value)
        return jnp.concatenate([jnp.where(left, value, zero), jnp.where(left, zero, value)], axis=0)

    def pair_back(queries, keys, values, probs, grad):
        count = queries.shape[0]
        stacked = stack(grad)
        spread = mul(stacked, values, 1, 1)
        wide_probs = wide(probs)
        product = wide_probs * spread
        scores = low(product - wide_probs * jnp.sum(product, axis=-1, keepdims=True))
        grad_values = low(mul(probs, stacked, 0, 0))
        both = mul(scores, keys)
        grad_queries = low(jnp.where(left, both[:count], both[count:]) * HEAD ** (-0.5))
        grad_keys = low(mul(scores, stack(queries * jnp.bfloat16(HEAD ** (-0.5))), 0, 0))
        return grad_queries, grad_keys, grad_values, scores

    def probs_copy(kind, pair):
        target = (probs_cross, probs_self)[kind]
        return pltpu.make_async_copy(
            probs_from[kind].at[:, pair], target.at[pair % 2], probs_sems.at[2 * kind + pair % 2]
        )

    def cross_back(pair):
        if pair + 1 < count_pairs:
            probs_copy(0, pair + 1).start()
        probs_copy(0, pair).wait()
        lanes = pl.ds(pair * LANES, LANES)

        def body(sequence, carry):
            at = pl.ds(pl.multiple_of(sequence * slot_rows, slot_rows), slot_rows)
            keys = pl.ds(pl.multiple_of(sequence * enc_rows, enc_rows), enc_rows)
            queries, pairs = vmem["queries"], vmem["pairs"]
            grads = pair_back(
                queries[at, lanes],
                pairs[0, keys, lanes],
                pairs[1, keys, lanes],
                probs_cross[pair % 2, sequence],
                grad_mixed[at, lanes],
            )
            queries[at, lanes], pairs[0, keys, lanes], pairs[1, keys, lanes] = grads[:3]
            return carry

        lax.fori_loop(0, seqs, body, 0)

    def self_back(pair):
        if pair + 1 < count_pairs:
            probs_copy(1, pair + 1).start()
        probs_copy(1, pair).wait()
        lanes = pl.ds(pair * LANES, LANES)
        total = 0.0
        for sequence in range(seqs):
            at = pl.ds(sequence * slot_rows, slot_rows)
            qkv = vmem["qkv"]
            grads = pair_back(
                qkv[0, at, lanes],
                qkv[1, at, lanes],
                qkv[2, at, lanes],
                probs_self[pair % 2, sequence],
                grad_mixed[at, lanes],
            )
            qkv[0, at, lanes], qkv[1, at, lanes], qkv[2, at, lanes] = grads[:3]
            total = total + wide(grads[3])
        period = spread_ids.shape[1]
        total = jnp.concatenate(
            [total, jnp.zeros((total.shape[0], period - slot_rows), jnp.float32)], axis=1
        )
        for head in range(2):
            sums = 0.0
            for group in range(slot_rows // 8):
                start = head * slot_rows + group * 8
                piece = total[start : start + 8]
                sums = sums + (pltpu.roll(piece, period - group * 8, 1) if group else piece)
            diag[2 * pair + head] = sums

    chain, produced = [], []

    def then(cost, step):
        chain.append((cost, step))

    def start_ffn():
        need("third", "grad_normed", "gains")
        norm_back(2, vmem["third"], vmem["branch"], False)

    def start_cross():
        probs_copy(0, 0).start()
        through(0, rounded.at[0], grad_mixed, False, True)
        need("queries", "pairs")

    def encoder_back():
        keys, values = weight(1), weight(2)
        for sequence in range(seqs):
            at = slice(sequence * enc_rows, (sequence + 1) * enc_rows)
            copy = pltpu.make_async_copy(grad_enc, grad_encoder.at[at], out_sems.at[0])
            if sequence:
                copy.wait()
            pairs = vmem["pairs"]
            grad_enc[...] = mul(pairs[0, at], keys(), 1, 1) + mul(pairs[1, at], values(), 1, 1)
            copy.start()
        release()
        release()

    def end_cross():
        need("second")
        through(3, vmem["queries"], vmem["grad_normed"], False, False)

    def start_self():
        norm_back(1, vmem["second"], dx, False)

    def self_mixed():
        probs_copy(1, 0).start()
        need("qkv")
        through(4, rounded.at[1], grad_mixed, False, True)

    def self_normed(part):
        through(5 + part, vmem["qkv"].at[part], vmem["grad_normed"], part > 0, False)

    def end_self():
        need("tokens")
        norm_back(0, vmem["tokens"], dx, True)
        pltpu.make_async_copy(dx, grad_tokens, out_sems.at[1]).start()

    then(1.5, start_ffn)
    marks = {}
    marks[5] = len(chain)
    then(1.5, start_cross)
    for pair in range(count_pairs):
        then(3.0, functools.partial(cross_back, pair))
    marks[2] = marks[4] = len(chain)
    then(4.0, encoder_back)
    then(1.5, end_cross)
    then(1.5, start_self)
    marks[3] = len(chain)
    then(1.5, self_mixed)
    for pair in range(count_pairs):
        then(3.0, functools.partial(self_back, pair))
    marks[1] = len(chain)
    for part in range(3):
        then(1.2, functools.partial(self_normed, part))
    then(1.5, end_self)
    marks[0] = len(chain)
    marks[6] = marks[7] = 0

    def pack_grad(u):
        slot = u % whole_slots.shape[0]
        period = spread_ids.shape[1]
        table = 0.0
        for row in range(8):
            part = diag[:, row, :]
            table = table + (pltpu.roll(part, period - row, 1) if row else part)
        spread = spread_ids[...]
        onehot = (lax.broadcasted_iota(jnp.int32, (LANES, period), 0) == spread).astype(jnp.bfloat16)
        high = low(table)
        rel = mul(high, onehot, 1, 1) + mul(low(table - wide(high)), onehot, 1, 1)
        for z in range(sizes[0]):
            for y in range(sizes[1]):
                at = slice((z * sizes[1] + y) * LANES, (z * sizes[1] + y + 1) * LANES)
                top = jnp.concatenate(
                    [gain_grads[:, at], jnp.zeros((HEADS - norms, LANES), jnp.float32)], axis=0
                )
                tile = low(jnp.concatenate([top, rel], axis=0))
                for x in range(sizes[2]):
                    for core in range(sizes[3]):
                        whole_slots[slot, z, y, x, core, :, 0:LANES] = tile

    groups = owned[7].shape[0] // 8

    def down_piece(spot):
        size = vmem["hidden"].shape[2]
        size = min(size, hidden_width - spot * size)
        start = spot * vmem["hidden"].shape[2] // 8
        block = mul(vmem["hidden"][spot, :, 0:size], vmem["branch"][...], 0, 0)
        down_grads[start : start + size // 8] = low(block.reshape(size // 8, 8, width))

    def down_grad(u):
        slot = u % whole_slots.shape[0]
        start = units[u].row // 8

        block_rows = whole_slots.shape[5]

        def body(device, carry):
            piece = down_grads[pl.ds(device * groups + start, block_rows // 8)]
            c, rest = device % sizes[3], device // sizes[3]
            x, rest = rest % sizes[2], rest // sizes[2]
            whole_slots[slot, rest // sizes[1], rest % sizes[1], x, c, :, :] = low(
                wide(piece).reshape(block_rows, width)
            )
            return carry

        lax.fori_loop(0, sizes[0] * sizes[1] * sizes[2] * sizes[3], body, 0)

    def grad_of(u):
        unit = units[u]
        owner = unit.owner
        part = unit.start // width
        if owner == 6:
            need("branch", "grad_gate_up")
            weight_grad(
                u, "normed_ffn", vmem["grad_gate_up"][unit.start // width, :, 0 : unit.shape[1]]
            )
        elif owner == 7:
            if unit.row == 0:
                need("hidden")
                down_grads[down_grads.shape[0] - 8 :] = jnp.zeros((8, 8, width), jnp.bfloat16)
                for spot in range(vmem["hidden"].shape[0]):
                    down_piece(spot)
            down_grad(u)
        elif owner == 5:
            weight_grad(u, "mixed_cross", rounded[0])
        elif owner == 2:
            weight_grad(u, "encoder", vmem["pairs"][part])
        elif owner == 4:
            weight_grad(u, "normed_cross", vmem["queries"][...])
        elif owner == 3:
            weight_grad(u, "mixed_self", rounded[1])
        elif owner == 1:
            weight_grad(u, "normed_self", vmem["qkv"][part])
        else:
            pack_grad(u)

    position = 0
    budget = 6.0
    for u, unit in enumerate(units):
        while position < marks[unit.owner]:
            chain[position][1]()
            position += 1
        grad_of(u)
        driver.advance()
        begin(("pairs", "encoder", "normed_self")[min(u, 2)])
        spent = 0.0
        while unit.owner in (6, 7) and position < len(chain) and spent < budget:
            spent += chain[position][0]
            chain[position][1]()
            position += 1
    while not driver.done():
        driver.advance()
    pltpu.make_async_copy(grad_enc, grad_encoder.at[0:enc_rows], out_sems.at[0]).wait()
    pltpu.make_async_copy(dx, grad_tokens, out_sems.at[1]).wait()


def backward_all(place, wholes, kept, probs, spread, data, blocks):
    tokens, encoder = data[:2]
    seqs, slot_rows, width = tokens.shape
    rows = seqs * slot_rows
    sources = dict(kept, tokens=tokens.reshape(rows, width), encoder=encoder.reshape(-1, width))
    low_type, wide_type = jnp.bfloat16, jnp.float32
    sizes = place.sizes
    block_rows = blocks[1][0]
    units = []
    for owner in BACK_ORDER:
        if owner == 7:
            height = blocks[7][0] * 8
            for row in range(0, height, block_rows):
                unit = Unit(7, (block_rows, width), 0, width, len(units) % 2)
                unit.row = row
                units.append(unit)
        else:
            units += make_units(blocks, PIECE, (owner,), len(units))
    total = copies_of(units, sizes)
    anywhere = pl.BlockSpec(memory_space=pl.ANY)
    inside = pl.BlockSpec(memory_space=pltpu.VMEM)
    down_rows = blocks[7][0] * 8
    owned = [(block[0], block[1]) for block in blocks[:7]] + [(down_rows, width)]
    count = sizes[0] * sizes[1] * sizes[2] * sizes[3]
    size = PIECE // block_rows
    rings = ring_shapes(sizes, block_rows, size)
    like = lambda array: pltpu.VMEM(array.shape, array.dtype)
    results = pl.pallas_call(
        functools.partial(backward_kernel, place, units, seqs, tuple(rings)),
        out_shape=[
            jax.ShapeDtypeStruct((rows, width), wide_type),
            jax.ShapeDtypeStruct((sources["encoder"].shape), wide_type),
        ]
        + [jax.ShapeDtypeStruct(block, wide_type) for block in owned],
        in_specs=[anywhere] * (5 + len(READ) + 2) + [inside],
        out_specs=[anywhere] * 2 + [inside] * len(owned),
        scratch_shapes=[like(sources[name]) for name in READ]
        + [
            pltpu.VMEM((2,) + probs[0].shape[:1] + probs[0].shape[2:], low_type),
            pltpu.VMEM((2,) + probs[1].shape[:1] + probs[1].shape[2:], low_type),
            pltpu.VMEM((rows, width), wide_type),
            pltpu.VMEM((2, rows, width), low_type),
            pltpu.VMEM((rows, width), low_type),
            pltpu.VMEM((encoder.shape[1], width), wide_type),
            pltpu.VMEM((count * blocks[7][0] + 8, 8, width), low_type),
            pltpu.VMEM((HEADS, 8, spread.shape[1]), wide_type),
            pltpu.VMEM(kept["gains"].shape, wide_type),
            pltpu.VMEM((2,) + sizes + (block_rows, width), low_type),
            pltpu.VMEM((2,) + sizes + (block_rows, size), low_type),
        ]
        + [pltpu.VMEM((RING,) + sizes[:3] + (block_rows, size), low_type)]
        + [pltpu.VMEM((RING,) + shape, low_type) for shape in rings.values()]
        + [
            pltpu.SemaphoreType.DMA((total,)),
            pltpu.SemaphoreType.DMA((total,)),
            pltpu.SemaphoreType.DMA((len(READ),)),
            pltpu.SemaphoreType.DMA((4,)),
            pltpu.SemaphoreType.DMA((2,)),
            pltpu.SemaphoreType.DMA((2,)),
        ],
        compiler_params=pltpu.CompilerParams(
            collective_id=1, has_side_effects=True, vmem_limit_bytes=63 * 2**20
        ),
        name="backward_all",
    )(*wholes[1:6], *[sources[name] for name in READ], *probs, spread)
    return results[0], results[1], results[2:]


def norm_scale(stream, gain):
    return stream * lax.rsqrt(jnp.mean(stream * stream, axis=-1, keepdims=True) + 1e-06) * gain


def gelu_tanh(values):
    return (
        0.5
        * values
        * (1.0 + jnp.tanh(0.7978845608028654 * (values + 0.044715 * values * values * values)))
    )


def gated(gate_up):
    half_width = gate_up.shape[1] // 2
    return gelu_tanh(gate_up[:, :half_width]) * gate_up[:, half_width:]


def product(spec, left, right):
    return jnp.einsum(spec, left, right, preferred_element_type=jnp.float32)


def attend(queries, key_rows, value_rows, pos_bias, keep_mask):
    scores = product("bihc,bjhc->bhij", queries, key_rows) * HEAD ** (-0.5)
    if pos_bias is not None:
        scores = scores + pos_bias
    masked = jnp.where(keep_mask[:, None], scores, -1e30)
    row_max = jnp.max(masked, axis=-1, keepdims=True)
    powers = jnp.exp(masked - row_max)
    probs = powers / jnp.sum(powers, axis=-1, keepdims=True)
    low_probs = probs.astype(jnp.bfloat16)
    mixed = product("bhij,bjhc->bihc", low_probs, value_rows)
    return mixed.astype(jnp.bfloat16), low_probs


def attend_back(queries, key_rows, value_rows, low_probs, grad_mixed):
    probs = low_probs.astype(jnp.float32)
    grad_values = product("bhij,bihc->bjhc", low_probs, grad_mixed)
    grad_probs = product("bihc,bjhc->bhij", grad_mixed, value_rows)
    grad_scores = (
        probs * (grad_probs - jnp.sum(probs * grad_probs, axis=-1, keepdims=True))
    ).astype(jnp.bfloat16)
    grad_queries = product("bhij,bjhc->bihc", grad_scores, key_rows) * HEAD ** (-0.5)
    grad_keys = product("bhij,bihc->bjhc", grad_scores, queries) * HEAD ** (-0.5)
    return grad_queries, grad_keys, grad_values, grad_scores


def toeplitz(table, size):
    lead = table.shape[:-1]
    row = jnp.concatenate(
        [table[..., ::-1], jnp.broadcast_to(table[..., :1], lead + (size,))], axis=-1
    )
    tiled = jnp.broadcast_to(row[..., None, :], lead + (size, 2 * size)).reshape(lead + (-1,))
    tiled = jnp.concatenate([tiled[..., size - 1 :], row[..., :1]], axis=-1)
    tiled = tiled[..., : size * (2 * size - 1)]
    return tiled.reshape(lead + (size, 2 * size - 1))[..., :size]


def layer(weights, gains, rel_bias, tokens, encoder, cotangent, lengths, enc_lengths, bucket_ids):
    self_qkv, self_out, cross_q, cross_kv, cross_out, ff_in, ff_out = weights
    count, slots, width = tokens.shape
    enc_count = encoder.shape[1]
    bucket_map = toeplitz(bucket_ids, slots).reshape(-1)
    onehot = (lax.iota(jnp.int32, BUCKETS)[:, None] == bucket_map[None, :]).astype(jnp.bfloat16)
    pos_bias = jnp.dot(rel_bias, onehot, preferred_element_type=jnp.float32).reshape(
        HEADS, slots, slots
    )
    row_ids = lax.iota(jnp.int32, slots)
    self_mask = (row_ids[None, None, :] <= row_ids[None, :, None]) & (
        row_ids[None, None, :] < lengths[:, None, None]
    )
    cross_mask = lax.iota(jnp.int32, enc_count)[None, None, :] < enc_lengths[:, None, None]
    enc_rows = encoder.reshape(count * enc_count, width)
    dot = functools.partial(jnp.dot, preferred_element_type=jnp.float32)
    low = lambda value: value.astype(jnp.bfloat16)
    stream = tokens.reshape(count * slots, width).astype(jnp.float32)
    normed_self, back_self = jax.vjp(norm_scale, stream, gains[0])
    normed_self = low(normed_self)
    qkv = low(dot(normed_self, self_qkv)).reshape(count, slots, 3, HEADS, HEAD)
    mixed_self, probs_self = attend(qkv[:, :, 0], qkv[:, :, 1], qkv[:, :, 2], pos_bias, self_mask)
    mixed_self = mixed_self.reshape(count * slots, width)
    second = stream + dot(mixed_self, self_out)
    normed_cross, back_cross = jax.vjp(norm_scale, second, gains[1])
    normed_cross = low(normed_cross)
    queries = low(dot(normed_cross, cross_q)).reshape(count, slots, HEADS, HEAD)
    pairs = low(dot(enc_rows, cross_kv)).reshape(count, enc_count, 2, HEADS, HEAD)
    mixed_cross, probs_cross = attend(queries, pairs[:, :, 0], pairs[:, :, 1], None, cross_mask)
    mixed_cross = mixed_cross.reshape(count * slots, width)
    third = second + dot(mixed_cross, cross_out)
    normed_ffn, back_ffn = jax.vjp(norm_scale, third, gains[2])
    normed_ffn = low(normed_ffn)
    gate_up = dot(normed_ffn, ff_in)
    activated, back_gate = jax.vjp(gated, gate_up)
    hidden = low(activated)
    outcome = third + dot(hidden, ff_out)

    valid = (row_ids[None, :] < lengths[:, None]).astype(jnp.float32)[:, :, None]
    grad_out = (cotangent.astype(jnp.float32) * valid).reshape(count * slots, width)
    branch = low(grad_out)
    grad_ff_out = product("lf,ld->fd", hidden, branch)
    grad_hidden = product("ld,fd->lf", branch, ff_out)
    (grad_gate_up,) = back_gate(grad_hidden)
    grad_gate_up = low(grad_gate_up)
    grad_ff_in = product("ld,lf->df", normed_ffn, grad_gate_up)
    grad_stream, gain_ffn = back_ffn(product("lf,df->ld", grad_gate_up, ff_in))
    grad_third = grad_out + grad_stream
    branch = low(grad_third)
    grad_cross_out = product("le,ld->ed", mixed_cross, branch)
    grad_mixed = low(product("ld,ed->le", branch, cross_out)).reshape(count, slots, HEADS, HEAD)
    grad_queries, grad_keys, grad_values, unused = attend_back(
        queries, pairs[:, :, 0], pairs[:, :, 1], probs_cross, grad_mixed
    )
    grad_query_rows = low(grad_queries.reshape(count * slots, width))
    grad_pair_rows = low(
        jnp.concatenate(
            [
                grad_keys.reshape(count * enc_count, width),
                grad_values.reshape(count * enc_count, width),
            ],
            axis=1,
        )
    )
    grad_cross_q = product("ld,le->de", normed_cross, grad_query_rows)
    grad_cross_kv = product("ed,ef->df", enc_rows, grad_pair_rows)
    grad_enc = product("ef,df->ed", grad_pair_rows, cross_kv)
    grad_stream, gain_cross = back_cross(product("le,de->ld", grad_query_rows, cross_q))
    grad_second = grad_third + grad_stream
    branch = low(grad_second)
    grad_self_out = product("le,ld->ed", mixed_self, branch)
    grad_mixed = low(product("ld,ed->le", branch, self_out)).reshape(count, slots, HEADS, HEAD)
    grad_queries, grad_keys, grad_values, grad_scores = attend_back(
        qkv[:, :, 0], qkv[:, :, 1], qkv[:, :, 2], probs_self, grad_mixed
    )
    score_sums = jnp.sum(grad_scores.astype(jnp.float32), axis=0).reshape(HEADS, slots * slots)
    grad_rel_bias = product("hn,bn->hb", low(score_sums), onehot)
    grad_qkv = low(
        jnp.concatenate(
            [part.reshape(count * slots, width) for part in (grad_queries, grad_keys, grad_values)],
            axis=1,
        )
    )
    grad_self_qkv = product("ld,lf->df", normed_self, grad_qkv)
    grad_stream, gain_self = back_self(product("lf,df->ld", grad_qkv, self_qkv))
    grad_tok = grad_second + grad_stream
    grad_gains = jnp.stack([gain_self, gain_cross, gain_ffn], axis=0)
    grads = (
        grad_self_qkv,
        grad_self_out,
        grad_cross_q,
        grad_cross_kv,
        grad_cross_out,
        grad_ff_in,
        grad_ff_out,
    )
    return (
        outcome.reshape(tokens.shape),
        grad_tok.reshape(tokens.shape),
        grad_enc.reshape(encoder.shape),
        grads,
        grad_gains,
        grad_rel_bias,
    )


AXES = ("dp", "fsdp")


def by_collectives(data, shards):
    whole = lambda shard, axis=0: lax.all_gather(shard, AXES, axis=axis, tiled=True)
    weights = tuple(whole(shard) for shard in shards[:7])
    gains = whole(shards[7], 1).astype(jnp.float32)
    rel_bias = whole(shards[8]).reshape(HEADS, BUCKETS)
    outcome, grad_tok, grad_enc, grads, grad_gains, grad_rel_bias = layer(
        weights, gains, rel_bias, *data
    )
    settle = lambda total, axis=0: lax.psum_scatter(
        total, AXES, scatter_dimension=axis, tiled=True
    )
    return (
        (outcome, grad_tok, grad_enc)
        + tuple(settle(grad) for grad in grads)
        + (settle(grad_gains, 1), settle(grad_rel_bias.reshape(-1)))
    )


def by_kernels(place, data, shards):
    norm_gains, rel_bias = shards[7:]
    count = place.sizes[0] * place.sizes[1] * place.sizes[2] * place.sizes[3]
    me = lax.axis_index(AXES)
    norms, per = norm_gains.shape
    group = LANES // per
    rel_per = rel_bias.shape[0]
    pack = jnp.zeros((PACK, LANES), jnp.bfloat16)
    pack = lax.dynamic_update_slice(pack, norm_gains, (0, (me % group) * per))
    rel_row, rel_column = HEADS + me * rel_per // BUCKETS, (me * rel_per) % BUCKETS
    pack = lax.dynamic_update_slice(pack, rel_bias.reshape(1, rel_per), (rel_row, rel_column))
    ff_rows, width = shards[6].shape
    ff_shape = (ff_rows // 8, 8, width)
    self_qkv, self_out, cross_q, cross_kv, cross_out, ff_in, ff_out = shards[:7]
    chunks = ff_in.shape[1] // (2 * CHUNK)
    laced = ff_in.reshape(-1, 2, chunks, CHUNK).transpose(0, 2, 1, 3).reshape(ff_in.shape)
    sent = (pack, self_qkv, cross_kv, self_out, cross_q, cross_out, laced, ff_out.reshape(ff_shape))
    blocks = [piece.shape for piece in sent]
    bucket_ids = data[5]
    spread = jnp.concatenate(
        [bucket_ids[:1], jnp.broadcast_to(bucket_ids[:1], bucket_ids.shape), bucket_ids[:0:-1]]
    )[None]
    wholes, outcome, kept = forward_all(place, sent, *data[:5], spread, norms)
    grad_tok, grad_enc, sums = backward_all(
        place,
        wholes,
        kept,
        (kept["probs_cross"], kept["probs_self"]),
        spread,
        data,
        blocks,
    )
    packed, g_qkv, g_kv, g_so, g_cq, g_co, g_in, g_out = sums
    owned = [g_qkv, g_so, g_cq, g_kv, g_co, g_in, g_out]
    own_gains = lax.dynamic_slice(packed, (0, (me % group) * per), (norms, per))
    own_rel = lax.dynamic_slice(packed, (rel_row, rel_column), (1, rel_per)).reshape(-1)
    shaped = (
        outcome.reshape(data[0].shape),
        grad_tok.reshape(data[0].shape),
        grad_enc.reshape(data[1].shape),
    )
    return shaped + tuple(owned) + (own_gains, own_rel)


def on_device(place, *args):
    data, shards = args[:6], args[6:]
    per = shards[7].shape[1]
    regular = all(shard.shape[0] % 16 == 0 for shard in shards[:6])
    if regular and shards[6].shape[0] % 8 == 0 and LANES % per == 0:
        return by_kernels(place, data, shards)
    return by_collectives(data, shards)


def solution(mesh):
    rows = P(AXES, None, None)
    flat = P(AXES)
    matrix = P(AXES, None)
    split = P(None, AXES)
    place = Place(mesh.shape["dp"], mesh.shape["fsdp"])
    return jax.shard_map(
        functools.partial(on_device, place),
        mesh=mesh,
        in_specs=(rows, rows, rows, flat, flat, P()) + (matrix,) * 7 + (split, flat),
        out_specs=(rows, rows, rows) + (matrix,) * 7 + (split, flat),
        check_vma=False,
    )
```

```python
import functools

import jax
import jax.numpy as jnp
from jax import lax
from jax.experimental import pallas as pl
from jax.experimental.pallas import tpu as pltpu
from jax.sharding import PartitionSpec as P

HEADS = 16
HEAD = 64
BUCKETS = 32
PACK = 32
LANES = 128
PIECE = 32 * 1024

MESH = pl.DeviceIdType.MESH


class Place:
    def __init__(self, dp, fsdp):
        self.sizes = (dp // 2, 2, fsdp // 2, 2)

    def locate(self):
        row, column = lax.axis_index("dp"), lax.axis_index("fsdp")
        sizes = self.sizes
        self.here = (row // sizes[1], row % sizes[1], column // sizes[3], column % sizes[3])

    def moved(self, axis, step):
        coords = list(self.here)
        coords[axis] = (coords[axis] + step) % self.sizes[axis]
        return coords

    def device(self, coords):
        return (coords[0] * self.sizes[1] + coords[1], coords[2] * self.sizes[3] + coords[3])

    def peers(self):
        return [(axis, step) for axis in range(4) for step in range(1, self.sizes[axis])]

    def greet(self):
        barrier = pltpu.get_barrier_semaphore()
        for axis, step in self.peers():
            pl.semaphore_signal(
                barrier, inc=1, device_id=self.device(self.moved(axis, step)), device_id_type=MESH
            )
        pl.semaphore_wait(barrier, len(self.peers()))


def split_lanes(width, parity):
    if width == 8 * LANES:
        more, less = (4 - parity) * LANES, (3 + parity) * LANES
        third = ((2, 1, 0), (1, 2, 0))[parity]
        return ((0, more, (0, 2, 1)), (more, less, (0, 1, 2)), (7 * LANES, LANES, third))
    if width % (2 * LANES) == 0:
        return ((0, width // 2, (0, 2, 1)), (width // 2, width // 2, (0, 1, 2)))
    return ((0, width, (0, 2, 1)),)


class Unit:
    def __init__(self, owner, block, start, count, parity=0):
        self.owner, self.start, self.count = owner, start, count
        self.grouped = len(block) == 3
        self.shape = (count,) + block[1:] if self.grouped else (block[0], count)
        self.paths = split_lanes(self.shape[-1], parity)

    def part(self, start=0, size=None):
        size = self.shape[-1] if size is None else size
        if self.grouped:
            return (pl.ds(self.start, self.count), slice(None), pl.ds(start, size))
        return (slice(None), pl.ds(self.start + start, size))


def make_units(blocks, piece, order, before=0):
    units = []
    for owner in order:
        block = blocks[owner]
        total, most = (block[0], piece // 8 // block[2] or 1) if len(block) == 3 else (block[1], piece // block[0])
        start = 0
        while start < total:
            count = min(most, total - start)
            units.append(Unit(owner, block, start, count, (before + len(units)) % 2))
            start += count
    return units


class Wires:
    def __init__(self, place, send_sems, recv_sems):
        self.place, self.send_sems, self.recv_sems = place, send_sems, recv_sems
        self.started = []

    def send(self, source, target, axis, step):
        spot = len(self.started)
        copy = pltpu.make_async_remote_copy(
            src_ref=source,
            dst_ref=target,
            send_sem=self.send_sems.at[spot],
            recv_sem=self.recv_sems.at[spot],
            device_id=self.place.device(self.place.moved(axis, step)),
            device_id_type=MESH,
        )
        copy.start()
        self.started.append(copy)
        return copy

    def along(self, axis, source, target):
        return [
            self.send(source, target, axis, step) for step in range(1, self.place.sizes[axis])
        ]

    def finish(self):
        for copy in self.started:
            copy.wait_send()


def gather_stages(place, units, shards, wholes, wires, own_copies):
    full = slice(None)
    pending = {}

    def settle(u):
        for copy in pending[u]:
            copy.wait_recv()
        pending[u] = []

    def first(u):
        unit = units[u]
        whole = wholes[unit.owner]
        if unit.owner == 6:
            for copy in own_copies[u]:
                copy.wait()
        pending[u] = []
        for start, size, axes in unit.paths:
            target = whole.at[place.here + unit.part(start, size)]
            source = target if unit.owner == 6 else shards[unit.owner].at[unit.part(start, size)]
            pending[u] += wires.along(axes[0], source, target)

    def later(u, stage):
        unit = units[u]
        if stage == 1 and unit.owner != 6:
            for copy in own_copies[u]:
                copy.wait()
        settle(u)
        for start, size, axes in unit.paths:
            index = tuple(
                full if axis in axes[:stage] else place.here[axis] for axis in range(3)
            ) + (place.here[3],)
            ref = wholes[unit.owner].at[index + unit.part(start, size)]
            pending[u] += wires.along(axes[stage], ref, ref)

    def across(u):
        settle(u)
        unit = units[u]
        ref = wholes[unit.owner].at[(full, full, full, place.here[3]) + unit.part()]
        pending[u] = wires.along(3, ref, ref)

    return (
        first,
        functools.partial(later, stage=1),
        functools.partial(later, stage=2),
        across,
        settle,
    )


def copies_of(units, sizes):
    return sum(1 + len(unit.paths) * (sizes[0] + sizes[1] + sizes[2] - 3) for unit in units)


def mul(left, right, left_dim=1, right_dim=0):
    return lax.dot_general(
        left, right, (((left_dim,), (right_dim,)), ((), ())), preferred_element_type=jnp.float32
    )


def low(value):
    return value.astype(jnp.bfloat16)


def wide(value):
    return value.astype(jnp.float32)


def rms_rows(source, target, gain, rows=64):
    def body(step, carry):
        at = pl.ds(pl.multiple_of(step * rows, rows), rows)
        value = wide(source[at, :])
        scale = lax.rsqrt(jnp.mean(value * value, axis=-1, keepdims=True) + 1e-06)
        target[at, :] = low(value * scale * gain)
        return carry

    lax.fori_loop(0, source.shape[0] // rows, body, 0)


def attend_pair(queries, key_rows, value_rows, bias, mask):
    rows = queries.shape[0]
    left = lax.broadcasted_iota(jnp.int32, (1, LANES), 1) < HEAD
    zero = jnp.zeros_like(queries)
    scaled = queries * jnp.bfloat16(HEAD ** (-0.5))
    stacked = jnp.concatenate(
        [jnp.where(left, scaled, zero), jnp.where(left, zero, scaled)], axis=0
    )
    scores = mul(stacked, key_rows, 1, 1)
    if bias is not None:
        scores = scores + bias
    scores = jnp.where(mask, scores, -1e30)
    powers = jnp.exp(scores - jnp.max(scores, axis=-1, keepdims=True))
    probs = low(powers / jnp.sum(powers, axis=-1, keepdims=True))
    none = jnp.zeros_like(value_rows)
    mixed = mul(probs[:rows], jnp.where(left, value_rows, none)) + mul(
        probs[rows:], jnp.where(left, none, value_rows)
    )
    return probs, low(mixed)


class Driver:
    def __init__(self, units, stages, lead):
        self.units, self.stages, self.lead = units, stages, lead
        self.tick, self.debt = 0, 0.0

    def done(self):
        return self.tick >= len(self.units) + len(self.stages) - 1

    def settled(self):
        return self.tick - len(self.stages)

    def advance(self):
        for lag, stage in enumerate(self.stages):
            if 0 <= self.tick - lag < len(self.units):
                stage(self.tick - lag)
        self.tick += 1

    def until(self, unit):
        while self.settled() < unit:
            self.advance()

    def spent(self, cost):
        self.debt += cost
        while self.debt >= self.lead:
            self.debt -= self.lead
            if not self.done():
                self.advance()


def ring_shapes(sizes, block_rows, width):
    shapes = {}
    for parity in range(2):
        for start, lanes, axes in split_lanes(width, parity):
            for hop in range(3):
                axis = axes[2 - hop]
                rest = tuple(sizes[other] for other in range(3) if other in axes[: 2 - hop])
                shape = (sizes[axis] - 1,) + rest + (block_rows,)
                key = (axes, hop)
                old = shapes.get(key, (0,))[-1]
                shapes[key] = shape + (max(lanes, old),)
    return shapes


def scatter_stages(place, units, whole_slots, arrived, rings, finish, wires):
    sizes, full = place.sizes, slice(None)
    here = place.here
    pending = {}

    def settle(u):
        for copy in pending[u]:
            copy.wait()
        pending[u] = []

    def lanes(u):
        return (full, pl.ds(0, units[u].shape[1]))

    def slot(u):
        return whole_slots.at[u % whole_slots.shape[0]]

    def spread(b, axes):
        coords = {}
        for axis in reversed(axes):
            coords[axis] = b % sizes[axis]
            b = b // sizes[axis]
        return coords

    def count(axes):
        total = 1
        for axis in axes:
            total *= sizes[axis]
        return total

    def held(u, path, hop):
        start, size, axes = path
        ring = u % RING
        if hop == 0:
            return lambda at: (arrived, (ring,) + tuple(at[a] for a in range(3)) + (full, pl.ds(start, size)))
        rest = sorted(axes[: 3 - hop])
        ref = rings[axes, hop - 1]
        return lambda at: (ref, (ring, 0) + tuple(at[a] for a in rest) + (full, pl.ds(0, size)))

    def first(u):
        source = slot(u).at[(full, full, full, (here[3] + 1) % 2) + lanes(u)]
        target = arrived.at[(u % RING, full, full, full) + lanes(u)]
        pending[u] = [wires.send(source, target, 3, 1)]

    def pass_on(u, hop):
        for path in units[u].paths:
            start, size, axes = path
            axis = axes[2 - hop]
            where = held(u, path, hop)
            ref = rings[axes, hop]
            rest = sorted(axes[: 2 - hop])
            for step in range(1, sizes[axis]):
                at = {a: full for a in rest}
                at[axis] = place.moved(axis, step)[axis]
                source, index = where(at)
                target = ref.at[
                    (u % RING, step - 1) + (full,) * len(rest) + (full, pl.ds(0, size))
                ]
                pending[u].append(wires.send(source.at[index], target, axis, step))

    def merge(u, path, hop):
        start, size, axes = path
        axis = axes[2 - hop]
        rest = sorted(axes[: 2 - hop])
        before, after = held(u, path, hop), held(u, path, hop + 1)
        ref = rings[axes, hop]

        def body(b, carry):
            at = spread(b, rest)
            source, index = before({**at, axis: here[axis]})
            value = wide(source[index])
            for step in range(sizes[axis] - 1):
                value = value + wide(
                    ref[(u % RING, step) + tuple(at[a] for a in rest) + (full, pl.ds(0, size))]
                )
            if hop == 2:
                finish(u, start, size, value)
            else:
                target, index = after(at)
                target[index] = low(value)
            return carry

        if hop == 2:
            body(0, 0)
        else:
            lax.fori_loop(0, count(rest), body, 0)

    def second(u):
        settle(u)
        ring, own = u % RING, slot(u)

        def body(b, carry):
            at = spread(b, (0, 1, 2))
            index = tuple(at[a] for a in range(3))
            target = (ring,) + index + lanes(u)
            arrived[target] = low(wide(arrived[target]) + wide(own[index + (here[3],) + lanes(u)]))
            return carry

        lax.fori_loop(0, count((0, 1, 2)), body, 0)
        pass_on(u, 0)

    def later(u, hop):
        settle(u)
        for path in units[u].paths:
            merge(u, path, hop)
        if hop < 2:
            pass_on(u, hop + 1)

    return (first, second) + tuple(functools.partial(later, hop=hop) for hop in range(3))


CHUNK = 256
RING = 5
ORDER = (0, 1, 2, 3, 4, 5, 7, 6)
BACK_ORDER = (6, 7, 5, 2, 4, 3, 1, 0)
BUFFERS = (
    "tokens", "encoder", "branch", "normed_self", "qkv", "mixed_self", "second", "normed_cross",
    "queries", "pairs", "mixed_cross", "third", "normed_ffn", "hidden", "grad_gate_up",
    "grad_normed", "gains",
)


def layer_kernel(place, units, back_units, count, seqs, ring_keys, *refs):
    shards, refs = refs[: count - 1], refs[count - 1 :]
    gain_shard, rel_shard, tokens_in, encoder_in, cotangent_in = refs[:5]
    lengths, enc_lengths, bucket_ids, refs = refs[5], refs[6], refs[7], refs[8:]
    wholes, refs = refs[:count], refs[count:]
    outcome_out, grad_tokens, grad_encoder, refs = refs[0], refs[1], refs[2], refs[3:]
    probs_out, refs = refs[:2], refs[2:]
    owned, refs = refs[: count - 1], refs[count - 1 :]
    own_gains, own_rel, refs = refs[0], refs[1], refs[2:]
    vmem, refs = dict(zip(BUFFERS, refs)), refs[len(BUFFERS) :]
    probs_slots, refs = refs[:2], refs[2:]
    dx, rounded, down_rows, diag, gain_grads = refs[:5]
    own_pack, packs_in, spread, bias_rows, slots, whole_slots, arrived = refs[5:12]
    refs = refs[12:]
    rings, refs = dict(zip(ring_keys, refs)), refs[len(ring_keys) :]
    gather_send, gather_recv, scatter_send, scatter_recv = refs[:4]
    local_sems, fetch_sems, read_sems, probs_sems, out_sems = refs[4:]
    place.locate()
    sizes = place.sizes
    devices = sizes[0] * sizes[1] * sizes[2] * sizes[3]
    me = place.device(place.here)
    me = me[0] * (sizes[2] * sizes[3]) + me[1]
    rows, width = dx.shape
    slot_rows, enc_rows = rows // seqs, vmem["encoder"].shape[0] // seqs
    count_pairs = width // LANES
    norms, per = gain_shard.shape
    rel_per = rel_shard.shape[1]
    gain_lane = (me % (LANES // per)) * per
    rel_row, rel_lane = me * rel_per // BUCKETS, (me * rel_per) % BUCKETS
    hidden_width = owned[5].shape[1] // 2
    outcome = dx

    reads = {}
    for at, (name, source) in enumerate(
        (("tokens", tokens_in), ("branch", cotangent_in), ("encoder", encoder_in))
    ):
        reads[name] = pltpu.make_async_copy(source, vmem[name], read_sems.at[at])
        reads[name].start()
    padded = jnp.concatenate(
        [wide(gain_shard[...]), jnp.zeros((PACK // 2 - norms, per), jnp.float32)], axis=0
    )
    padded = jnp.concatenate([padded, jnp.zeros((PACK // 2, LANES - per), jnp.float32)], axis=1)
    rel = jnp.concatenate(
        [wide(rel_shard[...]), jnp.zeros((1, LANES - rel_per), jnp.float32)], axis=1
    )
    rel = jnp.broadcast_to(rel, (PACK // 2, LANES))
    pack_rows = lax.broadcasted_iota(jnp.int32, (PACK // 2, LANES), 0)
    rel = jnp.where(pack_rows == rel_row, pltpu.roll(rel, rel_lane, 1), 0.0)
    own_pack[...] = low(jnp.concatenate([pltpu.roll(padded, gain_lane, 1), rel], axis=0))
    shards = (own_pack,) + tuple(shards)
    own_copies, serial = {}, 0
    for u, unit in enumerate(units):
        pieces = [(unit.part(), unit.part())]
        if unit.owner == 6:
            pieces = []
            for at in range(unit.start, unit.start + unit.shape[1], CHUNK):
                spot = at // CHUNK
                source = (spot % 2) * hidden_width + (spot // 2) * CHUNK
                pieces.append(
                    ((slice(None), pl.ds(source, CHUNK)), (slice(None), pl.ds(at, CHUNK)))
                )
        own_copies[u] = []
        for source, target in pieces:
            copy = pltpu.make_async_copy(
                shards[unit.owner].at[source],
                wholes[unit.owner].at[place.here + target],
                local_sems.at[serial],
            )
            serial += 1
            copy.start()
            own_copies[u].append(copy)
    place.greet()
    gather_wires = Wires(place, gather_send, gather_recv)
    wires = Wires(place, scatter_send, scatter_recv)
    driver = Driver(
        units, gather_stages(place, units, shards, wholes, gather_wires, own_copies), 5.0
    )

    first_of = {}
    for u, unit in enumerate(units):
        first_of.setdefault(unit.owner, u)
    last_of = {unit.owner: u for u, unit in enumerate(units)}
    wanted = [
        (unit.owner, unit.part(), unit.shape[1], u)
        for u, unit in enumerate(units)
        if unit.owner not in (0, 7)
    ]
    for owner, part in ((5, 0), (2, 0), (2, 1), (4, 0), (3, 0), (1, 0), (1, 1), (1, 2)):
        wanted.append((owner, (slice(None), pl.ds(part * width, width)), width, 0))
    depth = slots.shape[0]
    state = dict(fetched=0, used=0, taken=0, raw=False)

    def fetch(spot):
        owner, part, size, unit = wanted[spot]
        return pltpu.make_async_copy(
            wholes[owner].at[(slice(None),) * 4 + part],
            slots.at[(spot % depth,) + (slice(None),) * 5 + (pl.ds(0, size),)],
            fetch_sems.at[spot % depth],
        )

    def raw_copy():
        return pltpu.make_async_copy(
            wholes[7].reshape(devices * wholes[7].shape[4], 8, width),
            down_rows.at[0 : devices * wholes[7].shape[4]],
            fetch_sems.at[depth],
        )

    def pump():
        while (
            state["fetched"] < len(wanted)
            and wanted[state["fetched"]][3] <= driver.settled()
            and state["fetched"] < state["used"] + depth
        ):
            fetch(state["fetched"]).start()
            state["fetched"] += 1
        if not state["raw"] and driver.settled() >= last_of[7]:
            state["raw"] = True
            raw_copy().start()

    def spent(cost):
        driver.spent(cost)
        pump()

    def weight():
        spot = state["taken"]
        state["taken"] += 1
        driver.until(wanted[spot][3])
        pump()
        fetch(spot).wait()
        size = wanted[spot][2]
        return lambda: slots[spot % depth, :, :, :, :, :, 0:size].reshape(width, size)

    def release():
        state["used"] += 1
        pump()

    def project(source, target, cost):
        matrix = weight()
        target[...] = low(mul(source[...], matrix()))
        release()
        spent(cost)

    def residual(source, before, target, cost):
        matrix = weight()
        target[...] = wide(before[...]) + mul(source[...], matrix())
        release()
        spent(cost)

    reads["branch"].wait()
    for sequence in range(seqs):
        at = pl.ds(sequence * slot_rows, slot_rows)
        valid = lax.broadcasted_iota(jnp.int32, (slot_rows, 1), 0) < lengths[sequence]
        vmem["branch"][at, :] = low(jnp.where(valid, wide(vmem["branch"][at, :]), 0.0))
    period = 2 * slot_rows
    distance = lax.broadcasted_iota(jnp.int32, (slot_rows, period), 0)
    lane = lax.broadcasted_iota(jnp.int32, (slot_rows, period), 1)
    turned = (lane == (period - distance) % period).astype(jnp.bfloat16)
    buckets = lax.broadcasted_iota(jnp.int32, (LANES, slot_rows), 0)
    spread[...] = low(mul((buckets == bucket_ids[...]).astype(jnp.bfloat16), turned))
    driver.until(0)
    copy = pltpu.make_async_copy(wholes[0], packs_in, fetch_sems.at[depth + 1])
    copy.start()
    copy.wait()
    packs = wide(packs_in[...]).reshape(width // LANES, -1, PACK, LANES)
    summed = jnp.sum(packs, axis=1)
    for group in range(summed.shape[0]):
        vmem["gains"][:, group * LANES : (group + 1) * LANES] = summed[group, :norms]
    table = low(jnp.sum(summed, axis=0)[PACK // 2 :])
    bias_rows[...] = mul(table, spread[...])
    reads["tokens"].wait()
    rms_rows(vmem["tokens"], vmem["normed_self"], vmem["gains"][0:1])

    for part in range(3):
        project(vmem["normed_self"], vmem["qkv"].at[part], 1.5)
    reads["encoder"].wait()
    for part in range(2):
        project(vmem["encoder"], vmem["pairs"].at[part], 2.5)

    def probs_copy(kind, pair, out):
        near = probs_slots[kind].at[pair % 2]
        far = probs_out[kind].at[pair]
        source, target = (near, far) if out else (far, near)
        return pltpu.make_async_copy(source, target, probs_sems.at[2 * kind + pair % 2])

    def pairs_forward(kind, body, cost):
        for pair in range(count_pairs):
            if pair >= 2:
                probs_copy(kind, pair - 2, True).wait()
            lax.fori_loop(0, seqs, functools.partial(body, pair), 0)
            probs_copy(kind, pair, True).start()
            spent(cost)
        for pair in range(count_pairs - 2, count_pairs):
            probs_copy(kind, pair, True).wait()

    def sequence_rows(sequence, size):
        return pl.ds(pl.multiple_of(sequence * size, size & -size), size)

    def self_pair(pair, sequence, carry):
        lanes = pl.ds(pair * LANES, LANES)
        row = lax.broadcasted_iota(jnp.int32, (slot_rows, slot_rows), 0)
        column = lax.broadcasted_iota(jnp.int32, (slot_rows, slot_rows), 1)
        bias = jnp.concatenate(
            [
                pltpu.roll(
                    jnp.broadcast_to(bias_rows[2 * pair + head, :][None], (slot_rows, period)),
                    0,
                    1,
                    stride=1,
                    stride_axis=0,
                )[:, :slot_rows]
                for head in range(2)
            ],
            axis=0,
        )
        at = sequence_rows(sequence, slot_rows)
        mask = (column <= row) & (column < lengths[sequence])
        probs, mixed = attend_pair(
            vmem["qkv"][0, at, lanes],
            vmem["qkv"][1, at, lanes],
            vmem["qkv"][2, at, lanes],
            bias,
            jnp.concatenate([mask, mask], axis=0),
        )
        probs_slots[1][pair % 2, sequence] = probs
        vmem["mixed_self"][at, lanes] = mixed
        return carry

    pairs_forward(1, self_pair, 1.3)
    residual(vmem["mixed_self"], vmem["tokens"], vmem["second"], 1.5)
    rms_rows(vmem["second"], vmem["normed_cross"], vmem["gains"][1:2])
    project(vmem["normed_cross"], vmem["queries"], 2.0)

    def cross_pair(pair, sequence, carry):
        lanes = pl.ds(pair * LANES, LANES)
        column = lax.broadcasted_iota(jnp.int32, (1, enc_rows), 1)
        at = sequence_rows(sequence, slot_rows)
        keys = sequence_rows(sequence, enc_rows)
        probs, mixed = attend_pair(
            vmem["queries"][at, lanes],
            vmem["pairs"][0, keys, lanes],
            vmem["pairs"][1, keys, lanes],
            None,
            column < enc_lengths[sequence],
        )
        probs_slots[0][pair % 2, sequence] = probs
        vmem["mixed_cross"][at, lanes] = mixed
        return carry

    pairs_forward(0, cross_pair, 1.3)
    residual(vmem["mixed_cross"], vmem["second"], vmem["third"], 1.5)
    rms_rows(vmem["third"], vmem["normed_ffn"], vmem["gains"][2:3])
    driver.until(last_of[7])
    pump()
    raw_copy().wait()
    outcome[...] = vmem["third"][...]
    vmem["grad_normed"][...] = jnp.zeros_like(vmem["grad_normed"])

    def finish(u, start_lane, size, value):
        unit = back_units[u]
        start = unit.start + start_lane
        if unit.owner == 0:
            own_gains[...] = pltpu.roll(
                value[: PACK // 2], (LANES - gain_lane) % LANES, 1
            )[:norms, :per]
            row = jnp.sum(jnp.where(pack_rows == rel_row, value[PACK // 2 :], 0.0), axis=0)[None]
            own_rel[...] = pltpu.roll(
                jnp.broadcast_to(row, (8, LANES)), (LANES - rel_lane) % LANES, 1
            )[:1, :rel_per]
        elif unit.owner == 6:
            for at in range(start, start + size, LANES):
                spot, rest = at // CHUNK, at % CHUNK
                to = (spot % 2) * hidden_width + (spot // 2) * CHUNK + rest
                owned[5][:, to : to + LANES] = value[:, at - start : at - start + LANES]
        elif unit.owner == 7:
            kept = min(value.shape[0], owned[6].shape[0] - unit.row)
            owned[6][unit.row : unit.row + kept, start_lane : start_lane + size] = value[:kept]
        else:
            owned[unit.owner - 1][:, start : start + size] = value

    scatter = Driver(
        back_units,
        scatter_stages(place, back_units, whole_slots, arrived, rings, finish, wires),
        1.0,
    )

    def weight_grad(u, name, right):
        size = back_units[u].shape[1]
        block = low(mul(vmem[name][...], right, 0, 0))
        whole_slots[u % whole_slots.shape[0], :, :, :, :, :, 0:size] = block.reshape(
            sizes + (-1, size)
        )

    def activate(spot, gate_up, grad_hidden, chunk):
        gate = gate_up[:, 2 * chunk * CHUNK : (2 * chunk + 1) * CHUNK]
        up = gate_up[:, (2 * chunk + 1) * CHUNK : (2 * chunk + 2) * CHUNK]
        grad = grad_hidden[:, chunk * CHUNK : (chunk + 1) * CHUNK]
        square = gate * gate
        curve = jnp.tanh(0.7978845608028654 * gate * (1.0 + 0.044715 * square))
        half = 0.5 * (1.0 + curve)
        gelu = gate * half
        slope = half + 0.5 * gate * (1.0 - curve * curve) * (
            0.7978845608028654 * (1.0 + 3 * 0.044715 * square)
        )
        hidden, grads = vmem["hidden"], vmem["grad_gate_up"]
        hidden[spot, :, chunk * CHUNK : (chunk + 1) * CHUNK] = low(gelu * up)
        grads[spot, :, 2 * chunk * CHUNK : (2 * chunk + 1) * CHUNK] = low(grad * up * slope)
        grads[spot, :, (2 * chunk + 1) * CHUNK : (2 * chunk + 2) * CHUNK] = low(grad * gelu)

    steps = last_of[6] + 1 - first_of[6]
    for spot in range(steps):
        unit = units[first_of[6] + spot]
        size = unit.shape[1]
        matrix = weight()
        groups_at = slice(unit.start // 16, (unit.start + size) // 16)
        down = low(wide(down_rows[groups_at]).reshape(size // 2, width))
        gate_up = mul(vmem["normed_ffn"][...], matrix())
        grad_hidden = mul(vmem["branch"][...], down, 1, 1)
        for chunk in range(size // (2 * CHUNK)):
            activate(spot, gate_up, grad_hidden, chunk)
        spent(5.0)
        vmem["grad_normed"][...] += mul(vmem["grad_gate_up"][spot, :, 0:size], matrix(), 1, 1)
        release()
        outcome[...] += mul(vmem["hidden"][spot, :, 0 : size // 2], down)
        weight_grad(spot, "normed_ffn", vmem["grad_gate_up"][spot, :, 0:size])
        scatter.advance()
    while not driver.done():
        driver.advance()
    pump()
    outcome_copy = pltpu.make_async_copy(outcome, outcome_out, out_sems.at[2])
    outcome_copy.start()

    def norm_back(which, stream, before, last):
        gain = vmem["gains"][which : which + 1]
        step_rows = 64

        def body(step, total):
            at = pl.ds(pl.multiple_of(step * step_rows, step_rows), step_rows)
            value = wide(stream[at, :])
            scale = lax.rsqrt(jnp.mean(value * value, axis=-1, keepdims=True) + 1e-06)
            unit = value * scale
            grad = vmem["grad_normed"][at, :]
            scaled = grad * gain
            result = wide(before[at, :]) + scale * (
                scaled - unit * jnp.mean(scaled * unit, axis=-1, keepdims=True)
            )
            dx[at, :] = result
            if not last:
                rounded[2 - which, at, :] = low(result)
            return total + jnp.sum(grad * unit, axis=0, keepdims=True)

        total = lax.fori_loop(0, rows // step_rows, body, jnp.zeros((1, width), jnp.float32))
        gain_grads[which : which + 1, :] = total

    def through(source, target, add, rounding):
        value = mul(source[...], weight()(), 1, 1)
        if add:
            value = value + target[...]
        target[...] = low(value) if rounding else value
        release()

    left = lax.broadcasted_iota(jnp.int32, (1, LANES), 1) < HEAD

    def stack(value):
        zero = jnp.zeros_like(value)
        return jnp.concatenate([jnp.where(left, value, zero), jnp.where(left, zero, value)], axis=0)

    def pair_back(queries, keys, values, probs, grad):
        count = queries.shape[0]
        stacked = stack(grad)
        spread = mul(stacked, values, 1, 1)
        wide_probs = wide(probs)
        product = wide_probs * spread
        scores = low(product - wide_probs * jnp.sum(product, axis=-1, keepdims=True))
        grad_values = low(mul(probs, stacked, 0, 0))
        both = mul(scores, keys)
        grad_queries = low(jnp.where(left, both[:count], both[count:]) * HEAD ** (-0.5))
        grad_keys = low(mul(scores, stack(queries * jnp.bfloat16(HEAD ** (-0.5))), 0, 0))
        return grad_queries, grad_keys, grad_values, scores

    def cross_back(pair):
        if pair + 1 < count_pairs:
            probs_copy(0, pair + 1, False).start()
        probs_copy(0, pair, False).wait()
        lanes = pl.ds(pair * LANES, LANES)

        def body(sequence, carry):
            at = pl.ds(pl.multiple_of(sequence * slot_rows, slot_rows), slot_rows)
            keys = pl.ds(pl.multiple_of(sequence * enc_rows, enc_rows), enc_rows)
            queries, pairs = vmem["queries"], vmem["pairs"]
            grads = pair_back(
                queries[at, lanes],
                pairs[0, keys, lanes],
                pairs[1, keys, lanes],
                probs_slots[0][pair % 2, sequence],
                grad_mixed[at, lanes],
            )
            queries[at, lanes], pairs[0, keys, lanes], pairs[1, keys, lanes] = grads[:3]
            return carry

        lax.fori_loop(0, seqs, body, 0)

    def self_back(pair):
        if pair + 1 < count_pairs:
            probs_copy(1, pair + 1, False).start()
        probs_copy(1, pair, False).wait()
        lanes = pl.ds(pair * LANES, LANES)
        total = 0.0
        for sequence in range(seqs):
            at = pl.ds(sequence * slot_rows, slot_rows)
            qkv = vmem["qkv"]
            grads = pair_back(
                qkv[0, at, lanes],
                qkv[1, at, lanes],
                qkv[2, at, lanes],
                probs_slots[1][pair % 2, sequence],
                grad_mixed[at, lanes],
            )
            qkv[0, at, lanes], qkv[1, at, lanes], qkv[2, at, lanes] = grads[:3]
            total = total + wide(grads[3])
        total = jnp.concatenate(
            [total, jnp.zeros((total.shape[0], period - slot_rows), jnp.float32)], axis=1
        )
        for head in range(2):
            sums = 0.0
            for group in range(slot_rows // 8):
                start = head * slot_rows + group * 8
                piece = total[start : start + 8]
                sums = sums + (pltpu.roll(piece, period - group * 8, 1) if group else piece)
            diag[2 * pair + head] = sums

    grad_mixed = vmem["normed_ffn"]
    chain, marks = [], {6: 0, 7: 0}

    def then(cost, step):
        chain.append((cost, step))

    def start_ffn():
        outcome_copy.wait()
        norm_back(2, vmem["third"], vmem["branch"], False)

    def start_cross():
        probs_copy(0, 0, False).start()
        through(rounded.at[0], grad_mixed, False, True)

    def encoder_back():
        keys, values = weight(), weight()
        stage = vmem["third"]
        for sequence in range(seqs):
            at = slice(sequence * enc_rows, (sequence + 1) * enc_rows)
            copy = pltpu.make_async_copy(
                stage.at[0:enc_rows], grad_encoder.at[at], out_sems.at[0]
            )
            if sequence:
                copy.wait()
            pairs = vmem["pairs"]
            stage[0:enc_rows] = mul(pairs[0, at], keys(), 1, 1) + mul(pairs[1, at], values(), 1, 1)
            copy.start()
        release()
        release()

    def end_cross():
        through(vmem["queries"], vmem["grad_normed"], False, False)

    def start_self():
        norm_back(1, vmem["second"], dx, False)

    def self_mixed():
        probs_copy(1, 0, False).start()
        through(rounded.at[1], grad_mixed, False, True)

    def self_normed(part):
        through(vmem["qkv"].at[part], vmem["grad_normed"], part > 0, False)

    def end_self():
        norm_back(0, vmem["tokens"], dx, True)
        pltpu.make_async_copy(dx, grad_tokens, out_sems.at[1]).start()

    then(1.5, start_ffn)
    marks[5] = len(chain)
    then(1.2, start_cross)
    for pair in range(count_pairs):
        then(0.8, functools.partial(cross_back, pair))
    marks[2] = marks[4] = len(chain)
    then(4.5, encoder_back)
    then(1.2, end_cross)
    then(1.5, start_self)
    marks[3] = len(chain)
    then(1.2, self_mixed)
    for pair in range(count_pairs):
        then(0.8, functools.partial(self_back, pair))
    marks[1] = len(chain)
    for part in range(3):
        then(1.2, functools.partial(self_normed, part))
    then(1.5, end_self)
    marks[0] = len(chain)

    def pack_grad(u):
        slot = u % whole_slots.shape[0]
        table = 0.0
        for row in range(8):
            part = diag[:, row, :]
            table = table + (pltpu.roll(part, period - row, 1) if row else part)
        high = low(table)
        rel = mul(high, spread[...], 1, 1) + mul(low(table - wide(high)), spread[...], 1, 1)
        for z in range(sizes[0]):
            for y in range(sizes[1]):
                at = slice((z * sizes[1] + y) * LANES, (z * sizes[1] + y + 1) * LANES)
                top = jnp.concatenate(
                    [gain_grads[:, at], jnp.zeros((PACK // 2 - norms, LANES), jnp.float32)], axis=0
                )
                tile = low(jnp.concatenate([top, rel], axis=0))
                for x in range(sizes[2]):
                    for core in range(sizes[3]):
                        whole_slots[slot, z, y, x, core, :, 0:LANES] = tile

    groups = owned[6].shape[0] // 8

    def down_piece(spot):
        size = vmem["hidden"].shape[2]
        size = min(size, hidden_width - spot * size)
        start = spot * vmem["hidden"].shape[2] // 8
        block = mul(vmem["hidden"][spot, :, 0:size], vmem["branch"][...], 0, 0)
        down_rows[start : start + size // 8] = low(block.reshape(size // 8, 8, width))

    def down_grad(u):
        slot = u % whole_slots.shape[0]
        start = back_units[u].row // 8

        block_rows = whole_slots.shape[5]

        def body(device, carry):
            piece = down_rows[pl.ds(device * groups + start, block_rows // 8)]
            c, rest = device % sizes[3], device // sizes[3]
            x, rest = rest % sizes[2], rest // sizes[2]
            whole_slots[slot, rest // sizes[1], rest % sizes[1], x, c, :, :] = low(
                wide(piece).reshape(block_rows, width)
            )
            return carry

        lax.fori_loop(0, sizes[0] * sizes[1] * sizes[2] * sizes[3], body, 0)

    def grad_of(u):
        unit = back_units[u]
        owner = unit.owner
        part = unit.start // width
        if owner == 7:
            if unit.row == 0:
                for spot in range(vmem["hidden"].shape[0]):
                    down_piece(spot)
            down_grad(u)
        elif owner == 5:
            weight_grad(u, "mixed_cross", rounded[0])
        elif owner == 2:
            weight_grad(u, "encoder", vmem["pairs"][part])
        elif owner == 4:
            weight_grad(u, "normed_cross", vmem["queries"][...])
        elif owner == 3:
            weight_grad(u, "mixed_self", rounded[1])
        elif owner == 1:
            weight_grad(u, "normed_self", vmem["qkv"][part])
        else:
            pack_grad(u)

    position = 0
    budget = 5.0
    for u in range(steps, len(back_units)):
        owner = back_units[u].owner
        while position < marks[owner]:
            chain[position][1]()
            position += 1
        grad_of(u)
        scatter.advance()
        used = 0.0
        while owner == 7 and position < len(chain) and used < budget:
            used += chain[position][0]
            chain[position][1]()
            position += 1
    while not scatter.done():
        scatter.advance()
    pltpu.make_async_copy(
        vmem["third"].at[0:enc_rows], grad_encoder.at[0:enc_rows], out_sems.at[0]
    ).wait()
    pltpu.make_async_copy(dx, grad_tokens, out_sems.at[1]).wait()
    gather_wires.finish()


def layer_all(place, shards, norm_gains, rel_bias, data):
    tokens, encoder, cotangent, lengths, enc_lengths, bucket_ids = data
    blocks = [(PACK, LANES)] + [shard.shape for shard in shards]
    sizes = place.sizes
    seqs, slot_rows, width = tokens.shape
    rows, enc_rows = seqs * slot_rows, encoder.shape[1]
    block_rows = blocks[1][0]
    down_rows = blocks[7][0] * 8
    units = make_units(blocks, PIECE, ORDER)
    back_units = []
    for owner in BACK_ORDER:
        if owner == 7:
            for row in range(0, down_rows, block_rows):
                unit = Unit(7, (block_rows, width), 0, width, len(back_units) % 2)
                unit.row = row
                back_units.append(unit)
        else:
            back_units += make_units(blocks, PIECE, (owner,), len(back_units))
    devices = sizes[0] * sizes[1] * sizes[2] * sizes[3]
    piece = PIECE // block_rows
    rings = ring_shapes(sizes, block_rows, piece)
    low_type, wide_type = jnp.bfloat16, jnp.float32
    steps = sum(unit.owner == 6 for unit in units)
    shapes = {
        "tokens": ((rows, width), low_type),
        "encoder": ((seqs * enc_rows, width), low_type),
        "branch": ((rows, width), low_type),
        "normed_self": ((rows, width), low_type),
        "qkv": ((3, rows, width), low_type),
        "mixed_self": ((rows, width), low_type),
        "second": ((rows, width), wide_type),
        "normed_cross": ((rows, width), low_type),
        "queries": ((rows, width), low_type),
        "pairs": ((2, seqs * enc_rows, width), low_type),
        "mixed_cross": ((rows, width), low_type),
        "third": ((rows, width), wide_type),
        "normed_ffn": ((rows, width), low_type),
        "hidden": ((steps, rows, piece // 2), low_type),
        "grad_gate_up": ((steps, rows, piece), low_type),
        "grad_normed": ((rows, width), wide_type),
        "gains": ((norm_gains.shape[0], width), wide_type),
    }
    owned = [(block[0], block[1]) for block in blocks[1:7]] + [(down_rows, width)]
    pair_shapes = [(seqs, 2 * slot_rows, enc_rows), (seqs, 2 * slot_rows, slot_rows)]
    anywhere = pl.BlockSpec(memory_space=pl.ANY)
    inside = pl.BlockSpec(memory_space=pltpu.VMEM)
    scalars = pl.BlockSpec(memory_space=pltpu.SMEM)
    sends, returns = copies_of(units, sizes), copies_of(back_units, sizes)
    local = len(units) + blocks[6][1] // CHUNK
    depth = 3
    shaped = jax.ShapeDtypeStruct
    results = pl.pallas_call(
        functools.partial(
            layer_kernel, place, units, back_units, len(blocks), seqs, tuple(rings)
        ),
        out_shape=[shaped(sizes + block, low_type) for block in blocks]
        + [shaped((rows, width), wide_type)] * 2
        + [shaped((seqs * enc_rows, width), wide_type)]
        + [shaped((width // LANES,) + shape, low_type) for shape in pair_shapes]
        + [shaped(block, wide_type) for block in owned]
        + [shaped(norm_gains.shape, wide_type), shaped((1, rel_bias.shape[0]), wide_type)],
        in_specs=[anywhere] * (len(blocks) - 1)
        + [inside] * 2
        + [anywhere] * 3
        + [scalars] * 2
        + [inside],
        out_specs=[anywhere] * (len(blocks) + 5) + [inside] * (len(owned) + 2),
        scratch_shapes=[pltpu.VMEM(*shapes[name]) for name in BUFFERS]
        + [pltpu.VMEM((2,) + shape, low_type) for shape in pair_shapes]
        + [
            pltpu.VMEM((rows, width), wide_type),
            pltpu.VMEM((2, rows, width), low_type),
            pltpu.VMEM((devices * blocks[7][0] + 8, 8, width), low_type),
            pltpu.VMEM((HEADS, 8, 2 * slot_rows), wide_type),
            pltpu.VMEM((norm_gains.shape[0], width), wide_type),
            pltpu.VMEM((PACK, LANES), low_type),
            pltpu.VMEM(sizes + (PACK, LANES), low_type),
            pltpu.VMEM((LANES, 2 * slot_rows), low_type),
            pltpu.VMEM((HEADS, 2 * slot_rows), wide_type),
            pltpu.VMEM((depth,) + sizes + (block_rows, piece), low_type),
            pltpu.VMEM((2,) + sizes + (block_rows, piece), low_type),
            pltpu.VMEM((RING,) + sizes[:3] + (block_rows, piece), low_type),
        ]
        + [pltpu.VMEM((RING,) + shape, low_type) for shape in rings.values()]
        + [
            pltpu.SemaphoreType.DMA((number,))
            for number in (sends, sends, returns, returns, local, depth + 2, 3, 4, 3)
        ],
        compiler_params=pltpu.CompilerParams(
            collective_id=0, has_side_effects=True, vmem_limit_bytes=63 * 2**20
        ),
        name="layer_all",
    )(
        *shards,
        norm_gains,
        rel_bias.reshape(1, -1),
        tokens.reshape(rows, width),
        encoder.reshape(-1, width),
        cotangent.reshape(rows, width),
        lengths,
        enc_lengths,
        bucket_ids.reshape(1, -1),
    )
    return results[len(blocks) :]


def norm_scale(stream, gain):
    return stream * lax.rsqrt(jnp.mean(stream * stream, axis=-1, keepdims=True) + 1e-06) * gain


def gelu_tanh(values):
    return (
        0.5
        * values
        * (1.0 + jnp.tanh(0.7978845608028654 * (values + 0.044715 * values * values * values)))
    )


def gated(gate_up):
    half_width = gate_up.shape[1] // 2
    return gelu_tanh(gate_up[:, :half_width]) * gate_up[:, half_width:]


def product(spec, left, right):
    return jnp.einsum(spec, left, right, preferred_element_type=jnp.float32)


def attend(queries, key_rows, value_rows, pos_bias, keep_mask):
    scores = product("bihc,bjhc->bhij", queries, key_rows) * HEAD ** (-0.5)
    if pos_bias is not None:
        scores = scores + pos_bias
    masked = jnp.where(keep_mask[:, None], scores, -1e30)
    row_max = jnp.max(masked, axis=-1, keepdims=True)
    powers = jnp.exp(masked - row_max)
    probs = powers / jnp.sum(powers, axis=-1, keepdims=True)
    low_probs = probs.astype(jnp.bfloat16)
    mixed = product("bhij,bjhc->bihc", low_probs, value_rows)
    return mixed.astype(jnp.bfloat16), low_probs


def attend_back(queries, key_rows, value_rows, low_probs, grad_mixed):
    probs = low_probs.astype(jnp.float32)
    grad_values = product("bhij,bihc->bjhc", low_probs, grad_mixed)
    grad_probs = product("bihc,bjhc->bhij", grad_mixed, value_rows)
    grad_scores = (
        probs * (grad_probs - jnp.sum(probs * grad_probs, axis=-1, keepdims=True))
    ).astype(jnp.bfloat16)
    grad_queries = product("bhij,bjhc->bihc", grad_scores, key_rows) * HEAD ** (-0.5)
    grad_keys = product("bhij,bihc->bjhc", grad_scores, queries) * HEAD ** (-0.5)
    return grad_queries, grad_keys, grad_values, grad_scores


def toeplitz(table, size):
    lead = table.shape[:-1]
    row = jnp.concatenate(
        [table[..., ::-1], jnp.broadcast_to(table[..., :1], lead + (size,))], axis=-1
    )
    tiled = jnp.broadcast_to(row[..., None, :], lead + (size, 2 * size)).reshape(lead + (-1,))
    tiled = jnp.concatenate([tiled[..., size - 1 :], row[..., :1]], axis=-1)
    tiled = tiled[..., : size * (2 * size - 1)]
    return tiled.reshape(lead + (size, 2 * size - 1))[..., :size]


def layer(weights, gains, rel_bias, tokens, encoder, cotangent, lengths, enc_lengths, bucket_ids):
    self_qkv, self_out, cross_q, cross_kv, cross_out, ff_in, ff_out = weights
    count, slots, width = tokens.shape
    enc_count = encoder.shape[1]
    bucket_map = toeplitz(bucket_ids, slots).reshape(-1)
    onehot = (lax.iota(jnp.int32, BUCKETS)[:, None] == bucket_map[None, :]).astype(jnp.bfloat16)
    pos_bias = jnp.dot(rel_bias, onehot, preferred_element_type=jnp.float32).reshape(
        HEADS, slots, slots
    )
    row_ids = lax.iota(jnp.int32, slots)
    self_mask = (row_ids[None, None, :] <= row_ids[None, :, None]) & (
        row_ids[None, None, :] < lengths[:, None, None]
    )
    cross_mask = lax.iota(jnp.int32, enc_count)[None, None, :] < enc_lengths[:, None, None]
    enc_rows = encoder.reshape(count * enc_count, width)
    dot = functools.partial(jnp.dot, preferred_element_type=jnp.float32)
    low = lambda value: value.astype(jnp.bfloat16)
    stream = tokens.reshape(count * slots, width).astype(jnp.float32)
    normed_self, back_self = jax.vjp(norm_scale, stream, gains[0])
    normed_self = low(normed_self)
    qkv = low(dot(normed_self, self_qkv)).reshape(count, slots, 3, HEADS, HEAD)
    mixed_self, probs_self = attend(qkv[:, :, 0], qkv[:, :, 1], qkv[:, :, 2], pos_bias, self_mask)
    mixed_self = mixed_self.reshape(count * slots, width)
    second = stream + dot(mixed_self, self_out)
    normed_cross, back_cross = jax.vjp(norm_scale, second, gains[1])
    normed_cross = low(normed_cross)
    queries = low(dot(normed_cross, cross_q)).reshape(count, slots, HEADS, HEAD)
    pairs = low(dot(enc_rows, cross_kv)).reshape(count, enc_count, 2, HEADS, HEAD)
    mixed_cross, probs_cross = attend(queries, pairs[:, :, 0], pairs[:, :, 1], None, cross_mask)
    mixed_cross = mixed_cross.reshape(count * slots, width)
    third = second + dot(mixed_cross, cross_out)
    normed_ffn, back_ffn = jax.vjp(norm_scale, third, gains[2])
    normed_ffn = low(normed_ffn)
    gate_up = dot(normed_ffn, ff_in)
    activated, back_gate = jax.vjp(gated, gate_up)
    hidden = low(activated)
    outcome = third + dot(hidden, ff_out)

    valid = (row_ids[None, :] < lengths[:, None]).astype(jnp.float32)[:, :, None]
    grad_out = (cotangent.astype(jnp.float32) * valid).reshape(count * slots, width)
    branch = low(grad_out)
    grad_ff_out = product("lf,ld->fd", hidden, branch)
    grad_hidden = product("ld,fd->lf", branch, ff_out)
    (grad_gate_up,) = back_gate(grad_hidden)
    grad_gate_up = low(grad_gate_up)
    grad_ff_in = product("ld,lf->df", normed_ffn, grad_gate_up)
    grad_stream, gain_ffn = back_ffn(product("lf,df->ld", grad_gate_up, ff_in))
    grad_third = grad_out + grad_stream
    branch = low(grad_third)
    grad_cross_out = product("le,ld->ed", mixed_cross, branch)
    grad_mixed = low(product("ld,ed->le", branch, cross_out)).reshape(count, slots, HEADS, HEAD)
    grad_queries, grad_keys, grad_values, unused = attend_back(
        queries, pairs[:, :, 0], pairs[:, :, 1], probs_cross, grad_mixed
    )
    grad_query_rows = low(grad_queries.reshape(count * slots, width))
    grad_pair_rows = low(
        jnp.concatenate(
            [
                grad_keys.reshape(count * enc_count, width),
                grad_values.reshape(count * enc_count, width),
            ],
            axis=1,
        )
    )
    grad_cross_q = product("ld,le->de", normed_cross, grad_query_rows)
    grad_cross_kv = product("ed,ef->df", enc_rows, grad_pair_rows)
    grad_enc = product("ef,df->ed", grad_pair_rows, cross_kv)
    grad_stream, gain_cross = back_cross(product("le,de->ld", grad_query_rows, cross_q))
    grad_second = grad_third + grad_stream
    branch = low(grad_second)
    grad_self_out = product("le,ld->ed", mixed_self, branch)
    grad_mixed = low(product("ld,ed->le", branch, self_out)).reshape(count, slots, HEADS, HEAD)
    grad_queries, grad_keys, grad_values, grad_scores = attend_back(
        qkv[:, :, 0], qkv[:, :, 1], qkv[:, :, 2], probs_self, grad_mixed
    )
    score_sums = jnp.sum(grad_scores.astype(jnp.float32), axis=0).reshape(HEADS, slots * slots)
    grad_rel_bias = product("hn,bn->hb", low(score_sums), onehot)
    grad_qkv = low(
        jnp.concatenate(
            [part.reshape(count * slots, width) for part in (grad_queries, grad_keys, grad_values)],
            axis=1,
        )
    )
    grad_self_qkv = product("ld,lf->df", normed_self, grad_qkv)
    grad_stream, gain_self = back_self(product("lf,df->ld", grad_qkv, self_qkv))
    grad_tok = grad_second + grad_stream
    grad_gains = jnp.stack([gain_self, gain_cross, gain_ffn], axis=0)
    grads = (
        grad_self_qkv,
        grad_self_out,
        grad_cross_q,
        grad_cross_kv,
        grad_cross_out,
        grad_ff_in,
        grad_ff_out,
    )
    return (
        outcome.reshape(tokens.shape),
        grad_tok.reshape(tokens.shape),
        grad_enc.reshape(encoder.shape),
        grads,
        grad_gains,
        grad_rel_bias,
    )


AXES = ("dp", "fsdp")


def by_collectives(data, shards):
    whole = lambda shard, axis=0: lax.all_gather(shard, AXES, axis=axis, tiled=True)
    weights = tuple(whole(shard) for shard in shards[:7])
    gains = whole(shards[7], 1).astype(jnp.float32)
    rel_bias = whole(shards[8]).reshape(HEADS, BUCKETS)
    outcome, grad_tok, grad_enc, grads, grad_gains, grad_rel_bias = layer(
        weights, gains, rel_bias, *data
    )
    settle = lambda total, axis=0: lax.psum_scatter(
        total, AXES, scatter_dimension=axis, tiled=True
    )
    return (
        (outcome, grad_tok, grad_enc)
        + tuple(settle(grad) for grad in grads)
        + (settle(grad_gains, 1), settle(grad_rel_bias.reshape(-1)))
    )


def by_kernels(place, data, shards):
    self_qkv, self_out, cross_q, cross_kv, cross_out, ff_in, ff_out = shards[:7]
    ff_rows, width = ff_out.shape
    sent = (self_qkv, cross_kv, self_out, cross_q, cross_out, ff_in)
    sent += (ff_out.reshape(ff_rows // 8, 8, width),)
    results = layer_all(place, sent, shards[7], shards[8], data)
    outcome, grad_tok, grad_enc = (
        result.reshape(like.shape)
        for result, like in zip(results[:3], (data[0], data[0], data[1]))
    )
    g_qkv, g_kv, g_so, g_cq, g_co, g_in, g_out = results[5:12]
    owned = (g_qkv, g_so, g_cq, g_kv, g_co, g_in, g_out)
    return (outcome, grad_tok, grad_enc) + owned + (results[12], results[13].reshape(-1))


def on_device(place, *args):
    data, shards = args[:6], args[6:]
    per = shards[7].shape[1]
    regular = all(shard.shape[0] % 16 == 0 for shard in shards[:6])
    group = place.sizes[2] * place.sizes[3]
    if regular and shards[6].shape[0] % 8 == 0 and group * per == LANES:
        return by_kernels(place, data, shards)
    return by_collectives(data, shards)


def solution(mesh):
    rows = P(AXES, None, None)
    flat = P(AXES)
    matrix = P(AXES, None)
    split = P(None, AXES)
    place = Place(mesh.shape["dp"], mesh.shape["fsdp"])
    return jax.shard_map(
        functools.partial(on_device, place),
        mesh=mesh,
        in_specs=(rows, rows, rows, flat, flat, P()) + (matrix,) * 7 + (split, flat),
        out_specs=(rows, rows, rows) + (matrix,) * 7 + (split, flat),
        check_vma=False,
    )
```

```python
import functools

import jax
import jax.numpy as jnp
from jax import lax
from jax.experimental import pallas as pl
from jax.experimental.pallas import tpu as pltpu
from jax.sharding import PartitionSpec as P

HEADS = 16
HEAD = 64
BUCKETS = 32
PACK = 32
LANES = 128
PIECE = 32 * 1024

MESH = pl.DeviceIdType.MESH


class Place:
    def __init__(self, dp, fsdp):
        self.sizes = (dp // 2, 2, fsdp // 2, 2)

    def locate(self):
        row, column = lax.axis_index("dp"), lax.axis_index("fsdp")
        sizes = self.sizes
        self.here = (row // sizes[1], row % sizes[1], column // sizes[3], column % sizes[3])
        z = self.here[0]
        self.inner, self.outer = z % 3 != 0, z % 3 == 0
        self.twin, self.far, self.entry = z + 1 - 2 * (z % 2), 2 - 2 * (z // 2), 2 - z // 2

    def moved(self, axis, step):
        coords = list(self.here)
        coords[axis] = (coords[axis] + step) % self.sizes[axis]
        return coords

    def at(self, axis, coordinate):
        coords = list(self.here)
        coords[axis] = coordinate
        return coords

    def hops(self, axes):
        steps = []
        for axis in axes:
            steps += ["spread", "relay"] if axis == 0 and self.sizes[0] == 4 else [axis]
        return steps

    def device(self, coords):
        return (coords[0] * self.sizes[1] + coords[1], coords[2] * self.sizes[3] + coords[3])

    def peers(self):
        return [(axis, step) for axis in range(4) for step in range(1, self.sizes[axis])]

    def greet(self):
        barrier = pltpu.get_barrier_semaphore()
        for axis, step in self.peers():
            pl.semaphore_signal(
                barrier, inc=1, device_id=self.device(self.moved(axis, step)), device_id_type=MESH
            )
        pl.semaphore_wait(barrier, len(self.peers()))


def split_lanes(width, turn):
    if width == 8 * LANES:
        last = (1 if turn == 3 else 2) * LANES
        more, less = 5 * LANES - last, 3 * LANES
        order = (1, 2, 0) if turn % 2 else (2, 1, 0)
        return ((0, more, (0, 2, 1)), (more, less, (0, 1, 2)), (more + less, last, order))
    if width % (2 * LANES) == 0:
        return ((0, width // 2, (0, 2, 1)), (width // 2, width // 2, (0, 1, 2)))
    return ((0, width, (0, 2, 1)),)


class Unit:
    def __init__(self, owner, block, start, count, turn):
        self.owner, self.start, self.count = owner, start, count
        self.grouped = len(block) == 3
        self.shape = (count,) + block[1:] if self.grouped else (block[0], count)
        self.paths = split_lanes(self.shape[-1], turn)

    def part(self, start=0, size=None):
        size = self.shape[-1] if size is None else size
        if self.grouped:
            return (pl.ds(self.start, self.count), slice(None), pl.ds(start, size))
        return (slice(None), pl.ds(self.start + start, size))


def make_units(blocks, piece, order, before=0):
    units = []
    for owner in order:
        block = blocks[owner]
        total, most = (block[0], piece // 8 // block[2] or 1) if len(block) == 3 else (block[1], piece // block[0])
        start = 0
        while start < total:
            count = min(most, total - start)
            units.append(Unit(owner, block, start, count, (before + len(units)) % 4))
            start += count
    return units


def guarded(condition, action):
    if condition is True:
        action()
    elif condition is not False:
        pl.when(condition)(action)


class Message:
    def __init__(self, make, sends, receives):
        self.make, self.sends, self.receives = make, sends, receives

    def start(self):
        guarded(self.sends, lambda: self.make().start())

    def wait_send(self):
        guarded(self.sends, lambda: self.make().wait_send())

    def wait_recv(self):
        guarded(self.receives, lambda: self.make().wait_recv())

    def wait(self):
        self.wait_send()
        self.wait_recv()


class Wires:
    def __init__(self, place, send_sems, recv_sems):
        self.place, self.send_sems, self.recv_sems = place, send_sems, recv_sems
        self.started, self.spot = [], 0

    def send(self, source, target, coords, sends=True, receives=True, arrival=None):
        spot = self.spot
        self.spot += 1
        arrival = spot if arrival is None else arrival
        device = self.place.device(coords)

        def make():
            return pltpu.make_async_remote_copy(
                src_ref=source,
                dst_ref=target,
                send_sem=self.send_sems.at[spot],
                recv_sem=self.recv_sems.at[arrival],
                device_id=device,
                device_id_type=MESH,
            )

        message = Message(make, sends, receives)
        message.start()
        self.started.append(message)
        return message

    def along(self, axis, source, target):
        return [
            self.send(source, target, self.place.moved(axis, step))
            for step in range(1, self.place.sizes[axis])
        ]

    def spread(self, source, target):
        place = self.place
        messages = [self.send(source, target, place.at(0, place.twin))]
        first = self.spot
        arrival = first + place.here[0] % 2
        entry = place.at(0, place.entry)
        messages.append(self.send(source, target, entry, receives=False, arrival=arrival))
        for arrival in (first, first + 1):
            messages.append(
                self.send(source, target, entry, sends=False, receives=place.inner, arrival=arrival)
            )
        return messages

    def relay(self, ref):
        place = self.place
        twin = place.at(0, place.twin)
        return [self.send(ref, ref, twin, sends=place.inner, receives=place.outer)]

    def finish(self):
        for message in self.started:
            message.wait_send()


def gather_stages(place, units, shards, wholes, wires, own_copies):
    full = slice(None)
    pending = {}

    def settle(u):
        for copy in pending[u]:
            copy.wait_recv()
        pending[u] = []

    def move(u, stage):
        unit = units[u]
        whole = wholes[unit.owner]
        if stage == int(unit.owner != 6):
            for copy in own_copies[u]:
                copy.wait()
        if stage:
            settle(u)
        pending[u] = []
        for start, size, axes in unit.paths:
            steps = place.hops(axes)
            if stage >= len(steps):
                continue
            step, done = steps[stage], steps[:stage]
            part = unit.part(start, size)
            index = [full if axis in done else place.here[axis] for axis in range(3)]
            if "relay" in done:
                index[0] = full
            elif step == "relay":
                index[0] = pl.ds(place.far, 2)
            target = whole.at[tuple(index) + (place.here[3],) + part]
            source = target
            if stage == 0 and unit.owner != 6:
                source = shards[unit.owner].at[part]
            if step == "spread":
                pending[u] += wires.spread(source, target)
            elif step == "relay":
                pending[u] += wires.relay(target)
            else:
                pending[u] += wires.along(step, source, target)

    def across(u):
        settle(u)
        unit = units[u]
        ref = wholes[unit.owner].at[(full, full, full, place.here[3]) + unit.part()]
        pending[u] = wires.along(3, ref, ref)

    count = len(place.hops((0, 1, 2)))
    return tuple(functools.partial(move, stage=stage) for stage in range(count)) + (across, settle)


def copies_of(units, sizes):
    line = 4 if sizes[0] == 4 else sizes[0] - 1
    per_path = line + sizes[1] - 1 + sizes[2] - 1
    return sum(1 + len(unit.paths) * (per_path + 1) for unit in units)


def mul(left, right, left_dim=1, right_dim=0):
    return lax.dot_general(
        left, right, (((left_dim,), (right_dim,)), ((), ())), preferred_element_type=jnp.float32
    )


def low(value):
    return value.astype(jnp.bfloat16)


def wide(value):
    return value.astype(jnp.float32)


def rms_rows(source, target, gain, rows=64):
    def body(step, carry):
        at = pl.ds(pl.multiple_of(step * rows, rows), rows)
        value = wide(source[at, :])
        scale = lax.rsqrt(jnp.mean(value * value, axis=-1, keepdims=True) + 1e-06)
        target[at, :] = low(value * scale * gain)
        return carry

    lax.fori_loop(0, source.shape[0] // rows, body, 0)


def attend_pair(queries, key_rows, value_rows, bias, mask):
    rows = queries.shape[0]
    left = lax.broadcasted_iota(jnp.int32, (1, LANES), 1) < HEAD
    zero = jnp.zeros_like(queries)
    scaled = queries * jnp.bfloat16(HEAD ** (-0.5))
    stacked = jnp.concatenate(
        [jnp.where(left, scaled, zero), jnp.where(left, zero, scaled)], axis=0
    )
    scores = mul(stacked, key_rows, 1, 1)
    if bias is not None:
        scores = scores + bias
    scores = jnp.where(mask, scores, -1e30)
    powers = jnp.exp(scores - jnp.max(scores, axis=-1, keepdims=True))
    probs = low(powers / jnp.sum(powers, axis=-1, keepdims=True))
    none = jnp.zeros_like(value_rows)
    mixed = mul(probs[:rows], jnp.where(left, value_rows, none)) + mul(
        probs[rows:], jnp.where(left, none, value_rows)
    )
    return probs, low(mixed)


class Driver:
    def __init__(self, units, stages, lead):
        self.units, self.stages, self.lead = units, stages, lead
        self.tick, self.debt = 0, 0.0

    def done(self):
        return self.tick >= len(self.units) + len(self.stages) - 1

    def settled(self):
        return self.tick - len(self.stages)

    def advance(self):
        for lag, stage in enumerate(self.stages):
            if 0 <= self.tick - lag < len(self.units):
                stage(self.tick - lag)
        self.tick += 1

    def until(self, unit):
        while self.settled() < unit:
            self.advance()

    def spent(self, cost):
        self.debt += cost
        while self.debt >= self.lead:
            self.debt -= self.lead
            if not self.done():
                self.advance()


def scatter_hops(place, axes):
    names = {"spread": "last", "relay": "relay"}
    return [(names.get(step, "axis"), 0 if step in names else step) for step in place.hops(axes)[::-1]]


def ring_shapes(place, block_rows, width):
    sizes, shapes = place.sizes, {}
    for turn in range(4):
        for start, lanes, axes in split_lanes(width, turn):
            left = list(range(3))
            for hop, (step, axis) in enumerate(scatter_hops(place, axes)):
                senders = sizes[axis] - 1 if step == "axis" else 2
                rest = tuple(sizes[other] for other in left if other != axis)
                slots = RING + (hop == 1)
                lanes = max(lanes, shapes.get((axes, hop), (0,))[-1])
                shapes[axes, hop] = (slots, senders) + rest + (block_rows, lanes)
                if step != "relay":
                    left.remove(axis)
    return shapes


def scatter_stages(place, units, whole_slots, arrived, rings, finish, wires):
    sizes, full = place.sizes, slice(None)
    here = place.here
    pending = {}

    def settle(u):
        for copy in pending[u]:
            copy.wait()
        pending[u] = []

    def lanes(u):
        return (full, pl.ds(0, units[u].shape[1]))

    def slot(u):
        return whole_slots.at[u % whole_slots.shape[0]]

    def spread(b, axes):
        coords = {}
        for axis in reversed(axes):
            coords[axis] = b % sizes[axis]
            b = b // sizes[axis]
        return coords

    def count(axes):
        total = 1
        for axis in axes:
            total *= sizes[axis]
        return total

    def held(u, path, hop):
        start, size, axes = path
        steps = scatter_hops(place, axes)
        done = [h for h in range(hop) if steps[h][0] != "relay"]
        gone = [steps[h][1] for h in done]
        left = [axis for axis in range(3) if axis not in gone]
        if not done:
            ring = u % arrived.shape[0]
            return left, lambda at: (
                arrived,
                (ring,) + tuple(at[a] for a in left) + (full, pl.ds(start, size)),
            )
        ref = rings[axes, done[-1]]
        ring = u % ref.shape[0]
        return left, lambda at: (
            ref,
            (ring, 0) + tuple(at[a] for a in left) + (full, pl.ds(0, size)),
        )

    def landing(u, path, hop, sender, at=None):
        start, size, axes = path
        ref = rings[axes, hop]
        rest = len(ref.shape) - 4
        inner = (full,) * rest if at is None else at
        return ref, (u % ref.shape[0], sender) + inner + (full, pl.ds(0, size))

    def first(u):
        source = slot(u).at[(full, full, full, (here[3] + 1) % 2) + lanes(u)]
        target = arrived.at[(u % arrived.shape[0], full, full, full) + lanes(u)]
        pending[u] = [wires.send(source, target, place.moved(3, 1))]

    def pass_on(u, hop):
        for path in units[u].paths:
            steps = scatter_hops(place, path[2])
            if hop >= len(steps):
                continue
            step, axis = steps[hop]
            left, where = held(u, path, hop)

            def take(coordinate):
                ref, index = where({a: coordinate if a == axis else full for a in left})
                return ref.at[index]

            def put(sender):
                ref, index = landing(u, path, hop, sender)
                return ref.at[index]

            if step == "axis":
                for move in range(1, sizes[axis]):
                    coords = place.moved(axis, move)
                    pending[u].append(wires.send(take(coords[axis]), put(move - 1), coords))
            elif step == "relay":
                ref, index = landing(u, path, hop, pl.ds(0, 2))
                pending[u].append(
                    wires.send(
                        take(pl.ds(place.far, 2)),
                        ref.at[index],
                        place.at(0, place.twin),
                        sends=place.outer,
                        receives=place.inner,
                    )
                )
            else:
                pending[u].append(wires.send(take(place.twin), put(0), place.at(0, place.twin)))
                spot = wires.spot
                for other in range(2):
                    pending[u].append(
                        wires.send(
                            take(place.far + other),
                            put(1),
                            place.at(0, place.far + other),
                            sends=place.inner,
                            receives=other == 0,
                            arrival=spot,
                        )
                    )

    def merge(u, path, hop):
        start, size, axes = path
        steps = scatter_hops(place, axes)
        if hop >= len(steps):
            return
        step, axis = steps[hop]
        left, before = held(u, path, hop)
        rest = [a for a in left if a != axis]
        senders = rings[axes, hop].shape[1]

        def relayed(b, carry):
            at = spread(b % count(rest), rest)
            which = b // count(rest)
            ref, index = before({**at, axis: place.far + which})
            source, arrival = landing(u, path, hop, which, tuple(at[a] for a in rest))
            ref[index] = low(wide(ref[index]) + wide(source[arrival]))
            return carry

        def take_relay():
            lax.fori_loop(0, 2 * count(rest), relayed, 0)

        if step == "relay":
            guarded(place.inner, take_relay)
            return

        def body(b, carry):
            at = spread(b, rest)
            source, index = before({**at, axis: here[axis]})
            value = wide(source[index])
            for sender in range(senders):
                source, index = landing(u, path, hop, sender, tuple(at[a] for a in rest))
                value = value + wide(source[index])
            if hop == len(steps) - 1:
                finish(u, start, size, value)
            else:
                target, index = landing(u, path, hop, 0, tuple(at[a] for a in rest))
                target[index] = low(value)
            return carry

        if hop == len(steps) - 1:
            body(0, 0)
        else:
            lax.fori_loop(0, count(rest), body, 0)

    def second(u):
        settle(u)
        ring, own = u % arrived.shape[0], slot(u)

        def body(b, carry):
            at = spread(b, (0, 1, 2))
            index = tuple(at[a] for a in range(3))
            target = (ring,) + index + lanes(u)
            arrived[target] = low(wide(arrived[target]) + wide(own[index + (here[3],) + lanes(u)]))
            return carry

        lax.fori_loop(0, count((0, 1, 2)), body, 0)
        pass_on(u, 0)

    def later(u, hop):
        settle(u)
        for path in units[u].paths:
            merge(u, path, hop)
        pass_on(u, hop + 1)

    hops = len(scatter_hops(place, (0, 1, 2)))
    return (first, second) + tuple(functools.partial(later, hop=hop) for hop in range(hops))


CHUNK = 256
RING = 5
ORDER = (0, 1, 2, 3, 4, 5, 7, 6)
BACK_ORDER = (6, 7, 5, 2, 4, 3, 1, 0)
BUFFERS = (
    "branch", "normed_self", "qkv", "mixed_self", "second", "normed_cross",
    "queries", "pairs", "mixed_cross", "third", "normed_ffn", "hidden", "grad_gate_up",
    "grad_normed", "gains",
)


def layer_kernel(place, units, back_units, count, seqs, ring_keys, *refs):
    shards, refs = refs[: count - 1], refs[count - 1 :]
    gain_shard, rel_shard, tokens_in, encoder_in, cotangent_in = refs[:5]
    lengths, enc_lengths, bucket_ids, refs = refs[5], refs[6], refs[7], refs[8:]
    wholes, refs = refs[:count], refs[count:]
    outcome_out, grad_tokens, grad_encoder, refs = refs[0], refs[1], refs[2], refs[3:]
    probs_out, refs = refs[:2], refs[2:]
    owned, refs = refs[: count - 1], refs[count - 1 :]
    own_gains, own_rel, refs = refs[0], refs[1], refs[2:]
    vmem, refs = dict(zip(BUFFERS, refs)), refs[len(BUFFERS) :]
    probs_slots, refs = refs[:2], refs[2:]
    dx, down_rows, diag, gain_grads = refs[:4]
    own_pack, packs_in, spread, bias_rows, slots, whole_slots, arrived = refs[4:11]
    refs = refs[11:]
    rings, refs = dict(zip(ring_keys, refs)), refs[len(ring_keys) :]
    gather_send, gather_recv, scatter_send, scatter_recv = refs[:4]
    local_sems, fetch_sems, read_sems, probs_sems, out_sems = refs[4:]
    place.locate()
    sizes = place.sizes
    devices = sizes[0] * sizes[1] * sizes[2] * sizes[3]
    me = place.device(place.here)
    me = me[0] * (sizes[2] * sizes[3]) + me[1]
    rows, width = dx.shape
    slot_rows, enc_rows = rows // seqs, encoder_in.shape[0] // seqs
    shared = vmem["grad_gate_up"]
    parts = encoder_in.shape[0] // rows
    rounded, first_free = shared, 2
    count_pairs = width // LANES
    norms, per = gain_shard.shape
    rel_per = rel_shard.shape[1]
    gain_lane = (me % (LANES // per)) * per
    rel_row, rel_lane = me * rel_per // BUCKETS, (me * rel_per) % BUCKETS
    hidden_width = owned[5].shape[1] // 2
    outcome = dx

    def read_inputs(start, sems):
        sources = [(tokens_in, shared.at[start])]
        for part in range(parts):
            source = encoder_in.at[part * rows : (part + 1) * rows]
            sources.append((source, shared.at[start + 1 + part]))
        copies = [
            pltpu.make_async_copy(source, target, read_sems.at[sems + at])
            for at, (source, target) in enumerate(sources)
        ]
        for copy in copies:
            copy.start()
        return copies

    def encoder_rows(start):
        return shared[start + 1 : start + 1 + parts].reshape(parts * rows, width)

    reads = read_inputs(first_free, 1)
    branch_read = pltpu.make_async_copy(cotangent_in, vmem["branch"], read_sems.at[0])
    branch_read.start()
    padded = jnp.concatenate(
        [wide(gain_shard[...]), jnp.zeros((PACK // 2 - norms, per), jnp.float32)], axis=0
    )
    padded = jnp.concatenate([padded, jnp.zeros((PACK // 2, LANES - per), jnp.float32)], axis=1)
    rel = jnp.concatenate(
        [wide(rel_shard[...]), jnp.zeros((1, LANES - rel_per), jnp.float32)], axis=1
    )
    rel = jnp.broadcast_to(rel, (PACK // 2, LANES))
    pack_rows = lax.broadcasted_iota(jnp.int32, (PACK // 2, LANES), 0)
    rel = jnp.where(pack_rows == rel_row, pltpu.roll(rel, rel_lane, 1), 0.0)
    own_pack[...] = low(jnp.concatenate([pltpu.roll(padded, gain_lane, 1), rel], axis=0))
    shards = (own_pack,) + tuple(shards)
    own_copies, serial = {}, 0
    for u, unit in enumerate(units):
        pieces = [(unit.part(), unit.part())]
        if unit.owner == 6:
            pieces = []
            for at in range(unit.start, unit.start + unit.shape[1], CHUNK):
                spot = at // CHUNK
                source = (spot % 2) * hidden_width + (spot // 2) * CHUNK
                pieces.append(
                    ((slice(None), pl.ds(source, CHUNK)), (slice(None), pl.ds(at, CHUNK)))
                )
        own_copies[u] = []
        for source, target in pieces:
            copy = pltpu.make_async_copy(
                shards[unit.owner].at[source],
                wholes[unit.owner].at[place.here + target],
                local_sems.at[serial],
            )
            serial += 1
            copy.start()
            own_copies[u].append(copy)
    place.greet()
    gather_wires = Wires(place, gather_send, gather_recv)
    wires = Wires(place, scatter_send, scatter_recv)
    driver = Driver(
        units, gather_stages(place, units, shards, wholes, gather_wires, own_copies), 5.0
    )

    first_of = {}
    for u, unit in enumerate(units):
        first_of.setdefault(unit.owner, u)
    last_of = {unit.owner: u for u, unit in enumerate(units)}
    wanted = [
        (unit.owner, unit.part(), unit.shape[1], u)
        for u, unit in enumerate(units)
        if unit.owner not in (0, 7)
    ]
    for owner, part in ((5, 0), (2, 0), (2, 1), (4, 0), (3, 0), (1, 0), (1, 1), (1, 2)):
        wanted.append((owner, (slice(None), pl.ds(part * width, width)), width, 0))
    depth = slots.shape[0]
    state = dict(fetched=0, used=0, taken=0, raw=False)

    def fetch(spot):
        owner, part, size, unit = wanted[spot]
        return pltpu.make_async_copy(
            wholes[owner].at[(slice(None),) * 4 + part],
            slots.at[(spot % depth,) + (slice(None),) * 5 + (pl.ds(0, size),)],
            fetch_sems.at[spot % depth],
        )

    def raw_copy():
        return pltpu.make_async_copy(
            wholes[7].reshape(devices * wholes[7].shape[4], 8, width),
            down_rows.at[0 : devices * wholes[7].shape[4]],
            fetch_sems.at[depth],
        )

    def pump():
        while (
            state["fetched"] < len(wanted)
            and wanted[state["fetched"]][3] <= driver.settled()
            and state["fetched"] < state["used"] + depth
        ):
            fetch(state["fetched"]).start()
            state["fetched"] += 1
        if not state["raw"] and driver.settled() >= last_of[7]:
            state["raw"] = True
            raw_copy().start()

    def spent(cost):
        driver.spent(cost)
        pump()

    def weight():
        spot = state["taken"]
        state["taken"] += 1
        driver.until(wanted[spot][3])
        pump()
        fetch(spot).wait()
        size = wanted[spot][2]
        return lambda: slots[spot % depth, :, :, :, :, :, 0:size].reshape(width, size)

    def release():
        state["used"] += 1
        pump()

    def project(source, target, cost):
        matrix = weight()
        target[...] = low(mul(source[...], matrix()))
        release()
        spent(cost)

    def residual(source, before, target, cost):
        matrix = weight()
        target[...] = wide(before[...]) + mul(source[...], matrix())
        release()
        spent(cost)

    branch_read.wait()
    for sequence in range(seqs):
        at = pl.ds(sequence * slot_rows, slot_rows)
        valid = lax.broadcasted_iota(jnp.int32, (slot_rows, 1), 0) < lengths[sequence]
        vmem["branch"][at, :] = low(jnp.where(valid, wide(vmem["branch"][at, :]), 0.0))
    period = 2 * slot_rows
    distance = lax.broadcasted_iota(jnp.int32, (slot_rows, period), 0)
    lane = lax.broadcasted_iota(jnp.int32, (slot_rows, period), 1)
    turned = (lane == (period - distance) % period).astype(jnp.bfloat16)
    buckets = lax.broadcasted_iota(jnp.int32, (LANES, slot_rows), 0)
    spread[...] = low(mul((buckets == bucket_ids[...]).astype(jnp.bfloat16), turned))
    driver.until(0)
    copy = pltpu.make_async_copy(wholes[0], packs_in, fetch_sems.at[depth + 1])
    copy.start()
    copy.wait()
    packs = wide(packs_in[...]).reshape(width // LANES, -1, PACK, LANES)
    summed = jnp.sum(packs, axis=1)
    for group in range(summed.shape[0]):
        vmem["gains"][:, group * LANES : (group + 1) * LANES] = summed[group, :norms]
    table = low(jnp.sum(summed, axis=0)[PACK // 2 :])
    bias_rows[...] = mul(table, spread[...])
    reads[0].wait()
    rms_rows(shared.at[first_free], vmem["normed_self"], vmem["gains"][0:1])

    for part in range(3):
        project(vmem["normed_self"], vmem["qkv"].at[part], 1.5)
    for copy in reads[1:]:
        copy.wait()
    for part in range(2):
        project(encoder_rows(first_free), vmem["pairs"].at[part], 2.5)

    def probs_copy(kind, pair, out):
        near = probs_slots[kind].at[pair % 2]
        far = probs_out[kind].at[pair]
        source, target = (near, far) if out else (far, near)
        return pltpu.make_async_copy(source, target, probs_sems.at[2 * kind + pair % 2])

    def pairs_forward(kind, body, cost):
        for pair in range(count_pairs):
            if pair >= 2:
                probs_copy(kind, pair - 2, True).wait()
            lax.fori_loop(0, seqs, functools.partial(body, pair), 0)
            probs_copy(kind, pair, True).start()
            spent(cost)
        for pair in range(count_pairs - 2, count_pairs):
            probs_copy(kind, pair, True).wait()

    def sequence_rows(sequence, size):
        return pl.ds(pl.multiple_of(sequence * size, size & -size), size)

    def self_pair(pair, sequence, carry):
        lanes = pl.ds(pair * LANES, LANES)
        row = lax.broadcasted_iota(jnp.int32, (slot_rows, slot_rows), 0)
        column = lax.broadcasted_iota(jnp.int32, (slot_rows, slot_rows), 1)
        bias = jnp.concatenate(
            [
                pltpu.roll(
                    jnp.broadcast_to(bias_rows[2 * pair + head, :][None], (slot_rows, period)),
                    0,
                    1,
                    stride=1,
                    stride_axis=0,
                )[:, :slot_rows]
                for head in range(2)
            ],
            axis=0,
        )
        at = sequence_rows(sequence, slot_rows)
        mask = (column <= row) & (column < lengths[sequence])
        probs, mixed = attend_pair(
            vmem["qkv"][0, at, lanes],
            vmem["qkv"][1, at, lanes],
            vmem["qkv"][2, at, lanes],
            bias,
            jnp.concatenate([mask, mask], axis=0),
        )
        probs_slots[1][pair % 2, sequence] = probs
        vmem["mixed_self"][at, lanes] = mixed
        return carry

    pairs_forward(1, self_pair, 1.3)
    residual(vmem["mixed_self"], shared.at[first_free], vmem["second"], 1.5)
    rms_rows(vmem["second"], vmem["normed_cross"], vmem["gains"][1:2])
    project(vmem["normed_cross"], vmem["queries"], 2.0)

    def cross_pair(pair, sequence, carry):
        lanes = pl.ds(pair * LANES, LANES)
        column = lax.broadcasted_iota(jnp.int32, (1, enc_rows), 1)
        at = sequence_rows(sequence, slot_rows)
        keys = sequence_rows(sequence, enc_rows)
        probs, mixed = attend_pair(
            vmem["queries"][at, lanes],
            vmem["pairs"][0, keys, lanes],
            vmem["pairs"][1, keys, lanes],
            None,
            column < enc_lengths[sequence],
        )
        probs_slots[0][pair % 2, sequence] = probs
        vmem["mixed_cross"][at, lanes] = mixed
        return carry

    pairs_forward(0, cross_pair, 1.3)
    residual(vmem["mixed_cross"], vmem["second"], vmem["third"], 1.5)
    rms_rows(vmem["third"], vmem["normed_ffn"], vmem["gains"][2:3])
    driver.until(last_of[7])
    pump()
    raw_copy().wait()
    outcome[...] = vmem["third"][...]
    vmem["grad_normed"][...] = jnp.zeros_like(vmem["grad_normed"])

    def finish(u, start_lane, size, value):
        unit = back_units[u]
        start = unit.start + start_lane
        if unit.owner == 0:
            own_gains[...] = pltpu.roll(
                value[: PACK // 2], (LANES - gain_lane) % LANES, 1
            )[:norms, :per]
            row = jnp.sum(jnp.where(pack_rows == rel_row, value[PACK // 2 :], 0.0), axis=0)[None]
            own_rel[...] = pltpu.roll(
                jnp.broadcast_to(row, (8, LANES)), (LANES - rel_lane) % LANES, 1
            )[:1, :rel_per]
        elif unit.owner == 6:
            for at in range(start, start + size, LANES):
                spot, rest = at // CHUNK, at % CHUNK
                to = (spot % 2) * hidden_width + (spot // 2) * CHUNK + rest
                owned[5][:, to : to + LANES] = value[:, at - start : at - start + LANES]
        elif unit.owner == 7:
            kept = min(value.shape[0], owned[6].shape[0] - unit.row)
            owned[6][unit.row : unit.row + kept, start_lane : start_lane + size] = value[:kept]
        else:
            owned[unit.owner - 1][:, start : start + size] = value

    scatter = Driver(
        back_units,
        scatter_stages(place, back_units, whole_slots, arrived, rings, finish, wires),
        1.0,
    )

    def weight_grad(u, name, right):
        size = back_units[u].shape[1]
        left = encoder_rows(first_free) if name == "encoder" else vmem[name][...]
        block = low(mul(left, right, 0, 0))
        whole_slots[u % whole_slots.shape[0], :, :, :, :, :, 0:size] = block.reshape(
            sizes + (-1, size)
        )

    def activate(spot, gate_up, grad_hidden, chunk):
        gate = gate_up[:, 2 * chunk * CHUNK : (2 * chunk + 1) * CHUNK]
        up = gate_up[:, (2 * chunk + 1) * CHUNK : (2 * chunk + 2) * CHUNK]
        grad = grad_hidden[:, chunk * CHUNK : (chunk + 1) * CHUNK]
        square = gate * gate
        curve = jnp.tanh(0.7978845608028654 * gate * (1.0 + 0.044715 * square))
        half = 0.5 * (1.0 + curve)
        gelu = gate * half
        slope = half + 0.5 * gate * (1.0 - curve * curve) * (
            0.7978845608028654 * (1.0 + 3 * 0.044715 * square)
        )
        hidden, grads = vmem["hidden"], vmem["grad_gate_up"]
        hidden[spot, :, chunk * CHUNK : (chunk + 1) * CHUNK] = low(gelu * up)
        grads[spot, :, 2 * chunk * CHUNK : (2 * chunk + 1) * CHUNK] = low(grad * up * slope)
        grads[spot, :, (2 * chunk + 1) * CHUNK : (2 * chunk + 2) * CHUNK] = low(grad * gelu)

    steps = last_of[6] + 1 - first_of[6]
    for spot in range(steps):
        unit = units[first_of[6] + spot]
        size = unit.shape[1]
        matrix = weight()
        groups_at = slice(unit.start // 16, (unit.start + size) // 16)
        down = low(wide(down_rows[groups_at]).reshape(size // 2, width))
        gate_up = mul(vmem["normed_ffn"][...], matrix())
        grad_hidden = mul(vmem["branch"][...], down, 1, 1)
        for chunk in range(size // (2 * CHUNK)):
            activate(spot, gate_up, grad_hidden, chunk)
        spent(5.0)
        vmem["grad_normed"][...] += mul(vmem["grad_gate_up"][spot, :, 0:size], matrix(), 1, 1)
        release()
        outcome[...] += mul(vmem["hidden"][spot, :, 0 : size // 2], down)
        weight_grad(spot, "normed_ffn", vmem["grad_gate_up"][spot, :, 0:size])
        scatter.advance()
    while not driver.done():
        driver.advance()
    pump()
    outcome_copy = pltpu.make_async_copy(outcome, outcome_out, out_sems.at[2])
    outcome_copy.start()
    reads = read_inputs(first_free, 1)

    def norm_back(which, stream, before, last):
        gain = vmem["gains"][which : which + 1]
        step_rows = 64

        def body(step, total):
            at = pl.ds(pl.multiple_of(step * step_rows, step_rows), step_rows)
            value = wide(stream[at, :])
            scale = lax.rsqrt(jnp.mean(value * value, axis=-1, keepdims=True) + 1e-06)
            unit = value * scale
            grad = vmem["grad_normed"][at, :]
            scaled = grad * gain
            result = wide(before[at, :]) + scale * (
                scaled - unit * jnp.mean(scaled * unit, axis=-1, keepdims=True)
            )
            dx[at, :] = result
            if not last:
                rounded[2 - which, at, :] = low(result)
            return total + jnp.sum(grad * unit, axis=0, keepdims=True)

        total = lax.fori_loop(0, rows // step_rows, body, jnp.zeros((1, width), jnp.float32))
        gain_grads[which : which + 1, :] = total

    def through(source, target, add, rounding):
        value = mul(source[...], weight()(), 1, 1)
        if add:
            value = value + target[...]
        target[...] = low(value) if rounding else value
        release()

    left = lax.broadcasted_iota(jnp.int32, (1, LANES), 1) < HEAD

    def stack(value):
        zero = jnp.zeros_like(value)
        return jnp.concatenate([jnp.where(left, value, zero), jnp.where(left, zero, value)], axis=0)

    def pair_back(queries, keys, values, probs, grad):
        count = queries.shape[0]
        stacked = stack(grad)
        spread = mul(stacked, values, 1, 1)
        wide_probs = wide(probs)
        product = wide_probs * spread
        scores = low(product - wide_probs * jnp.sum(product, axis=-1, keepdims=True))
        grad_values = low(mul(probs, stacked, 0, 0))
        both = mul(scores, keys)
        grad_queries = low(jnp.where(left, both[:count], both[count:]) * HEAD ** (-0.5))
        grad_keys = low(mul(scores, stack(queries * jnp.bfloat16(HEAD ** (-0.5))), 0, 0))
        return grad_queries, grad_keys, grad_values, scores

    def cross_back(pair):
        if pair + 1 < count_pairs:
            probs_copy(0, pair + 1, False).start()
        probs_copy(0, pair, False).wait()
        lanes = pl.ds(pair * LANES, LANES)

        def body(sequence, carry):
            at = pl.ds(pl.multiple_of(sequence * slot_rows, slot_rows), slot_rows)
            keys = pl.ds(pl.multiple_of(sequence * enc_rows, enc_rows), enc_rows)
            queries, pairs = vmem["queries"], vmem["pairs"]
            grads = pair_back(
                queries[at, lanes],
                pairs[0, keys, lanes],
                pairs[1, keys, lanes],
                probs_slots[0][pair % 2, sequence],
                grad_mixed[at, lanes],
            )
            queries[at, lanes], pairs[0, keys, lanes], pairs[1, keys, lanes] = grads[:3]
            return carry

        lax.fori_loop(0, seqs, body, 0)

    def self_back(pair):
        if pair + 1 < count_pairs:
            probs_copy(1, pair + 1, False).start()
        probs_copy(1, pair, False).wait()
        lanes = pl.ds(pair * LANES, LANES)
        total = 0.0
        for sequence in range(seqs):
            at = pl.ds(sequence * slot_rows, slot_rows)
            qkv = vmem["qkv"]
            grads = pair_back(
                qkv[0, at, lanes],
                qkv[1, at, lanes],
                qkv[2, at, lanes],
                probs_slots[1][pair % 2, sequence],
                grad_mixed[at, lanes],
            )
            qkv[0, at, lanes], qkv[1, at, lanes], qkv[2, at, lanes] = grads[:3]
            total = total + wide(grads[3])
        total = jnp.concatenate(
            [total, jnp.zeros((total.shape[0], period - slot_rows), jnp.float32)], axis=1
        )
        for head in range(2):
            sums = 0.0
            for group in range(slot_rows // 8):
                start = head * slot_rows + group * 8
                piece = total[start : start + 8]
                sums = sums + (pltpu.roll(piece, period - group * 8, 1) if group else piece)
            diag[2 * pair + head] = sums

    grad_mixed = vmem["normed_ffn"]
    chain, marks = [], {6: 0, 7: 0}

    def then(cost, step):
        chain.append((cost, step))

    def start_ffn():
        outcome_copy.wait()
        norm_back(2, vmem["third"], vmem["branch"], False)

    def start_cross():
        probs_copy(0, 0, False).start()
        through(rounded.at[0], grad_mixed, False, True)

    def encoder_back():
        keys, values = weight(), weight()
        stage = vmem["third"]
        for sequence in range(seqs):
            at = slice(sequence * enc_rows, (sequence + 1) * enc_rows)
            copy = pltpu.make_async_copy(
                stage.at[0:enc_rows], grad_encoder.at[at], out_sems.at[0]
            )
            if sequence:
                copy.wait()
            pairs = vmem["pairs"]
            stage[0:enc_rows] = mul(pairs[0, at], keys(), 1, 1) + mul(pairs[1, at], values(), 1, 1)
            copy.start()
        release()
        release()

    def end_cross():
        through(vmem["queries"], vmem["grad_normed"], False, False)

    def start_self():
        norm_back(1, vmem["second"], dx, False)

    def self_mixed():
        probs_copy(1, 0, False).start()
        through(rounded.at[1], grad_mixed, False, True)

    def self_normed(part):
        through(vmem["qkv"].at[part], vmem["grad_normed"], part > 0, False)

    def end_self():
        reads[0].wait()
        norm_back(0, shared.at[first_free], dx, True)
        pltpu.make_async_copy(dx, grad_tokens, out_sems.at[1]).start()

    then(1.5, start_ffn)
    marks[5] = len(chain)
    then(1.2, start_cross)
    for pair in range(count_pairs):
        then(0.8, functools.partial(cross_back, pair))
    marks[2] = marks[4] = len(chain)
    then(4.5, encoder_back)
    then(1.2, end_cross)
    then(1.5, start_self)
    marks[3] = len(chain)
    then(1.2, self_mixed)
    for pair in range(count_pairs):
        then(0.8, functools.partial(self_back, pair))
    marks[1] = len(chain)
    for part in range(3):
        then(1.2, functools.partial(self_normed, part))
    then(1.5, end_self)
    marks[0] = len(chain)

    def pack_grad(u):
        slot = u % whole_slots.shape[0]
        table = 0.0
        for row in range(8):
            part = diag[:, row, :]
            table = table + (pltpu.roll(part, period - row, 1) if row else part)
        high = low(table)
        rel = mul(high, spread[...], 1, 1) + mul(low(table - wide(high)), spread[...], 1, 1)
        for z in range(sizes[0]):
            for y in range(sizes[1]):
                at = slice((z * sizes[1] + y) * LANES, (z * sizes[1] + y + 1) * LANES)
                top = jnp.concatenate(
                    [gain_grads[:, at], jnp.zeros((PACK // 2 - norms, LANES), jnp.float32)], axis=0
                )
                tile = low(jnp.concatenate([top, rel], axis=0))
                for x in range(sizes[2]):
                    for core in range(sizes[3]):
                        whole_slots[slot, z, y, x, core, :, 0:LANES] = tile

    groups = owned[6].shape[0] // 8

    def down_piece(spot):
        size = vmem["hidden"].shape[2]
        size = min(size, hidden_width - spot * size)
        start = spot * vmem["hidden"].shape[2] // 8
        block = mul(vmem["hidden"][spot, :, 0:size], vmem["branch"][...], 0, 0)
        down_rows[start : start + size // 8] = low(block.reshape(size // 8, 8, width))

    def down_grad(u):
        slot = u % whole_slots.shape[0]
        start = back_units[u].row // 8

        block_rows = whole_slots.shape[5]

        def body(device, carry):
            piece = down_rows[pl.ds(device * groups + start, block_rows // 8)]
            c, rest = device % sizes[3], device // sizes[3]
            x, rest = rest % sizes[2], rest // sizes[2]
            whole_slots[slot, rest // sizes[1], rest % sizes[1], x, c, :, :] = low(
                wide(piece).reshape(block_rows, width)
            )
            return carry

        lax.fori_loop(0, sizes[0] * sizes[1] * sizes[2] * sizes[3], body, 0)

    def grad_of(u):
        unit = back_units[u]
        owner = unit.owner
        part = unit.start // width
        if owner == 7:
            if unit.row == 0:
                for spot in range(vmem["hidden"].shape[0]):
                    down_piece(spot)
            down_grad(u)
        elif owner == 5:
            weight_grad(u, "mixed_cross", rounded[0])
        elif owner == 2:
            if part == 0:
                for copy in reads[1:]:
                    copy.wait()
            weight_grad(u, "encoder", vmem["pairs"][part])
        elif owner == 4:
            weight_grad(u, "normed_cross", vmem["queries"][...])
        elif owner == 3:
            weight_grad(u, "mixed_self", rounded[1])
        elif owner == 1:
            weight_grad(u, "normed_self", vmem["qkv"][part])
        else:
            pack_grad(u)

    position = 0
    budget = 3.0
    for u in range(steps, len(back_units)):
        owner = back_units[u].owner
        while position < marks[owner]:
            chain[position][1]()
            position += 1
        grad_of(u)
        scatter.advance()
        used = 0.0
        while position < len(chain) and used < budget:
            used += chain[position][0]
            chain[position][1]()
            position += 1
    while not scatter.done():
        scatter.advance()
    pltpu.make_async_copy(
        vmem["third"].at[0:enc_rows], grad_encoder.at[0:enc_rows], out_sems.at[0]
    ).wait()
    pltpu.make_async_copy(dx, grad_tokens, out_sems.at[1]).wait()
    gather_wires.finish()


def layer_all(place, shards, norm_gains, rel_bias, data):
    tokens, encoder, cotangent, lengths, enc_lengths, bucket_ids = data
    blocks = [(PACK, LANES)] + [shard.shape for shard in shards]
    sizes = place.sizes
    seqs, slot_rows, width = tokens.shape
    rows, enc_rows = seqs * slot_rows, encoder.shape[1]
    block_rows = blocks[1][0]
    down_rows = blocks[7][0] * 8
    units = make_units(blocks, PIECE, ORDER)
    back_units = []
    for owner in BACK_ORDER:
        if owner == 7:
            for row in range(0, down_rows, block_rows):
                unit = Unit(7, (block_rows, width), 0, width, len(back_units) % 4)
                unit.row = row
                back_units.append(unit)
        else:
            back_units += make_units(blocks, PIECE, (owner,), len(back_units))
    devices = sizes[0] * sizes[1] * sizes[2] * sizes[3]
    piece = PIECE // block_rows
    rings = ring_shapes(place, block_rows, piece)
    low_type, wide_type = jnp.bfloat16, jnp.float32
    steps = sum(unit.owner == 6 for unit in units)
    shapes = {
        "branch": ((rows, width), low_type),
        "normed_self": ((rows, width), low_type),
        "qkv": ((3, rows, width), low_type),
        "mixed_self": ((rows, width), low_type),
        "second": ((rows, width), wide_type),
        "normed_cross": ((rows, width), low_type),
        "queries": ((rows, width), low_type),
        "pairs": ((2, seqs * enc_rows, width), low_type),
        "mixed_cross": ((rows, width), low_type),
        "third": ((rows, width), wide_type),
        "normed_ffn": ((rows, width), low_type),
        "hidden": ((steps, rows, piece // 2), low_type),
        "grad_gate_up": ((steps, rows, piece), low_type),
        "grad_normed": ((rows, width), wide_type),
        "gains": ((norm_gains.shape[0], width), wide_type),
    }
    owned = [(block[0], block[1]) for block in blocks[1:7]] + [(down_rows, width)]
    pair_shapes = [(seqs, 2 * slot_rows, enc_rows), (seqs, 2 * slot_rows, slot_rows)]
    anywhere = pl.BlockSpec(memory_space=pl.ANY)
    inside = pl.BlockSpec(memory_space=pltpu.VMEM)
    scalars = pl.BlockSpec(memory_space=pltpu.SMEM)
    sends, returns = copies_of(units, sizes), copies_of(back_units, sizes)
    local = len(units) + blocks[6][1] // CHUNK
    depth = 3
    shaped = jax.ShapeDtypeStruct
    results = pl.pallas_call(
        functools.partial(
            layer_kernel, place, units, back_units, len(blocks), seqs, tuple(rings)
        ),
        out_shape=[shaped(sizes + block, low_type) for block in blocks]
        + [shaped((rows, width), wide_type)] * 2
        + [shaped((seqs * enc_rows, width), wide_type)]
        + [shaped((width // LANES,) + shape, low_type) for shape in pair_shapes]
        + [shaped(block, wide_type) for block in owned]
        + [shaped(norm_gains.shape, wide_type), shaped((1, rel_bias.shape[0]), wide_type)],
        in_specs=[anywhere] * (len(blocks) - 1)
        + [inside] * 2
        + [anywhere] * 3
        + [scalars] * 2
        + [inside],
        out_specs=[anywhere] * (len(blocks) + 5) + [inside] * (len(owned) + 2),
        scratch_shapes=[pltpu.VMEM(*shapes[name]) for name in BUFFERS]
        + [pltpu.VMEM((2,) + shape, low_type) for shape in pair_shapes]
        + [
            pltpu.VMEM((rows, width), wide_type),
            pltpu.VMEM((devices * blocks[7][0] + 8, 8, width), low_type),
            pltpu.VMEM((HEADS, 8, 2 * slot_rows), wide_type),
            pltpu.VMEM((norm_gains.shape[0], width), wide_type),
            pltpu.VMEM((PACK, LANES), low_type),
            pltpu.VMEM(sizes + (PACK, LANES), low_type),
            pltpu.VMEM((LANES, 2 * slot_rows), low_type),
            pltpu.VMEM((HEADS, 2 * slot_rows), wide_type),
            pltpu.VMEM((depth,) + sizes + (block_rows, piece), low_type),
            pltpu.VMEM((2,) + sizes + (block_rows, piece), low_type),
            pltpu.VMEM((RING + 1,) + sizes[:3] + (block_rows, piece), low_type),
        ]
        + [pltpu.VMEM(shape, low_type) for shape in rings.values()]
        + [
            pltpu.SemaphoreType.DMA((number,))
            for number in (sends, sends, returns, returns, local, depth + 2, 2 + seqs * enc_rows // rows, 4, 3)
        ],
        compiler_params=pltpu.CompilerParams(
            collective_id=0, has_side_effects=True, vmem_limit_bytes=63 * 2**20
        ),
        name="layer_all",
    )(
        *shards,
        norm_gains,
        rel_bias.reshape(1, -1),
        tokens.reshape(rows, width),
        encoder.reshape(-1, width),
        cotangent.reshape(rows, width),
        lengths,
        enc_lengths,
        bucket_ids.reshape(1, -1),
    )
    return results[len(blocks) :]


def norm_scale(stream, gain):
    return stream * lax.rsqrt(jnp.mean(stream * stream, axis=-1, keepdims=True) + 1e-06) * gain


def gelu_tanh(values):
    return (
        0.5
        * values
        * (1.0 + jnp.tanh(0.7978845608028654 * (values + 0.044715 * values * values * values)))
    )


def gated(gate_up):
    half_width = gate_up.shape[1] // 2
    return gelu_tanh(gate_up[:, :half_width]) * gate_up[:, half_width:]


def product(spec, left, right):
    return jnp.einsum(spec, left, right, preferred_element_type=jnp.float32)


def attend(queries, key_rows, value_rows, pos_bias, keep_mask):
    scores = product("bihc,bjhc->bhij", queries, key_rows) * HEAD ** (-0.5)
    if pos_bias is not None:
        scores = scores + pos_bias
    masked = jnp.where(keep_mask[:, None], scores, -1e30)
    row_max = jnp.max(masked, axis=-1, keepdims=True)
    powers = jnp.exp(masked - row_max)
    probs = powers / jnp.sum(powers, axis=-1, keepdims=True)
    low_probs = probs.astype(jnp.bfloat16)
    mixed = product("bhij,bjhc->bihc", low_probs, value_rows)
    return mixed.astype(jnp.bfloat16), low_probs


def attend_back(queries, key_rows, value_rows, low_probs, grad_mixed):
    probs = low_probs.astype(jnp.float32)
    grad_values = product("bhij,bihc->bjhc", low_probs, grad_mixed)
    grad_probs = product("bihc,bjhc->bhij", grad_mixed, value_rows)
    grad_scores = (
        probs * (grad_probs - jnp.sum(probs * grad_probs, axis=-1, keepdims=True))
    ).astype(jnp.bfloat16)
    grad_queries = product("bhij,bjhc->bihc", grad_scores, key_rows) * HEAD ** (-0.5)
    grad_keys = product("bhij,bihc->bjhc", grad_scores, queries) * HEAD ** (-0.5)
    return grad_queries, grad_keys, grad_values, grad_scores


def toeplitz(table, size):
    lead = table.shape[:-1]
    row = jnp.concatenate(
        [table[..., ::-1], jnp.broadcast_to(table[..., :1], lead + (size,))], axis=-1
    )
    tiled = jnp.broadcast_to(row[..., None, :], lead + (size, 2 * size)).reshape(lead + (-1,))
    tiled = jnp.concatenate([tiled[..., size - 1 :], row[..., :1]], axis=-1)
    tiled = tiled[..., : size * (2 * size - 1)]
    return tiled.reshape(lead + (size, 2 * size - 1))[..., :size]


def layer(weights, gains, rel_bias, tokens, encoder, cotangent, lengths, enc_lengths, bucket_ids):
    self_qkv, self_out, cross_q, cross_kv, cross_out, ff_in, ff_out = weights
    count, slots, width = tokens.shape
    enc_count = encoder.shape[1]
    bucket_map = toeplitz(bucket_ids, slots).reshape(-1)
    onehot = (lax.iota(jnp.int32, BUCKETS)[:, None] == bucket_map[None, :]).astype(jnp.bfloat16)
    pos_bias = jnp.dot(rel_bias, onehot, preferred_element_type=jnp.float32).reshape(
        HEADS, slots, slots
    )
    row_ids = lax.iota(jnp.int32, slots)
    self_mask = (row_ids[None, None, :] <= row_ids[None, :, None]) & (
        row_ids[None, None, :] < lengths[:, None, None]
    )
    cross_mask = lax.iota(jnp.int32, enc_count)[None, None, :] < enc_lengths[:, None, None]
    enc_rows = encoder.reshape(count * enc_count, width)
    dot = functools.partial(jnp.dot, preferred_element_type=jnp.float32)
    low = lambda value: value.astype(jnp.bfloat16)
    stream = tokens.reshape(count * slots, width).astype(jnp.float32)
    normed_self, back_self = jax.vjp(norm_scale, stream, gains[0])
    normed_self = low(normed_self)
    qkv = low(dot(normed_self, self_qkv)).reshape(count, slots, 3, HEADS, HEAD)
    mixed_self, probs_self = attend(qkv[:, :, 0], qkv[:, :, 1], qkv[:, :, 2], pos_bias, self_mask)
    mixed_self = mixed_self.reshape(count * slots, width)
    second = stream + dot(mixed_self, self_out)
    normed_cross, back_cross = jax.vjp(norm_scale, second, gains[1])
    normed_cross = low(normed_cross)
    queries = low(dot(normed_cross, cross_q)).reshape(count, slots, HEADS, HEAD)
    pairs = low(dot(enc_rows, cross_kv)).reshape(count, enc_count, 2, HEADS, HEAD)
    mixed_cross, probs_cross = attend(queries, pairs[:, :, 0], pairs[:, :, 1], None, cross_mask)
    mixed_cross = mixed_cross.reshape(count * slots, width)
    third = second + dot(mixed_cross, cross_out)
    normed_ffn, back_ffn = jax.vjp(norm_scale, third, gains[2])
    normed_ffn = low(normed_ffn)
    gate_up = dot(normed_ffn, ff_in)
    activated, back_gate = jax.vjp(gated, gate_up)
    hidden = low(activated)
    outcome = third + dot(hidden, ff_out)

    valid = (row_ids[None, :] < lengths[:, None]).astype(jnp.float32)[:, :, None]
    grad_out = (cotangent.astype(jnp.float32) * valid).reshape(count * slots, width)
    branch = low(grad_out)
    grad_ff_out = product("lf,ld->fd", hidden, branch)
    grad_hidden = product("ld,fd->lf", branch, ff_out)
    (grad_gate_up,) = back_gate(grad_hidden)
    grad_gate_up = low(grad_gate_up)
    grad_ff_in = product("ld,lf->df", normed_ffn, grad_gate_up)
    grad_stream, gain_ffn = back_ffn(product("lf,df->ld", grad_gate_up, ff_in))
    grad_third = grad_out + grad_stream
    branch = low(grad_third)
    grad_cross_out = product("le,ld->ed", mixed_cross, branch)
    grad_mixed = low(product("ld,ed->le", branch, cross_out)).reshape(count, slots, HEADS, HEAD)
    grad_queries, grad_keys, grad_values, unused = attend_back(
        queries, pairs[:, :, 0], pairs[:, :, 1], probs_cross, grad_mixed
    )
    grad_query_rows = low(grad_queries.reshape(count * slots, width))
    grad_pair_rows = low(
        jnp.concatenate(
            [
                grad_keys.reshape(count * enc_count, width),
                grad_values.reshape(count * enc_count, width),
            ],
            axis=1,
        )
    )
    grad_cross_q = product("ld,le->de", normed_cross, grad_query_rows)
    grad_cross_kv = product("ed,ef->df", enc_rows, grad_pair_rows)
    grad_enc = product("ef,df->ed", grad_pair_rows, cross_kv)
    grad_stream, gain_cross = back_cross(product("le,de->ld", grad_query_rows, cross_q))
    grad_second = grad_third + grad_stream
    branch = low(grad_second)
    grad_self_out = product("le,ld->ed", mixed_self, branch)
    grad_mixed = low(product("ld,ed->le", branch, self_out)).reshape(count, slots, HEADS, HEAD)
    grad_queries, grad_keys, grad_values, grad_scores = attend_back(
        qkv[:, :, 0], qkv[:, :, 1], qkv[:, :, 2], probs_self, grad_mixed
    )
    score_sums = jnp.sum(grad_scores.astype(jnp.float32), axis=0).reshape(HEADS, slots * slots)
    grad_rel_bias = product("hn,bn->hb", low(score_sums), onehot)
    grad_qkv = low(
        jnp.concatenate(
            [part.reshape(count * slots, width) for part in (grad_queries, grad_keys, grad_values)],
            axis=1,
        )
    )
    grad_self_qkv = product("ld,lf->df", normed_self, grad_qkv)
    grad_stream, gain_self = back_self(product("lf,df->ld", grad_qkv, self_qkv))
    grad_tok = grad_second + grad_stream
    grad_gains = jnp.stack([gain_self, gain_cross, gain_ffn], axis=0)
    grads = (
        grad_self_qkv,
        grad_self_out,
        grad_cross_q,
        grad_cross_kv,
        grad_cross_out,
        grad_ff_in,
        grad_ff_out,
    )
    return (
        outcome.reshape(tokens.shape),
        grad_tok.reshape(tokens.shape),
        grad_enc.reshape(encoder.shape),
        grads,
        grad_gains,
        grad_rel_bias,
    )


AXES = ("dp", "fsdp")


def by_collectives(data, shards):
    whole = lambda shard, axis=0: lax.all_gather(shard, AXES, axis=axis, tiled=True)
    weights = tuple(whole(shard) for shard in shards[:7])
    gains = whole(shards[7], 1).astype(jnp.float32)
    rel_bias = whole(shards[8]).reshape(HEADS, BUCKETS)
    outcome, grad_tok, grad_enc, grads, grad_gains, grad_rel_bias = layer(
        weights, gains, rel_bias, *data
    )
    settle = lambda total, axis=0: lax.psum_scatter(
        total, AXES, scatter_dimension=axis, tiled=True
    )
    return (
        (outcome, grad_tok, grad_enc)
        + tuple(settle(grad) for grad in grads)
        + (settle(grad_gains, 1), settle(grad_rel_bias.reshape(-1)))
    )


def by_kernels(place, data, shards):
    self_qkv, self_out, cross_q, cross_kv, cross_out, ff_in, ff_out = shards[:7]
    ff_rows, width = ff_out.shape
    sent = (self_qkv, cross_kv, self_out, cross_q, cross_out, ff_in)
    sent += (ff_out.reshape(ff_rows // 8, 8, width),)
    results = layer_all(place, sent, shards[7], shards[8], data)
    outcome, grad_tok, grad_enc = (
        result.reshape(like.shape)
        for result, like in zip(results[:3], (data[0], data[0], data[1]))
    )
    g_qkv, g_kv, g_so, g_cq, g_co, g_in, g_out = results[5:12]
    owned = (g_qkv, g_so, g_cq, g_kv, g_co, g_in, g_out)
    return (outcome, grad_tok, grad_enc) + owned + (results[12], results[13].reshape(-1))


def on_device(place, *args):
    data, shards = args[:6], args[6:]
    per = shards[7].shape[1]
    regular = all(shard.shape[0] % 16 == 0 for shard in shards[:6])
    group = place.sizes[2] * place.sizes[3]
    seqs, slots, enc_slots = args[0].shape[0], args[0].shape[1], args[1].shape[1]
    regular = regular and enc_slots <= seqs * slots and seqs * enc_slots % (seqs * slots) == 0
    if regular and shards[6].shape[0] % 8 == 0 and group * per == LANES:
        return by_kernels(place, data, shards)
    return by_collectives(data, shards)


def solution(mesh):
    rows = P(AXES, None, None)
    flat = P(AXES)
    matrix = P(AXES, None)
    split = P(None, AXES)
    place = Place(mesh.shape["dp"], mesh.shape["fsdp"])
    return jax.shard_map(
        functools.partial(on_device, place),
        mesh=mesh,
        in_specs=(rows, rows, rows, flat, flat, P()) + (matrix,) * 7 + (split, flat),
        out_specs=(rows, rows, rows) + (matrix,) * 7 + (split, flat),
        check_vma=False,
    )
```

```python
import functools

import jax
import jax.numpy as jnp
from jax import lax
from jax.experimental import pallas as pl
from jax.experimental.pallas import tpu as pltpu
from jax.sharding import PartitionSpec as P

HEADS = 16
HEAD = 64
BUCKETS = 32
PACK = 32
LANES = 128
PIECE = 32 * 1024
GATHER_WIDTHS = {1: (1024, 2048), 4: (2048, 1024), None: (2048,)}
SCATTER_WIDTHS = {None: (1024,)}

MESH = pl.DeviceIdType.MESH


class Place:
    def __init__(self, dp, fsdp):
        self.sizes = (dp // 2, 2, fsdp // 2, 2)

    def locate(self):
        row, column = lax.axis_index("dp"), lax.axis_index("fsdp")
        sizes = self.sizes
        self.here = (row // sizes[1], row % sizes[1], column // sizes[3], column % sizes[3])
        z = self.here[0]
        self.inner, self.outer = z % 3 != 0, z % 3 == 0
        self.twin, self.far, self.entry = z + 1 - 2 * (z % 2), 2 - 2 * (z // 2), 2 - z // 2

    def moved(self, axis, step):
        coords = list(self.here)
        coords[axis] = (coords[axis] + step) % self.sizes[axis]
        return coords

    def at(self, axis, coordinate):
        coords = list(self.here)
        coords[axis] = coordinate
        return coords

    def hops(self, axes):
        steps = []
        for axis in axes:
            steps += ["spread", "relay"] if axis == 0 and self.sizes[0] == 4 else [axis]
        return steps

    def device(self, coords):
        return (coords[0] * self.sizes[1] + coords[1], coords[2] * self.sizes[3] + coords[3])

    def peers(self):
        return [(axis, step) for axis in range(4) for step in range(1, self.sizes[axis])]

    def greet(self):
        barrier = pltpu.get_barrier_semaphore()
        for axis, step in self.peers():
            pl.semaphore_signal(
                barrier, inc=1, device_id=self.device(self.moved(axis, step)), device_id_type=MESH
            )
        pl.semaphore_wait(barrier, len(self.peers()))


def split_lanes(width, turn):
    if width % (4 * LANES) == 0:
        last = width // 4
        more = -(-(width - last) // (2 * LANES)) * LANES
        less = width - last - more
        order = (1, 2, 0) if turn % 2 else (2, 1, 0)
        return ((0, more, (0, 2, 1)), (more, less, (0, 1, 2)), (more + less, last, order))
    return ((0, width, (0, 2, 1)),)


class Unit:
    def __init__(self, owner, block, start, count, turn):
        self.owner, self.start, self.count = owner, start, count
        self.grouped = len(block) == 3
        self.shape = (count,) + block[1:] if self.grouped else (block[0], count)
        self.paths = split_lanes(self.shape[-1], turn)

    def part(self, start=0, size=None):
        size = self.shape[-1] if size is None else size
        if self.grouped:
            return (pl.ds(self.start, self.count), slice(None), pl.ds(start, size))
        return (slice(None), pl.ds(self.start + start, size))


def make_units(blocks, order, widths, before=0):
    units = []
    for owner in order:
        block = blocks[owner]
        grouped = len(block) == 3
        total = block[0] if grouped else block[1]
        turns = widths.get(owner, widths[None])
        start = 0
        while start < total:
            most = turns[0]
            turns = turns[1:] or turns
            most = max(most // 256, 1) if grouped else most
            count = min(most, total - start)
            units.append(Unit(owner, block, start, count, (before + len(units)) % 4))
            start += count
    return units


def guarded(condition, action):
    if condition is True:
        action()
    elif condition is not False:
        pl.when(condition)(action)


class Message:
    def __init__(self, make, sends, receives):
        self.make, self.sends, self.receives = make, sends, receives

    def start(self):
        guarded(self.sends, lambda: self.make().start())

    def wait_send(self):
        guarded(self.sends, lambda: self.make().wait_send())

    def wait_recv(self):
        guarded(self.receives, lambda: self.make().wait_recv())

    def wait(self):
        self.wait_send()
        self.wait_recv()


class Wires:
    def __init__(self, place, send_sems, recv_sems):
        self.place, self.send_sems, self.recv_sems = place, send_sems, recv_sems
        self.started, self.spot = [], 0

    def send(self, source, target, coords, sends=True, receives=True, arrival=None):
        spot = self.spot
        self.spot += 1
        arrival = spot if arrival is None else arrival
        device = self.place.device(coords)

        def make():
            return pltpu.make_async_remote_copy(
                src_ref=source,
                dst_ref=target,
                send_sem=self.send_sems.at[spot],
                recv_sem=self.recv_sems.at[arrival],
                device_id=device,
                device_id_type=MESH,
            )

        message = Message(make, sends, receives)
        message.start()
        self.started.append(message)
        return message

    def along(self, axis, source, target):
        return [
            self.send(source, target, self.place.moved(axis, step))
            for step in range(1, self.place.sizes[axis])
        ]

    def spread(self, source, target):
        place = self.place
        messages = [self.send(source, target, place.at(0, place.twin))]
        first = self.spot
        arrival = first + place.here[0] % 2
        entry = place.at(0, place.entry)
        messages.append(self.send(source, target, entry, receives=False, arrival=arrival))
        for arrival in (first, first + 1):
            messages.append(
                self.send(source, target, entry, sends=False, receives=place.inner, arrival=arrival)
            )
        return messages

    def relay(self, ref):
        place = self.place
        twin = place.at(0, place.twin)
        return [self.send(ref, ref, twin, sends=place.inner, receives=place.outer)]

    def finish(self):
        for message in self.started:
            message.wait_send()


def gather_stages(place, units, shards, wholes, wires, own_copies):
    full = slice(None)
    pending = {}

    def settle(u):
        for copy in pending[u]:
            copy.wait_recv()
        pending[u] = []

    def move(u, stage):
        unit = units[u]
        whole = wholes[unit.owner]
        if stage == int(unit.owner in shards):
            for copy in own_copies[u]:
                copy.wait()
        if stage:
            settle(u)
        pending[u] = []
        for start, size, axes in unit.paths:
            steps = place.hops(axes)
            if stage >= len(steps):
                continue
            step, done = steps[stage], steps[:stage]
            part = unit.part(start, size)
            index = [full if axis in done else place.here[axis] for axis in range(3)]
            if "relay" in done:
                index[0] = full
            elif step == "relay":
                index[0] = pl.ds(place.far, 2)
            target = whole.at[tuple(index) + (place.here[3],) + part]
            source = target
            if stage == 0 and unit.owner in shards:
                source = shards[unit.owner].at[part]
            if step == "spread":
                pending[u] += wires.spread(source, target)
            elif step == "relay":
                pending[u] += wires.relay(target)
            else:
                pending[u] += wires.along(step, source, target)

    def across(u):
        settle(u)
        unit = units[u]
        ref = wholes[unit.owner].at[(full, full, full, place.here[3]) + unit.part()]
        pending[u] = wires.along(3, ref, ref)

    count = len(place.hops((0, 1, 2)))
    return tuple(functools.partial(move, stage=stage) for stage in range(count)) + (across, settle)


def copies_of(units, sizes):
    line = 4 if sizes[0] == 4 else sizes[0] - 1
    per_path = line + sizes[1] - 1 + sizes[2] - 1
    return sum(1 + len(unit.paths) * (per_path + 1) for unit in units)


def mul(left, right, left_dim=1, right_dim=0):
    return lax.dot_general(
        left, right, (((left_dim,), (right_dim,)), ((), ())), preferred_element_type=jnp.float32
    )


def low(value):
    return value.astype(jnp.bfloat16)


def wide(value):
    return value.astype(jnp.float32)


def rms_rows(source, target, gain, rows=64):
    def body(step, carry):
        at = pl.ds(pl.multiple_of(step * rows, rows), rows)
        value = wide(source[at, :])
        scale = lax.rsqrt(jnp.mean(value * value, axis=-1, keepdims=True) + 1e-06)
        target[at, :] = low(value * scale * gain)
        return carry

    lax.fori_loop(0, source.shape[0] // rows, body, 0)


def attend_pair(queries, key_rows, value_rows, bias, mask):
    rows = queries.shape[0]
    left = lax.broadcasted_iota(jnp.int32, (1, LANES), 1) < HEAD
    zero = jnp.zeros_like(queries)
    scaled = queries * jnp.bfloat16(HEAD ** (-0.5))
    stacked = jnp.concatenate(
        [jnp.where(left, scaled, zero), jnp.where(left, zero, scaled)], axis=0
    )
    scores = mul(stacked, key_rows, 1, 1)
    if bias is not None:
        scores = scores + bias
    scores = jnp.where(mask, scores, -1e30)
    powers = jnp.exp(scores - jnp.max(scores, axis=-1, keepdims=True))
    probs = low(powers / jnp.sum(powers, axis=-1, keepdims=True))
    none = jnp.zeros_like(value_rows)
    mixed = mul(probs[:rows], jnp.where(left, value_rows, none)) + mul(
        probs[rows:], jnp.where(left, none, value_rows)
    )
    return probs, low(mixed)


class Driver:
    def __init__(self, units, stages, lead):
        self.units, self.stages, self.lead = units, stages, lead
        self.tick, self.debt = 0, 0.0

    def done(self):
        return self.tick >= len(self.units) + len(self.stages) - 1

    def settled(self):
        return self.tick - len(self.stages)

    def advance(self):
        for lag, stage in enumerate(self.stages):
            if 0 <= self.tick - lag < len(self.units):
                stage(self.tick - lag)
        self.tick += 1

    def until(self, unit):
        while self.settled() < unit:
            self.advance()

    def spent(self, cost):
        self.debt += cost
        while self.debt >= self.lead:
            self.debt -= self.lead
            if not self.done():
                self.advance()


def scatter_hops(place, axes):
    names = {"spread": "last", "relay": "relay"}
    return [(names.get(step, "axis"), 0 if step in names else step) for step in place.hops(axes)[::-1]]


def ring_shapes(place, block_rows, width):
    sizes, shapes = place.sizes, {}
    for turn in range(4):
        for start, lanes, axes in split_lanes(width, turn):
            left = list(range(3))
            for hop, (step, axis) in enumerate(scatter_hops(place, axes)):
                senders = sizes[axis] - 1 if step == "axis" else 2
                rest = tuple(sizes[other] for other in left if other != axis)
                slots = RING + (hop == 1)
                lanes = max(lanes, shapes.get((axes, hop), (0,))[-1])
                shapes[axes, hop] = (slots, senders) + rest + (block_rows, lanes)
                if step != "relay":
                    left.remove(axis)
    return shapes


def scatter_stages(place, units, whole_slots, arrived, rings, finish, wires):
    sizes, full = place.sizes, slice(None)
    here = place.here
    pending = {}

    def settle(u):
        for copy in pending[u]:
            copy.wait()
        pending[u] = []

    def lanes(u):
        return (full, pl.ds(0, units[u].shape[1]))

    def slot(u):
        return whole_slots.at[u % whole_slots.shape[0]]

    def spread(b, axes):
        coords = {}
        for axis in reversed(axes):
            coords[axis] = b % sizes[axis]
            b = b // sizes[axis]
        return coords

    def count(axes):
        total = 1
        for axis in axes:
            total *= sizes[axis]
        return total

    def held(u, path, hop):
        start, size, axes = path
        steps = scatter_hops(place, axes)
        done = [h for h in range(hop) if steps[h][0] != "relay"]
        gone = [steps[h][1] for h in done]
        left = [axis for axis in range(3) if axis not in gone]
        if not done:
            ring = u % arrived.shape[0]
            return left, lambda at: (
                arrived,
                (ring,) + tuple(at[a] for a in left) + (full, pl.ds(start, size)),
            )
        ref = rings[axes, done[-1]]
        ring = u % ref.shape[0]
        return left, lambda at: (
            ref,
            (ring, 0) + tuple(at[a] for a in left) + (full, pl.ds(0, size)),
        )

    def landing(u, path, hop, sender, at=None):
        start, size, axes = path
        ref = rings[axes, hop]
        rest = len(ref.shape) - 4
        inner = (full,) * rest if at is None else at
        return ref, (u % ref.shape[0], sender) + inner + (full, pl.ds(0, size))

    def first(u):
        source = slot(u).at[(full, full, full, (here[3] + 1) % 2) + lanes(u)]
        target = arrived.at[(u % arrived.shape[0], full, full, full) + lanes(u)]
        pending[u] = [wires.send(source, target, place.moved(3, 1))]

    def pass_on(u, hop):
        for path in units[u].paths:
            steps = scatter_hops(place, path[2])
            if hop >= len(steps):
                continue
            step, axis = steps[hop]
            left, where = held(u, path, hop)

            def take(coordinate):
                ref, index = where({a: coordinate if a == axis else full for a in left})
                return ref.at[index]

            def put(sender):
                ref, index = landing(u, path, hop, sender)
                return ref.at[index]

            if step == "axis":
                for move in range(1, sizes[axis]):
                    coords = place.moved(axis, move)
                    pending[u].append(wires.send(take(coords[axis]), put(move - 1), coords))
            elif step == "relay":
                ref, index = landing(u, path, hop, pl.ds(0, 2))
                pending[u].append(
                    wires.send(
                        take(pl.ds(place.far, 2)),
                        ref.at[index],
                        place.at(0, place.twin),
                        sends=place.outer,
                        receives=place.inner,
                    )
                )
            else:
                pending[u].append(wires.send(take(place.twin), put(0), place.at(0, place.twin)))
                spot = wires.spot
                for other in range(2):
                    pending[u].append(
                        wires.send(
                            take(place.far + other),
                            put(1),
                            place.at(0, place.far + other),
                            sends=place.inner,
                            receives=other == 0,
                            arrival=spot,
                        )
                    )

    def merge(u, path, hop):
        start, size, axes = path
        steps = scatter_hops(place, axes)
        if hop >= len(steps):
            return
        step, axis = steps[hop]
        left, before = held(u, path, hop)
        rest = [a for a in left if a != axis]
        senders = rings[axes, hop].shape[1]

        def relayed(b, carry):
            at = spread(b % count(rest), rest)
            which = b // count(rest)
            ref, index = before({**at, axis: place.far + which})
            source, arrival = landing(u, path, hop, which, tuple(at[a] for a in rest))
            ref[index] = low(wide(ref[index]) + wide(source[arrival]))
            return carry

        def take_relay():
            lax.fori_loop(0, 2 * count(rest), relayed, 0)

        if step == "relay":
            guarded(place.inner, take_relay)
            return

        def body(b, carry):
            at = spread(b, rest)
            source, index = before({**at, axis: here[axis]})
            value = wide(source[index])
            for sender in range(senders):
                source, index = landing(u, path, hop, sender, tuple(at[a] for a in rest))
                value = value + wide(source[index])
            if hop == len(steps) - 1:
                finish(u, start, size, value)
            else:
                target, index = landing(u, path, hop, 0, tuple(at[a] for a in rest))
                target[index] = low(value)
            return carry

        if hop == len(steps) - 1:
            body(0, 0)
        else:
            lax.fori_loop(0, count(rest), body, 0)

    def second(u):
        settle(u)
        ring, own = u % arrived.shape[0], slot(u)

        def body(b, carry):
            at = spread(b, (0, 1, 2))
            index = tuple(at[a] for a in range(3))
            target = (ring,) + index + lanes(u)
            arrived[target] = low(wide(arrived[target]) + wide(own[index + (here[3],) + lanes(u)]))
            return carry

        lax.fori_loop(0, count((0, 1, 2)), body, 0)
        pass_on(u, 0)

    def later(u, hop):
        settle(u)
        for path in units[u].paths:
            merge(u, path, hop)
        pass_on(u, hop + 1)

    hops = len(scatter_hops(place, (0, 1, 2)))
    return (first, second) + tuple(functools.partial(later, hop=hop) for hop in range(hops))


CHUNK = 256
RING = 5
ORDER = (0, 1, 2, 3, 5, 4)
BACK_ORDER = (6, 7, 5, 2, 4, 3, 1, 0)
BUFFERS = (
    "branch", "normed_self", "qkv", "mixed_self", "second", "normed_cross",
    "queries", "pairs", "mixed_cross", "third", "normed_ffn", "hidden", "grad_gate_up",
    "grad_normed", "gains",
)


def layer_kernel(place, units, back_units, count, seqs, ring_keys, *refs):
    shards, refs = refs[:7], refs[7:]
    gain_shard, rel_shard, tokens_in, encoder_in, cotangent_in = refs[:5]
    lengths, enc_lengths, bucket_ids, refs = refs[5], refs[6], refs[7], refs[8:]
    wholes, refs = refs[:count], refs[count:]
    outcome_out, grad_tokens, grad_encoder, refs = refs[0], refs[1], refs[2], refs[3:]
    probs_out, refs = refs[:2], refs[2:]
    owned, refs = refs[:7], refs[7:]
    own_gains, own_rel, refs = refs[0], refs[1], refs[2:]
    vmem, refs = dict(zip(BUFFERS, refs)), refs[len(BUFFERS) :]
    probs_slots, refs = refs[:2], refs[2:]
    dx, down_rows, diag, gain_grads = refs[:4]
    own_pack, packs_in, spread, bias_rows, slots, whole_slots, arrived = refs[4:11]
    refs = refs[11:]
    rings, refs = dict(zip(ring_keys, refs)), refs[len(ring_keys) :]
    gather_send, gather_recv, scatter_send, scatter_recv = refs[:4]
    local_sems, fetch_sems, read_sems, probs_sems, out_sems = refs[4:]
    place.locate()
    sizes = place.sizes
    devices = sizes[0] * sizes[1] * sizes[2] * sizes[3]
    me = place.device(place.here)
    me = me[0] * (sizes[2] * sizes[3]) + me[1]
    rows, width = dx.shape
    slot_rows, enc_rows = rows // seqs, encoder_in.shape[0] // seqs
    shared = vmem["grad_gate_up"]
    parts = encoder_in.shape[0] // rows
    rounded, first_free = shared, 2
    count_pairs = width // LANES
    norms, per = gain_shard.shape
    rel_per = rel_shard.shape[1]
    gain_lane = (me % (LANES // per)) * per
    rel_row, rel_lane = me * rel_per // BUCKETS, (me * rel_per) % BUCKETS
    hidden_width = owned[5].shape[1] // 2
    outcome = dx

    def read_inputs(start, sems):
        sources = [(tokens_in, shared.at[start])]
        for part in range(parts):
            source = encoder_in.at[part * rows : (part + 1) * rows]
            sources.append((source, shared.at[start + 1 + part]))
        copies = [
            pltpu.make_async_copy(source, target, read_sems.at[sems + at])
            for at, (source, target) in enumerate(sources)
        ]
        for copy in copies:
            copy.start()
        return copies

    def encoder_rows(start):
        return shared[start + 1 : start + 1 + parts].reshape(parts * rows, width)

    reads = read_inputs(first_free, 1)
    branch_read = pltpu.make_async_copy(cotangent_in, vmem["branch"], read_sems.at[0])
    branch_read.start()
    padded = jnp.concatenate(
        [wide(gain_shard[...]), jnp.zeros((PACK // 2 - norms, per), jnp.float32)], axis=0
    )
    padded = jnp.concatenate([padded, jnp.zeros((PACK // 2, LANES - per), jnp.float32)], axis=1)
    rel = jnp.concatenate(
        [wide(rel_shard[...]), jnp.zeros((1, LANES - rel_per), jnp.float32)], axis=1
    )
    rel = jnp.broadcast_to(rel, (PACK // 2, LANES))
    pack_rows = lax.broadcasted_iota(jnp.int32, (PACK // 2, LANES), 0)
    rel = jnp.where(pack_rows == rel_row, pltpu.roll(rel, rel_lane, 1), 0.0)
    own_pack[...] = low(jnp.concatenate([pltpu.roll(padded, gain_lane, 1), rel], axis=0))
    self_qkv, cross_kv, self_out, cross_q, cross_out, ff_in, ff_out = shards
    shards = {0: own_pack, 1: self_qkv, 2: cross_kv, 5: ff_out}
    own_copies, serial = {}, 0
    for u, unit in enumerate(units):
        end = unit.start + unit.shape[-1]
        pieces = []
        if unit.owner == 3:
            for at in range(unit.start, end, width):
                target = (slice(None), pl.ds(at, width))
                pieces.append(((self_out, cross_q, cross_out)[at // width], target))
        elif unit.owner == 4:
            for at in range(unit.start, end, CHUNK):
                spot = at // CHUNK
                source = (spot % 2) * hidden_width + (spot // 2) * CHUNK
                target = (slice(None), pl.ds(at, CHUNK))
                pieces.append((ff_in.at[:, source : source + CHUNK], target))
        else:
            pieces.append((shards[unit.owner].at[unit.part()], unit.part()))
        own_copies[u] = []
        for source, target in pieces:
            copy = pltpu.make_async_copy(
                source, wholes[unit.owner].at[place.here + target], local_sems.at[serial]
            )
            serial += 1
            copy.start()
            own_copies[u].append(copy)
    place.greet()
    gather_wires = Wires(place, gather_send, gather_recv)
    wires = Wires(place, scatter_send, scatter_recv)
    driver = Driver(
        units, gather_stages(place, units, shards, wholes, gather_wires, own_copies), 8.0
    )

    last_of = {unit.owner: u for u, unit in enumerate(units)}
    wanted = []
    at = {}
    for u, unit in enumerate(units):
        if unit.owner not in (0, 5):
            start, end = at.get(unit.owner, 0), unit.start + unit.shape[1]
            total = wholes[unit.owner].shape[-1]
            while start < end and min(start + width, total) <= end:
                size = min(width, total - start)
                wanted.append((unit.owner, (slice(None), pl.ds(start, size)), size, u))
                start += size
            at[unit.owner] = start
    for owner, part in ((3, 2), (2, 0), (2, 1), (3, 1), (3, 0), (1, 0), (1, 1), (1, 2)):
        wanted.append((owner, (slice(None), pl.ds(part * width, width)), width, 0))
    depth = slots.shape[0]
    state = dict(fetched=0, used=0, taken=0, raw=False)

    def fetch(spot):
        owner, part, size, unit = wanted[spot]
        return pltpu.make_async_copy(
            wholes[owner].at[(slice(None),) * 4 + part],
            slots.at[(spot % depth,) + (slice(None),) * 5 + (pl.ds(0, size),)],
            fetch_sems.at[spot % depth],
        )

    def raw_copy():
        return pltpu.make_async_copy(
            wholes[5].reshape(devices * wholes[5].shape[4], 8, width),
            down_rows.at[0 : devices * wholes[5].shape[4]],
            fetch_sems.at[depth],
        )

    def pump():
        while (
            state["fetched"] < len(wanted)
            and wanted[state["fetched"]][3] <= driver.settled()
            and state["fetched"] < state["used"] + depth
        ):
            fetch(state["fetched"]).start()
            state["fetched"] += 1
        if not state["raw"] and driver.settled() >= last_of[5]:
            state["raw"] = True
            raw_copy().start()

    def spent(cost):
        driver.spent(cost)
        pump()

    def weight():
        spot = state["taken"]
        state["taken"] += 1
        driver.until(wanted[spot][3])
        pump()
        fetch(spot).wait()
        size = wanted[spot][2]
        return lambda: slots[spot % depth, :, :, :, :, :, 0:size].reshape(width, size)

    def release():
        state["used"] += 1
        pump()

    def project(source, target, cost):
        matrix = weight()
        target[...] = low(mul(source[...], matrix()))
        release()
        spent(cost)

    def residual(source, before, target, cost):
        matrix = weight()
        target[...] = wide(before[...]) + mul(source[...], matrix())
        release()
        spent(cost)

    branch_read.wait()
    for sequence in range(seqs):
        at = pl.ds(sequence * slot_rows, slot_rows)
        valid = lax.broadcasted_iota(jnp.int32, (slot_rows, 1), 0) < lengths[sequence]
        vmem["branch"][at, :] = low(jnp.where(valid, wide(vmem["branch"][at, :]), 0.0))
    period = 2 * slot_rows
    distance = lax.broadcasted_iota(jnp.int32, (slot_rows, period), 0)
    lane = lax.broadcasted_iota(jnp.int32, (slot_rows, period), 1)
    turned = (lane == (period - distance) % period).astype(jnp.bfloat16)
    buckets = lax.broadcasted_iota(jnp.int32, (LANES, slot_rows), 0)
    spread[...] = low(mul((buckets == bucket_ids[...]).astype(jnp.bfloat16), turned))
    driver.until(0)
    copy = pltpu.make_async_copy(wholes[0], packs_in, fetch_sems.at[depth + 1])
    copy.start()
    copy.wait()
    packs = wide(packs_in[...]).reshape(width // LANES, -1, PACK, LANES)
    summed = jnp.sum(packs, axis=1)
    for group in range(summed.shape[0]):
        vmem["gains"][:, group * LANES : (group + 1) * LANES] = summed[group, :norms]
    table = low(jnp.sum(summed, axis=0)[PACK // 2 :])
    bias_rows[...] = mul(table, spread[...])
    reads[0].wait()
    rms_rows(shared.at[first_free], vmem["normed_self"], vmem["gains"][0:1])

    for part in range(3):
        project(vmem["normed_self"], vmem["qkv"].at[part], 1.5)
    for copy in reads[1:]:
        copy.wait()
    for part in range(2):
        project(encoder_rows(first_free), vmem["pairs"].at[part], 2.5)

    def probs_copy(kind, pair, out):
        near = probs_slots[kind].at[pair % 2]
        far = probs_out[kind].at[pair]
        source, target = (near, far) if out else (far, near)
        return pltpu.make_async_copy(source, target, probs_sems.at[2 * kind + pair % 2])

    def pairs_forward(kind, body, cost):
        for pair in range(count_pairs):
            if pair >= 2:
                probs_copy(kind, pair - 2, True).wait()
            lax.fori_loop(0, seqs, functools.partial(body, pair), 0)
            probs_copy(kind, pair, True).start()
            spent(cost)
        for pair in range(count_pairs - 2, count_pairs):
            probs_copy(kind, pair, True).wait()

    def sequence_rows(sequence, size):
        return pl.ds(pl.multiple_of(sequence * size, size & -size), size)

    def self_pair(pair, sequence, carry):
        lanes = pl.ds(pair * LANES, LANES)
        row = lax.broadcasted_iota(jnp.int32, (slot_rows, slot_rows), 0)
        column = lax.broadcasted_iota(jnp.int32, (slot_rows, slot_rows), 1)
        bias = jnp.concatenate(
            [
                pltpu.roll(
                    jnp.broadcast_to(bias_rows[2 * pair + head, :][None], (slot_rows, period)),
                    0,
                    1,
                    stride=1,
                    stride_axis=0,
                )[:, :slot_rows]
                for head in range(2)
            ],
            axis=0,
        )
        at = sequence_rows(sequence, slot_rows)
        mask = (column <= row) & (column < lengths[sequence])
        probs, mixed = attend_pair(
            vmem["qkv"][0, at, lanes],
            vmem["qkv"][1, at, lanes],
            vmem["qkv"][2, at, lanes],
            bias,
            jnp.concatenate([mask, mask], axis=0),
        )
        probs_slots[1][pair % 2, sequence] = probs
        vmem["mixed_self"][at, lanes] = mixed
        return carry

    pairs_forward(1, self_pair, 1.3)
    residual(vmem["mixed_self"], shared.at[first_free], vmem["second"], 1.5)
    rms_rows(vmem["second"], vmem["normed_cross"], vmem["gains"][1:2])
    project(vmem["normed_cross"], vmem["queries"], 2.0)

    def cross_pair(pair, sequence, carry):
        lanes = pl.ds(pair * LANES, LANES)
        column = lax.broadcasted_iota(jnp.int32, (1, enc_rows), 1)
        at = sequence_rows(sequence, slot_rows)
        keys = sequence_rows(sequence, enc_rows)
        probs, mixed = attend_pair(
            vmem["queries"][at, lanes],
            vmem["pairs"][0, keys, lanes],
            vmem["pairs"][1, keys, lanes],
            None,
            column < enc_lengths[sequence],
        )
        probs_slots[0][pair % 2, sequence] = probs
        vmem["mixed_cross"][at, lanes] = mixed
        return carry

    pairs_forward(0, cross_pair, 1.3)
    residual(vmem["mixed_cross"], vmem["second"], vmem["third"], 1.5)
    rms_rows(vmem["third"], vmem["normed_ffn"], vmem["gains"][2:3])
    driver.until(last_of[5])
    pump()
    raw_copy().wait()
    outcome[...] = vmem["third"][...]
    vmem["grad_normed"][...] = jnp.zeros_like(vmem["grad_normed"])

    def finish(u, start_lane, size, value):
        unit = back_units[u]
        start = unit.start + start_lane
        if unit.owner == 0:
            own_gains[...] = pltpu.roll(
                value[: PACK // 2], (LANES - gain_lane) % LANES, 1
            )[:norms, :per]
            row = jnp.sum(jnp.where(pack_rows == rel_row, value[PACK // 2 :], 0.0), axis=0)[None]
            own_rel[...] = pltpu.roll(
                jnp.broadcast_to(row, (8, LANES)), (LANES - rel_lane) % LANES, 1
            )[:1, :rel_per]
        elif unit.owner == 6:
            for at in range(start, start + size, LANES):
                spot, rest = at // CHUNK, at % CHUNK
                to = (spot % 2) * hidden_width + (spot // 2) * CHUNK + rest
                owned[5][:, to : to + LANES] = value[:, at - start : at - start + LANES]
        elif unit.owner == 7:
            kept = min(value.shape[0], owned[6].shape[0] - unit.row)
            owned[6][unit.row : unit.row + kept, start_lane : start_lane + size] = value[:kept]
        else:
            owned[unit.owner - 1][:, start : start + size] = value

    scatter = Driver(
        back_units,
        scatter_stages(place, back_units, whole_slots, arrived, rings, finish, wires),
        1.0,
    )

    def weight_grad(u, name, right):
        size = back_units[u].shape[1]
        left = encoder_rows(first_free) if name == "encoder" else vmem[name][...]
        block = low(mul(left, right, 0, 0))
        whole_slots[u % whole_slots.shape[0], :, :, :, :, :, 0:size] = block.reshape(
            sizes + (-1, size)
        )

    def activate(spot, gate_up, grad_hidden, chunk):
        gate = gate_up[:, 2 * chunk * CHUNK : (2 * chunk + 1) * CHUNK]
        up = gate_up[:, (2 * chunk + 1) * CHUNK : (2 * chunk + 2) * CHUNK]
        grad = grad_hidden[:, chunk * CHUNK : (chunk + 1) * CHUNK]
        square = gate * gate
        curve = jnp.tanh(0.7978845608028654 * gate * (1.0 + 0.044715 * square))
        half = 0.5 * (1.0 + curve)
        gelu = gate * half
        slope = half + 0.5 * gate * (1.0 - curve * curve) * (
            0.7978845608028654 * (1.0 + 3 * 0.044715 * square)
        )
        hidden, grads = vmem["hidden"], vmem["grad_gate_up"]
        hidden[spot, :, chunk * CHUNK : (chunk + 1) * CHUNK] = low(gelu * up)
        grads[spot, :, 2 * chunk * CHUNK : (2 * chunk + 1) * CHUNK] = low(grad * up * slope)
        grads[spot, :, (2 * chunk + 1) * CHUNK : (2 * chunk + 2) * CHUNK] = low(grad * gelu)

    steps = sum(unit.owner == 6 for unit in back_units)
    for spot in range(steps):
        unit = back_units[spot]
        size = unit.shape[1]
        matrix = weight()
        groups_at = slice(unit.start // 16, (unit.start + size) // 16)
        down = low(wide(down_rows[groups_at]).reshape(size // 2, width))
        gate_up = mul(vmem["normed_ffn"][...], matrix())
        grad_hidden = mul(vmem["branch"][...], down, 1, 1)
        for chunk in range(size // (2 * CHUNK)):
            activate(spot, gate_up, grad_hidden, chunk)
        spent(4.0)
        vmem["grad_normed"][...] += mul(vmem["grad_gate_up"][spot, :, 0:size], matrix(), 1, 1)
        release()
        outcome[...] += mul(vmem["hidden"][spot, :, 0 : size // 2], down)
        spent(4.0)
        weight_grad(spot, "normed_ffn", vmem["grad_gate_up"][spot, :, 0:size])
        scatter.advance()
    while not driver.done():
        driver.advance()
    pump()
    outcome_copy = pltpu.make_async_copy(outcome, outcome_out, out_sems.at[2])
    outcome_copy.start()
    reads = read_inputs(first_free, 1)

    def norm_back(which, stream, before, last):
        gain = vmem["gains"][which : which + 1]
        step_rows = 64

        def body(step, total):
            at = pl.ds(pl.multiple_of(step * step_rows, step_rows), step_rows)
            value = wide(stream[at, :])
            scale = lax.rsqrt(jnp.mean(value * value, axis=-1, keepdims=True) + 1e-06)
            unit = value * scale
            grad = vmem["grad_normed"][at, :]
            scaled = grad * gain
            result = wide(before[at, :]) + scale * (
                scaled - unit * jnp.mean(scaled * unit, axis=-1, keepdims=True)
            )
            dx[at, :] = result
            if not last:
                rounded[2 - which, at, :] = low(result)
            return total + jnp.sum(grad * unit, axis=0, keepdims=True)

        total = lax.fori_loop(0, rows // step_rows, body, jnp.zeros((1, width), jnp.float32))
        gain_grads[which : which + 1, :] = total

    def through(source, target, add, rounding):
        value = mul(source[...], weight()(), 1, 1)
        if add:
            value = value + target[...]
        target[...] = low(value) if rounding else value
        release()

    left = lax.broadcasted_iota(jnp.int32, (1, LANES), 1) < HEAD

    def stack(value):
        zero = jnp.zeros_like(value)
        return jnp.concatenate([jnp.where(left, value, zero), jnp.where(left, zero, value)], axis=0)

    def pair_back(queries, keys, values, probs, grad):
        count = queries.shape[0]
        stacked = stack(grad)
        spread = mul(stacked, values, 1, 1)
        wide_probs = wide(probs)
        product = wide_probs * spread
        scores = low(product - wide_probs * jnp.sum(product, axis=-1, keepdims=True))
        grad_values = low(mul(probs, stacked, 0, 0))
        both = mul(scores, keys)
        grad_queries = low(jnp.where(left, both[:count], both[count:]) * HEAD ** (-0.5))
        grad_keys = low(mul(scores, stack(queries * jnp.bfloat16(HEAD ** (-0.5))), 0, 0))
        return grad_queries, grad_keys, grad_values, scores

    def cross_back(pair):
        if pair + 1 < count_pairs:
            probs_copy(0, pair + 1, False).start()
        probs_copy(0, pair, False).wait()
        lanes = pl.ds(pair * LANES, LANES)

        def body(sequence, carry):
            at = pl.ds(pl.multiple_of(sequence * slot_rows, slot_rows), slot_rows)
            keys = pl.ds(pl.multiple_of(sequence * enc_rows, enc_rows), enc_rows)
            queries, pairs = vmem["queries"], vmem["pairs"]
            grads = pair_back(
                queries[at, lanes],
                pairs[0, keys, lanes],
                pairs[1, keys, lanes],
                probs_slots[0][pair % 2, sequence],
                grad_mixed[at, lanes],
            )
            queries[at, lanes], pairs[0, keys, lanes], pairs[1, keys, lanes] = grads[:3]
            return carry

        lax.fori_loop(0, seqs, body, 0)

    def self_back(pair):
        if pair + 1 < count_pairs:
            probs_copy(1, pair + 1, False).start()
        probs_copy(1, pair, False).wait()
        lanes = pl.ds(pair * LANES, LANES)
        total = 0.0
        for sequence in range(seqs):
            at = pl.ds(sequence * slot_rows, slot_rows)
            qkv = vmem["qkv"]
            grads = pair_back(
                qkv[0, at, lanes],
                qkv[1, at, lanes],
                qkv[2, at, lanes],
                probs_slots[1][pair % 2, sequence],
                grad_mixed[at, lanes],
            )
            qkv[0, at, lanes], qkv[1, at, lanes], qkv[2, at, lanes] = grads[:3]
            total = total + wide(grads[3])
        total = jnp.concatenate(
            [total, jnp.zeros((total.shape[0], period - slot_rows), jnp.float32)], axis=1
        )
        for head in range(2):
            sums = 0.0
            for group in range(slot_rows // 8):
                start = head * slot_rows + group * 8
                piece = total[start : start + 8]
                sums = sums + (pltpu.roll(piece, period - group * 8, 1) if group else piece)
            diag[2 * pair + head] = sums

    grad_mixed = vmem["normed_ffn"]
    chain, marks = [], {6: 0, 7: 0}

    def then(cost, step):
        chain.append((cost, step))

    def start_ffn():
        outcome_copy.wait()
        norm_back(2, vmem["third"], vmem["branch"], False)

    def start_cross():
        probs_copy(0, 0, False).start()
        through(rounded.at[0], grad_mixed, False, True)

    def encoder_back():
        keys, values = weight(), weight()
        stage = vmem["third"]
        for sequence in range(seqs):
            at = slice(sequence * enc_rows, (sequence + 1) * enc_rows)
            copy = pltpu.make_async_copy(
                stage.at[0:enc_rows], grad_encoder.at[at], out_sems.at[0]
            )
            if sequence:
                copy.wait()
            pairs = vmem["pairs"]
            stage[0:enc_rows] = mul(pairs[0, at], keys(), 1, 1) + mul(pairs[1, at], values(), 1, 1)
            copy.start()
        release()
        release()

    def end_cross():
        through(vmem["queries"], vmem["grad_normed"], False, False)

    def start_self():
        norm_back(1, vmem["second"], dx, False)

    def self_mixed():
        probs_copy(1, 0, False).start()
        through(rounded.at[1], grad_mixed, False, True)

    def self_normed(part):
        through(vmem["qkv"].at[part], vmem["grad_normed"], part > 0, False)

    def end_self():
        reads[0].wait()
        norm_back(0, shared.at[first_free], dx, True)
        pltpu.make_async_copy(dx, grad_tokens, out_sems.at[1]).start()

    then(1.5, start_ffn)
    marks[5] = len(chain)
    then(1.2, start_cross)
    for pair in range(count_pairs):
        then(0.8, functools.partial(cross_back, pair))
    marks[2] = marks[4] = len(chain)
    then(4.5, encoder_back)
    then(1.2, end_cross)
    then(1.5, start_self)
    marks[3] = len(chain)
    then(1.2, self_mixed)
    for pair in range(count_pairs):
        then(0.8, functools.partial(self_back, pair))
    marks[1] = len(chain)
    for part in range(3):
        then(1.2, functools.partial(self_normed, part))
    then(1.5, end_self)
    marks[0] = len(chain)

    def pack_grad(u):
        slot = u % whole_slots.shape[0]
        table = 0.0
        for row in range(8):
            part = diag[:, row, :]
            table = table + (pltpu.roll(part, period - row, 1) if row else part)
        high = low(table)
        rel = mul(high, spread[...], 1, 1) + mul(low(table - wide(high)), spread[...], 1, 1)
        for z in range(sizes[0]):
            for y in range(sizes[1]):
                at = slice((z * sizes[1] + y) * LANES, (z * sizes[1] + y + 1) * LANES)
                top = jnp.concatenate(
                    [gain_grads[:, at], jnp.zeros((PACK // 2 - norms, LANES), jnp.float32)], axis=0
                )
                tile = low(jnp.concatenate([top, rel], axis=0))
                for x in range(sizes[2]):
                    for core in range(sizes[3]):
                        whole_slots[slot, z, y, x, core, :, 0:LANES] = tile

    groups = owned[6].shape[0] // 8

    def down_piece(spot):
        size = vmem["hidden"].shape[2]
        size = min(size, hidden_width - spot * size)
        start = spot * vmem["hidden"].shape[2] // 8
        block = mul(vmem["hidden"][spot, :, 0:size], vmem["branch"][...], 0, 0)
        down_rows[start : start + size // 8] = low(block.reshape(size // 8, 8, width))

    def down_grad(u):
        slot = u % whole_slots.shape[0]
        start = back_units[u].row // 8

        block_rows = whole_slots.shape[5]

        def body(device, carry):
            piece = down_rows[pl.ds(device * groups + start, block_rows // 8)]
            c, rest = device % sizes[3], device // sizes[3]
            x, rest = rest % sizes[2], rest // sizes[2]
            whole_slots[slot, rest // sizes[1], rest % sizes[1], x, c, :, :] = low(
                wide(piece).reshape(block_rows, width)
            )
            return carry

        lax.fori_loop(0, sizes[0] * sizes[1] * sizes[2] * sizes[3], body, 0)

    def grad_of(u):
        unit = back_units[u]
        owner = unit.owner
        part = unit.start // width
        if owner == 7:
            if unit.row == 0:
                for spot in range(vmem["hidden"].shape[0]):
                    down_piece(spot)
            down_grad(u)
        elif owner == 5:
            weight_grad(u, "mixed_cross", rounded[0])
        elif owner == 2:
            if part == 0:
                for copy in reads[1:]:
                    copy.wait()
            weight_grad(u, "encoder", vmem["pairs"][part])
        elif owner == 4:
            weight_grad(u, "normed_cross", vmem["queries"][...])
        elif owner == 3:
            weight_grad(u, "mixed_self", rounded[1])
        elif owner == 1:
            lane = unit.start % width
            weight_grad(u, "normed_self", vmem["qkv"][part, :, lane : lane + unit.shape[1]])
        else:
            pack_grad(u)

    position = 0
    budget = 2.0
    for u in range(steps, len(back_units)):
        owner = back_units[u].owner
        while position < marks[owner]:
            chain[position][1]()
            position += 1
        grad_of(u)
        scatter.advance()
        used = 0.0
        while position < len(chain) and used < budget:
            used += chain[position][0]
            chain[position][1]()
            position += 1
    while not scatter.done():
        scatter.advance()
    pltpu.make_async_copy(
        vmem["third"].at[0:enc_rows], grad_encoder.at[0:enc_rows], out_sems.at[0]
    ).wait()
    pltpu.make_async_copy(dx, grad_tokens, out_sems.at[1]).wait()
    gather_wires.finish()


def layer_all(place, shards, norm_gains, rel_bias, data):
    tokens, encoder, cotangent, lengths, enc_lengths, bucket_ids = data
    blocks = [(PACK, LANES)] + [shard.shape for shard in shards]
    sizes = place.sizes
    seqs, slot_rows, width = tokens.shape
    rows, enc_rows = seqs * slot_rows, encoder.shape[1]
    block_rows = blocks[1][0]
    down_rows = blocks[7][0] * 8
    gathered = blocks[:3] + [(block_rows, 3 * width)] + blocks[6:]
    units = make_units(gathered, ORDER, GATHER_WIDTHS)
    back_units = []
    for owner in BACK_ORDER:
        if owner == 7:
            for row in range(0, down_rows, block_rows):
                unit = Unit(7, (block_rows, width), 0, width, len(back_units) % 4)
                unit.row = row
                back_units.append(unit)
        else:
            back_units += make_units(blocks, (owner,), SCATTER_WIDTHS, len(back_units))
    devices = sizes[0] * sizes[1] * sizes[2] * sizes[3]
    piece = PIECE // block_rows
    rings = ring_shapes(place, block_rows, piece)
    low_type, wide_type = jnp.bfloat16, jnp.float32
    steps = sum(unit.owner == 6 for unit in back_units)
    shapes = {
        "branch": ((rows, width), low_type),
        "normed_self": ((rows, width), low_type),
        "qkv": ((3, rows, width), low_type),
        "mixed_self": ((rows, width), low_type),
        "second": ((rows, width), wide_type),
        "normed_cross": ((rows, width), low_type),
        "queries": ((rows, width), low_type),
        "pairs": ((2, seqs * enc_rows, width), low_type),
        "mixed_cross": ((rows, width), low_type),
        "third": ((rows, width), wide_type),
        "normed_ffn": ((rows, width), low_type),
        "hidden": ((steps, rows, piece // 2), low_type),
        "grad_gate_up": ((steps, rows, piece), low_type),
        "grad_normed": ((rows, width), wide_type),
        "gains": ((norm_gains.shape[0], width), wide_type),
    }
    owned = [(block[0], block[1]) for block in blocks[1:7]] + [(down_rows, width)]
    pair_shapes = [(seqs, 2 * slot_rows, enc_rows), (seqs, 2 * slot_rows, slot_rows)]
    anywhere = pl.BlockSpec(memory_space=pl.ANY)
    inside = pl.BlockSpec(memory_space=pltpu.VMEM)
    scalars = pl.BlockSpec(memory_space=pltpu.SMEM)
    sends, returns = copies_of(units, sizes), copies_of(back_units, sizes)
    local = len(units) + 3 + blocks[6][1] // CHUNK
    depth = 3
    shaped = jax.ShapeDtypeStruct
    results = pl.pallas_call(
        functools.partial(
            layer_kernel, place, units, back_units, len(gathered), seqs, tuple(rings)
        ),
        out_shape=[shaped(sizes + block, low_type) for block in gathered]
        + [shaped((rows, width), wide_type)] * 2
        + [shaped((seqs * enc_rows, width), wide_type)]
        + [shaped((width // LANES,) + shape, low_type) for shape in pair_shapes]
        + [shaped(block, wide_type) for block in owned]
        + [shaped(norm_gains.shape, wide_type), shaped((1, rel_bias.shape[0]), wide_type)],
        in_specs=[anywhere] * (len(blocks) - 1)
        + [inside] * 2
        + [anywhere] * 3
        + [scalars] * 2
        + [inside],
        out_specs=[anywhere] * (len(gathered) + 5) + [inside] * (len(owned) + 2),
        scratch_shapes=[pltpu.VMEM(*shapes[name]) for name in BUFFERS]
        + [pltpu.VMEM((2,) + shape, low_type) for shape in pair_shapes]
        + [
            pltpu.VMEM((rows, width), wide_type),
            pltpu.VMEM((devices * blocks[7][0] + 8, 8, width), low_type),
            pltpu.VMEM((HEADS, 8, 2 * slot_rows), wide_type),
            pltpu.VMEM((norm_gains.shape[0], width), wide_type),
            pltpu.VMEM((PACK, LANES), low_type),
            pltpu.VMEM(sizes + (PACK, LANES), low_type),
            pltpu.VMEM((LANES, 2 * slot_rows), low_type),
            pltpu.VMEM((HEADS, 2 * slot_rows), wide_type),
            pltpu.VMEM((depth,) + sizes + (block_rows, piece), low_type),
            pltpu.VMEM((2,) + sizes + (block_rows, piece), low_type),
            pltpu.VMEM((RING + 1,) + sizes[:3] + (block_rows, piece), low_type),
        ]
        + [pltpu.VMEM(shape, low_type) for shape in rings.values()]
        + [
            pltpu.SemaphoreType.DMA((number,))
            for number in (sends, sends, returns, returns, local, depth + 2, 2 + seqs * enc_rows // rows, 4, 3)
        ],
        compiler_params=pltpu.CompilerParams(
            collective_id=0, has_side_effects=True, vmem_limit_bytes=63 * 2**20
        ),
        name="layer_all",
    )(
        *shards,
        norm_gains,
        rel_bias.reshape(1, -1),
        tokens.reshape(rows, width),
        encoder.reshape(-1, width),
        cotangent.reshape(rows, width),
        lengths,
        enc_lengths,
        bucket_ids.reshape(1, -1),
    )
    return results[len(gathered) :]


def norm_scale(stream, gain):
    return stream * lax.rsqrt(jnp.mean(stream * stream, axis=-1, keepdims=True) + 1e-06) * gain


def gelu_tanh(values):
    return (
        0.5
        * values
        * (1.0 + jnp.tanh(0.7978845608028654 * (values + 0.044715 * values * values * values)))
    )


def gated(gate_up):
    half_width = gate_up.shape[1] // 2
    return gelu_tanh(gate_up[:, :half_width]) * gate_up[:, half_width:]


def product(spec, left, right):
    return jnp.einsum(spec, left, right, preferred_element_type=jnp.float32)


def attend(queries, key_rows, value_rows, pos_bias, keep_mask):
    scores = product("bihc,bjhc->bhij", queries, key_rows) * HEAD ** (-0.5)
    if pos_bias is not None:
        scores = scores + pos_bias
    masked = jnp.where(keep_mask[:, None], scores, -1e30)
    row_max = jnp.max(masked, axis=-1, keepdims=True)
    powers = jnp.exp(masked - row_max)
    probs = powers / jnp.sum(powers, axis=-1, keepdims=True)
    low_probs = probs.astype(jnp.bfloat16)
    mixed = product("bhij,bjhc->bihc", low_probs, value_rows)
    return mixed.astype(jnp.bfloat16), low_probs


def attend_back(queries, key_rows, value_rows, low_probs, grad_mixed):
    probs = low_probs.astype(jnp.float32)
    grad_values = product("bhij,bihc->bjhc", low_probs, grad_mixed)
    grad_probs = product("bihc,bjhc->bhij", grad_mixed, value_rows)
    grad_scores = (
        probs * (grad_probs - jnp.sum(probs * grad_probs, axis=-1, keepdims=True))
    ).astype(jnp.bfloat16)
    grad_queries = product("bhij,bjhc->bihc", grad_scores, key_rows) * HEAD ** (-0.5)
    grad_keys = product("bhij,bihc->bjhc", grad_scores, queries) * HEAD ** (-0.5)
    return grad_queries, grad_keys, grad_values, grad_scores


def toeplitz(table, size):
    lead = table.shape[:-1]
    row = jnp.concatenate(
        [table[..., ::-1], jnp.broadcast_to(table[..., :1], lead + (size,))], axis=-1
    )
    tiled = jnp.broadcast_to(row[..., None, :], lead + (size, 2 * size)).reshape(lead + (-1,))
    tiled = jnp.concatenate([tiled[..., size - 1 :], row[..., :1]], axis=-1)
    tiled = tiled[..., : size * (2 * size - 1)]
    return tiled.reshape(lead + (size, 2 * size - 1))[..., :size]


def layer(weights, gains, rel_bias, tokens, encoder, cotangent, lengths, enc_lengths, bucket_ids):
    self_qkv, self_out, cross_q, cross_kv, cross_out, ff_in, ff_out = weights
    count, slots, width = tokens.shape
    enc_count = encoder.shape[1]
    bucket_map = toeplitz(bucket_ids, slots).reshape(-1)
    onehot = (lax.iota(jnp.int32, BUCKETS)[:, None] == bucket_map[None, :]).astype(jnp.bfloat16)
    pos_bias = jnp.dot(rel_bias, onehot, preferred_element_type=jnp.float32).reshape(
        HEADS, slots, slots
    )
    row_ids = lax.iota(jnp.int32, slots)
    self_mask = (row_ids[None, None, :] <= row_ids[None, :, None]) & (
        row_ids[None, None, :] < lengths[:, None, None]
    )
    cross_mask = lax.iota(jnp.int32, enc_count)[None, None, :] < enc_lengths[:, None, None]
    enc_rows = encoder.reshape(count * enc_count, width)
    dot = functools.partial(jnp.dot, preferred_element_type=jnp.float32)
    low = lambda value: value.astype(jnp.bfloat16)
    stream = tokens.reshape(count * slots, width).astype(jnp.float32)
    normed_self, back_self = jax.vjp(norm_scale, stream, gains[0])
    normed_self = low(normed_self)
    qkv = low(dot(normed_self, self_qkv)).reshape(count, slots, 3, HEADS, HEAD)
    mixed_self, probs_self = attend(qkv[:, :, 0], qkv[:, :, 1], qkv[:, :, 2], pos_bias, self_mask)
    mixed_self = mixed_self.reshape(count * slots, width)
    second = stream + dot(mixed_self, self_out)
    normed_cross, back_cross = jax.vjp(norm_scale, second, gains[1])
    normed_cross = low(normed_cross)
    queries = low(dot(normed_cross, cross_q)).reshape(count, slots, HEADS, HEAD)
    pairs = low(dot(enc_rows, cross_kv)).reshape(count, enc_count, 2, HEADS, HEAD)
    mixed_cross, probs_cross = attend(queries, pairs[:, :, 0], pairs[:, :, 1], None, cross_mask)
    mixed_cross = mixed_cross.reshape(count * slots, width)
    third = second + dot(mixed_cross, cross_out)
    normed_ffn, back_ffn = jax.vjp(norm_scale, third, gains[2])
    normed_ffn = low(normed_ffn)
    gate_up = dot(normed_ffn, ff_in)
    activated, back_gate = jax.vjp(gated, gate_up)
    hidden = low(activated)
    outcome = third + dot(hidden, ff_out)

    valid = (row_ids[None, :] < lengths[:, None]).astype(jnp.float32)[:, :, None]
    grad_out = (cotangent.astype(jnp.float32) * valid).reshape(count * slots, width)
    branch = low(grad_out)
    grad_ff_out = product("lf,ld->fd", hidden, branch)
    grad_hidden = product("ld,fd->lf", branch, ff_out)
    (grad_gate_up,) = back_gate(grad_hidden)
    grad_gate_up = low(grad_gate_up)
    grad_ff_in = product("ld,lf->df", normed_ffn, grad_gate_up)
    grad_stream, gain_ffn = back_ffn(product("lf,df->ld", grad_gate_up, ff_in))
    grad_third = grad_out + grad_stream
    branch = low(grad_third)
    grad_cross_out = product("le,ld->ed", mixed_cross, branch)
    grad_mixed = low(product("ld,ed->le", branch, cross_out)).reshape(count, slots, HEADS, HEAD)
    grad_queries, grad_keys, grad_values, unused = attend_back(
        queries, pairs[:, :, 0], pairs[:, :, 1], probs_cross, grad_mixed
    )
    grad_query_rows = low(grad_queries.reshape(count * slots, width))
    grad_pair_rows = low(
        jnp.concatenate(
            [
                grad_keys.reshape(count * enc_count, width),
                grad_values.reshape(count * enc_count, width),
            ],
            axis=1,
        )
    )
    grad_cross_q = product("ld,le->de", normed_cross, grad_query_rows)
    grad_cross_kv = product("ed,ef->df", enc_rows, grad_pair_rows)
    grad_enc = product("ef,df->ed", grad_pair_rows, cross_kv)
    grad_stream, gain_cross = back_cross(product("le,de->ld", grad_query_rows, cross_q))
    grad_second = grad_third + grad_stream
    branch = low(grad_second)
    grad_self_out = product("le,ld->ed", mixed_self, branch)
    grad_mixed = low(product("ld,ed->le", branch, self_out)).reshape(count, slots, HEADS, HEAD)
    grad_queries, grad_keys, grad_values, grad_scores = attend_back(
        qkv[:, :, 0], qkv[:, :, 1], qkv[:, :, 2], probs_self, grad_mixed
    )
    score_sums = jnp.sum(grad_scores.astype(jnp.float32), axis=0).reshape(HEADS, slots * slots)
    grad_rel_bias = product("hn,bn->hb", low(score_sums), onehot)
    grad_qkv = low(
        jnp.concatenate(
            [part.reshape(count * slots, width) for part in (grad_queries, grad_keys, grad_values)],
            axis=1,
        )
    )
    grad_self_qkv = product("ld,lf->df", normed_self, grad_qkv)
    grad_stream, gain_self = back_self(product("lf,df->ld", grad_qkv, self_qkv))
    grad_tok = grad_second + grad_stream
    grad_gains = jnp.stack([gain_self, gain_cross, gain_ffn], axis=0)
    grads = (
        grad_self_qkv,
        grad_self_out,
        grad_cross_q,
        grad_cross_kv,
        grad_cross_out,
        grad_ff_in,
        grad_ff_out,
    )
    return (
        outcome.reshape(tokens.shape),
        grad_tok.reshape(tokens.shape),
        grad_enc.reshape(encoder.shape),
        grads,
        grad_gains,
        grad_rel_bias,
    )


AXES = ("dp", "fsdp")


def by_collectives(data, shards):
    whole = lambda shard, axis=0: lax.all_gather(shard, AXES, axis=axis, tiled=True)
    weights = tuple(whole(shard) for shard in shards[:7])
    gains = whole(shards[7], 1).astype(jnp.float32)
    rel_bias = whole(shards[8]).reshape(HEADS, BUCKETS)
    outcome, grad_tok, grad_enc, grads, grad_gains, grad_rel_bias = layer(
        weights, gains, rel_bias, *data
    )
    settle = lambda total, axis=0: lax.psum_scatter(
        total, AXES, scatter_dimension=axis, tiled=True
    )
    return (
        (outcome, grad_tok, grad_enc)
        + tuple(settle(grad) for grad in grads)
        + (settle(grad_gains, 1), settle(grad_rel_bias.reshape(-1)))
    )


def by_kernels(place, data, shards):
    self_qkv, self_out, cross_q, cross_kv, cross_out, ff_in, ff_out = shards[:7]
    ff_rows, width = ff_out.shape
    sent = (self_qkv, cross_kv, self_out, cross_q, cross_out, ff_in)
    sent += (ff_out.reshape(ff_rows // 8, 8, width),)
    results = layer_all(place, sent, shards[7], shards[8], data)
    outcome, grad_tok, grad_enc = (
        result.reshape(like.shape)
        for result, like in zip(results[:3], (data[0], data[0], data[1]))
    )
    g_qkv, g_kv, g_so, g_cq, g_co, g_in, g_out = results[5:12]
    owned = (g_qkv, g_so, g_cq, g_kv, g_co, g_in, g_out)
    return (outcome, grad_tok, grad_enc) + owned + (results[12], results[13].reshape(-1))


def on_device(place, *args):
    data, shards = args[:6], args[6:]
    per = shards[7].shape[1]
    regular = all(shard.shape[0] % 16 == 0 for shard in shards[:6])
    group = place.sizes[2] * place.sizes[3]
    seqs, slots, enc_slots = args[0].shape[0], args[0].shape[1], args[1].shape[1]
    regular = regular and enc_slots <= seqs * slots and seqs * enc_slots % (seqs * slots) == 0
    if regular and shards[6].shape[0] % 8 == 0 and group * per == LANES:
        return by_kernels(place, data, shards)
    return by_collectives(data, shards)


def solution(mesh):
    rows = P(AXES, None, None)
    flat = P(AXES)
    matrix = P(AXES, None)
    split = P(None, AXES)
    place = Place(mesh.shape["dp"], mesh.shape["fsdp"])
    return jax.shard_map(
        functools.partial(on_device, place),
        mesh=mesh,
        in_specs=(rows, rows, rows, flat, flat, P()) + (matrix,) * 7 + (split, flat),
        out_specs=(rows, rows, rows) + (matrix,) * 7 + (split, flat),
        check_vma=False,
    )
```

```python
import functools

import jax
import jax.numpy as jnp
from jax import lax
from jax.experimental import pallas as pl
from jax.experimental.pallas import tpu as pltpu
from jax.sharding import PartitionSpec as P

HEADS = 16
HEAD = 64
BUCKETS = 32
PACK = 32
LANES = 128
PIECE = 32 * 1024
GATHER_WIDTHS = {1: (1024, 2048), 4: (2048, 1024), None: (2048,)}
SCATTER_WIDTHS = {None: (1024,)}

MESH = pl.DeviceIdType.MESH


class Place:
    def __init__(self, dp, fsdp):
        self.sizes = (dp // 2, 2, fsdp // 2, 2)

    def locate(self):
        row, column = lax.axis_index("dp"), lax.axis_index("fsdp")
        sizes = self.sizes
        self.here = (row // sizes[1], row % sizes[1], column // sizes[3], column % sizes[3])
        z = self.here[0]
        self.inner, self.outer = z % 3 != 0, z % 3 == 0
        self.twin, self.far, self.entry = z + 1 - 2 * (z % 2), 2 - 2 * (z // 2), 2 - z // 2

    def moved(self, axis, step):
        coords = list(self.here)
        coords[axis] = (coords[axis] + step) % self.sizes[axis]
        return coords

    def at(self, axis, coordinate):
        coords = list(self.here)
        coords[axis] = coordinate
        return coords

    def hops(self, axes):
        steps = []
        for axis in axes:
            steps += ["spread", "relay"] if axis == 0 and self.sizes[0] == 4 else [axis]
        return steps

    def device(self, coords):
        return (coords[0] * self.sizes[1] + coords[1], coords[2] * self.sizes[3] + coords[3])

    def peers(self):
        return [(axis, step) for axis in range(4) for step in range(1, self.sizes[axis])]

    def greet(self):
        barrier = pltpu.get_barrier_semaphore()
        for axis, step in self.peers():
            pl.semaphore_signal(
                barrier, inc=1, device_id=self.device(self.moved(axis, step)), device_id_type=MESH
            )
        pl.semaphore_wait(barrier, len(self.peers()))


def split_lanes(width, turn):
    if width % (4 * LANES) == 0:
        last = width // 4
        more = -(-(width - last) // (2 * LANES)) * LANES
        less = width - last - more
        order = (1, 2, 0) if turn % 2 else (2, 1, 0)
        return ((0, more, (0, 2, 1)), (more, less, (0, 1, 2)), (more + less, last, order))
    return ((0, width, (0, 2, 1)),)


class Unit:
    def __init__(self, owner, block, start, count, turn):
        self.owner, self.start, self.count = owner, start, count
        self.grouped = len(block) == 3
        self.shape = (count,) + block[1:] if self.grouped else (block[0], count)
        self.paths = split_lanes(self.shape[-1], turn)

    def part(self, start=0, size=None):
        size = self.shape[-1] if size is None else size
        if self.grouped:
            return (pl.ds(self.start, self.count), slice(None), pl.ds(start, size))
        return (slice(None), pl.ds(self.start + start, size))


def make_units(blocks, order, widths, before=0):
    units = []
    for owner in order:
        block = blocks[owner]
        grouped = len(block) == 3
        total = block[0] if grouped else block[1]
        turns = widths.get(owner, widths[None])
        start = 0
        while start < total:
            most = turns[0]
            turns = turns[1:] or turns
            most = max(most // 256, 1) if grouped else most
            count = min(most, total - start)
            units.append(Unit(owner, block, start, count, (before + len(units)) % 4))
            start += count
    return units


def guarded(condition, action):
    if condition is True:
        action()
    elif condition is not False:
        pl.when(condition)(action)


class Message:
    def __init__(self, make, sends, receives):
        self.make, self.sends, self.receives = make, sends, receives

    def start(self):
        guarded(self.sends, lambda: self.make().start())

    def wait_send(self):
        guarded(self.sends, lambda: self.make().wait_send())

    def wait_recv(self):
        guarded(self.receives, lambda: self.make().wait_recv())

    def wait(self):
        self.wait_send()
        self.wait_recv()


class Wires:
    def __init__(self, place, send_sems, recv_sems):
        self.place, self.send_sems, self.recv_sems = place, send_sems, recv_sems
        self.started, self.spot = [], 0

    def send(self, source, target, coords, sends=True, receives=True, arrival=None):
        spot = self.spot
        self.spot += 1
        arrival = spot if arrival is None else arrival
        device = self.place.device(coords)

        def make():
            return pltpu.make_async_remote_copy(
                src_ref=source,
                dst_ref=target,
                send_sem=self.send_sems.at[spot],
                recv_sem=self.recv_sems.at[arrival],
                device_id=device,
                device_id_type=MESH,
            )

        message = Message(make, sends, receives)
        message.start()
        self.started.append(message)
        return message

    def along(self, axis, source, target):
        return [
            self.send(source, target, self.place.moved(axis, step))
            for step in range(1, self.place.sizes[axis])
        ]

    def spread(self, source, target):
        place = self.place
        messages = [self.send(source, target, place.at(0, place.twin))]
        first = self.spot
        arrival = first + place.here[0] % 2
        entry = place.at(0, place.entry)
        messages.append(self.send(source, target, entry, receives=False, arrival=arrival))
        for arrival in (first, first + 1):
            messages.append(
                self.send(source, target, entry, sends=False, receives=place.inner, arrival=arrival)
            )
        return messages

    def relay(self, ref):
        place = self.place
        twin = place.at(0, place.twin)
        return [self.send(ref, ref, twin, sends=place.inner, receives=place.outer)]

    def finish(self):
        for message in self.started:
            message.wait_send()


def gather_stages(place, units, shards, wholes, wires, own_copies):
    full = slice(None)
    pending = {}

    def settle(u):
        for copy in pending[u]:
            copy.wait_recv()
        pending[u] = []

    def move(u, stage):
        unit = units[u]
        whole = wholes[unit.owner]
        if stage == int(unit.owner in shards):
            for copy in own_copies[u]:
                copy.wait()
        if stage:
            settle(u)
        pending[u] = []
        for start, size, axes in unit.paths:
            steps = place.hops(axes)
            if stage >= len(steps):
                continue
            step, done = steps[stage], steps[:stage]
            part = unit.part(start, size)
            index = [full if axis in done else place.here[axis] for axis in range(3)]
            if "relay" in done:
                index[0] = full
            elif step == "relay":
                index[0] = pl.ds(place.far, 2)
            target = whole.at[tuple(index) + (place.here[3],) + part]
            source = target
            if stage == 0 and unit.owner in shards:
                source = shards[unit.owner].at[part]
            if step == "spread":
                pending[u] += wires.spread(source, target)
            elif step == "relay":
                pending[u] += wires.relay(target)
            else:
                pending[u] += wires.along(step, source, target)

    def across(u):
        settle(u)
        unit = units[u]
        ref = wholes[unit.owner].at[(full, full, full, place.here[3]) + unit.part()]
        pending[u] = wires.along(3, ref, ref)

    count = len(place.hops((0, 1, 2)))
    return tuple(functools.partial(move, stage=stage) for stage in range(count)) + (across, settle)


def copies_of(units, sizes):
    line = 4 if sizes[0] == 4 else sizes[0] - 1
    per_path = line + sizes[1] - 1 + sizes[2] - 1
    return sum(1 + len(unit.paths) * (per_path + 1) for unit in units)


def mul(left, right, left_dim=1, right_dim=0):
    return lax.dot_general(
        left, right, (((left_dim,), (right_dim,)), ((), ())), preferred_element_type=jnp.float32
    )


def low(value):
    return value.astype(jnp.bfloat16)


def wide(value):
    return value.astype(jnp.float32)


def rms_rows(source, target, gain, rows=64):
    def body(step, carry):
        at = pl.ds(pl.multiple_of(step * rows, rows), rows)
        value = wide(source[at, :])
        scale = lax.rsqrt(jnp.mean(value * value, axis=-1, keepdims=True) + 1e-06)
        target[at, :] = low(value * scale * gain)
        return carry

    lax.fori_loop(0, source.shape[0] // rows, body, 0)


def attend_pair(queries, key_rows, value_rows, bias, mask):
    rows = queries.shape[0]
    left = lax.broadcasted_iota(jnp.int32, (1, LANES), 1) < HEAD
    zero = jnp.zeros_like(queries)
    scaled = queries * jnp.bfloat16(HEAD ** (-0.5))
    stacked = jnp.concatenate(
        [jnp.where(left, scaled, zero), jnp.where(left, zero, scaled)], axis=0
    )
    scores = mul(stacked, key_rows, 1, 1)
    if bias is not None:
        scores = scores + bias
    scores = jnp.where(mask, scores, -1e30)
    powers = jnp.exp(scores - jnp.max(scores, axis=-1, keepdims=True))
    probs = low(powers / jnp.sum(powers, axis=-1, keepdims=True))
    none = jnp.zeros_like(value_rows)
    mixed = mul(probs[:rows], jnp.where(left, value_rows, none)) + mul(
        probs[rows:], jnp.where(left, none, value_rows)
    )
    return probs, low(mixed)


class Driver:
    def __init__(self, units, stages, lead):
        self.units, self.stages, self.lead = units, stages, lead
        self.tick, self.debt = 0, 0.0

    def done(self):
        return self.tick >= len(self.units) + len(self.stages) - 1

    def settled(self):
        return self.tick - len(self.stages)

    def advance(self):
        for lag, stage in enumerate(self.stages):
            if 0 <= self.tick - lag < len(self.units):
                stage(self.tick - lag)
        self.tick += 1

    def until(self, unit):
        while self.settled() < unit:
            self.advance()

    def spent(self, cost):
        self.debt += cost
        while self.debt >= self.lead:
            self.debt -= self.lead
            if not self.done():
                self.advance()


def scatter_hops(place, axes):
    names = {"spread": "last", "relay": "relay"}
    return [(names.get(step, "axis"), 0 if step in names else step) for step in place.hops(axes)[::-1]]


def ring_shapes(place, block_rows, width):
    sizes, shapes = place.sizes, {}
    for turn in range(4):
        for start, lanes, axes in split_lanes(width, turn):
            left = list(range(3))
            for hop, (step, axis) in enumerate(scatter_hops(place, axes)):
                senders = sizes[axis] - 1 if step == "axis" else 2
                rest = tuple(sizes[other] for other in left if other != axis)
                slots = RING + (hop == 1)
                lanes = max(lanes, shapes.get((axes, hop), (0,))[-1])
                shapes[axes, hop] = (slots, senders) + rest + (block_rows, lanes)
                if step != "relay":
                    left.remove(axis)
    return shapes


def scatter_stages(place, units, whole_slots, arrived, rings, finish, wires):
    sizes, full = place.sizes, slice(None)
    here = place.here
    pending = {}

    def settle(u):
        for copy in pending[u]:
            copy.wait()
        pending[u] = []

    def lanes(u):
        return (full, pl.ds(0, units[u].shape[1]))

    def slot(u):
        return whole_slots.at[u % whole_slots.shape[0]]

    def spread(b, axes):
        coords = {}
        for axis in reversed(axes):
            coords[axis] = b % sizes[axis]
            b = b // sizes[axis]
        return coords

    def count(axes):
        total = 1
        for axis in axes:
            total *= sizes[axis]
        return total

    def held(u, path, hop):
        start, size, axes = path
        steps = scatter_hops(place, axes)
        done = [h for h in range(hop) if steps[h][0] != "relay"]
        gone = [steps[h][1] for h in done]
        left = [axis for axis in range(3) if axis not in gone]
        if not done:
            ring = u % arrived.shape[0]
            return left, lambda at: (
                arrived,
                (ring,) + tuple(at[a] for a in left) + (full, pl.ds(start, size)),
            )
        ref = rings[axes, done[-1]]
        ring = u % ref.shape[0]
        return left, lambda at: (
            ref,
            (ring, 0) + tuple(at[a] for a in left) + (full, pl.ds(0, size)),
        )

    def landing(u, path, hop, sender, at=None):
        start, size, axes = path
        ref = rings[axes, hop]
        rest = len(ref.shape) - 4
        inner = (full,) * rest if at is None else at
        return ref, (u % ref.shape[0], sender) + inner + (full, pl.ds(0, size))

    def first(u):
        source = slot(u).at[(full, full, full, (here[3] + 1) % 2) + lanes(u)]
        target = arrived.at[(u % arrived.shape[0], full, full, full) + lanes(u)]
        pending[u] = [wires.send(source, target, place.moved(3, 1))]

    def pass_on(u, hop):
        for path in units[u].paths:
            steps = scatter_hops(place, path[2])
            if hop >= len(steps):
                continue
            step, axis = steps[hop]
            left, where = held(u, path, hop)

            def take(coordinate):
                ref, index = where({a: coordinate if a == axis else full for a in left})
                return ref.at[index]

            def put(sender):
                ref, index = landing(u, path, hop, sender)
                return ref.at[index]

            if step == "axis":
                for move in range(1, sizes[axis]):
                    coords = place.moved(axis, move)
                    pending[u].append(wires.send(take(coords[axis]), put(move - 1), coords))
            elif step == "relay":
                ref, index = landing(u, path, hop, pl.ds(0, 2))
                pending[u].append(
                    wires.send(
                        take(pl.ds(place.far, 2)),
                        ref.at[index],
                        place.at(0, place.twin),
                        sends=place.outer,
                        receives=place.inner,
                    )
                )
            else:
                pending[u].append(wires.send(take(place.twin), put(0), place.at(0, place.twin)))
                spot = wires.spot
                for other in range(2):
                    pending[u].append(
                        wires.send(
                            take(place.far + other),
                            put(1),
                            place.at(0, place.far + other),
                            sends=place.inner,
                            receives=other == 0,
                            arrival=spot,
                        )
                    )

    def merge(u, path, hop):
        start, size, axes = path
        steps = scatter_hops(place, axes)
        if hop >= len(steps):
            return
        step, axis = steps[hop]
        left, before = held(u, path, hop)
        rest = [a for a in left if a != axis]
        senders = rings[axes, hop].shape[1]

        def relayed(b, carry):
            at = spread(b % count(rest), rest)
            which = b // count(rest)
            ref, index = before({**at, axis: place.far + which})
            source, arrival = landing(u, path, hop, which, tuple(at[a] for a in rest))
            ref[index] = low(wide(ref[index]) + wide(source[arrival]))
            return carry

        def take_relay():
            lax.fori_loop(0, 2 * count(rest), relayed, 0)

        if step == "relay":
            guarded(place.inner, take_relay)
            return

        def body(b, carry):
            at = spread(b, rest)
            source, index = before({**at, axis: here[axis]})
            value = wide(source[index])
            for sender in range(senders):
                source, index = landing(u, path, hop, sender, tuple(at[a] for a in rest))
                value = value + wide(source[index])
            if hop == len(steps) - 1:
                finish(u, start, size, value)
            else:
                target, index = landing(u, path, hop, 0, tuple(at[a] for a in rest))
                target[index] = low(value)
            return carry

        if hop == len(steps) - 1:
            body(0, 0)
        else:
            lax.fori_loop(0, count(rest), body, 0)

    def second(u):
        settle(u)
        ring, own = u % arrived.shape[0], slot(u)

        def body(b, carry):
            at = spread(b, (0, 1, 2))
            index = tuple(at[a] for a in range(3))
            target = (ring,) + index + lanes(u)
            arrived[target] = low(wide(arrived[target]) + wide(own[index + (here[3],) + lanes(u)]))
            return carry

        lax.fori_loop(0, count((0, 1, 2)), body, 0)
        pass_on(u, 0)

    def later(u, hop):
        settle(u)
        for path in units[u].paths:
            merge(u, path, hop)
        pass_on(u, hop + 1)

    hops = len(scatter_hops(place, (0, 1, 2)))
    return (first, second) + tuple(functools.partial(later, hop=hop) for hop in range(hops))


CHUNK = 256
RING = 5
ORDER = (0, 1, 2, 3, 5, 4)
BACK_ORDER = (6, 7, 5, 2, 4, 3, 1, 0)
BUFFERS = (
    "branch", "normed_self", "qkv", "mixed_self", "second", "normed_cross",
    "queries", "pairs", "mixed_cross", "third", "normed_ffn", "hidden", "grad_gate_up",
    "grad_normed", "gains",
)


def layer_kernel(place, units, back_units, count, seqs, ring_keys, *refs):
    shards, refs = refs[:7], refs[7:]
    gain_shard, rel_shard, tokens_in, encoder_in, cotangent_in = refs[:5]
    lengths, enc_lengths, bucket_ids, refs = refs[5], refs[6], refs[7], refs[8:]
    wholes, refs = refs[:count], refs[count:]
    outcome_out, grad_tokens, grad_encoder, refs = refs[0], refs[1], refs[2], refs[3:]
    probs_out, refs = refs[:2], refs[2:]
    owned_out, refs = refs[:7], refs[7:]
    own_gains, own_rel, refs = refs[0], refs[1], refs[2:]
    owned, refs = refs[:7], refs[7:]
    vmem, refs = dict(zip(BUFFERS, refs)), refs[len(BUFFERS) :]
    probs_slots, refs = refs[:2], refs[2:]
    dx, down_rows, diag, gain_grads = refs[:4]
    own_pack, packs_in, spread, bias_rows, slots, whole_slots, arrived = refs[4:11]
    refs = refs[11:]
    rings, refs = dict(zip(ring_keys, refs)), refs[len(ring_keys) :]
    gather_send, gather_recv, scatter_send, scatter_recv = refs[:4]
    local_sems, fetch_sems, read_sems, probs_sems, out_sems = refs[4:]
    place.locate()
    sizes = place.sizes
    devices = sizes[0] * sizes[1] * sizes[2] * sizes[3]
    me = place.device(place.here)
    me = me[0] * (sizes[2] * sizes[3]) + me[1]
    rows, width = dx.shape
    slot_rows, enc_rows = rows // seqs, encoder_in.shape[0] // seqs
    shared = vmem["grad_gate_up"]
    parts = encoder_in.shape[0] // rows
    rounded, first_free = shared, 2
    count_pairs = width // LANES
    norms, per = gain_shard.shape
    rel_per = rel_shard.shape[1]
    gain_lane = (me % (LANES // per)) * per
    rel_row, rel_lane = me * rel_per // BUCKETS, (me * rel_per) % BUCKETS
    hidden_width = owned[5].shape[1] // 2
    outcome = dx

    def read_inputs(start, sems):
        sources = [(tokens_in, shared.at[start])]
        for part in range(parts):
            source = encoder_in.at[part * rows : (part + 1) * rows]
            sources.append((source, shared.at[start + 1 + part]))
        copies = [
            pltpu.make_async_copy(source, target, read_sems.at[sems + at])
            for at, (source, target) in enumerate(sources)
        ]
        for copy in copies:
            copy.start()
        return copies

    def encoder_rows(start):
        return shared[start + 1 : start + 1 + parts].reshape(parts * rows, width)

    reads = read_inputs(first_free, 1)
    branch_read = pltpu.make_async_copy(cotangent_in, vmem["branch"], read_sems.at[0])
    branch_read.start()
    padded = jnp.concatenate(
        [wide(gain_shard[...]), jnp.zeros((PACK // 2 - norms, per), jnp.float32)], axis=0
    )
    padded = jnp.concatenate([padded, jnp.zeros((PACK // 2, LANES - per), jnp.float32)], axis=1)
    rel = jnp.concatenate(
        [wide(rel_shard[...]), jnp.zeros((1, LANES - rel_per), jnp.float32)], axis=1
    )
    rel = jnp.broadcast_to(rel, (PACK // 2, LANES))
    pack_rows = lax.broadcasted_iota(jnp.int32, (PACK // 2, LANES), 0)
    rel = jnp.where(pack_rows == rel_row, pltpu.roll(rel, rel_lane, 1), 0.0)
    own_pack[...] = low(jnp.concatenate([pltpu.roll(padded, gain_lane, 1), rel], axis=0))
    self_qkv, cross_kv, self_out, cross_q, cross_out, ff_in, ff_out = shards
    shards = {0: own_pack, 1: self_qkv, 2: cross_kv, 5: ff_out}
    own_copies, serial = {}, 0
    for u, unit in enumerate(units):
        end = unit.start + unit.shape[-1]
        pieces = []
        if unit.owner == 3:
            for at in range(unit.start, end, width):
                target = (slice(None), pl.ds(at, width))
                pieces.append(((self_out, cross_q, cross_out)[at // width], target))
        elif unit.owner == 4:
            for at in range(unit.start, end, CHUNK):
                spot = at // CHUNK
                source = (spot % 2) * hidden_width + (spot // 2) * CHUNK
                target = (slice(None), pl.ds(at, CHUNK))
                pieces.append((ff_in.at[:, source : source + CHUNK], target))
        else:
            pieces.append((shards[unit.owner].at[unit.part()], unit.part()))
        own_copies[u] = []
        for source, target in pieces:
            copy = pltpu.make_async_copy(
                source, wholes[unit.owner].at[place.here + target], local_sems.at[serial]
            )
            serial += 1
            copy.start()
            own_copies[u].append(copy)
    place.greet()
    gather_wires = Wires(place, gather_send, gather_recv)
    wires = Wires(place, scatter_send, scatter_recv)
    driver = Driver(
        units, gather_stages(place, units, shards, wholes, gather_wires, own_copies), 8.0
    )

    last_of = {unit.owner: u for u, unit in enumerate(units)}
    wanted = []
    at = {}
    for u, unit in enumerate(units):
        if unit.owner not in (0, 5):
            start, end = at.get(unit.owner, 0), unit.start + unit.shape[1]
            total = wholes[unit.owner].shape[-1]
            while start < end and min(start + width, total) <= end:
                size = min(width, total - start)
                wanted.append((unit.owner, (slice(None), pl.ds(start, size)), size, u))
                start += size
            at[unit.owner] = start
    for owner, part in ((3, 2), (2, 0), (2, 1), (3, 1), (3, 0), (1, 0), (1, 1), (1, 2)):
        wanted.append((owner, (slice(None), pl.ds(part * width, width)), width, 0))
    depth = slots.shape[0]
    state = dict(fetched=0, used=0, taken=0, raw=False)

    def fetch(spot):
        owner, part, size, unit = wanted[spot]
        return pltpu.make_async_copy(
            wholes[owner].at[(slice(None),) * 4 + part],
            slots.at[(spot % depth,) + (slice(None),) * 5 + (pl.ds(0, size),)],
            fetch_sems.at[spot % depth],
        )

    def raw_copy():
        return pltpu.make_async_copy(
            wholes[5].reshape(devices * wholes[5].shape[4], 8, width),
            down_rows.at[0 : devices * wholes[5].shape[4]],
            fetch_sems.at[depth],
        )

    def pump():
        while (
            state["fetched"] < len(wanted)
            and wanted[state["fetched"]][3] <= driver.settled()
            and state["fetched"] < state["used"] + depth
        ):
            fetch(state["fetched"]).start()
            state["fetched"] += 1
        if not state["raw"] and driver.settled() >= last_of[5]:
            state["raw"] = True
            raw_copy().start()

    def spent(cost):
        driver.spent(cost)
        pump()

    def weight():
        spot = state["taken"]
        state["taken"] += 1
        driver.until(wanted[spot][3])
        pump()
        fetch(spot).wait()
        size = wanted[spot][2]
        return lambda: slots[spot % depth, :, :, :, :, :, 0:size].reshape(width, size)

    def release():
        state["used"] += 1
        pump()

    def project(source, target, cost):
        matrix = weight()
        target[...] = low(mul(source[...], matrix()))
        release()
        spent(cost)

    def residual(source, before, target, cost):
        matrix = weight()
        target[...] = wide(before[...]) + mul(source[...], matrix())
        release()
        spent(cost)

    branch_read.wait()
    for sequence in range(seqs):
        at = pl.ds(sequence * slot_rows, slot_rows)
        valid = lax.broadcasted_iota(jnp.int32, (slot_rows, 1), 0) < lengths[sequence]
        vmem["branch"][at, :] = low(jnp.where(valid, wide(vmem["branch"][at, :]), 0.0))
    period = 2 * slot_rows
    distance = lax.broadcasted_iota(jnp.int32, (slot_rows, period), 0)
    lane = lax.broadcasted_iota(jnp.int32, (slot_rows, period), 1)
    turned = (lane == (period - distance) % period).astype(jnp.bfloat16)
    buckets = lax.broadcasted_iota(jnp.int32, (LANES, slot_rows), 0)
    spread[...] = low(mul((buckets == bucket_ids[...]).astype(jnp.bfloat16), turned))
    driver.until(0)
    copy = pltpu.make_async_copy(wholes[0], packs_in, fetch_sems.at[depth + 1])
    copy.start()
    copy.wait()
    packs = wide(packs_in[...]).reshape(width // LANES, -1, PACK, LANES)
    summed = jnp.sum(packs, axis=1)
    for group in range(summed.shape[0]):
        vmem["gains"][:, group * LANES : (group + 1) * LANES] = summed[group, :norms]
    table = low(jnp.sum(summed, axis=0)[PACK // 2 :])
    bias_rows[...] = mul(table, spread[...])
    reads[0].wait()
    rms_rows(shared.at[first_free], vmem["normed_self"], vmem["gains"][0:1])

    for part in range(3):
        project(vmem["normed_self"], vmem["qkv"].at[part], 1.5)
    for copy in reads[1:]:
        copy.wait()
    for part in range(2):
        project(encoder_rows(first_free), vmem["pairs"].at[part], 2.5)

    def probs_copy(kind, pair, out):
        near = probs_slots[kind].at[pair % 2]
        far = probs_out[kind].at[pair]
        source, target = (near, far) if out else (far, near)
        return pltpu.make_async_copy(source, target, probs_sems.at[2 * kind + pair % 2])

    def pairs_forward(kind, body, cost):
        for pair in range(count_pairs):
            if pair >= 2:
                probs_copy(kind, pair - 2, True).wait()
            lax.fori_loop(0, seqs, functools.partial(body, pair), 0)
            probs_copy(kind, pair, True).start()
            spent(cost)
        for pair in range(count_pairs - 2, count_pairs):
            probs_copy(kind, pair, True).wait()

    def sequence_rows(sequence, size):
        return pl.ds(pl.multiple_of(sequence * size, size & -size), size)

    def self_pair(pair, sequence, carry):
        lanes = pl.ds(pair * LANES, LANES)
        row = lax.broadcasted_iota(jnp.int32, (slot_rows, slot_rows), 0)
        column = lax.broadcasted_iota(jnp.int32, (slot_rows, slot_rows), 1)
        bias = jnp.concatenate(
            [
                pltpu.roll(
                    jnp.broadcast_to(bias_rows[2 * pair + head, :][None], (slot_rows, period)),
                    0,
                    1,
                    stride=1,
                    stride_axis=0,
                )[:, :slot_rows]
                for head in range(2)
            ],
            axis=0,
        )
        at = sequence_rows(sequence, slot_rows)
        mask = (column <= row) & (column < lengths[sequence])
        probs, mixed = attend_pair(
            vmem["qkv"][0, at, lanes],
            vmem["qkv"][1, at, lanes],
            vmem["qkv"][2, at, lanes],
            bias,
            jnp.concatenate([mask, mask], axis=0),
        )
        probs_slots[1][pair % 2, sequence] = probs
        vmem["mixed_self"][at, lanes] = mixed
        return carry

    pairs_forward(1, self_pair, 1.3)
    residual(vmem["mixed_self"], shared.at[first_free], vmem["second"], 1.5)
    rms_rows(vmem["second"], vmem["normed_cross"], vmem["gains"][1:2])
    project(vmem["normed_cross"], vmem["queries"], 2.0)

    def cross_pair(pair, sequence, carry):
        lanes = pl.ds(pair * LANES, LANES)
        column = lax.broadcasted_iota(jnp.int32, (1, enc_rows), 1)
        at = sequence_rows(sequence, slot_rows)
        keys = sequence_rows(sequence, enc_rows)
        probs, mixed = attend_pair(
            vmem["queries"][at, lanes],
            vmem["pairs"][0, keys, lanes],
            vmem["pairs"][1, keys, lanes],
            None,
            column < enc_lengths[sequence],
        )
        probs_slots[0][pair % 2, sequence] = probs
        vmem["mixed_cross"][at, lanes] = mixed
        return carry

    pairs_forward(0, cross_pair, 1.3)
    residual(vmem["mixed_cross"], vmem["second"], vmem["third"], 1.5)
    rms_rows(vmem["third"], vmem["normed_ffn"], vmem["gains"][2:3])
    driver.until(last_of[5])
    pump()
    raw_copy().wait()
    outcome[...] = vmem["third"][...]
    vmem["grad_normed"][...] = jnp.zeros_like(vmem["grad_normed"])

    last_back = {unit.owner: u for u, unit in enumerate(back_units)}
    leaving = []

    def finish(u, start_lane, size, value):
        unit = back_units[u]
        store(unit, start_lane, size, value)
        if unit.owner and u == last_back[unit.owner] and start_lane + size == unit.shape[1]:
            at = unit.owner - 1
            copy = pltpu.make_async_copy(owned[at], owned_out[at], out_sems.at[3 + at])
            copy.start()
            leaving.append(copy)

    def store(unit, start_lane, size, value):
        start = unit.start + start_lane
        if unit.owner == 0:
            own_gains[...] = pltpu.roll(
                value[: PACK // 2], (LANES - gain_lane) % LANES, 1
            )[:norms, :per]
            row = jnp.sum(jnp.where(pack_rows == rel_row, value[PACK // 2 :], 0.0), axis=0)[None]
            own_rel[...] = pltpu.roll(
                jnp.broadcast_to(row, (8, LANES)), (LANES - rel_lane) % LANES, 1
            )[:1, :rel_per]
        elif unit.owner == 6:
            for at in range(start, start + size, LANES):
                spot, rest = at // CHUNK, at % CHUNK
                to = (spot % 2) * hidden_width + (spot // 2) * CHUNK + rest
                owned[5][:, to : to + LANES] = value[:, at - start : at - start + LANES]
        elif unit.owner == 7:
            kept = min(value.shape[0], owned[6].shape[0] - unit.row)
            owned[6][unit.row : unit.row + kept, start_lane : start_lane + size] = value[:kept]
        else:
            owned[unit.owner - 1][:, start : start + size] = value

    scatter = Driver(
        back_units,
        scatter_stages(place, back_units, whole_slots, arrived, rings, finish, wires),
        1.0,
    )

    def weight_grad(u, name, right):
        size = back_units[u].shape[1]
        left = encoder_rows(first_free) if name == "encoder" else vmem[name][...]
        block = low(mul(left, right, 0, 0))
        whole_slots[u % whole_slots.shape[0], :, :, :, :, :, 0:size] = block.reshape(
            sizes + (-1, size)
        )

    def activate(spot, gate_up, grad_hidden, chunk):
        gate = gate_up[:, 2 * chunk * CHUNK : (2 * chunk + 1) * CHUNK]
        up = gate_up[:, (2 * chunk + 1) * CHUNK : (2 * chunk + 2) * CHUNK]
        grad = grad_hidden[:, chunk * CHUNK : (chunk + 1) * CHUNK]
        square = gate * gate
        curve = jnp.tanh(0.7978845608028654 * gate * (1.0 + 0.044715 * square))
        half = 0.5 * (1.0 + curve)
        gelu = gate * half
        slope = half + 0.5 * gate * (1.0 - curve * curve) * (
            0.7978845608028654 * (1.0 + 3 * 0.044715 * square)
        )
        hidden, grads = vmem["hidden"], vmem["grad_gate_up"]
        hidden[spot, :, chunk * CHUNK : (chunk + 1) * CHUNK] = low(gelu * up)
        grads[spot, :, 2 * chunk * CHUNK : (2 * chunk + 1) * CHUNK] = low(grad * up * slope)
        grads[spot, :, (2 * chunk + 1) * CHUNK : (2 * chunk + 2) * CHUNK] = low(grad * gelu)

    steps = sum(unit.owner == 6 for unit in back_units)
    for spot in range(steps):
        unit = back_units[spot]
        size = unit.shape[1]
        matrix = weight()
        groups_at = slice(unit.start // 16, (unit.start + size) // 16)
        down = low(wide(down_rows[groups_at]).reshape(size // 2, width))
        gate_up = mul(vmem["normed_ffn"][...], matrix())
        grad_hidden = mul(vmem["branch"][...], down, 1, 1)
        for chunk in range(size // (2 * CHUNK)):
            activate(spot, gate_up, grad_hidden, chunk)
        spent(4.0)
        vmem["grad_normed"][...] += mul(vmem["grad_gate_up"][spot, :, 0:size], matrix(), 1, 1)
        release()
        outcome[...] += mul(vmem["hidden"][spot, :, 0 : size // 2], down)
        spent(4.0)
        weight_grad(spot, "normed_ffn", vmem["grad_gate_up"][spot, :, 0:size])
        scatter.advance()
    while not driver.done():
        driver.advance()
    pump()
    outcome_copy = pltpu.make_async_copy(outcome, outcome_out, out_sems.at[2])
    outcome_copy.start()
    reads = read_inputs(first_free, 1)

    def norm_back(which, stream, before, last):
        gain = vmem["gains"][which : which + 1]
        step_rows = 64

        def body(step, total):
            at = pl.ds(pl.multiple_of(step * step_rows, step_rows), step_rows)
            value = wide(stream[at, :])
            scale = lax.rsqrt(jnp.mean(value * value, axis=-1, keepdims=True) + 1e-06)
            unit = value * scale
            grad = vmem["grad_normed"][at, :]
            scaled = grad * gain
            result = wide(before[at, :]) + scale * (
                scaled - unit * jnp.mean(scaled * unit, axis=-1, keepdims=True)
            )
            dx[at, :] = result
            if not last:
                rounded[2 - which, at, :] = low(result)
            return total + jnp.sum(grad * unit, axis=0, keepdims=True)

        total = lax.fori_loop(0, rows // step_rows, body, jnp.zeros((1, width), jnp.float32))
        gain_grads[which : which + 1, :] = total

    def through(source, target, add, rounding):
        value = mul(source[...], weight()(), 1, 1)
        if add:
            value = value + target[...]
        target[...] = low(value) if rounding else value
        release()

    left = lax.broadcasted_iota(jnp.int32, (1, LANES), 1) < HEAD

    def stack(value):
        zero = jnp.zeros_like(value)
        return jnp.concatenate([jnp.where(left, value, zero), jnp.where(left, zero, value)], axis=0)

    def pair_back(queries, keys, values, probs, grad):
        count = queries.shape[0]
        stacked = stack(grad)
        spread = mul(stacked, values, 1, 1)
        wide_probs = wide(probs)
        product = wide_probs * spread
        scores = low(product - wide_probs * jnp.sum(product, axis=-1, keepdims=True))
        grad_values = low(mul(probs, stacked, 0, 0))
        both = mul(scores, keys)
        grad_queries = low(jnp.where(left, both[:count], both[count:]) * HEAD ** (-0.5))
        grad_keys = low(mul(scores, stack(queries * jnp.bfloat16(HEAD ** (-0.5))), 0, 0))
        return grad_queries, grad_keys, grad_values, scores

    def cross_back(pair):
        if pair + 1 < count_pairs:
            probs_copy(0, pair + 1, False).start()
        probs_copy(0, pair, False).wait()
        lanes = pl.ds(pair * LANES, LANES)

        def body(sequence, carry):
            at = pl.ds(pl.multiple_of(sequence * slot_rows, slot_rows), slot_rows)
            keys = pl.ds(pl.multiple_of(sequence * enc_rows, enc_rows), enc_rows)
            queries, pairs = vmem["queries"], vmem["pairs"]
            grads = pair_back(
                queries[at, lanes],
                pairs[0, keys, lanes],
                pairs[1, keys, lanes],
                probs_slots[0][pair % 2, sequence],
                grad_mixed[at, lanes],
            )
            queries[at, lanes], pairs[0, keys, lanes], pairs[1, keys, lanes] = grads[:3]
            return carry

        lax.fori_loop(0, seqs, body, 0)

    def self_back(pair):
        if pair + 1 < count_pairs:
            probs_copy(1, pair + 1, False).start()
        probs_copy(1, pair, False).wait()
        lanes = pl.ds(pair * LANES, LANES)
        total = 0.0
        for sequence in range(seqs):
            at = pl.ds(sequence * slot_rows, slot_rows)
            qkv = vmem["qkv"]
            grads = pair_back(
                qkv[0, at, lanes],
                qkv[1, at, lanes],
                qkv[2, at, lanes],
                probs_slots[1][pair % 2, sequence],
                grad_mixed[at, lanes],
            )
            qkv[0, at, lanes], qkv[1, at, lanes], qkv[2, at, lanes] = grads[:3]
            total = total + wide(grads[3])
        total = jnp.concatenate(
            [total, jnp.zeros((total.shape[0], period - slot_rows), jnp.float32)], axis=1
        )
        for head in range(2):
            sums = 0.0
            for group in range(slot_rows // 8):
                start = head * slot_rows + group * 8
                piece = total[start : start + 8]
                sums = sums + (pltpu.roll(piece, period - group * 8, 1) if group else piece)
            diag[2 * pair + head] = sums

    grad_mixed = vmem["normed_ffn"]
    chain, marks = [], {6: 0, 7: 0}

    def then(cost, step):
        chain.append((cost, step))

    def start_ffn():
        outcome_copy.wait()
        norm_back(2, vmem["third"], vmem["branch"], False)

    def start_cross():
        probs_copy(0, 0, False).start()
        through(rounded.at[0], grad_mixed, False, True)

    def encoder_back():
        keys, values = weight(), weight()
        stage = vmem["third"]
        for sequence in range(seqs):
            at = slice(sequence * enc_rows, (sequence + 1) * enc_rows)
            copy = pltpu.make_async_copy(
                stage.at[0:enc_rows], grad_encoder.at[at], out_sems.at[0]
            )
            if sequence:
                copy.wait()
            pairs = vmem["pairs"]
            stage[0:enc_rows] = mul(pairs[0, at], keys(), 1, 1) + mul(pairs[1, at], values(), 1, 1)
            copy.start()
        release()
        release()

    def end_cross():
        through(vmem["queries"], vmem["grad_normed"], False, False)

    def start_self():
        norm_back(1, vmem["second"], dx, False)

    def self_mixed():
        probs_copy(1, 0, False).start()
        through(rounded.at[1], grad_mixed, False, True)

    def self_normed(part):
        through(vmem["qkv"].at[part], vmem["grad_normed"], part > 0, False)

    def end_self():
        reads[0].wait()
        norm_back(0, shared.at[first_free], dx, True)
        pltpu.make_async_copy(dx, grad_tokens, out_sems.at[1]).start()

    then(1.5, start_ffn)
    marks[5] = len(chain)
    then(1.2, start_cross)
    for pair in range(count_pairs):
        then(0.8, functools.partial(cross_back, pair))
    marks[2] = marks[4] = len(chain)
    then(4.5, encoder_back)
    then(1.2, end_cross)
    then(1.5, start_self)
    marks[3] = len(chain)
    then(1.2, self_mixed)
    for pair in range(count_pairs):
        then(0.8, functools.partial(self_back, pair))
    marks[1] = len(chain)
    for part in range(3):
        then(1.2, functools.partial(self_normed, part))
    then(1.5, end_self)
    marks[0] = len(chain)

    def pack_grad(u):
        slot = u % whole_slots.shape[0]
        table = 0.0
        for row in range(8):
            part = diag[:, row, :]
            table = table + (pltpu.roll(part, period - row, 1) if row else part)
        high = low(table)
        rel = mul(high, spread[...], 1, 1) + mul(low(table - wide(high)), spread[...], 1, 1)
        for z in range(sizes[0]):
            for y in range(sizes[1]):
                at = slice((z * sizes[1] + y) * LANES, (z * sizes[1] + y + 1) * LANES)
                top = jnp.concatenate(
                    [gain_grads[:, at], jnp.zeros((PACK // 2 - norms, LANES), jnp.float32)], axis=0
                )
                tile = low(jnp.concatenate([top, rel], axis=0))
                for x in range(sizes[2]):
                    for core in range(sizes[3]):
                        whole_slots[slot, z, y, x, core, :, 0:LANES] = tile

    groups = owned[6].shape[0] // 8

    def down_piece(spot):
        size = vmem["hidden"].shape[2]
        size = min(size, hidden_width - spot * size)
        start = spot * vmem["hidden"].shape[2] // 8
        block = mul(vmem["hidden"][spot, :, 0:size], vmem["branch"][...], 0, 0)
        down_rows[start : start + size // 8] = low(block.reshape(size // 8, 8, width))

    def down_grad(u):
        slot = u % whole_slots.shape[0]
        start = back_units[u].row // 8

        block_rows = whole_slots.shape[5]

        def body(device, carry):
            piece = down_rows[pl.ds(device * groups + start, block_rows // 8)]
            c, rest = device % sizes[3], device // sizes[3]
            x, rest = rest % sizes[2], rest // sizes[2]
            whole_slots[slot, rest // sizes[1], rest % sizes[1], x, c, :, :] = low(
                wide(piece).reshape(block_rows, width)
            )
            return carry

        lax.fori_loop(0, sizes[0] * sizes[1] * sizes[2] * sizes[3], body, 0)

    def grad_of(u):
        unit = back_units[u]
        owner = unit.owner
        part = unit.start // width
        if owner == 7:
            if unit.row == 0:
                for spot in range(vmem["hidden"].shape[0]):
                    down_piece(spot)
            down_grad(u)
        elif owner == 5:
            weight_grad(u, "mixed_cross", rounded[0])
        elif owner == 2:
            if part == 0:
                for copy in reads[1:]:
                    copy.wait()
            weight_grad(u, "encoder", vmem["pairs"][part])
        elif owner == 4:
            weight_grad(u, "normed_cross", vmem["queries"][...])
        elif owner == 3:
            weight_grad(u, "mixed_self", rounded[1])
        elif owner == 1:
            lane = unit.start % width
            weight_grad(u, "normed_self", vmem["qkv"][part, :, lane : lane + unit.shape[1]])
        else:
            pack_grad(u)

    position = 0
    budget = 2.0
    for u in range(steps, len(back_units)):
        owner = back_units[u].owner
        while position < marks[owner]:
            chain[position][1]()
            position += 1
        grad_of(u)
        scatter.advance()
        used = 0.0
        while position < len(chain) and used < budget:
            used += chain[position][0]
            chain[position][1]()
            position += 1
    while not scatter.done():
        scatter.advance()
    pltpu.make_async_copy(
        vmem["third"].at[0:enc_rows], grad_encoder.at[0:enc_rows], out_sems.at[0]
    ).wait()
    pltpu.make_async_copy(dx, grad_tokens, out_sems.at[1]).wait()
    for copy in leaving:
        copy.wait()
    gather_wires.finish()


def layer_all(place, shards, norm_gains, rel_bias, data):
    tokens, encoder, cotangent, lengths, enc_lengths, bucket_ids = data
    blocks = [(PACK, LANES)] + [shard.shape for shard in shards]
    sizes = place.sizes
    seqs, slot_rows, width = tokens.shape
    rows, enc_rows = seqs * slot_rows, encoder.shape[1]
    block_rows = blocks[1][0]
    down_rows = blocks[7][0] * 8
    gathered = blocks[:3] + [(block_rows, 3 * width)] + blocks[6:]
    units = make_units(gathered, ORDER, GATHER_WIDTHS)
    back_units = []
    for owner in BACK_ORDER:
        if owner == 7:
            for row in range(0, down_rows, block_rows):
                unit = Unit(7, (block_rows, width), 0, width, len(back_units) % 4)
                unit.row = row
                back_units.append(unit)
        else:
            back_units += make_units(blocks, (owner,), SCATTER_WIDTHS, len(back_units))
    devices = sizes[0] * sizes[1] * sizes[2] * sizes[3]
    piece = PIECE // block_rows
    rings = ring_shapes(place, block_rows, piece)
    low_type, wide_type = jnp.bfloat16, jnp.float32
    steps = sum(unit.owner == 6 for unit in back_units)
    shapes = {
        "branch": ((rows, width), low_type),
        "normed_self": ((rows, width), low_type),
        "qkv": ((3, rows, width), low_type),
        "mixed_self": ((rows, width), low_type),
        "second": ((rows, width), wide_type),
        "normed_cross": ((rows, width), low_type),
        "queries": ((rows, width), low_type),
        "pairs": ((2, seqs * enc_rows, width), low_type),
        "mixed_cross": ((rows, width), low_type),
        "third": ((rows, width), wide_type),
        "normed_ffn": ((rows, width), low_type),
        "hidden": ((steps, rows, piece // 2), low_type),
        "grad_gate_up": ((steps, rows, piece), low_type),
        "grad_normed": ((rows, width), wide_type),
        "gains": ((norm_gains.shape[0], width), wide_type),
    }
    owned = [(block[0], block[1]) for block in blocks[1:7]] + [(down_rows, width)]
    pair_shapes = [(seqs, 2 * slot_rows, enc_rows), (seqs, 2 * slot_rows, slot_rows)]
    anywhere = pl.BlockSpec(memory_space=pl.ANY)
    inside = pl.BlockSpec(memory_space=pltpu.VMEM)
    scalars = pl.BlockSpec(memory_space=pltpu.SMEM)
    sends, returns = copies_of(units, sizes), copies_of(back_units, sizes)
    local = len(units) + 3 + blocks[6][1] // CHUNK
    depth = 3
    shaped = jax.ShapeDtypeStruct
    results = pl.pallas_call(
        functools.partial(
            layer_kernel, place, units, back_units, len(gathered), seqs, tuple(rings)
        ),
        out_shape=[shaped(sizes + block, low_type) for block in gathered]
        + [shaped((rows, width), wide_type)] * 2
        + [shaped((seqs * enc_rows, width), wide_type)]
        + [shaped((width // LANES,) + shape, low_type) for shape in pair_shapes]
        + [shaped(block, wide_type) for block in owned]
        + [shaped(norm_gains.shape, wide_type), shaped((1, rel_bias.shape[0]), wide_type)],
        in_specs=[anywhere] * (len(blocks) - 1)
        + [inside] * 2
        + [anywhere] * 3
        + [scalars] * 2
        + [inside],
        out_specs=[anywhere] * (len(gathered) + 5 + len(owned)) + [inside] * 2,
        scratch_shapes=[pltpu.VMEM(block, wide_type) for block in owned]
        + [pltpu.VMEM(*shapes[name]) for name in BUFFERS]
        + [pltpu.VMEM((2,) + shape, low_type) for shape in pair_shapes]
        + [
            pltpu.VMEM((rows, width), wide_type),
            pltpu.VMEM((devices * blocks[7][0] + 8, 8, width), low_type),
            pltpu.VMEM((HEADS, 8, 2 * slot_rows), wide_type),
            pltpu.VMEM((norm_gains.shape[0], width), wide_type),
            pltpu.VMEM((PACK, LANES), low_type),
            pltpu.VMEM(sizes + (PACK, LANES), low_type),
            pltpu.VMEM((LANES, 2 * slot_rows), low_type),
            pltpu.VMEM((HEADS, 2 * slot_rows), wide_type),
            pltpu.VMEM((depth,) + sizes + (block_rows, piece), low_type),
            pltpu.VMEM((2,) + sizes + (block_rows, piece), low_type),
            pltpu.VMEM((RING + 1,) + sizes[:3] + (block_rows, piece), low_type),
        ]
        + [pltpu.VMEM(shape, low_type) for shape in rings.values()]
        + [
            pltpu.SemaphoreType.DMA((number,))
            for number in (sends, sends, returns, returns, local, depth + 2, 2 + seqs * enc_rows // rows, 4, 10)
        ],
        compiler_params=pltpu.CompilerParams(
            collective_id=0, has_side_effects=True, vmem_limit_bytes=63 * 2**20
        ),
        name="layer_all",
    )(
        *shards,
        norm_gains,
        rel_bias.reshape(1, -1),
        tokens.reshape(rows, width),
        encoder.reshape(-1, width),
        cotangent.reshape(rows, width),
        lengths,
        enc_lengths,
        bucket_ids.reshape(1, -1),
    )
    return results[len(gathered) :]


def norm_scale(stream, gain):
    return stream * lax.rsqrt(jnp.mean(stream * stream, axis=-1, keepdims=True) + 1e-06) * gain


def gelu_tanh(values):
    return (
        0.5
        * values
        * (1.0 + jnp.tanh(0.7978845608028654 * (values + 0.044715 * values * values * values)))
    )


def gated(gate_up):
    half_width = gate_up.shape[1] // 2
    return gelu_tanh(gate_up[:, :half_width]) * gate_up[:, half_width:]


def product(spec, left, right):
    return jnp.einsum(spec, left, right, preferred_element_type=jnp.float32)


def attend(queries, key_rows, value_rows, pos_bias, keep_mask):
    scores = product("bihc,bjhc->bhij", queries, key_rows) * HEAD ** (-0.5)
    if pos_bias is not None:
        scores = scores + pos_bias
    masked = jnp.where(keep_mask[:, None], scores, -1e30)
    row_max = jnp.max(masked, axis=-1, keepdims=True)
    powers = jnp.exp(masked - row_max)
    probs = powers / jnp.sum(powers, axis=-1, keepdims=True)
    low_probs = probs.astype(jnp.bfloat16)
    mixed = product("bhij,bjhc->bihc", low_probs, value_rows)
    return mixed.astype(jnp.bfloat16), low_probs


def attend_back(queries, key_rows, value_rows, low_probs, grad_mixed):
    probs = low_probs.astype(jnp.float32)
    grad_values = product("bhij,bihc->bjhc", low_probs, grad_mixed)
    grad_probs = product("bihc,bjhc->bhij", grad_mixed, value_rows)
    grad_scores = (
        probs * (grad_probs - jnp.sum(probs * grad_probs, axis=-1, keepdims=True))
    ).astype(jnp.bfloat16)
    grad_queries = product("bhij,bjhc->bihc", grad_scores, key_rows) * HEAD ** (-0.5)
    grad_keys = product("bhij,bihc->bjhc", grad_scores, queries) * HEAD ** (-0.5)
    return grad_queries, grad_keys, grad_values, grad_scores


def toeplitz(table, size):
    lead = table.shape[:-1]
    row = jnp.concatenate(
        [table[..., ::-1], jnp.broadcast_to(table[..., :1], lead + (size,))], axis=-1
    )
    tiled = jnp.broadcast_to(row[..., None, :], lead + (size, 2 * size)).reshape(lead + (-1,))
    tiled = jnp.concatenate([tiled[..., size - 1 :], row[..., :1]], axis=-1)
    tiled = tiled[..., : size * (2 * size - 1)]
    return tiled.reshape(lead + (size, 2 * size - 1))[..., :size]


def layer(weights, gains, rel_bias, tokens, encoder, cotangent, lengths, enc_lengths, bucket_ids):
    self_qkv, self_out, cross_q, cross_kv, cross_out, ff_in, ff_out = weights
    count, slots, width = tokens.shape
    enc_count = encoder.shape[1]
    bucket_map = toeplitz(bucket_ids, slots).reshape(-1)
    onehot = (lax.iota(jnp.int32, BUCKETS)[:, None] == bucket_map[None, :]).astype(jnp.bfloat16)
    pos_bias = jnp.dot(rel_bias, onehot, preferred_element_type=jnp.float32).reshape(
        HEADS, slots, slots
    )
    row_ids = lax.iota(jnp.int32, slots)
    self_mask = (row_ids[None, None, :] <= row_ids[None, :, None]) & (
        row_ids[None, None, :] < lengths[:, None, None]
    )
    cross_mask = lax.iota(jnp.int32, enc_count)[None, None, :] < enc_lengths[:, None, None]
    enc_rows = encoder.reshape(count * enc_count, width)
    dot = functools.partial(jnp.dot, preferred_element_type=jnp.float32)
    low = lambda value: value.astype(jnp.bfloat16)
    stream = tokens.reshape(count * slots, width).astype(jnp.float32)
    normed_self, back_self = jax.vjp(norm_scale, stream, gains[0])
    normed_self = low(normed_self)
    qkv = low(dot(normed_self, self_qkv)).reshape(count, slots, 3, HEADS, HEAD)
    mixed_self, probs_self = attend(qkv[:, :, 0], qkv[:, :, 1], qkv[:, :, 2], pos_bias, self_mask)
    mixed_self = mixed_self.reshape(count * slots, width)
    second = stream + dot(mixed_self, self_out)
    normed_cross, back_cross = jax.vjp(norm_scale, second, gains[1])
    normed_cross = low(normed_cross)
    queries = low(dot(normed_cross, cross_q)).reshape(count, slots, HEADS, HEAD)
    pairs = low(dot(enc_rows, cross_kv)).reshape(count, enc_count, 2, HEADS, HEAD)
    mixed_cross, probs_cross = attend(queries, pairs[:, :, 0], pairs[:, :, 1], None, cross_mask)
    mixed_cross = mixed_cross.reshape(count * slots, width)
    third = second + dot(mixed_cross, cross_out)
    normed_ffn, back_ffn = jax.vjp(norm_scale, third, gains[2])
    normed_ffn = low(normed_ffn)
    gate_up = dot(normed_ffn, ff_in)
    activated, back_gate = jax.vjp(gated, gate_up)
    hidden = low(activated)
    outcome = third + dot(hidden, ff_out)

    valid = (row_ids[None, :] < lengths[:, None]).astype(jnp.float32)[:, :, None]
    grad_out = (cotangent.astype(jnp.float32) * valid).reshape(count * slots, width)
    branch = low(grad_out)
    grad_ff_out = product("lf,ld->fd", hidden, branch)
    grad_hidden = product("ld,fd->lf", branch, ff_out)
    (grad_gate_up,) = back_gate(grad_hidden)
    grad_gate_up = low(grad_gate_up)
    grad_ff_in = product("ld,lf->df", normed_ffn, grad_gate_up)
    grad_stream, gain_ffn = back_ffn(product("lf,df->ld", grad_gate_up, ff_in))
    grad_third = grad_out + grad_stream
    branch = low(grad_third)
    grad_cross_out = product("le,ld->ed", mixed_cross, branch)
    grad_mixed = low(product("ld,ed->le", branch, cross_out)).reshape(count, slots, HEADS, HEAD)
    grad_queries, grad_keys, grad_values, unused = attend_back(
        queries, pairs[:, :, 0], pairs[:, :, 1], probs_cross, grad_mixed
    )
    grad_query_rows = low(grad_queries.reshape(count * slots, width))
    grad_pair_rows = low(
        jnp.concatenate(
            [
                grad_keys.reshape(count * enc_count, width),
                grad_values.reshape(count * enc_count, width),
            ],
            axis=1,
        )
    )
    grad_cross_q = product("ld,le->de", normed_cross, grad_query_rows)
    grad_cross_kv = product("ed,ef->df", enc_rows, grad_pair_rows)
    grad_enc = product("ef,df->ed", grad_pair_rows, cross_kv)
    grad_stream, gain_cross = back_cross(product("le,de->ld", grad_query_rows, cross_q))
    grad_second = grad_third + grad_stream
    branch = low(grad_second)
    grad_self_out = product("le,ld->ed", mixed_self, branch)
    grad_mixed = low(product("ld,ed->le", branch, self_out)).reshape(count, slots, HEADS, HEAD)
    grad_queries, grad_keys, grad_values, grad_scores = attend_back(
        qkv[:, :, 0], qkv[:, :, 1], qkv[:, :, 2], probs_self, grad_mixed
    )
    score_sums = jnp.sum(grad_scores.astype(jnp.float32), axis=0).reshape(HEADS, slots * slots)
    grad_rel_bias = product("hn,bn->hb", low(score_sums), onehot)
    grad_qkv = low(
        jnp.concatenate(
            [part.reshape(count * slots, width) for part in (grad_queries, grad_keys, grad_values)],
            axis=1,
        )
    )
    grad_self_qkv = product("ld,lf->df", normed_self, grad_qkv)
    grad_stream, gain_self = back_self(product("lf,df->ld", grad_qkv, self_qkv))
    grad_tok = grad_second + grad_stream
    grad_gains = jnp.stack([gain_self, gain_cross, gain_ffn], axis=0)
    grads = (
        grad_self_qkv,
        grad_self_out,
        grad_cross_q,
        grad_cross_kv,
        grad_cross_out,
        grad_ff_in,
        grad_ff_out,
    )
    return (
        outcome.reshape(tokens.shape),
        grad_tok.reshape(tokens.shape),
        grad_enc.reshape(encoder.shape),
        grads,
        grad_gains,
        grad_rel_bias,
    )


AXES = ("dp", "fsdp")


def by_collectives(data, shards):
    whole = lambda shard, axis=0: lax.all_gather(shard, AXES, axis=axis, tiled=True)
    weights = tuple(whole(shard) for shard in shards[:7])
    gains = whole(shards[7], 1).astype(jnp.float32)
    rel_bias = whole(shards[8]).reshape(HEADS, BUCKETS)
    outcome, grad_tok, grad_enc, grads, grad_gains, grad_rel_bias = layer(
        weights, gains, rel_bias, *data
    )
    settle = lambda total, axis=0: lax.psum_scatter(
        total, AXES, scatter_dimension=axis, tiled=True
    )
    return (
        (outcome, grad_tok, grad_enc)
        + tuple(settle(grad) for grad in grads)
        + (settle(grad_gains, 1), settle(grad_rel_bias.reshape(-1)))
    )


def by_kernels(place, data, shards):
    self_qkv, self_out, cross_q, cross_kv, cross_out, ff_in, ff_out = shards[:7]
    ff_rows, width = ff_out.shape
    sent = (self_qkv, cross_kv, self_out, cross_q, cross_out, ff_in)
    sent += (ff_out.reshape(ff_rows // 8, 8, width),)
    results = layer_all(place, sent, shards[7], shards[8], data)
    outcome, grad_tok, grad_enc = (
        result.reshape(like.shape)
        for result, like in zip(results[:3], (data[0], data[0], data[1]))
    )
    g_qkv, g_kv, g_so, g_cq, g_co, g_in, g_out = results[5:12]
    owned = (g_qkv, g_so, g_cq, g_kv, g_co, g_in, g_out)
    return (outcome, grad_tok, grad_enc) + owned + (results[12], results[13].reshape(-1))


def on_device(place, *args):
    data, shards = args[:6], args[6:]
    per = shards[7].shape[1]
    regular = all(shard.shape[0] % 16 == 0 for shard in shards[:6])
    group = place.sizes[2] * place.sizes[3]
    seqs, slots, enc_slots = args[0].shape[0], args[0].shape[1], args[1].shape[1]
    regular = regular and enc_slots <= seqs * slots and seqs * enc_slots % (seqs * slots) == 0
    if regular and shards[6].shape[0] % 8 == 0 and group * per == LANES:
        return by_kernels(place, data, shards)
    return by_collectives(data, shards)


def solution(mesh):
    rows = P(AXES, None, None)
    flat = P(AXES)
    matrix = P(AXES, None)
    split = P(None, AXES)
    place = Place(mesh.shape["dp"], mesh.shape["fsdp"])
    return jax.shard_map(
        functools.partial(on_device, place),
        mesh=mesh,
        in_specs=(rows, rows, rows, flat, flat, P()) + (matrix,) * 7 + (split, flat),
        out_specs=(rows, rows, rows) + (matrix,) * 7 + (split, flat),
        check_vma=False,
    )
```
